128 devices in a mesh: wide: 64 (over z, y, x_hi, core), narrow: 2 (over x_lo).
Axes of the slice: x: 4 (x_hi: 2, x_lo: 2; x = x_hi * 2 + x_lo), y: 4, z: 4, core: 2. Of those that a mesh axis runs over, the one named last changes fastest.
Arguments:
- layer_in: bfloat16 [8192, 1536], P('wide'), may hold values from -16 to 16
- lengths: int32 [4], replicated, may hold values from 1 to 8127, as said below
- norm_attn: float32 [1536], replicated, may hold values from 0.1 to 1.9
- w_qkv: bfloat16 [1536, 2048], P(None, 'narrow'), may hold values from -0.15625 to 0.15625
- qkv_bias: float32 [2, 1024], P('narrow'), may hold values from -3 to 3
- w_out: bfloat16 [1536, 1536], P('narrow'), may hold values from -4 to 4
- norm_mlp: float32 [1536], replicated, may hold values from 0.1 to 1.9
- w_gate: bfloat16 [1536, 8960], P(None, 'narrow'), may hold values from -0.15625 to 0.15625
- w_up: bfloat16 [1536, 8960], P(None, 'narrow'), may hold values from -0.15625 to 0.15625
- w_down: bfloat16 [8960, 1536], P('narrow'), may hold values from -0.0625 to 0.0625
- out_grad: bfloat16 [8192, 1536], P('wide'), may hold values from -16 to 16
Outputs:
- layer_out: bfloat16 [8192, 1536], P('wide')
- in_grad: bfloat16 [8192, 1536], P('wide')
- grad_norm_attn: float32 [1536], P('wide')
- grad_qkv: float32 [1536, 2048], P('wide', 'narrow')
- grad_bias: float32 [2, 7, 128], P('narrow', None, 'wide')
- grad_value_bias: float32 [2, 128], P('narrow', 'wide')
- grad_out: float32 [1536, 1536], P('narrow', 'wide')
- grad_norm_mlp: float32 [1536], P('wide')
- grad_gate: float32 [1536, 8960], P('wide', 'narrow')
- grad_up: float32 [1536, 8960], P('wide', 'narrow')
- grad_down: float32 [8960, 1536], P('narrow', 'wide')
The draws below stay inside these ranges and needn't reach their ends.
Inputs may be any that keep to these rules, and one draw needn't show every extreme that they name: 4 sequences packed one after another; their lengths sum to 8192; one of them, which one is drawn, reaches from the first token shard of wide to the last.
All inputs are finite; a program needn't handle non-finite values.
Results may differ from the reference program's by a relative error of at most 0.022.
Values may be sent and summed in bfloat16 or wider, within the bound.
A program may use at most 384 MiB of HBM per device.

```python
import math
import jax
import jax.numpy as jnp
from jax import lax

D = 1536
FF = 8960
HD = 128
QH = 12
KVH = 2
TOK_DEV = 128
SEQS = 4
TOKENS = 8192
GW = 1024
QKV = 2048


def draw_lengths(key, part):
    key = jax.random.fold_in(key, 11)
    key_pair, key_pick, key_order = jax.random.split(key, 3)
    middle = TOK_DEV // SEQS
    pair_count = (SEQS - 1) // 2
    paired = jax.random.randint(key_pair, (max(pair_count, 1),), 1, 2 * middle, dtype=jnp.int32)
    chosen = jax.random.randint(key_pick, (), 0, SEQS, dtype=jnp.int32)
    seq_index = jnp.arange(SEQS, dtype=jnp.int32)
    shuffled = jax.random.permutation(key_order, SEQS - 1).astype(jnp.int32)
    rank = seq_index - (seq_index > chosen).astype(jnp.int32)
    rank = jnp.clip(rank, 0, SEQS - 2)
    slot = jnp.take(shuffled, rank)
    pair_slot = jnp.clip(slot // 2, 0, max(pair_count, 1) - 1)
    pair_value = jnp.take(paired, pair_slot)
    short = jnp.where(slot % 2 == 0, pair_value, 2 * middle - pair_value)
    short = jnp.where(slot >= 2 * pair_count, 1, short).astype(jnp.int32)
    longest = TOKENS - 2 * pair_count * middle - (SEQS - 1) % 2
    return jnp.where(seq_index == chosen, longest, short).astype(jnp.int32)


def spiked(values, key, source, target, blocks, factor):
    def block_of(dim):
        return (jnp.arange(values.shape[dim]) // (values.shape[dim] // blocks)).reshape((-1,) + (1,) * (values.ndim - 1 - dim))

    first = jax.random.permutation(key, blocks)[block_of(target)]
    far = (block_of(target) + blocks // 2) % blocks
    return jnp.where((block_of(source) == first) | (block_of(source) == far), factor * values, values)


def levels(key, shape, pieces, least, largest):
    loudness, own = 1.0, jax.random.fold_in(key, 6)
    for dim, blocks in pieces:
        heights = jnp.exp(jax.random.uniform(jax.random.fold_in(own, dim), (blocks,), jnp.float32, least / len(pieces), largest / len(pieces)))
        loudness = loudness * jnp.repeat(heights, shape[dim] // blocks).reshape([-1 if axis == dim else 1 for axis in range(len(shape))])
    return loudness


def normal_values(rng, dims, spread, bound, pieces=(), kind=jnp.bfloat16):
    level = levels(rng, dims, pieces, -0.22, 0.18) if pieces else 1.0
    entries = jax.random.normal(rng, dims, jnp.float32) * spread * level
    return jnp.minimum(jnp.maximum(entries, -bound), bound).astype(kind)


def noise_with(stream_key, extent, deviation, limit, shards, heavy, held_as=jnp.bfloat16):
    entries = deviation * jax.random.normal(stream_key, extent, jnp.float32)
    if shards:
        entries = entries * levels(stream_key, extent, shards, -0.22, 0.18)
    return jnp.clip(spiked(entries, jax.random.fold_in(stream_key, 3), *heavy), -limit, limit).astype(held_as)


def setup_inputs(seed: int = 0) -> dict:
    keys = jax.random.split(jax.random.key(seed), 12)
    layer_in = noise_with(keys[0], (TOKENS, D), 1.0, 16.0, ((0, 64),), (0, 1, 64, 4.0))
    lengths = draw_lengths(jax.random.fold_in(keys[11], 71), 0)
    norm_attn = jnp.clip(1.0 + 0.18 * jax.random.normal(keys[2], (D,), jnp.float32), 0.1, 1.9)
    w_qkv = normal_values(keys[3], (D, QKV), D ** -0.5, 0.15625, ((1, 2),))
    qkv_bias = normal_values(keys[4], (KVH, GW), 0.5, 3.0, ((0, 2),), jnp.float32)
    w_out = normal_values(keys[5], (QH * HD, D), (max(2, 8 * QH * HD // TOKENS)) ** -0.5, 4.0, ((0, 2),))
    norm_mlp = jnp.clip(1.0 + 0.18 * jax.random.normal(keys[6], (D,), jnp.float32), 0.1, 1.9)
    w_gate = normal_values(keys[7], (D, FF), D ** -0.5, 0.15625, ((1, 2),))
    w_up = normal_values(keys[8], (D, FF), D ** -0.5, 0.15625, ((1, 2),))
    w_down = normal_values(keys[9], (FF, D), FF ** -0.5, 0.0625, ((0, 2),))
    out_grad = noise_with(keys[10], (TOKENS, D), 1.0, 16.0, ((0, 64),), (0, 1, 64, 4.0))
    return {"layer_in": layer_in, "lengths": lengths, "norm_attn": norm_attn, "w_qkv": w_qkv, "qkv_bias": qkv_bias, "w_out": w_out, "norm_mlp": norm_mlp, "w_gate": w_gate, "w_up": w_up, "w_down": w_down, "out_grad": out_grad}


rms_eps = 1e-06
rope_base = 10000.0
big_negative = -1e+30
highest = lax.Precision.HIGHEST

@jax.custom_vjp
def low(v):
    return lax.optimization_barrier(v.astype(jnp.bfloat16)).astype(jnp.float32)

@jax.custom_vjp
def low_back(v):
    return v

def low_keep(v):
    return (low(v), None)

def low_pass(kept, grad):
    return (grad,)

def back_keep(v):
    return (v, None)

def back_low(kept, grad):
    return (low(grad),)
low.defvjp(low_keep, low_pass)
low_back.defvjp(back_keep, back_low)

def row_starts(lengths, token_ids):
    ends = jnp.cumsum(lengths).astype(jnp.int32)
    before = ends[None, :] <= token_ids[:, None]
    return lax.optimization_barrier(jnp.sum(jnp.where(before, lengths[None, :], 0), axis=1)).astype(jnp.int32)

def rope_tables(positions, head_size):
    half_size = head_size // 2
    freqs = rope_base ** (-2.0 * jnp.arange(half_size, dtype=jnp.float32) / head_size)
    angles = positions.astype(jnp.float32)[:, None] * freqs[None, :]
    return (jnp.cos(angles), jnp.sin(angles))

def rotate(values, cosine, sine):
    half_size = values.shape[-1] // 2
    first_half = values[..., :half_size]
    second_half = values[..., half_size:]
    cos_heads = cosine[:, None, :]
    sin_heads = sine[:, None, :]
    return jnp.concatenate([first_half * cos_heads - second_half * sin_heads, second_half * cos_heads + first_half * sin_heads], axis=-1)

def normalize(values):
    return values * lax.rsqrt(lax.optimization_barrier(jnp.mean(values * values, axis=-1, keepdims=True)) + rms_eps)

def forward(layer_in, norm_attn, w_qkv, qkv_bias, w_out, norm_mlp, w_gate, w_up, w_down, token_ids, seq_starts):
    group_heads = QH // KVH
    query_width = group_heads * HD
    act_attn = low(normalize(layer_in) * norm_attn)
    projected = low_back(jnp.dot(act_attn, w_qkv, precision=highest) + qkv_bias.reshape(-1))
    cosine, sine = rope_tables(token_ids - seq_starts, HD)
    grouped = projected.reshape(TOKENS, KVH, GW)
    queries = low(rotate(grouped[:, :, :query_width].reshape(TOKENS, QH, HD), cosine, sine))
    key_heads = low(rotate(grouped[:, :, query_width:query_width + HD], cosine, sine))
    value_heads = low(grouped[:, :, query_width + HD:])
    q_block = math.gcd(512, TOKENS)
    block_count = TOKENS // q_block
    scale = HD ** (-0.5)

    @jax.checkpoint
    def attend(inputs):
        query_rows, query_ids, query_starts = inputs
        grouped_rows = query_rows.reshape(q_block, KVH, group_heads, HD)
        raw = low_back(jnp.einsum('qghd,kgd->ghqk', grouped_rows, key_heads, precision=highest)) * scale
        allowed = (token_ids[None, :] <= query_ids[:, None]) & (token_ids[None, :] >= query_starts[:, None])
        probs = jax.nn.softmax(jnp.where(allowed, raw, big_negative), axis=-1)
        probs_low = low(jnp.where(allowed, probs, 0.0))
        mixed = jnp.einsum('ghqk,kgd->qghd', probs_low, value_heads, precision=highest)
        return mixed.reshape(q_block, QH * HD)
    blocks = lax.map(attend, (queries.reshape(block_count, q_block, QH, HD), token_ids.reshape(block_count, q_block), seq_starts.reshape(block_count, q_block)))
    attn_low = low(low_back(blocks.reshape(TOKENS, QH * HD)))
    attn_out = low_back(jnp.dot(attn_low, w_out, precision=highest))
    resid = layer_in + attn_out
    act_mlp = low(normalize(resid) * norm_mlp)
    gate_proj = low_back(jnp.dot(act_mlp, w_gate, precision=highest))
    up_proj = low_back(jnp.dot(act_mlp, w_up, precision=highest))
    hidden = low(jax.nn.silu(gate_proj) * up_proj)
    return resid + jnp.dot(hidden, w_down, precision=highest)

def reference(layer_in, lengths, norm_attn, w_qkv, qkv_bias, w_out, norm_mlp, w_gate, w_up, w_down, out_grad):
    token_ids = jnp.arange(TOKENS, dtype=jnp.int32)
    seq_starts = row_starts(lengths.astype(jnp.int32), token_ids)
    floats = tuple((array_in.astype(jnp.float32) for array_in in (layer_in, norm_attn, w_qkv, qkv_bias, w_out, norm_mlp, w_gate, w_up, w_down)))

    def layer(*params):
        return forward(*params, token_ids, seq_starts)
    result, pullback = jax.vjp(layer, *floats)
    grads = pullback(out_grad.astype(jnp.float32))
    bias_grid = grads[3].reshape(KVH, QH // KVH + 2, HD)
    return (result.astype(jnp.bfloat16), grads[0].astype(jnp.bfloat16), grads[1], grads[2], bias_grid[:, :QH // KVH + 1], bias_grid[:, QH // KVH + 1], grads[4], grads[5], grads[6], grads[7], grads[8])
```

```python
import functools
import math

import jax
import jax.numpy as jnp
from jax import lax
from jax.experimental import pallas as pl
from jax.experimental.pallas import tpu as pltpu
from jax.sharding import Mesh
from jax.sharding import PartitionSpec as P

HD = 128
QH = 12
KVH = 2
HEADS = QH // KVH
D = 1536
FF = 8960
TOK = 128
TOKENS = 8192
NQ = HEADS * TOK
GROUP = 8
UNITS = FF // 2 // GROUP
OUT_COLS = HEADS * HD // GROUP

AXES = ("z", "y", "xh", "c", "n")
SIZE = {"z": 4, "y": 4, "xh": 2, "c": 2, "n": 2}
WIDE = ("z", "y", "xh", "c")
MESH = pl.DeviceIdType.MESH

rms_eps = 1e-06
rope_base = 10000.0
big_negative = -1e30
SCALE = HD ** (-0.5)
SCALE_LOG2 = SCALE * math.log2(math.e)
KEY_BLOCK = 512
BLOCK_SHARDS = KEY_BLOCK // TOK
Q_CHUNK = 256

bf16 = jnp.bfloat16
f32 = jnp.float32
VMEM = pl.BlockSpec(memory_space=pltpu.VMEM)
SMEM = pl.BlockSpec(memory_space=pltpu.SMEM)
ANY = pl.BlockSpec(memory_space=pl.ANY)


def nn(a, b):
    return lax.dot_general(a, b, (((1,), (0,)), ((), ())), preferred_element_type=f32)


def nt(a, b):
    return lax.dot_general(a, b, (((1,), (1,)), ((), ())), preferred_element_type=f32)


def tn(a, b):
    return lax.dot_general(a, b, (((0,), (0,)), ((), ())), preferred_element_type=f32)


def here():
    return {a: lax.axis_index(a) for a in AXES}


def step(me, axis, by):
    return lax.rem(me[axis] + by, SIZE[axis])


def at(me, **moved):
    return tuple(step(me, a, moved[a]) if a in moved else me[a] for a in AXES)


def greet(peers):
    barrier = pltpu.get_barrier_semaphore()
    for p in peers:
        pl.semaphore_signal(barrier, inc=1, device_id=p, device_id_type=MESH)
    pl.semaphore_wait(barrier, len(peers))


class Copies:
    def __init__(self, send_sems, recv_sems):
        self.send_sems, self.recv_sems, self.used, self.started = send_sems, recv_sems, 0, []

    def make(self, src, dst, target):
        k = self.used
        self.used += 1
        return pltpu.make_async_remote_copy(
            src_ref=src,
            dst_ref=dst,
            send_sem=self.send_sems.at[k],
            recv_sem=self.recv_sems.at[k],
            device_id=target,
            device_id_type=MESH,
        )

    def send(self, src, dst, target):
        copy = self.make(src, dst, target)
        copy.start()
        self.started.append(copy)
        return copy

    def finish(self):
        for copy in self.started:
            copy.wait_send()


def sems(count):
    return [pltpu.SemaphoreType.DMA((count,)), pltpu.SemaphoreType.DMA((count,))]


def params(ident, mib=60):
    return pltpu.CompilerParams(
        collective_id=ident, has_side_effects=True, vmem_limit_bytes=mib * 2**20
    )


def kv_gather_kernel(x, o, send_sems, recv_sems):
    me = here()
    z, y, xh, c = me["z"], me["y"], me["xh"], me["c"]
    partner, across = at(me, c=1), at(me, xh=1)
    ys = {d: at(me, y=d) for d in (1, 2, 3)}
    zs = {d: at(me, z=d) for d in (1, 2, 3)}
    o[z, y, xh, c] = x[...]
    greet([partner, across, *ys.values(), *zs.values()])
    copies = Copies(send_sems, recv_sems)
    mine = o.at[z, y, xh, c]
    first = copies.send(mine, mine, across)
    to_core = [copies.send(mine, mine, partner)]
    first.wait_recv()
    theirs = o.at[z, y, 1 - xh, c]
    to_core.append(copies.send(theirs, theirs, partner))
    half = TOK // 2
    low, high = pl.ds(0, half), pl.ds(half, half)

    def slot(zi, yi, rows):
        return o.at[zi, yi, :, c, rows]

    first_low, first_high = {}, {}
    for d in (1, 3, 2):
        first_low[d] = copies.send(slot(z, y, low), slot(z, y, low), ys[d])
        first_high[d] = copies.send(slot(z, y, high), slot(z, y, high), zs[d])
    second_low, second_high = {}, {}
    for e in (0, 1, 3, 2):
        yi, zi = lax.rem(y + (4 - e), 4), lax.rem(z + (4 - e), 4)
        if e:
            first_low[e].wait_recv()
            to_core.append(copies.send(slot(z, yi, low), slot(z, yi, low), partner))
            first_high[e].wait_recv()
            to_core.append(copies.send(slot(zi, y, high), slot(zi, y, high), partner))
        for d in (1, 3, 2):
            second_low[e, d] = copies.send(slot(z, yi, low), slot(z, yi, low), zs[d])
            second_high[e, d] = copies.send(slot(zi, y, high), slot(zi, y, high), ys[d])
    for e in (0, 1, 3, 2):
        for d in (1, 3, 2):
            yi, zi = lax.rem(y + (4 - e), 4), lax.rem(z + (4 - e), 4)
            yd, zd = lax.rem(y + (4 - d), 4), lax.rem(z + (4 - d), 4)
            second_low[e, d].wait_recv()
            to_core.append(copies.send(slot(zd, yi, low), slot(zd, yi, low), partner))
            second_high[e, d].wait_recv()
            to_core.append(copies.send(slot(zi, yd, high), slot(zi, yd, high), partner))
    for copy in to_core:
        copy.wait_recv()
    copies.finish()


def kv_gather(kv):
    return pl.pallas_call(
        kv_gather_kernel,
        out_shape=jax.ShapeDtypeStruct((4, 4, 2, 2, TOK, 2 * HD), bf16),
        in_specs=[VMEM],
        out_specs=VMEM,
        scratch_shapes=sems(80),
        compiler_params=params(1),
    )(kv)


def kv_reduce_kernel(p, o, cb, s, r1a, r1b, ta, tb, r2a, r2b, u, r3, send_sems, recv_sems):
    me = here()
    z, y, xh, c = me["z"], me["y"], me["xh"], me["c"]
    partner, across = at(me, c=1), at(me, xh=1)
    ys = {d: at(me, y=d) for d in (1, 2, 3)}
    zs = {d: at(me, z=d) for d in (1, 2, 3)}
    greet([partner, across, *ys.values(), *zs.values()])
    copies = Copies(send_sems, recv_sems)
    half = TOK // 2
    low, high = pl.ds(0, half), pl.ds(half, half)
    cores = [
        copies.send(p.at[:, :, :, 1 - c, rows], cb.at[:, :, :, rows], partner)
        for rows in (low, high)
    ]
    first_a, first_b = {}, {}
    cores[0].wait_recv()
    for zi in range(4):
        s[zi, :, :, low] = (p[zi, :, :, c, low].astype(f32) + cb[zi, :, :, low].astype(f32)).astype(bf16)
    for d in (1, 3, 2):
        first_a[d] = copies.send(s.at[step(me, "z", d), :, :, low], r1a.at[d - 1], zs[d])
    cores[1].wait_recv()
    for zi in range(4):
        s[zi, :, :, high] = (p[zi, :, :, c, high].astype(f32) + cb[zi, :, :, high].astype(f32)).astype(bf16)
    for d in (1, 3, 2):
        first_b[d] = copies.send(s.at[:, step(me, "y", d), :, high], r1b.at[d - 1], ys[d])
    for d in (1, 3, 2):
        first_a[d].wait_recv()
    ta[...] = (s[z, :, :, low].astype(f32) + r1a[0].astype(f32) + r1a[1].astype(f32) + r1a[2].astype(f32)).astype(bf16)
    second_a, second_b = {}, {}
    for d in (1, 3, 2):
        second_a[d] = copies.send(ta.at[step(me, "y", d)], r2a.at[d - 1], ys[d])
    for d in (1, 3, 2):
        first_b[d].wait_recv()
    tb[...] = (s[:, y, :, high].astype(f32) + r1b[0].astype(f32) + r1b[1].astype(f32) + r1b[2].astype(f32)).astype(bf16)
    for d in (1, 3, 2):
        second_b[d] = copies.send(tb.at[step(me, "z", d)], r2b.at[d - 1], zs[d])
    for d in (1, 3, 2):
        second_a[d].wait_recv()
        second_b[d].wait_recv()
    ua = ta[y].astype(f32) + r2a[0].astype(f32) + r2a[1].astype(f32) + r2a[2].astype(f32)
    ub = tb[z].astype(f32) + r2b[0].astype(f32) + r2b[1].astype(f32) + r2b[2].astype(f32)
    u[:, low] = ua.astype(bf16)
    u[:, high] = ub.astype(bf16)
    last = copies.send(u.at[1 - xh], r3, across)
    last.wait_recv()
    o[...] = u[xh].astype(f32) + r3[...].astype(f32)
    copies.finish()


def kv_reduce(terms):
    half = TOK // 2
    wide = 2 * HD
    return pl.pallas_call(
        kv_reduce_kernel,
        out_shape=jax.ShapeDtypeStruct((TOK, wide), f32),
        in_specs=[VMEM],
        out_specs=VMEM,
        scratch_shapes=[
            pltpu.VMEM((4, 4, 2, TOK, wide), bf16),
            pltpu.VMEM((4, 4, 2, TOK, wide), bf16),
            pltpu.VMEM((3, 4, 2, half, wide), bf16),
            pltpu.VMEM((3, 4, 2, half, wide), bf16),
            pltpu.VMEM((4, 2, half, wide), bf16),
            pltpu.VMEM((4, 2, half, wide), bf16),
            pltpu.VMEM((3, 2, half, wide), bf16),
            pltpu.VMEM((3, 2, half, wide), bf16),
            pltpu.VMEM((2, TOK, wide), bf16),
            pltpu.VMEM((TOK, wide), bf16),
            *sems(16),
        ],
        compiler_params=params(2),
    )(terms)


def group_gather_kernel(count, *refs):
    xs, os, (send_sems, recv_sems, local_sems) = refs[:count], refs[count : 2 * count], refs[2 * count :]
    me = here()
    y, c = me["y"], me["c"]
    partner = at(me, c=1)
    ys = {d: at(me, y=d) for d in (1, 2, 3)}
    greet([partner, *ys.values()])
    copies = Copies(send_sems, recv_sems)
    arrive, to_core, local = {}, [], []
    for i, (x, o) in enumerate(zip(xs, os)):
        for d in (1, 3, 2):
            arrive[i, d] = copies.send(x, o.at[y, c], ys[d])
        to_core.append(copies.send(x, o.at[y, c], partner))
        local.append(pltpu.make_async_copy(x, o.at[y, c], local_sems.at[i]))
        local[-1].start()
    for i, o in enumerate(os):
        for d in (1, 3, 2):
            arrive[i, d].wait_recv()
            got = o.at[lax.rem(y + (4 - d), 4), c]
            to_core.append(copies.send(got, got, partner))
    for copy in to_core:
        copy.wait_recv()
    for copy in local:
        copy.wait()
    copies.finish()


def group_gather(ident, arrays):
    count = len(arrays)
    return pl.pallas_call(
        functools.partial(group_gather_kernel, count),
        out_shape=[jax.ShapeDtypeStruct((4, 2, *a.shape), a.dtype) for a in arrays],
        in_specs=[ANY] * count,
        out_specs=[ANY] * count,
        scratch_shapes=[*sems(7 * count), pltpu.SemaphoreType.DMA((count,))],
        compiler_params=params(ident),
    )(*arrays)


def group_swap_kernel(count, *refs):
    xs, os, (send_sems, recv_sems, local_sems) = refs[:count], refs[count : 2 * count], refs[2 * count :]
    me = here()
    y, c = me["y"], me["c"]
    moves = [(d, e) for d in (1, 3, 2, 0) for e in (0, 1) if d or e]
    greet([at(me, y=d, c=e) for d, e in moves])
    copies = Copies(send_sems, recv_sems)
    local = []
    for i, (x, o) in enumerate(zip(xs, os)):
        for d, e in moves:
            copies.send(x.at[step(me, "y", d), step(me, "c", e)], o.at[y, c], at(me, y=d, c=e))
        local.append(pltpu.make_async_copy(x.at[y, c], o.at[y, c], local_sems.at[i]))
        local[-1].start()
    for copy in local:
        copy.wait()
    for copy in copies.started:
        copy.wait_recv()
    copies.finish()


def group_swap(ident, arrays):
    count = len(arrays)
    return pl.pallas_call(
        functools.partial(group_swap_kernel, count),
        out_shape=[jax.ShapeDtypeStruct(a.shape, a.dtype) for a in arrays],
        in_specs=[ANY] * count,
        out_specs=[ANY] * count,
        scratch_shapes=[*sems(7 * count), pltpu.SemaphoreType.DMA((count,))],
        compiler_params=params(ident),
    )(*arrays)


def group_reduce_kernel(count, *refs):
    ps, os = refs[:count], refs[count : 2 * count]
    cb, sb, rb, nb, rn, send_sems, recv_sems = refs[2 * count :]
    me = here()
    y, c = me["y"], me["c"]
    partner, other = at(me, c=1), at(me, n=1)
    ys = {d: at(me, y=d) for d in (1, 2, 3)}
    greet([partner, other, *ys.values()])
    copies = Copies(send_sems, recv_sems)
    cores, sent = {}, {}
    for i in range(count):
        for d in (2, 1, 3, 0):
            yi = step(me, "y", d)
            cores[i, d] = copies.send(ps[i].at[yi, 1 - c], cb.at[i, d], partner)
    for i in range(count):
        for d in (2, 1, 3):
            cores[i, d].wait_recv()
            sb[i, d - 1] = (ps[i][step(me, "y", d), c].astype(f32) + cb[i, d].astype(f32)).astype(bf16)
            sent[i, d] = copies.send(sb.at[i, d - 1], rb.at[i, d - 1], ys[d])
    last = []
    for i in range(count):
        cores[i, 0].wait_recv()
        total = ps[i][y, c].astype(f32) + cb[i, 0].astype(f32)
        for d in (1, 3, 2):
            sent[i, d].wait_recv()
            total = total + rb[i, d - 1].astype(f32)
        nb[i] = total.astype(bf16)
        last.append(copies.send(nb.at[i], rn.at[i], other))
    for i in range(count):
        last[i].wait_recv()
        os[i][...] = nb[i].astype(f32) + rn[i].astype(f32)
    copies.finish()


def group_reduce(ident, arrays):
    count = len(arrays)
    return pl.pallas_call(
        functools.partial(group_reduce_kernel, count),
        out_shape=[jax.ShapeDtypeStruct((TOK, D), f32) for _ in arrays],
        in_specs=[VMEM] * count,
        out_specs=[VMEM] * count,
        scratch_shapes=[
            pltpu.VMEM((count, 4, TOK, D), bf16),
            pltpu.VMEM((count, 3, TOK, D), bf16),
            pltpu.VMEM((count, 3, TOK, D), bf16),
            pltpu.VMEM((count, TOK, D), bf16),
            pltpu.VMEM((count, TOK, D), bf16),
            *sems(8 * count),
        ],
        compiler_params=params(ident),
    )(*arrays)


def narrow_sum_kernel(x, o, rn, send_sems, recv_sems):
    me = here()
    other = at(me, n=1)
    greet([other])
    copies = Copies(send_sems, recv_sems)
    copies.send(x, rn, other).wait_recv()
    o[...] = x[...].astype(f32) + rn[...].astype(f32)
    copies.finish()


def narrow_sum(ident, array):
    return pl.pallas_call(
        narrow_sum_kernel,
        out_shape=jax.ShapeDtypeStruct(array.shape, f32),
        in_specs=[VMEM],
        out_specs=VMEM,
        scratch_shapes=[pltpu.VMEM(array.shape, bf16), *sems(1)],
        compiler_params=params(ident),
    )(array)


def weight_reduce_kernel(count, *refs):
    ps, small = refs[:count], refs[count]
    os, small_out = refs[count + 1 : 2 * count + 1], refs[2 * count + 1]
    scratch = refs[2 * count + 2 :]
    r1, s1, r2, t2, r3 = (scratch[k * count : (k + 1) * count] for k in range(5))
    e1, e2, e3, f1, f2, send_sems, recv_sems = scratch[5 * count :]
    me = here()
    z, y, xh, c = me["z"], me["y"], me["xh"], me["c"]
    partner = at(me, c=1)
    zs = {d: at(me, z=d) for d in (1, 2, 3)}
    moves = [(d, e) for d in (1, 3, 2, 0) for e in (0, 1) if d or e]
    near = {m: at(me, y=m[0], xh=m[1]) for m in moves}
    greet([partner, *zs.values(), *near.values()])
    copies = Copies(send_sems, recv_sems)
    first, first_small = {}, {}
    for d in (1, 3, 2):
        first_small[d] = copies.send(small, e1.at[d - 1], zs[d])
    for i in range(count):
        for d in (1, 3, 2):
            first[i, d] = copies.send(ps[i].at[step(me, "z", d)], r1[i].at[d - 1], zs[d])
    for d in (1, 3, 2):
        first_small[d].wait_recv()
    f1[...] = small[...] + e1[0] + e1[1] + e1[2]
    second_small = {m: copies.send(f1, e2.at[k], near[m]) for k, m in enumerate(moves)}
    second = {}
    for i in range(count):
        for d in (1, 3, 2):
            first[i, d].wait_recv()
        for yi in range(4):
            for xi in range(2):
                rows = pl.ds(96 * yi + 48 * xi, 48)
                total = ps[i][z, rows].astype(f32)
                for d in range(3):
                    total = total + r1[i][d, rows].astype(f32)
                s1[i][yi, xi] = total.astype(bf16)
        for m in moves:
            second[i, m] = copies.send(
                s1[i].at[step(me, "y", m[0]), step(me, "xh", m[1])], r2[i].at[y, xh], near[m]
            )
        r2[i][y, xh] = s1[i][y, xh]
    for m in moves:
        second_small[m].wait_recv()
    f2[...] = f1[...]
    for k in range(len(moves)):
        f2[...] = f2[...] + e2[k]
    third_small = copies.send(f2, e3, partner)
    third = []
    keep, give = pl.ds(pl.multiple_of(24 * c, 8), 24), pl.ds(pl.multiple_of(24 * (1 - c), 8), 24)
    for i in range(count):
        for m in moves:
            second[i, m].wait_recv()
        t2[i][...] = r2[i][:, 0].astype(f32) + r2[i][:, 1].astype(f32)
        third.append(copies.send(t2[i].at[:, give], r3[i], partner))
        os[i][:, c] = t2[i][:, keep]
    for i in range(count):
        third[i].wait_recv()
        os[i][:, 1 - c] = r3[i][...]
    third_small.wait_recv()
    small_out[...] = f2[...] + e3[...]
    copies.finish()


def weight_reduce(ident, arrays, small):
    count = len(arrays)
    cols = [a.shape[-1] for a in arrays]
    rows = small.shape[0]
    return pl.pallas_call(
        functools.partial(weight_reduce_kernel, count),
        out_shape=[jax.ShapeDtypeStruct((4, 2, 24, n), f32) for n in cols]
        + [jax.ShapeDtypeStruct(small.shape, f32)],
        in_specs=[VMEM] * (count + 1),
        out_specs=[VMEM] * (count + 1),
        scratch_shapes=[
            *[pltpu.VMEM((3, 384, n), bf16) for n in cols],
            *[pltpu.VMEM((4, 2, 48, n), bf16) for n in cols],
            *[pltpu.VMEM((4, 2, 48, n), bf16) for n in cols],
            *[pltpu.VMEM((4, 48, n), f32) for n in cols],
            *[pltpu.VMEM((4, 24, n), f32) for n in cols],
            pltpu.VMEM((3, rows, D), f32),
            pltpu.VMEM((7, rows, D), f32),
            pltpu.VMEM((rows, D), f32),
            pltpu.VMEM((rows, D), f32),
            pltpu.VMEM((rows, D), f32),
            *sems(11 * (count + 1)),
        ],
        compiler_params=params(ident),
    )(*arrays, small)


def heads_in(ref, scratch):
    for h in range(HEADS):
        scratch[pl.ds(h * TOK, TOK), :] = ref[:, pl.ds(h * HD, HD)]


def attend_kernel(q_in, kv, start, ids, o, exact, lse, q, top, total, acc, low_acc):
    me = here()
    shard = ((me["z"] * 4 + me["y"]) * 2 + me["xh"]) * 2 + me["c"]
    last = shard // BLOCK_SHARDS
    heads_in(q_in, q)
    top[...] = jnp.full_like(top, big_negative)
    total[...] = jnp.zeros_like(total)
    acc[...] = jnp.zeros_like(acc)
    low_acc[...] = jnp.zeros_like(low_acc)

    def block(index, masked):
        offset = pl.multiple_of(index * KEY_BLOCK, KEY_BLOCK)
        rows = pl.ds(offset, KEY_BLOCK)
        keys = kv[rows, pl.ds(0, HD)]
        values = kv[rows, pl.ds(HD, HD)].T
        for chunk in range(NQ // Q_CHUNK):
            cs = pl.ds(chunk * Q_CHUNK, Q_CHUNK)
            scores = nt(keys, q[cs, :]) * SCALE_LOG2
            if masked:
                key_ids = offset + lax.broadcasted_iota(jnp.int32, (KEY_BLOCK, Q_CHUNK), 0)
                allowed = (key_ids >= start[:, cs]) & (key_ids <= ids[:, cs])
                scores = jnp.where(allowed, scores, big_negative)
            old = top[:, cs]
            new = jnp.maximum(old, jnp.max(scores, axis=0, keepdims=True))
            probs = jnp.exp2(scores - new)
            if masked:
                probs = jnp.where(allowed, probs, 0.0)
            fade = jnp.exp2(old - new)
            top[:, cs] = new
            total[:, cs] = total[:, cs] * fade + jnp.sum(probs, axis=0, keepdims=True)
            high = probs.astype(bf16)
            rest = (probs - high.astype(f32)).astype(bf16)
            acc[:, cs] = acc[:, cs] * fade + nn(values, high)
            low_acc[:, cs] = low_acc[:, cs] * fade + nn(values, rest)

    @pl.when(last > 0)
    def _():
        block(0, True)

        @pl.loop(1, last)
        def _(index):
            block(index, False)

        kept = start[...] < last * KEY_BLOCK
        top[...] = jnp.where(kept, top[...], big_negative)
        kept = kept.astype(f32)
        total[...] = total[...] * kept
        acc[...] = acc[...] * kept
        low_acc[...] = low_acc[...] * kept

    block(last, True)
    inverse = 1.0 / total[...]
    rows = acc[...] * inverse
    exact[...] = rows + low_acc[...] * inverse
    rows = rows.T.astype(bf16)
    for h in range(HEADS):
        o[:, pl.ds(h * HD, HD)] = rows[h * TOK : (h + 1) * TOK]
    lse[...] = top[...] + jnp.log2(total[...])


def attend(queries, kv, start, ids):
    return pl.pallas_call(
        attend_kernel,
        out_shape=(
            jax.ShapeDtypeStruct((TOK, HEADS * HD), bf16),
            jax.ShapeDtypeStruct((HD, NQ), f32),
            jax.ShapeDtypeStruct((1, NQ), f32),
        ),
        in_specs=[VMEM] * 4,
        out_specs=(VMEM,) * 3,
        scratch_shapes=[
            pltpu.VMEM((NQ, HD), bf16),
            pltpu.VMEM((1, NQ), f32),
            pltpu.VMEM((1, NQ), f32),
            pltpu.VMEM((HD, NQ), f32),
            pltpu.VMEM((HD, NQ), f32),
        ],
        compiler_params=pltpu.CompilerParams(vmem_limit_bytes=60 * 2**20),
    )(queries, kv, start, ids)


def attend_back_kernel(q_in, kv, g_in, exact, start, ids, lse, dq, dkv, q, g, acc):
    me = here()
    shard = ((me["z"] * 4 + me["y"]) * 2 + me["xh"]) * 2 + me["c"]
    last = shard // BLOCK_SHARDS
    heads_in(q_in, q)
    heads_in(g_in, g)
    balance = jnp.sum(g[...].astype(f32).T * exact[...], axis=0, keepdims=True)
    acc[...] = jnp.zeros_like(acc)
    total = lse[...]
    earlier = jnp.where(start[...] < last * KEY_BLOCK, total, -big_negative)

    def block(index, masked, shift):
        offset = pl.multiple_of(index * KEY_BLOCK, KEY_BLOCK)
        rows = pl.ds(offset, KEY_BLOCK)
        keys, values = kv[rows, pl.ds(0, HD)], kv[rows, pl.ds(HD, HD)]
        keys_t = keys.T
        dk = jnp.zeros((KEY_BLOCK, HD), f32)
        dv = jnp.zeros((KEY_BLOCK, HD), f32)
        for chunk in range(NQ // Q_CHUNK):
            cs = pl.ds(chunk * Q_CHUNK, Q_CHUNK)
            part = slice(chunk * Q_CHUNK, (chunk + 1) * Q_CHUNK)
            qc, gc = q[cs, :], g[cs, :]
            probs = jnp.exp2(nt(keys, qc) * SCALE_LOG2 - shift[:, part])
            if masked:
                key_ids = offset + lax.broadcasted_iota(jnp.int32, (KEY_BLOCK, Q_CHUNK), 0)
                allowed = (key_ids >= start[:, cs]) & (key_ids <= ids[:, cs])
                probs = jnp.where(allowed, probs, 0.0)
            grads = (probs * (nt(values, gc) - balance[:, part])).astype(bf16)
            dv = dv + nn(probs.astype(bf16), gc)
            dk = dk + nn(grads, qc)
            acc[:, cs] = acc[:, cs] + nn(keys_t, grads)
        dkv[rows, pl.ds(0, HD)] = (dk * SCALE).astype(bf16)
        dkv[rows, pl.ds(HD, HD)] = dv.astype(bf16)

    @pl.when(last > 0)
    def _():
        block(0, True, earlier)

        @pl.loop(1, last)
        def _(index):
            block(index, False, earlier)

    block(last, True, total)

    @pl.loop(last + 1, TOKENS // KEY_BLOCK)
    def _(index):
        dkv[pl.ds(pl.multiple_of(index * KEY_BLOCK, KEY_BLOCK), KEY_BLOCK), :] = jnp.zeros(
            (KEY_BLOCK, 2 * HD), bf16
        )

    rows = (acc[...] * SCALE).T
    for h in range(HEADS):
        dq[:, pl.ds(h * HD, HD)] = rows[h * TOK : (h + 1) * TOK]


def attend_back(queries, kv, grads, exact, start, ids, lse):
    return pl.pallas_call(
        attend_back_kernel,
        out_shape=(
            jax.ShapeDtypeStruct((TOK, HEADS * HD), f32),
            jax.ShapeDtypeStruct((TOKENS, 2 * HD), bf16),
        ),
        in_specs=[VMEM] * 7,
        out_specs=(VMEM,) * 2,
        scratch_shapes=[
            pltpu.VMEM((NQ, HD), bf16),
            pltpu.VMEM((NQ, HD), bf16),
            pltpu.VMEM((HD, NQ), f32),
        ],
        compiler_params=pltpu.CompilerParams(vmem_limit_bytes=60 * 2**20),
    )(queries, kv, grads, exact, start, ids, lse)


def row_starts(lengths, token_ids):
    ends = jnp.cumsum(lengths)
    before = ends[None, :] <= token_ids[:, None]
    return jnp.sum(jnp.where(before, lengths[None, :], 0), axis=1)


def rope_tables(positions):
    half = HD // 2
    freqs = rope_base ** (-2.0 * jnp.arange(half, dtype=f32) / HD)
    angles = positions.astype(f32)[:, None] * freqs[None, :]
    cosine, sine = jnp.cos(angles), jnp.sin(angles)
    return jnp.concatenate([cosine, cosine], 1), jnp.concatenate([-sine, sine], 1)


def rotate(values, cosine, sine):
    heads = []
    for h in range(values.shape[1] // HD):
        one = values[:, h * HD : (h + 1) * HD]
        swapped = jnp.concatenate([one[:, HD // 2 :], one[:, : HD // 2]], axis=1)
        heads.append(one * cosine + swapped * sine)
    return jnp.concatenate(heads, axis=1)


def normalize(values):
    inverse = lax.rsqrt(jnp.mean(values * values, axis=-1) + rms_eps)
    return (values * inverse[:, None], inverse)


def norm_back(grad_normed, normed, inverse):
    inner = jnp.mean(grad_normed * normed, axis=-1, keepdims=True)
    return inverse[:, None] * (grad_normed - normed * inner)


def shards(
    layer_in, lengths, norm_attn, w_qkv, qkv_bias, w_out, norm_mlp, w_gate, w_up, w_down, out_grad
):
    shard = lax.axis_index(WIDE)
    member = lax.axis_index(("y", "c"))
    own_ids = shard * TOK + jnp.arange(TOK, dtype=jnp.int32)
    seq_starts = row_starts(lengths, own_ids)
    cosine, sine = rope_tables(own_ids - seq_starts)
    start = jnp.tile(seq_starts, HEADS)[None]
    ids = jnp.tile(own_ids, HEADS)[None]
    gate_w = lax.dynamic_slice(w_gate, (0, member * UNITS), (D, UNITS))
    up_w = lax.dynamic_slice(w_up, (0, member * UNITS), (D, UNITS))
    down_w = lax.dynamic_slice(w_down, (member * UNITS, 0), (UNITS, D))

    input_f32 = layer_in.astype(f32)
    normed_attn, inverse_attn = normalize(input_f32)
    act_attn = (normed_attn * norm_attn).astype(bf16)
    projected = nn(act_attn, w_qkv) + qkv_bias[0]
    turned = rotate(projected[:, : (HEADS + 1) * HD], cosine, sine).astype(bf16)
    queries = turned[:, : HEADS * HD]
    kv_own = jnp.concatenate(
        [turned[:, HEADS * HD :], projected[:, (HEADS + 1) * HD :].astype(bf16)], axis=1
    )
    kv = kv_gather(kv_own).reshape(TOKENS, 2 * HD)
    attn_low, exact, lse = attend(queries, kv, start, ids)

    resid = input_f32 + narrow_sum(3, nn(attn_low, w_out).astype(bf16))
    normed_mlp, inverse_mlp = normalize(resid)
    act_mlp = (normed_mlp * norm_mlp).astype(bf16)
    act_all, out_grad_all = (
        a.reshape(GROUP * TOK, D) for a in group_gather(4, [act_mlp, out_grad])
    )
    gate = nn(act_all, gate_w)
    up = nn(act_all, up_w)
    sigmoid = jax.nn.sigmoid(gate)
    silu = gate * sigmoid
    hidden = (silu * up).astype(bf16)
    grad_hidden = nt(out_grad_all, down_w)
    grad_gate_pre = (grad_hidden * up * (sigmoid * (1.0 + gate * (1.0 - sigmoid)))).astype(bf16)
    grad_up_pre = (grad_hidden * silu).astype(bf16)
    down_terms = nn(hidden, down_w).astype(bf16).reshape(4, 2, TOK, D)
    back_terms = (nt(grad_gate_pre, gate_w) + nt(grad_up_pre, up_w)).astype(bf16)
    mlp_out, grad_act_mlp = group_reduce(5, [down_terms, back_terms.reshape(4, 2, TOK, D)])
    layer_out = (resid + mlp_out).astype(bf16)
    grad_norm_mlp = jnp.sum(grad_act_mlp * normed_mlp, axis=0)
    grad_resid = out_grad.astype(f32) + norm_back(
        grad_act_mlp * norm_mlp, normed_mlp, inverse_mlp
    )
    grad_branch = grad_resid.astype(bf16)
    grad_attn = nt(grad_branch, w_out).astype(bf16)
    grad_q, grad_kv_terms = attend_back(queries, kv, grad_attn, exact, start, ids, lse)
    grad_kv = kv_reduce(grad_kv_terms.reshape(4, 4, 2, 2, TOK, 2 * HD))
    grad_turned = jnp.concatenate([grad_q, grad_kv[:, :HD]], axis=1)
    grad_projected = jnp.concatenate(
        [rotate(grad_turned, cosine, -sine), grad_kv[:, HD:]], axis=1
    ).astype(bf16)
    grad_act_attn = narrow_sum(6, nt(grad_projected, w_qkv).astype(bf16))
    grad_norm_attn = jnp.sum(grad_act_attn * normed_attn, axis=0)
    in_grad = (
        grad_resid + norm_back(grad_act_attn * norm_attn, normed_attn, inverse_attn)
    ).astype(bf16)

    act_attn_all, branch_all = (
        a.reshape(GROUP * TOK, D) for a in group_gather(7, [act_attn, grad_branch])
    )
    by_head = grad_projected.reshape(TOK, 4, 2, HD).transpose(1, 2, 0, 3)
    low_cols = attn_low.reshape(TOK, 4, 2, OUT_COLS).transpose(1, 2, 0, 3)
    head_grads, low_all = (
        a.reshape(GROUP * TOK, -1) for a in group_swap(8, [by_head, low_cols])
    )
    bias_sums = jnp.sum(grad_projected.astype(f32), axis=0)
    small = jnp.concatenate(
        [
            grad_norm_attn[None],
            grad_norm_mlp[None],
            jnp.pad(bias_sums, (0, D - bias_sums.shape[0]))[None],
            jnp.zeros((5, D), f32),
        ]
    )
    terms = [
        tn(act_all, grad_gate_pre),
        tn(act_all, grad_up_pre),
        tn(out_grad_all, hidden),
        tn(act_attn_all, head_grads),
        tn(branch_all, low_all),
    ]
    *sums, small = weight_reduce(
        9, [t.astype(bf16).reshape(4, D // 4, t.shape[1]) for t in terms], small
    )
    sum_gate, sum_up, sum_down, sum_qkv, sum_out = (
        s.transpose(2, 0, 1, 3).reshape(24, -1) for s in sums
    )
    norms = lax.dynamic_slice(small, (0, shard * 24), (2, 24))
    bias = lax.dynamic_slice(
        small[2, : (HEADS + 2) * HD].reshape(HEADS + 2, HD), (0, shard * 2), (HEADS + 2, 2)
    )
    return (
        layer_out,
        in_grad,
        norms[0],
        sum_qkv,
        bias[None, : HEADS + 1],
        bias[HEADS + 1 :],
        sum_out.T,
        norms[1],
        sum_gate,
        sum_up,
        sum_down.T,
    )


def solution(mesh):
    torus = Mesh(mesh.devices.reshape(4, 4, 2, 2, 2), AXES)
    in_specs = (
        P(WIDE, None),
        P(),
        P(),
        P(None, "n"),
        P("n", None),
        P("n", None),
        P(),
        P(None, "n"),
        P(None, "n"),
        P("n", None),
        P(WIDE, None),
    )
    out_specs = (
        P(WIDE, None),
        P(WIDE, None),
        P(WIDE),
        P(WIDE, "n"),
        P("n", None, WIDE),
        P("n", WIDE),
        P("n", WIDE),
        P(WIDE),
        P(WIDE, "n"),
        P(WIDE, "n"),
        P("n", WIDE),
    )
    return jax.shard_map(
        shards, mesh=torus, in_specs=in_specs, out_specs=out_specs, check_vma=False
    )
```

```python
import functools
import math

import jax
import jax.numpy as jnp
from jax import lax
from jax.experimental import pallas as pl
from jax.experimental.pallas import tpu as pltpu
from jax.sharding import Mesh
from jax.sharding import PartitionSpec as P

HD = 128
QH = 12
KVH = 2
HEADS = QH // KVH
D = 1536
FF = 8960
TOK = 128
TOKENS = 8192
NQ = HEADS * TOK
GROUP = 8
UNITS = FF // 2 // GROUP

AXES = ("z", "y", "xh", "c", "n")
SIZE = {"z": 4, "y": 4, "xh": 2, "c": 2, "n": 2}
WIDE = ("z", "y", "xh", "c")
MESH = pl.DeviceIdType.MESH

rms_eps = 1e-06
rope_base = 10000.0
big_negative = -1e30
SCALE = HD ** (-0.5)
SCALE_LOG2 = SCALE * math.log2(math.e)
KEY_BLOCK = 512
BLOCK_SHARDS = KEY_BLOCK // TOK
Q_CHUNK = 256

bf16 = jnp.bfloat16
f32 = jnp.float32
VMEM = pl.BlockSpec(memory_space=pltpu.VMEM)
SMEM = pl.BlockSpec(memory_space=pltpu.SMEM)
ANY = pl.BlockSpec(memory_space=pl.ANY)


def nn(a, b):
    return lax.dot_general(a, b, (((1,), (0,)), ((), ())), preferred_element_type=f32)


def nt(a, b):
    return lax.dot_general(a, b, (((1,), (1,)), ((), ())), preferred_element_type=f32)


def tn(a, b):
    return lax.dot_general(a, b, (((0,), (0,)), ((), ())), preferred_element_type=f32)


def here():
    return {a: lax.axis_index(a) for a in AXES}


def step(me, axis, by):
    return lax.rem(me[axis] + by, SIZE[axis])


def at(me, **moved):
    return tuple(step(me, a, moved[a]) if a in moved else me[a] for a in AXES)


def greet(peers):
    barrier = pltpu.get_barrier_semaphore()
    for p in peers:
        pl.semaphore_signal(barrier, inc=1, device_id=p, device_id_type=MESH)
    pl.semaphore_wait(barrier, len(peers))


class Copies:
    def __init__(self, send_sems, recv_sems):
        self.send_sems, self.recv_sems, self.used, self.started = send_sems, recv_sems, 0, []

    def make(self, src, dst, target):
        k = self.used
        self.used += 1
        return pltpu.make_async_remote_copy(
            src_ref=src,
            dst_ref=dst,
            send_sem=self.send_sems.at[k],
            recv_sem=self.recv_sems.at[k],
            device_id=target,
            device_id_type=MESH,
        )

    def send(self, src, dst, target):
        copy = self.make(src, dst, target)
        copy.start()
        self.started.append(copy)
        return copy

    def finish(self):
        for copy in self.started:
            copy.wait_send()


def sems(count):
    return [pltpu.SemaphoreType.DMA((count,)), pltpu.SemaphoreType.DMA((count,))]


def params(ident, mib=60):
    return pltpu.CompilerParams(
        collective_id=ident, has_side_effects=True, vmem_limit_bytes=mib * 2**20
    )


def kv_gather_kernel(x, o, send_sems, recv_sems):
    me = here()
    z, y, xh, c = me["z"], me["y"], me["xh"], me["c"]
    partner, across = at(me, c=1), at(me, xh=1)
    ys = {d: at(me, y=d) for d in (1, 2, 3)}
    zs = {d: at(me, z=d) for d in (1, 2, 3)}
    o[z, y, xh, c] = x[...]
    greet([partner, across, *ys.values(), *zs.values()])
    copies = Copies(send_sems, recv_sems)
    mine = o.at[z, y, xh, c]
    first = copies.send(mine, mine, across)
    to_core = [copies.send(mine, mine, partner)]
    first.wait_recv()
    theirs = o.at[z, y, 1 - xh, c]
    to_core.append(copies.send(theirs, theirs, partner))
    half = TOK // 2
    low, high = pl.ds(0, half), pl.ds(half, half)

    def slot(zi, yi, rows):
        return o.at[zi, yi, :, c, rows]

    first_low, first_high = {}, {}
    for d in (1, 3, 2):
        first_low[d] = copies.send(slot(z, y, low), slot(z, y, low), ys[d])
        first_high[d] = copies.send(slot(z, y, high), slot(z, y, high), zs[d])
    second_low, second_high = {}, {}
    for e in (0, 1, 3, 2):
        yi, zi = lax.rem(y + (4 - e), 4), lax.rem(z + (4 - e), 4)
        if e:
            first_low[e].wait_recv()
            to_core.append(copies.send(slot(z, yi, low), slot(z, yi, low), partner))
            first_high[e].wait_recv()
            to_core.append(copies.send(slot(zi, y, high), slot(zi, y, high), partner))
        for d in (1, 3, 2):
            second_low[e, d] = copies.send(slot(z, yi, low), slot(z, yi, low), zs[d])
            second_high[e, d] = copies.send(slot(zi, y, high), slot(zi, y, high), ys[d])
    for e in (0, 1, 3, 2):
        for d in (1, 3, 2):
            yi, zi = lax.rem(y + (4 - e), 4), lax.rem(z + (4 - e), 4)
            yd, zd = lax.rem(y + (4 - d), 4), lax.rem(z + (4 - d), 4)
            second_low[e, d].wait_recv()
            to_core.append(copies.send(slot(zd, yi, low), slot(zd, yi, low), partner))
            second_high[e, d].wait_recv()
            to_core.append(copies.send(slot(zi, yd, high), slot(zi, yd, high), partner))
    for copy in to_core:
        copy.wait_recv()
    copies.finish()


def kv_gather(kv):
    return pl.pallas_call(
        kv_gather_kernel,
        out_shape=jax.ShapeDtypeStruct((4, 4, 2, 2, TOK, 2 * HD), bf16),
        in_specs=[VMEM],
        out_specs=VMEM,
        scratch_shapes=sems(80),
        compiler_params=params(1),
    )(kv)


def group_gather_kernel(count, *refs):
    xs, os, (send_sems, recv_sems, local_sems) = refs[:count], refs[count : 2 * count], refs[2 * count :]
    me = here()
    y, c = me["y"], me["c"]
    partner = at(me, c=1)
    ys = {d: at(me, y=d) for d in (1, 2, 3)}
    greet([partner, *ys.values()])
    copies = Copies(send_sems, recv_sems)
    arrive, to_core, local = {}, [], []
    for i, (x, o) in enumerate(zip(xs, os)):
        for d in (1, 3, 2):
            arrive[i, d] = copies.send(x, o.at[y, c], ys[d])
        to_core.append(copies.send(x, o.at[y, c], partner))
        local.append(pltpu.make_async_copy(x, o.at[y, c], local_sems.at[i]))
        local[-1].start()
    for i, o in enumerate(os):
        for d in (1, 3, 2):
            arrive[i, d].wait_recv()
            got = o.at[lax.rem(y + (4 - d), 4), c]
            to_core.append(copies.send(got, got, partner))
    for copy in to_core:
        copy.wait_recv()
    for copy in local:
        copy.wait()
    copies.finish()


def group_gather(ident, arrays):
    count = len(arrays)
    return pl.pallas_call(
        functools.partial(group_gather_kernel, count),
        out_shape=[jax.ShapeDtypeStruct((4, 2, *a.shape), a.dtype) for a in arrays],
        in_specs=[ANY] * count,
        out_specs=[ANY] * count,
        scratch_shapes=[*sems(7 * count), pltpu.SemaphoreType.DMA((count,))],
        compiler_params=params(ident),
    )(*arrays)


def group_reduce_kernel(count, *refs):
    ps, os = refs[:count], refs[count : 2 * count]
    cb, sb, rb, nb, rn, send_sems, recv_sems = refs[2 * count :]
    me = here()
    y, c = me["y"], me["c"]
    partner, other = at(me, c=1), at(me, n=1)
    ys = {d: at(me, y=d) for d in (1, 2, 3)}
    greet([partner, other, *ys.values()])
    copies = Copies(send_sems, recv_sems)
    cores, sent = {}, {}
    for i in range(count):
        for d in (2, 1, 3, 0):
            yi = step(me, "y", d)
            cores[i, d] = copies.send(ps[i].at[yi, 1 - c], cb.at[i, d], partner)
    for i in range(count):
        for d in (2, 1, 3):
            cores[i, d].wait_recv()
            sb[i, d - 1] = (ps[i][step(me, "y", d), c].astype(f32) + cb[i, d].astype(f32)).astype(bf16)
            sent[i, d] = copies.send(sb.at[i, d - 1], rb.at[i, d - 1], ys[d])
    last = []
    for i in range(count):
        cores[i, 0].wait_recv()
        total = ps[i][y, c].astype(f32) + cb[i, 0].astype(f32)
        for d in (1, 3, 2):
            sent[i, d].wait_recv()
            total = total + rb[i, d - 1].astype(f32)
        nb[i] = total.astype(bf16)
        last.append(copies.send(nb.at[i], rn.at[i], other))
    for i in range(count):
        last[i].wait_recv()
        os[i][...] = nb[i].astype(f32) + rn[i].astype(f32)
    copies.finish()


def group_reduce(ident, arrays):
    count = len(arrays)
    return pl.pallas_call(
        functools.partial(group_reduce_kernel, count),
        out_shape=[jax.ShapeDtypeStruct((TOK, D), f32) for _ in arrays],
        in_specs=[VMEM] * count,
        out_specs=[VMEM] * count,
        scratch_shapes=[
            pltpu.VMEM((count, 4, TOK, D), bf16),
            pltpu.VMEM((count, 3, TOK, D), bf16),
            pltpu.VMEM((count, 3, TOK, D), bf16),
            pltpu.VMEM((count, TOK, D), bf16),
            pltpu.VMEM((count, TOK, D), bf16),
            *sems(8 * count),
        ],
        compiler_params=params(ident),
    )(*arrays)


def narrow_sum_kernel(x, o, rn, send_sems, recv_sems):
    me = here()
    other = at(me, n=1)
    greet([other])
    copies = Copies(send_sems, recv_sems)
    copies.send(x, rn, other).wait_recv()
    o[...] = x[...].astype(f32) + rn[...].astype(f32)
    copies.finish()


def narrow_sum(ident, array):
    return pl.pallas_call(
        narrow_sum_kernel,
        out_shape=jax.ShapeDtypeStruct(array.shape, f32),
        in_specs=[VMEM],
        out_specs=VMEM,
        scratch_shapes=[pltpu.VMEM(array.shape, bf16), *sems(1)],
        compiler_params=params(ident),
    )(array)


def heads_in(ref, scratch):
    for h in range(HEADS):
        scratch[pl.ds(h * TOK, TOK), :] = ref[:, pl.ds(h * HD, HD)]


def attend_kernel(q_in, kv, start, ids, o, exact, lse, q, top, total, acc, low_acc):
    me = here()
    shard = ((me["z"] * 4 + me["y"]) * 2 + me["xh"]) * 2 + me["c"]
    last = shard // BLOCK_SHARDS
    heads_in(q_in, q)
    top[...] = jnp.full_like(top, big_negative)
    total[...] = jnp.zeros_like(total)
    acc[...] = jnp.zeros_like(acc)
    low_acc[...] = jnp.zeros_like(low_acc)

    def block(index, masked):
        offset = pl.multiple_of(index * KEY_BLOCK, KEY_BLOCK)
        rows = pl.ds(offset, KEY_BLOCK)
        keys = kv[rows, pl.ds(0, HD)]
        values = kv[rows, pl.ds(HD, HD)].T
        for chunk in range(NQ // Q_CHUNK):
            cs = pl.ds(chunk * Q_CHUNK, Q_CHUNK)
            scores = nt(keys, q[cs, :]) * SCALE_LOG2
            if masked:
                key_ids = offset + lax.broadcasted_iota(jnp.int32, (KEY_BLOCK, Q_CHUNK), 0)
                allowed = (key_ids >= start[:, cs]) & (key_ids <= ids[:, cs])
                scores = jnp.where(allowed, scores, big_negative)
            old = top[:, cs]
            new = jnp.maximum(old, jnp.max(scores, axis=0, keepdims=True))
            probs = jnp.exp2(scores - new)
            if masked:
                probs = jnp.where(allowed, probs, 0.0)
            fade = jnp.exp2(old - new)
            top[:, cs] = new
            total[:, cs] = total[:, cs] * fade + jnp.sum(probs, axis=0, keepdims=True)
            high = probs.astype(bf16)
            rest = (probs - high.astype(f32)).astype(bf16)
            acc[:, cs] = acc[:, cs] * fade + nn(values, high)
            low_acc[:, cs] = low_acc[:, cs] * fade + nn(values, rest)

    @pl.when(last > 0)
    def _():
        block(0, True)

        @pl.loop(1, last)
        def _(index):
            block(index, False)

        kept = start[...] < last * KEY_BLOCK
        top[...] = jnp.where(kept, top[...], big_negative)
        kept = kept.astype(f32)
        total[...] = total[...] * kept
        acc[...] = acc[...] * kept
        low_acc[...] = low_acc[...] * kept

    block(last, True)
    inverse = 1.0 / total[...]
    rows = acc[...] * inverse
    exact[...] = rows + low_acc[...] * inverse
    rows = rows.T.astype(bf16)
    for h in range(HEADS):
        o[:, pl.ds(h * HD, HD)] = rows[h * TOK : (h + 1) * TOK]
    lse[...] = top[...] + jnp.log2(total[...])


def attend(queries, kv, start, ids):
    return pl.pallas_call(
        attend_kernel,
        out_shape=(
            jax.ShapeDtypeStruct((TOK, HEADS * HD), bf16),
            jax.ShapeDtypeStruct((HD, NQ), f32),
            jax.ShapeDtypeStruct((1, NQ), f32),
        ),
        in_specs=[VMEM] * 4,
        out_specs=(VMEM,) * 3,
        scratch_shapes=[
            pltpu.VMEM((NQ, HD), bf16),
            pltpu.VMEM((1, NQ), f32),
            pltpu.VMEM((1, NQ), f32),
            pltpu.VMEM((HD, NQ), f32),
            pltpu.VMEM((HD, NQ), f32),
        ],
        compiler_params=pltpu.CompilerParams(vmem_limit_bytes=60 * 2**20),
    )(queries, kv, start, ids)


def three(ref):
    return ref[0].astype(f32) + ref[1].astype(f32) + ref[2].astype(f32)


def back_kernel(*refs):
    (q_in, kv, exact, start, ids, lse, grad_resid, w_out, attn_low, cosine, sine, normed, inverse) = refs[:13]
    gain, resid, mlp_gain_terms, w_qkv_hbm, act_hbm, *terms, down_terms = refs[13:22]
    in_grad, layer_out, sum_gate, sum_up, sum_down, sum_qkv, sum_out, small_out = refs[22:30]
    (q, g, acc, dkv, cb, s, r1a, r1b, ta, tb, r2a, r2b, u, r3, w_qkv, act_all, gb_all, al_heads, al_all) = refs[30:49]
    gp, gp_flat, gp_all, part, part_other, small, e1, e2, e3, f1, f2 = refs[49:60]
    own, first_in, mid, second_in, summed, third_in = (refs[60 + 3 * k : 63 + 3 * k] for k in range(6))
    q_terms, q_first, q_mid, q_second, q_summed, q_third = refs[78:84]
    down_own, down_core, down_sent, down_in, down_part, down_other, send_sems, recv_sems, local_sems = refs[84:]

    me = here()
    z, y, xh, c, n = (me[a] for a in AXES)
    shard = ((z * 4 + y) * 2 + xh) * 2 + c
    partner, across, other = at(me, c=1), at(me, xh=1), at(me, n=1)
    ys = {d: at(me, y=d) for d in (1, 2, 3)}
    zs = {d: at(me, z=d) for d in (1, 2, 3)}
    near_moves = [(d, e) for d in (1, 3, 2, 0) for e in (0, 1) if d or e]
    near = {m: at(me, y=m[0], xh=m[1]) for m in near_moves}
    group = {m: at(me, y=m[0], c=m[1]) for m in near_moves}
    greet([other, *zs.values(), *near.values(), *(group[m] for m in near_moves if m[1])])
    copies = Copies(send_sems, recv_sems)
    half = TOK // 2
    low, high = pl.ds(0, half), pl.ds(half, half)

    local = []

    def load(src, dst):
        copy = pltpu.make_async_copy(src, dst, local_sems.at[len(local)])
        copy.start()
        local.append(copy)
        return copy

    def z_rows(d):
        return pl.ds(pl.multiple_of(step(me, "z", d) * 384, 384), 384)

    first = {}

    def send_first(i, d):
        first[i, d] = copies.send(terms[i].at[z_rows(d)], first_in[i].at[d - 1], zs[d])

    for d in (1, 3, 2):
        send_first(0, d)
    for d in (1, 3):
        send_first(1, d)

    branch = grad_resid[...].astype(bf16)
    gb_all[y, c] = branch
    mine = pl.ds(pl.multiple_of(half * n, half), half)
    theirs = pl.ds(pl.multiple_of(half * (1 - n), half), half)
    gathered = {d: copies.send(gb_all.at[y, c, mine], gb_all.at[y, c, mine], ys[d]) for d in (1, 3, 2)}
    gb_core = [copies.send(gb_all.at[y, c], gb_all.at[y, c], partner)]
    for h in range(HEADS):
        al_heads[h] = attn_low[:, pl.ds(h * HD, HD)]

    def head_of(d, e):
        taker = step(me, "y", d) * 2 + step(me, "c", e)
        return jnp.where(taker < HEADS, taker, 0)

    al_moves = [
        copies.send(al_heads.at[head_of(*m)], al_all.at[y, c], group[m]) for m in near_moves
    ]
    al_all[y, c] = al_heads[head_of(0, 0)]
    load_w = load(w_qkv_hbm, w_qkv)
    load_act = load(act_hbm, act_all)
    load_own = [load(terms[i].at[z_rows(0)], own[i]) for i in range(3)]
    down_cores = {}
    load_down = {}
    for d in (2, 1, 3, 0):
        yi = step(me, "y", d)
        down_cores[d] = copies.send(down_terms.at[yi, 1 - c], down_core.at[d], partner)
        load_down[d] = load(down_terms.at[yi, c], down_own.at[d])

    heads_in(q_in, q)
    grads_in = nt(branch, w_out[...]).astype(bf16)
    for h in range(HEADS):
        g[pl.ds(h * TOK, TOK), :] = grads_in[:, h * HD : (h + 1) * HD]
    balance = jnp.sum(g[...].astype(f32).T * exact[...], axis=0, keepdims=True)
    acc[...] = jnp.zeros_like(acc)
    last = shard // BLOCK_SHARDS
    log_total = lse[...]
    earlier = jnp.where(start[...] < last * KEY_BLOCK, log_total, -big_negative)

    def block(index, masked, shift):
        offset = pl.multiple_of(index * KEY_BLOCK, KEY_BLOCK)
        rows = pl.ds(offset, KEY_BLOCK)
        keys, values = kv[rows, pl.ds(0, HD)], kv[rows, pl.ds(HD, HD)]
        keys_t = keys.T
        dk = jnp.zeros((KEY_BLOCK, HD), f32)
        dv = jnp.zeros((KEY_BLOCK, HD), f32)
        for chunk in range(NQ // Q_CHUNK):
            cs = pl.ds(chunk * Q_CHUNK, Q_CHUNK)
            piece = slice(chunk * Q_CHUNK, (chunk + 1) * Q_CHUNK)
            qc, gc = q[cs, :], g[cs, :]
            probs = jnp.exp2(nt(keys, qc) * SCALE_LOG2 - shift[:, piece])
            if masked:
                key_ids = offset + lax.broadcasted_iota(jnp.int32, (KEY_BLOCK, Q_CHUNK), 0)
                allowed = (key_ids >= start[:, cs]) & (key_ids <= ids[:, cs])
                probs = jnp.where(allowed, probs, 0.0)
            grads = (probs * (nt(values, gc) - balance[:, piece])).astype(bf16)
            dv = dv + nn(probs.astype(bf16), gc)
            dk = dk + nn(grads, qc)
            acc[:, cs] = acc[:, cs] + nn(keys_t, grads)
        zi, yi = index // 4, lax.rem(index, 4)
        shape = (2, 2, TOK, HD)
        dkv[zi, yi, :, :, :, pl.ds(0, HD)] = (dk * SCALE).astype(bf16).reshape(shape)
        dkv[zi, yi, :, :, :, pl.ds(HD, HD)] = dv.astype(bf16).reshape(shape)

    @pl.when(last > 0)
    def _():
        block(0, True, earlier)

        @pl.loop(1, last)
        def _(index):
            block(index, False, earlier)

    block(last, True, log_total)

    @pl.loop(last + 1, TOKENS // KEY_BLOCK)
    def _(index):
        dkv[index // 4, lax.rem(index, 4)] = jnp.zeros((2, 2, TOK, 2 * HD), bf16)

    kv_cores = [
        copies.send(dkv.at[:, :, :, 1 - c, rows], cb.at[:, :, :, rows], partner)
        for rows in (low, high)
    ]
    first_a, first_b, second_a, second_b = {}, {}, {}, {}
    for rows, core in ((low, kv_cores[0]), (high, kv_cores[1])):
        core.wait_recv()
        for zi in range(4):
            s[zi, :, :, rows] = (dkv[zi, :, :, c, rows].astype(f32) + cb[zi, :, :, rows].astype(f32)).astype(bf16)
        for d in (1, 3, 2):
            if rows is low:
                first_a[d] = copies.send(s.at[step(me, "z", d), :, :, low], r1a.at[d - 1], zs[d])
            else:
                first_b[d] = copies.send(s.at[:, step(me, "y", d), :, high], r1b.at[d - 1], ys[d])

    for i, d in ((1, 2), (2, 1), (2, 3), (2, 2)):
        send_first(i, d)
    turned_back = (acc[...] * SCALE).T

    def revert(rows):
        return rows * cosine[...] - pltpu.roll(rows, HD // 2, 1) * sine[...]

    def keep_head(h, rows):
        low_rows = rows.astype(bf16)
        gp[h] = low_rows
        gp_flat[:, pl.ds(h * HD, HD)] = low_rows
        small[pl.ds(2, 1), pl.ds(h * HD, HD)] = jnp.sum(low_rows.astype(f32), axis=0, keepdims=True)

    small[...] = jnp.zeros_like(small)
    small[pl.ds(1, 1), :] = mlp_gain_terms[...]
    for h in range(HEADS):
        keep_head(h, revert(turned_back[h * TOK : (h + 1) * TOK]))
    gb_other = {}
    for d in (1, 3, 2):
        gathered[d].wait_recv()
        slot = gb_all.at[lax.rem(y + (4 - d), 4), c, mine]
        gb_other[d] = copies.send(slot, slot, other)
        gb_core.append(copies.send(slot, slot, partner))
    load_w.wait()
    front = HEADS * HD
    partial = nt(gp_flat[:, pl.ds(0, front)], w_qkv[:, pl.ds(0, front)])

    for d in (1, 3, 2):
        first_a[d].wait_recv()
    ta[...] = (s[z, :, :, low].astype(f32) + three(r1a)).astype(bf16)
    for d in (1, 3, 2):
        second_a[d] = copies.send(ta.at[step(me, "y", d)], r2a.at[d - 1], ys[d])
    for d in (1, 3, 2):
        first_b[d].wait_recv()
    tb[...] = (s[:, y, :, high].astype(f32) + three(r1b)).astype(bf16)
    for d in (1, 3, 2):
        second_b[d] = copies.send(tb.at[step(me, "z", d)], r2b.at[d - 1], zs[d])
    for d in (1, 3, 2):
        second_a[d].wait_recv()
        second_b[d].wait_recv()
    ua = ta[y].astype(f32) + three(r2a)
    ub = tb[z].astype(f32) + three(r2b)
    u[:, low] = ua.astype(bf16)
    u[:, high] = ub.astype(bf16)
    kv_last = copies.send(u.at[1 - xh], r3, across)

    down_moves = {}
    for d in (2, 1, 3):
        down_cores[d].wait_recv()
        load_down[d].wait()
        down_sent[d - 1] = (down_own[d].astype(f32) + down_core[d].astype(f32)).astype(bf16)

    kv_last.wait_recv()
    grad_kv = u[xh].astype(f32) + r3[...].astype(f32)
    keep_head(HEADS, revert(grad_kv[:, :HD]))
    keep_head(HEADS + 1, grad_kv[:, HD:])
    gp_moves = [
        copies.send(gp.at[step(me, "y", m[0]) * 2 + step(me, "c", m[1])], gp_all.at[y, c], group[m])
        for m in near_moves
    ]
    gp_all[y, c] = gp[y * 2 + c]
    back = pl.ds(front, 2 * HD)
    part[...] = (partial + nt(gp_flat[:, back], w_qkv[:, back])).astype(bf16)
    swap = copies.send(part, part_other, other)
    for d in (2, 1, 3):
        down_moves[d] = copies.send(down_sent.at[d - 1], down_in.at[d - 1], ys[d])

    for d in (1, 3, 2):
        gb_other[d].wait_recv()
        slot = gb_all.at[lax.rem(y + (4 - d), 4), c, theirs]
        gb_core.append(copies.send(slot, slot, partner))
    load_act.wait()
    for copy in gp_moves:
        copy.wait_recv()
    q_terms[pl.ds(0, HD), :] = tn(
        gp_all[...].reshape(GROUP * TOK, HD), act_all[...].reshape(GROUP * TOK, D)
    ).astype(bf16)

    def z_cols(d):
        return pl.ds(pl.multiple_of(step(me, "z", d) * 384, 384), 384)

    q_one = {d: copies.send(q_terms.at[pl.ds(0, HD), z_cols(d)], q_first.at[d - 1, pl.ds(0, HD)], zs[d]) for d in (1, 3, 2)}
    for copy in al_moves + gb_core:
        copy.wait_recv()
    q_terms[pl.ds(HD, HD), :] = tn(
        al_all[...].reshape(GROUP * TOK, HD), gb_all[...].reshape(GROUP * TOK, D)
    ).astype(bf16)
    q_two = {d: copies.send(q_terms.at[pl.ds(HD, HD), z_cols(d)], q_first.at[d - 1, pl.ds(HD, HD)], zs[d]) for d in (1, 3, 2)}

    swap.wait_recv()
    grad_act = part[...].astype(f32) + part_other[...].astype(f32)
    small[pl.ds(0, 1), :] = jnp.sum(grad_act * normed[...], axis=0, keepdims=True)
    small_one = {d: copies.send(small, e1.at[d - 1], zs[d]) for d in (1, 3, 2)}
    grad_normed = grad_act * gain[...]
    inner = jnp.mean(grad_normed * normed[...], axis=-1, keepdims=True)
    in_grad[...] = (grad_resid[...] + inverse[...] * (grad_normed - normed[...] * inner)).astype(bf16)

    second = {}

    def send_second(i, mid_ref, in_ref):
        for m in near_moves:
            second[i, m] = copies.send(
                mid_ref.at[step(me, "y", m[0]), step(me, "xh", m[1])], in_ref.at[y, xh], near[m]
            )
        in_ref[y, xh] = mid_ref[y, xh]

    for d in (1, 3, 2):
        small_one[d].wait_recv()
    f1[...] = small[...] + three(e1)
    small_two = {m: copies.send(f1, e2.at[k], near[m]) for k, m in enumerate(near_moves)}
    for i in range(3):
        load_own[i].wait()
        for d in (1, 3, 2):
            first[i, d].wait_recv()
        for yi in range(4):
            for xi in range(2):
                rows = pl.ds(96 * yi + 48 * xi, 48)
                total = own[i][rows].astype(f32)
                for d in range(3):
                    total = total + first_in[i][d, rows].astype(f32)
                mid[i][yi, xi] = total.astype(bf16)
        send_second(i, mid[i], second_in[i])
    for d in (1, 3, 2):
        q_one[d].wait_recv()
        q_two[d].wait_recv()
    q_sum = (q_terms[:, z_cols(0)].astype(f32) + three(q_first)).T.astype(bf16)
    for yi in range(4):
        for xi in range(2):
            q_mid[yi, xi] = q_sum[96 * yi + 48 * xi : 96 * yi + 48 * xi + 48]
    send_second(3, q_mid, q_second)

    load_down[0].wait()
    down_cores[0].wait_recv()
    mlp_out = down_own[0].astype(f32) + down_core[0].astype(f32)
    for d in (1, 3, 2):
        down_moves[d].wait_recv()
        mlp_out = mlp_out + down_in[d - 1].astype(f32)
    down_part[...] = mlp_out.astype(bf16)
    down_swap = copies.send(down_part, down_other, other)

    for m in near_moves:
        small_two[m].wait_recv()
    f2[...] = f1[...]
    for k in range(len(near_moves)):
        f2[...] = f2[...] + e2[k]
    small_three = copies.send(f2, e3, partner)
    keep, give = pl.ds(pl.multiple_of(24 * c, 8), 24), pl.ds(pl.multiple_of(24 * (1 - c), 8), 24)
    third = []
    all_summed = [*summed, q_summed]
    all_second = [*second_in, q_second]
    all_third = [*third_in, q_third]
    for i in range(4):
        for m in near_moves:
            second[i, m].wait_recv()
        all_summed[i][...] = all_second[i][:, 0].astype(f32) + all_second[i][:, 1].astype(f32)
        third.append(copies.send(all_summed[i].at[:, give], all_third[i], partner))
    for i, outs in enumerate(((sum_gate,), (sum_up,), (sum_down,), (sum_qkv, sum_out))):
        third[i].wait_recv()
        for yi in range(4):
            mine_sum, their_sum = all_summed[i][yi, keep], all_third[i][yi]
            pair = (jnp.where(c == 0, mine_sum, their_sum), jnp.where(c == 0, their_sum, mine_sum))
            for e in range(2):
                k = 2 * yi + e
                if i < 3:
                    outs[0][:, pl.ds(k * UNITS, UNITS)] = pair[e]
                else:
                    outs[0][:, pl.ds(k * HD, HD)] = pair[e][:, :HD]
                    if k < HEADS:
                        outs[1][:, pl.ds(k * HD, HD)] = pair[e][:, HD:]
    small_three.wait_recv()
    small_out[...] = f2[...] + e3[...]
    down_swap.wait_recv()
    layer_out[...] = (
        resid[...] + (down_part[...].astype(f32) + down_other[...].astype(f32))
    ).astype(bf16)
    copies.finish()


def back(*arrays):
    half = TOK // 2
    wide = 2 * HD
    return pl.pallas_call(
        back_kernel,
        out_shape=[
            jax.ShapeDtypeStruct((TOK, D), bf16),
            jax.ShapeDtypeStruct((TOK, D), bf16),
            *[jax.ShapeDtypeStruct((24, FF // 2), f32)] * 3,
            jax.ShapeDtypeStruct((24, (HEADS + 2) * HD), f32),
            jax.ShapeDtypeStruct((24, HEADS * HD), f32),
            jax.ShapeDtypeStruct((8, D), f32),
        ],
        in_specs=[VMEM] * 16 + [ANY] * 6,
        out_specs=[VMEM] * 8,
        scratch_shapes=[
            pltpu.VMEM((NQ, HD), bf16),
            pltpu.VMEM((NQ, HD), bf16),
            pltpu.VMEM((HD, NQ), f32),
            pltpu.VMEM((4, 4, 2, 2, TOK, wide), bf16),
            pltpu.VMEM((4, 4, 2, TOK, wide), bf16),
            pltpu.VMEM((4, 4, 2, TOK, wide), bf16),
            pltpu.VMEM((3, 4, 2, half, wide), bf16),
            pltpu.VMEM((3, 4, 2, half, wide), bf16),
            pltpu.VMEM((4, 2, half, wide), bf16),
            pltpu.VMEM((4, 2, half, wide), bf16),
            pltpu.VMEM((3, 2, half, wide), bf16),
            pltpu.VMEM((3, 2, half, wide), bf16),
            pltpu.VMEM((2, TOK, wide), bf16),
            pltpu.VMEM((TOK, wide), bf16),
            pltpu.VMEM((D, (HEADS + 2) * HD), bf16),
            pltpu.VMEM((4, 2, TOK, D), bf16),
            pltpu.VMEM((4, 2, TOK, D), bf16),
            pltpu.VMEM((HEADS, TOK, HD), bf16),
            pltpu.VMEM((4, 2, TOK, HD), bf16),
            pltpu.VMEM((HEADS + 2, TOK, HD), bf16),
            pltpu.VMEM((TOK, (HEADS + 2) * HD), bf16),
            pltpu.VMEM((4, 2, TOK, HD), bf16),
            pltpu.VMEM((TOK, D), bf16),
            pltpu.VMEM((TOK, D), bf16),
            pltpu.VMEM((8, D), f32),
            pltpu.VMEM((3, 8, D), f32),
            pltpu.VMEM((7, 8, D), f32),
            pltpu.VMEM((8, D), f32),
            pltpu.VMEM((8, D), f32),
            pltpu.VMEM((8, D), f32),
            *[pltpu.VMEM((384, UNITS), bf16)] * 3,
            *[pltpu.VMEM((3, 384, UNITS), bf16)] * 3,
            *[pltpu.VMEM((4, 2, 48, UNITS), bf16)] * 3,
            *[pltpu.VMEM((4, 2, 48, UNITS), bf16)] * 3,
            *[pltpu.VMEM((4, 48, UNITS), f32)] * 3,
            *[pltpu.VMEM((4, 24, UNITS), f32)] * 3,
            pltpu.VMEM((wide, D), bf16),
            pltpu.VMEM((3, wide, 384), bf16),
            pltpu.VMEM((4, 2, 48, wide), bf16),
            pltpu.VMEM((4, 2, 48, wide), bf16),
            pltpu.VMEM((4, 48, wide), f32),
            pltpu.VMEM((4, 24, wide), f32),
            pltpu.VMEM((4, TOK, D), bf16),
            pltpu.VMEM((4, TOK, D), bf16),
            pltpu.VMEM((3, TOK, D), bf16),
            pltpu.VMEM((3, TOK, D), bf16),
            pltpu.VMEM((TOK, D), bf16),
            pltpu.VMEM((TOK, D), bf16),
            *sems(140),
            pltpu.SemaphoreType.DMA((9,)),
        ],
        compiler_params=params(9, 62),
    )(*arrays)


def row_starts(lengths, token_ids):
    ends = jnp.cumsum(lengths)
    before = ends[None, :] <= token_ids[:, None]
    return jnp.sum(jnp.where(before, lengths[None, :], 0), axis=1)


def rope_tables(positions):
    half = HD // 2
    freqs = rope_base ** (-2.0 * jnp.arange(half, dtype=f32) / HD)
    angles = positions.astype(f32)[:, None] * freqs[None, :]
    cosine, sine = jnp.cos(angles), jnp.sin(angles)
    return jnp.concatenate([cosine, cosine], 1), jnp.concatenate([-sine, sine], 1)


def rotate(values, cosine, sine):
    heads = []
    for h in range(values.shape[1] // HD):
        one = values[:, h * HD : (h + 1) * HD]
        swapped = jnp.concatenate([one[:, HD // 2 :], one[:, : HD // 2]], axis=1)
        heads.append(one * cosine + swapped * sine)
    return jnp.concatenate(heads, axis=1)


def normalize(values):
    inverse = lax.rsqrt(jnp.mean(values * values, axis=-1) + rms_eps)
    return (values * inverse[:, None], inverse)


def norm_back(grad_normed, normed, inverse):
    inner = jnp.mean(grad_normed * normed, axis=-1, keepdims=True)
    return inverse[:, None] * (grad_normed - normed * inner)


def shards(
    layer_in, lengths, norm_attn, w_qkv, qkv_bias, w_out, norm_mlp, w_gate, w_up, w_down, out_grad
):
    shard = lax.axis_index(WIDE)
    member = lax.axis_index(("y", "c"))
    own_ids = shard * TOK + jnp.arange(TOK, dtype=jnp.int32)
    seq_starts = row_starts(lengths, own_ids)
    cosine, sine = rope_tables(own_ids - seq_starts)
    start = jnp.tile(seq_starts, HEADS)[None]
    ids = jnp.tile(own_ids, HEADS)[None]
    gate_w = lax.dynamic_slice(w_gate, (0, member * UNITS), (D, UNITS))
    up_w = lax.dynamic_slice(w_up, (0, member * UNITS), (D, UNITS))
    down_w = lax.dynamic_slice(w_down, (member * UNITS, 0), (UNITS, D))

    input_f32 = layer_in.astype(f32)
    normed_attn, inverse_attn = normalize(input_f32)
    act_attn = (normed_attn * norm_attn).astype(bf16)
    projected = nn(act_attn, w_qkv) + qkv_bias[0]
    turned = rotate(projected[:, : (HEADS + 1) * HD], cosine, sine).astype(bf16)
    queries = turned[:, : HEADS * HD]
    kv_own = jnp.concatenate(
        [turned[:, HEADS * HD :], projected[:, (HEADS + 1) * HD :].astype(bf16)], axis=1
    )
    kv = kv_gather(kv_own).reshape(TOKENS, 2 * HD)
    attn_low, exact, lse = attend(queries, kv, start, ids)

    resid = input_f32 + narrow_sum(3, nn(attn_low, w_out).astype(bf16))
    normed_mlp, inverse_mlp = normalize(resid)
    act_mlp = (normed_mlp * norm_mlp).astype(bf16)
    act_all, out_grad_all, act_attn_all = group_gather(4, [act_mlp, out_grad, act_attn])
    act_all, out_grad_all = act_all.reshape(GROUP * TOK, D), out_grad_all.reshape(GROUP * TOK, D)
    gate = nn(act_all, gate_w)
    up = nn(act_all, up_w)
    sigmoid = jax.nn.sigmoid(gate)
    silu = gate * sigmoid
    hidden = (silu * up).astype(bf16)
    grad_hidden = nt(out_grad_all, down_w)
    grad_gate_pre = (grad_hidden * up * (sigmoid * (1.0 + gate * (1.0 - sigmoid)))).astype(bf16)
    grad_up_pre = (grad_hidden * silu).astype(bf16)
    down_terms = nn(hidden, down_w).astype(bf16).reshape(4, 2, TOK, D)
    back_terms = (nt(grad_gate_pre, gate_w) + nt(grad_up_pre, up_w)).astype(bf16)
    (grad_act_mlp,) = group_reduce(5, [back_terms.reshape(4, 2, TOK, D)])
    grad_norm_mlp = jnp.sum(grad_act_mlp * normed_mlp, axis=0)
    grad_resid = out_grad.astype(f32) + norm_back(
        grad_act_mlp * norm_mlp, normed_mlp, inverse_mlp
    )
    terms = [
        t.astype(bf16)
        for t in (tn(act_all, grad_gate_pre), tn(act_all, grad_up_pre), tn(out_grad_all, hidden))
    ]
    in_grad, layer_out, sum_gate, sum_up, sum_down, sum_qkv, sum_out, small = back(
        queries, kv, exact, start, ids, lse, grad_resid, w_out, attn_low, cosine, sine, normed_attn,
        inverse_attn[:, None], norm_attn[None], resid, grad_norm_mlp[None],
        w_qkv, act_attn_all, *terms, down_terms,
    )
    norms = lax.dynamic_slice(small, (0, shard * 24), (2, 24))
    bias = lax.dynamic_slice(
        small[2, : (HEADS + 2) * HD].reshape(HEADS + 2, HD), (0, shard * 2), (HEADS + 2, 2)
    )
    return (
        layer_out,
        in_grad,
        norms[0],
        sum_qkv,
        bias[None, : HEADS + 1],
        bias[HEADS + 1 :],
        sum_out.T,
        norms[1],
        sum_gate,
        sum_up,
        sum_down.T,
    )


def solution(mesh):
    torus = Mesh(mesh.devices.reshape(4, 4, 2, 2, 2), AXES)
    in_specs = (
        P(WIDE, None),
        P(),
        P(),
        P(None, "n"),
        P("n", None),
        P("n", None),
        P(),
        P(None, "n"),
        P(None, "n"),
        P("n", None),
        P(WIDE, None),
    )
    out_specs = (
        P(WIDE, None),
        P(WIDE, None),
        P(WIDE),
        P(WIDE, "n"),
        P("n", None, WIDE),
        P("n", WIDE),
        P("n", WIDE),
        P(WIDE),
        P(WIDE, "n"),
        P(WIDE, "n"),
        P("n", WIDE),
    )
    return jax.shard_map(
        shards, mesh=torus, in_specs=in_specs, out_specs=out_specs, check_vma=False
    )
```

```python
import functools
import math

import jax
import jax.numpy as jnp
from jax import lax
from jax.experimental import pallas as pl
from jax.experimental.pallas import tpu as pltpu
from jax.sharding import Mesh
from jax.sharding import PartitionSpec as P

HD = 128
QH = 12
KVH = 2
HEADS = QH // KVH
D = 1536
FF = 8960
TOK = 128
TOKENS = 8192
NQ = HEADS * TOK
GROUP = 8
UNITS = FF // 2 // GROUP

AXES = ("z", "y", "xh", "c", "n")
SIZE = {"z": 4, "y": 4, "xh": 2, "c": 2, "n": 2}
WIDE = ("z", "y", "xh", "c")
MESH = pl.DeviceIdType.MESH

rms_eps = 1e-06
rope_base = 10000.0
big_negative = -1e30
SCALE = HD ** (-0.5)
SCALE_LOG2 = SCALE * math.log2(math.e)
KEY_BLOCK = 512
BLOCK_SHARDS = KEY_BLOCK // TOK
Q_CHUNK = 256

bf16 = jnp.bfloat16
f32 = jnp.float32
VMEM = pl.BlockSpec(memory_space=pltpu.VMEM)
SMEM = pl.BlockSpec(memory_space=pltpu.SMEM)
ANY = pl.BlockSpec(memory_space=pl.ANY)


def nn(a, b):
    return lax.dot_general(a, b, (((1,), (0,)), ((), ())), preferred_element_type=f32)


def nt(a, b):
    return lax.dot_general(a, b, (((1,), (1,)), ((), ())), preferred_element_type=f32)


def tn(a, b):
    return lax.dot_general(a, b, (((0,), (0,)), ((), ())), preferred_element_type=f32)


def here():
    return {a: lax.axis_index(a) for a in AXES}


def step(me, axis, by):
    return lax.rem(me[axis] + by, SIZE[axis])


def at(me, **moved):
    return tuple(step(me, a, moved[a]) if a in moved else me[a] for a in AXES)


def greet(peers):
    barrier = pltpu.get_barrier_semaphore()
    for p in peers:
        pl.semaphore_signal(barrier, inc=1, device_id=p, device_id_type=MESH)
    pl.semaphore_wait(barrier, len(peers))


class Copies:
    def __init__(self, send_sems, recv_sems):
        self.send_sems, self.recv_sems, self.used, self.started = send_sems, recv_sems, 0, []

    def make(self, src, dst, target):
        k = self.used
        self.used += 1
        return pltpu.make_async_remote_copy(
            src_ref=src,
            dst_ref=dst,
            send_sem=self.send_sems.at[k],
            recv_sem=self.recv_sems.at[k],
            device_id=target,
            device_id_type=MESH,
        )

    def send(self, src, dst, target):
        copy = self.make(src, dst, target)
        copy.start()
        self.started.append(copy)
        return copy

    def finish(self):
        for copy in self.started:
            copy.wait_send()


def sems(count):
    return [pltpu.SemaphoreType.DMA((count,)), pltpu.SemaphoreType.DMA((count,))]


def params(ident, mib=60):
    return pltpu.CompilerParams(
        collective_id=ident, has_side_effects=True, vmem_limit_bytes=mib * 2**20
    )


def three(ref):
    return ref[0].astype(f32) + ref[1].astype(f32) + ref[2].astype(f32)


def heads_in(ref, scratch):
    for h in range(HEADS):
        scratch[pl.ds(h * TOK, TOK), :] = ref[:, pl.ds(h * HD, HD)]


def shard_of(me):
    return ((me["z"] * 4 + me["y"]) * 2 + me["xh"]) * 2 + me["c"]


class Rows:
    def __init__(self, me, copies, source, slots):
        self.me, self.copies, self.slots = me, copies, slots
        half = TOK // 2
        n = me["n"]
        self.mine = pl.ds(pl.multiple_of(half * n, half), half)
        self.theirs = pl.ds(pl.multiple_of(half * (1 - n), half), half)
        y, c = me["y"], me["c"]
        own = slots.at[y, c]
        self.far = {
            d: copies.send(source.at[self.mine], own.at[self.mine], at(me, y=d)) for d in (1, 3, 2)
        }
        self.near = [copies.send(source, own, at(me, c=1))]
        self.across = {}

    def slot(self, d, rows):
        return self.slots.at[lax.rem(self.me["y"] + (4 - d), 4), self.me["c"], rows]

    def pass_on(self):
        for d in (1, 3, 2):
            self.far[d].wait_recv()
            got = self.slot(d, self.mine)
            self.across[d] = self.copies.send(got, got, at(self.me, n=1))
            self.near.append(self.copies.send(got, got, at(self.me, c=1)))

    def complete(self):
        for d in (1, 3, 2):
            self.across[d].wait_recv()
            got = self.slot(d, self.theirs)
            self.near.append(self.copies.send(got, got, at(self.me, c=1)))

    def wait(self):
        for copy in self.near:
            copy.wait_recv()


def attend_kernel(
    x, q_in, start, ids, og, aa, kv, o, exact, lse, og_all, aa_all,
    q, top, total, acc, low_acc, send_sems, recv_sems, local_sems,
):
    me = here()
    z, y, xh, c = me["z"], me["y"], me["xh"], me["c"]
    partner, across, other = at(me, c=1), at(me, xh=1), at(me, n=1)
    ys = {d: at(me, y=d) for d in (1, 2, 3)}
    zs = {d: at(me, z=d) for d in (1, 2, 3)}
    kv[z, y, xh, c] = x[...]
    greet([partner, across, other, *ys.values(), *zs.values()])
    copies = Copies(send_sems, recv_sems)
    mine = kv.at[z, y, xh, c]
    first = copies.send(mine, mine, across)
    to_core = [copies.send(mine, mine, partner)]
    heads_in(q_in, q)
    top[...] = jnp.full_like(top, big_negative)
    total[...] = jnp.zeros_like(total)
    acc[...] = jnp.zeros_like(acc)
    low_acc[...] = jnp.zeros_like(low_acc)
    first.wait_recv()
    theirs = kv.at[z, y, 1 - xh, c]
    to_core.append(copies.send(theirs, theirs, partner))
    half = TOK // 2
    low, high = pl.ds(0, half), pl.ds(half, half)

    def slot(zi, yi, rows):
        return kv.at[zi, yi, :, c, rows]

    first_low, first_high = {}, {}
    for d in (1, 3, 2):
        first_low[d] = copies.send(slot(z, y, low), slot(z, y, low), ys[d])
        first_high[d] = copies.send(slot(z, y, high), slot(z, y, high), zs[d])
    second_low, second_high = {}, {}
    for e in (0, 1, 3, 2):
        yi, zi = lax.rem(y + (4 - e), 4), lax.rem(z + (4 - e), 4)
        if e:
            first_low[e].wait_recv()
            to_core.append(copies.send(slot(z, yi, low), slot(z, yi, low), partner))
            first_high[e].wait_recv()
            to_core.append(copies.send(slot(zi, y, high), slot(zi, y, high), partner))
        for d in (1, 3, 2):
            second_low[e, d] = copies.send(slot(z, yi, low), slot(z, yi, low), zs[d])
            second_high[e, d] = copies.send(slot(zi, y, high), slot(zi, y, high), ys[d])
    local = []
    for i, (source, slots) in enumerate(((og, og_all), (aa, aa_all))):
        local.append(pltpu.make_async_copy(source, slots.at[y, c], local_sems.at[i]))
        local[-1].start()
    for e in (0, 1, 3, 2):
        for d in (1, 3, 2):
            yi, zi = lax.rem(y + (4 - e), 4), lax.rem(z + (4 - e), 4)
            yd, zd = lax.rem(y + (4 - d), 4), lax.rem(z + (4 - d), 4)
            second_low[e, d].wait_recv()
            to_core.append(copies.send(slot(zd, yi, low), slot(zd, yi, low), partner))
            second_high[e, d].wait_recv()
            to_core.append(copies.send(slot(zi, yd, high), slot(zi, yd, high), partner))
    for copy in to_core:
        copy.wait_recv()
    gathers = [Rows(me, copies, og, og_all), Rows(me, copies, aa, aa_all)]

    last = shard_of(me) // BLOCK_SHARDS

    def block(index, masked):
        zi, yi = index // 4, lax.rem(index, 4)
        shape = (KEY_BLOCK, HD)
        keys = kv[zi, yi, :, :, :, pl.ds(0, HD)].reshape(shape)
        values = kv[zi, yi, :, :, :, pl.ds(HD, HD)].reshape(shape).T
        for chunk in range(NQ // Q_CHUNK):
            cs = pl.ds(chunk * Q_CHUNK, Q_CHUNK)
            scores = nt(keys, q[cs, :]) * SCALE_LOG2
            if masked:
                key_ids = index * KEY_BLOCK + lax.broadcasted_iota(jnp.int32, (KEY_BLOCK, Q_CHUNK), 0)
                allowed = (key_ids >= start[:, cs]) & (key_ids <= ids[:, cs])
                scores = jnp.where(allowed, scores, big_negative)
            old = top[:, cs]
            new = jnp.maximum(old, jnp.max(scores, axis=0, keepdims=True))
            probs = jnp.exp2(scores - new)
            if masked:
                probs = jnp.where(allowed, probs, 0.0)
            fade = jnp.exp2(old - new)
            top[:, cs] = new
            total[:, cs] = total[:, cs] * fade + jnp.sum(probs, axis=0, keepdims=True)
            upper = probs.astype(bf16)
            rest = (probs - upper.astype(f32)).astype(bf16)
            acc[:, cs] = acc[:, cs] * fade + nn(values, upper)
            low_acc[:, cs] = low_acc[:, cs] * fade + nn(values, rest)

    middle = (last + 1) // 2

    @pl.when(last > 0)
    def _():
        block(0, True)

    @pl.loop(1, middle)
    def _(index):
        block(index, False)

    for rows in gathers:
        rows.pass_on()

    @pl.loop(jnp.maximum(middle, 1), last)
    def _(index):
        block(index, False)

    kept = start[...] < last * KEY_BLOCK
    top[...] = jnp.where(kept, top[...], big_negative)
    kept = kept.astype(f32)
    total[...] = total[...] * kept
    acc[...] = acc[...] * kept
    low_acc[...] = low_acc[...] * kept
    block(last, True)
    inverse = 1.0 / total[...]
    rows = acc[...] * inverse
    exact[...] = rows + low_acc[...] * inverse
    rows = rows.T.astype(bf16)
    for h in range(HEADS):
        o[:, pl.ds(h * HD, HD)] = rows[h * TOK : (h + 1) * TOK]
    lse[...] = top[...] + jnp.log2(total[...])
    for rows in gathers:
        rows.complete()
    for rows in gathers:
        rows.wait()
    for copy in local:
        copy.wait()
    copies.finish()


def attend(*arrays):
    slots = jax.ShapeDtypeStruct((4, 2, TOK, D), bf16)
    return pl.pallas_call(
        attend_kernel,
        out_shape=(
            jax.ShapeDtypeStruct((4, 4, 2, 2, TOK, 2 * HD), bf16),
            jax.ShapeDtypeStruct((TOK, HEADS * HD), bf16),
            jax.ShapeDtypeStruct((HD, NQ), f32),
            jax.ShapeDtypeStruct((1, NQ), f32),
            slots,
            slots,
        ),
        in_specs=[VMEM] * 6,
        out_specs=(VMEM,) * 4 + (ANY,) * 2,
        scratch_shapes=[
            pltpu.VMEM((NQ, HD), bf16),
            pltpu.VMEM((1, NQ), f32),
            pltpu.VMEM((1, NQ), f32),
            pltpu.VMEM((HD, NQ), f32),
            pltpu.VMEM((HD, NQ), f32),
            *sems(110),
            pltpu.SemaphoreType.DMA((2,)),
        ],
        compiler_params=params(1),
    )(*arrays)


def mlp_kernel(*refs):
    attn_low, w_out, x, gain, gate_w, up_w, og, og_hbm, w_down_hbm = refs[:9]
    resid, grad_resid, gain_terms, up_terms, down_terms, gate_sum, down_sum = refs[9:16]
    pa, pb, wd, og_all, act_all, grad_hidden, hidden, ggp, gup, bk, dn, bk_core, dn_core, bk_sent, bk_in = refs[16:31]
    nb, rn, gate_terms, gate_in, send_sems, recv_sems, local_sems = refs[31:]
    me = here()
    z, y, c = me["z"], me["y"], me["c"]
    partner, other = at(me, c=1), at(me, n=1)
    ys = {d: at(me, y=d) for d in (1, 2, 3)}
    zs = {d: at(me, z=d) for d in (1, 2, 3)}
    greet([partner, other, *ys.values(), *zs.values()])
    copies = Copies(send_sems, recv_sems)
    units = pl.ds(pl.multiple_of((y * 2 + c) * UNITS, 16), UNITS)
    load_down = pltpu.make_async_copy(w_down_hbm.at[units], wd, local_sems.at[0])
    load_down.start()
    load_og = pltpu.make_async_copy(og_hbm, og_all, local_sems.at[1])
    load_og.start()
    pa[...] = nn(attn_low[...], w_out[...]).astype(bf16)
    swap = copies.send(pa, pb, other)
    load_down.wait()
    load_og.wait()
    pair = (2 * TOK, D)
    for yi in range(4):
        grad_hidden[yi] = nt(og_all[yi].reshape(pair), wd[...])
    swap.wait_recv()
    total = x[...].astype(f32) + (pa[...].astype(f32) + pb[...].astype(f32))
    resid[...] = total
    inverse = lax.rsqrt(jnp.mean(total * total, axis=-1, keepdims=True) + rms_eps)
    act_all[y, c] = (total * inverse * gain[...]).astype(bf16)

    own = act_all.at[y, c]
    far = {d: copies.send(own, own, ys[d]) for d in (1, 3)}
    to_core = {0: [copies.send(own, own, partner)]}
    bk_cores, dn_cores, bk_moves = {}, {}, {}

    def block(d):
        yi = step(me, "y", d)
        rows = act_all[yi].reshape(pair)
        gate = nn(rows, gate_w[...])
        up = nn(rows, up_w[...])
        sigmoid = 1.0 / (1.0 + jnp.exp(-gate))
        silu = gate * sigmoid
        grads = grad_hidden[yi]
        hidden[yi] = (silu * up).astype(bf16)
        ggp[yi] = (grads * up * (sigmoid * (1.0 + gate * (1.0 - sigmoid)))).astype(bf16)
        gup[yi] = (grads * silu).astype(bf16)
        both = nt(ggp[yi], gate_w[...]) + nt(gup[yi], up_w[...])
        bk[yi] = both.astype(bf16).reshape(2, TOK, D)
        bk_cores[d] = copies.send(bk.at[yi, 1 - c], bk_core.at[yi], partner)
        dn[yi] = nn(hidden[yi], wd[...]).astype(bf16).reshape(2, TOK, D)
        dn_cores[d] = copies.send(dn.at[yi, 1 - c], dn_core.at[yi], partner)

    def pass_block(d):
        yi = step(me, "y", d)
        bk_cores[d].wait_recv()
        bk_sent[yi] = (bk[yi, c].astype(f32) + bk_core[yi].astype(f32)).astype(bf16)
        if d:
            bk_moves[d] = copies.send(bk_sent.at[yi], bk_in.at[d - 1], ys[d])

    def sum_down(d):
        yi = step(me, "y", d)
        dn_cores[d].wait_recv()
        down_sum[yi] = (dn[yi, c].astype(f32) + dn_core[yi].astype(f32)).astype(bf16)

    half = TOK // 2
    low, high = pl.ds(0, half), pl.ds(half, half)
    to_core[0][0].wait_recv()
    block(0)
    relay = {}
    for d, rows in ((1, low), (3, high)):
        far[d].wait_recv()
        yi = lax.rem(y + (4 - d), 4)
        got = act_all.at[yi, c]
        relay[d] = copies.send(got.at[rows], got.at[rows], ys[d])
        to_core[4 - d] = [copies.send(got, got, partner)]
    to_core[3][0].wait_recv()
    block(3)
    pass_block(0)
    to_core[2] = []
    for d, rows in ((1, low), (3, high)):
        relay[d].wait_recv()
        got = act_all.at[step(me, "y", 2), c, rows]
        to_core[2].append(copies.send(got, got, partner))
    to_core[1][0].wait_recv()
    block(1)
    pass_block(3)
    for copy in to_core[2]:
        copy.wait_recv()
    block(2)
    pass_block(1)
    pass_block(2)

    everything = (GROUP * TOK, D)
    all_units = (GROUP * TOK, UNITS)
    gate_terms[...] = tn(ggp[...].reshape(all_units), act_all[...].reshape(everything)).astype(bf16)

    def z_cols(d):
        return pl.ds(pl.multiple_of(step(me, "z", d) * 384, 384), 384)

    gate_moves = {
        d: copies.send(gate_terms.at[:, z_cols(d)], gate_in.at[d - 1], zs[d]) for d in (1, 3, 2)
    }
    up_terms[...] = tn(gup[...].reshape(all_units), act_all[...].reshape(everything)).astype(bf16)
    back = bk_sent[y].astype(f32)
    for d in (1, 3, 2):
        bk_moves[d].wait_recv()
        back = back + bk_in[d - 1].astype(f32)
    nb[...] = back.astype(bf16)
    swap_back = copies.send(nb, rn, other)
    down_terms[...] = tn(hidden[...].reshape(all_units), og_all[...].reshape(everything)).astype(bf16)
    for d in range(4):
        sum_down(d)
    swap_back.wait_recv()
    grad_act = nb[...].astype(f32) + rn[...].astype(f32)
    normed = resid[...] * inverse
    gain_terms[...] = jnp.sum(grad_act * normed, axis=0, keepdims=True)
    grad_normed = grad_act * gain[...]
    inner = jnp.mean(grad_normed * normed, axis=-1, keepdims=True)
    grad_resid[...] = og[...].astype(f32) + inverse * (grad_normed - normed * inner)
    for d in (1, 3, 2):
        gate_moves[d].wait_recv()
    gate_sum[...] = (gate_terms[:, z_cols(0)].astype(f32) + three(gate_in)).T.astype(bf16)
    copies.finish()


def feed_forward(*arrays):
    rows = pltpu.VMEM((TOK, D), bf16)
    return pl.pallas_call(
        mlp_kernel,
        out_shape=[
            jax.ShapeDtypeStruct((TOK, D), f32),
            jax.ShapeDtypeStruct((TOK, D), f32),
            jax.ShapeDtypeStruct((1, D), f32),
            jax.ShapeDtypeStruct((UNITS, D), bf16),
            jax.ShapeDtypeStruct((UNITS, D), bf16),
            jax.ShapeDtypeStruct((D // 4, UNITS), bf16),
            jax.ShapeDtypeStruct((4, TOK, D), bf16),
        ],
        in_specs=[VMEM] * 7 + [ANY] * 2,
        out_specs=[VMEM] * 7,
        scratch_shapes=[
            rows,
            rows,
            pltpu.VMEM((UNITS, D), bf16),
            pltpu.VMEM((4, 2, TOK, D), bf16),
            pltpu.VMEM((4, 2, TOK, D), bf16),
            pltpu.VMEM((4, 2 * TOK, UNITS), f32),
            *[pltpu.VMEM((4, 2 * TOK, UNITS), bf16)] * 3,
            *[pltpu.VMEM((4, 2, TOK, D), bf16)] * 2,
            *[pltpu.VMEM((4, TOK, D), bf16)] * 3,
            pltpu.VMEM((3, TOK, D), bf16),
            rows,
            rows,
            pltpu.VMEM((UNITS, D), bf16),
            pltpu.VMEM((3, UNITS, D // 4), bf16),
            *sems(40),
            pltpu.SemaphoreType.DMA((2,)),
        ],
        compiler_params=params(2),
    )(*arrays)


def back_kernel(*refs):
    (q_in, kv, exact, start, ids, lse, grad_resid, w_out, attn_low, cosine, sine, normed, inverse) = refs[:13]
    gain, resid, mlp_gain_terms, gate_sum, w_qkv_hbm, act_hbm, *terms, down_terms = refs[13:22]
    in_grad, layer_out, sum_gate, sum_up, sum_down, sum_qkv, sum_out, small_out = refs[22:30]
    (q, g, acc, dkv, cb, s, r1a, r1b, ta, tb, r2a, r2b, u, r3, w_qkv, act_all, gb_all, al_heads, al_all) = refs[30:49]
    gp, gp_flat, gp_all, part, part_other, small, e1, e2, e3, f1, f2 = refs[49:60]
    own, first_in, mid = refs[60:62], refs[62:64], refs[64:66]
    second_in, summed, third_in = (refs[66 + 3 * k : 69 + 3 * k] for k in range(3))
    q_terms, q_first, q_mid, q_second, q_summed, q_third = refs[75:81]
    down_own, down_in, down_part, down_other, send_sems, recv_sems, local_sems = refs[81:]

    me = here()
    z, y, xh, c, n = (me[a] for a in AXES)
    partner, across, other = at(me, c=1), at(me, xh=1), at(me, n=1)
    ys = {d: at(me, y=d) for d in (1, 2, 3)}
    zs = {d: at(me, z=d) for d in (1, 2, 3)}
    near_moves = [(d, e) for d in (1, 3, 2, 0) for e in (0, 1) if d or e]
    near = {m: at(me, y=m[0], xh=m[1]) for m in near_moves}
    group = {m: at(me, y=m[0], c=m[1]) for m in near_moves}
    greet([other, *zs.values(), *near.values(), *(group[m] for m in near_moves if m[1])])
    copies = Copies(send_sems, recv_sems)
    half = TOK // 2
    low, high = pl.ds(0, half), pl.ds(half, half)

    local = []

    def load(src, dst):
        copy = pltpu.make_async_copy(src, dst, local_sems.at[len(local)])
        copy.start()
        local.append(copy)
        return copy

    def z_cols(d):
        return pl.ds(pl.multiple_of(step(me, "z", d) * 384, 384), 384)

    second = {}

    def send_second(i, source, in_ref):
        for m in near_moves:
            second[i, m] = copies.send(
                source(step(me, "y", m[0]), step(me, "xh", m[1])), in_ref.at[y, xh], near[m]
            )

    def strip(yi, xi):
        return pl.ds(pl.multiple_of(96 * yi + 48 * xi, 48), 48)

    send_second(0, lambda yi, xi: gate_sum.at[strip(yi, xi)], second_in[0])
    second_in[0][y, xh] = gate_sum[strip(y, xh), :]
    first = {}

    def send_first(i, d):
        first[i, d] = copies.send(terms[i].at[:, z_cols(d)], first_in[i].at[d - 1], zs[d])

    for d in (1, 3, 2):
        send_first(0, d)
    for d in (1, 3):
        send_first(1, d)

    gb_all[y, c] = grad_resid[...].astype(bf16)
    branch = gb_all[y, c]
    branches = Rows(me, copies, gb_all.at[y, c], gb_all)
    down_moves = {
        d: copies.send(down_terms.at[step(me, "y", d)], down_in.at[d - 1], ys[d]) for d in (1, 3, 2)
    }
    load_down = load(down_terms.at[y], down_own)
    for h in range(HEADS):
        al_heads[h] = attn_low[:, pl.ds(h * HD, HD)]

    def head_of(d, e):
        taker = step(me, "y", d) * 2 + step(me, "c", e)
        return jnp.where(taker < HEADS, taker, 0)

    al_moves = [
        copies.send(al_heads.at[head_of(*m)], al_all.at[y, c], group[m]) for m in near_moves
    ]
    al_all[y, c] = al_heads[head_of(0, 0)]
    load_w = load(w_qkv_hbm, w_qkv)
    load_act = load(act_hbm, act_all)
    load_own = [load(terms[i].at[:, z_cols(0)], own[i]) for i in range(2)]

    heads_in(q_in, q)
    grads_in = nt(branch, w_out[...]).astype(bf16)
    for h in range(HEADS):
        g[pl.ds(h * TOK, TOK), :] = grads_in[:, h * HD : (h + 1) * HD]
    balance = jnp.sum(g[...].astype(f32).T * exact[...], axis=0, keepdims=True)
    acc[...] = jnp.zeros_like(acc)
    last = shard_of(me) // BLOCK_SHARDS
    log_total = lse[...]
    earlier = jnp.where(start[...] < last * KEY_BLOCK, log_total, -big_negative)

    def block(index, masked, shift):
        zi, yi = index // 4, lax.rem(index, 4)
        shape = (2, 2, TOK, HD)
        keys = kv[zi, yi, :, :, :, pl.ds(0, HD)].reshape(KEY_BLOCK, HD)
        values = kv[zi, yi, :, :, :, pl.ds(HD, HD)].reshape(KEY_BLOCK, HD)
        keys_t = keys.T
        dk = jnp.zeros((KEY_BLOCK, HD), f32)
        dv = jnp.zeros((KEY_BLOCK, HD), f32)
        for chunk in range(NQ // Q_CHUNK):
            cs = pl.ds(chunk * Q_CHUNK, Q_CHUNK)
            piece = slice(chunk * Q_CHUNK, (chunk + 1) * Q_CHUNK)
            qc, gc = q[cs, :], g[cs, :]
            probs = jnp.exp2(nt(keys, qc) * SCALE_LOG2 - shift[:, piece])
            if masked:
                key_ids = index * KEY_BLOCK + lax.broadcasted_iota(jnp.int32, (KEY_BLOCK, Q_CHUNK), 0)
                allowed = (key_ids >= start[:, cs]) & (key_ids <= ids[:, cs])
                probs = jnp.where(allowed, probs, 0.0)
            grads = (probs * (nt(values, gc) - balance[:, piece])).astype(bf16)
            dv = dv + nn(probs.astype(bf16), gc)
            dk = dk + nn(grads, qc)
            acc[:, cs] = acc[:, cs] + nn(keys_t, grads)
        dkv[zi, yi, :, :, :, pl.ds(0, HD)] = (dk * SCALE).astype(bf16).reshape(shape)
        dkv[zi, yi, :, :, :, pl.ds(HD, HD)] = dv.astype(bf16).reshape(shape)

    middle = (last + 1) // 2

    @pl.when(last > 0)
    def _():
        block(0, True, earlier)

    @pl.loop(1, middle)
    def _(index):
        block(index, False, earlier)

    branches.pass_on()

    @pl.loop(jnp.maximum(middle, 1), last)
    def _(index):
        block(index, False, earlier)

    block(last, True, log_total)

    @pl.loop(last + 1, TOKENS // KEY_BLOCK)
    def _(index):
        dkv[index // 4, lax.rem(index, 4)] = jnp.zeros((2, 2, TOK, 2 * HD), bf16)

    kv_cores = [
        copies.send(dkv.at[:, :, :, 1 - c, rows], cb.at[:, :, :, rows], partner)
        for rows in (low, high)
    ]
    first_a, first_b, second_a, second_b = {}, {}, {}, {}
    for rows, core in ((low, kv_cores[0]), (high, kv_cores[1])):
        core.wait_recv()
        for zi in range(4):
            s[zi, :, :, rows] = (dkv[zi, :, :, c, rows].astype(f32) + cb[zi, :, :, rows].astype(f32)).astype(bf16)
        for d in (1, 3, 2):
            if rows is low:
                first_a[d] = copies.send(s.at[step(me, "z", d), :, :, low], r1a.at[d - 1], zs[d])
            else:
                first_b[d] = copies.send(s.at[:, step(me, "y", d), :, high], r1b.at[d - 1], ys[d])

    send_first(1, 2)
    load_down.wait()
    mlp_out = down_own[...].astype(f32)
    for d in (1, 3, 2):
        down_moves[d].wait_recv()
        mlp_out = mlp_out + down_in[d - 1].astype(f32)
    down_part[...] = mlp_out.astype(bf16)
    down_swap = copies.send(down_part, down_other, other)
    turned_back = (acc[...] * SCALE).T

    def revert(rows):
        return rows * cosine[...] - pltpu.roll(rows, HD // 2, 1) * sine[...]

    def keep_head(h, rows):
        low_rows = rows.astype(bf16)
        gp[h] = low_rows
        gp_flat[:, pl.ds(h * HD, HD)] = low_rows
        small[pl.ds(2, 1), pl.ds(h * HD, HD)] = jnp.sum(low_rows.astype(f32), axis=0, keepdims=True)

    small[...] = jnp.zeros_like(small)
    small[pl.ds(1, 1), :] = mlp_gain_terms[...]
    for h in range(HEADS):
        keep_head(h, revert(turned_back[h * TOK : (h + 1) * TOK]))
    load_w.wait()
    front = HEADS * HD
    partial = nt(gp_flat[:, pl.ds(0, front)], w_qkv[:, pl.ds(0, front)])

    for d in (1, 3, 2):
        first_a[d].wait_recv()
    ta[...] = (s[z, :, :, low].astype(f32) + three(r1a)).astype(bf16)
    for d in (1, 3, 2):
        second_a[d] = copies.send(ta.at[step(me, "y", d)], r2a.at[d - 1], ys[d])
    for d in (1, 3, 2):
        first_b[d].wait_recv()
    tb[...] = (s[:, y, :, high].astype(f32) + three(r1b)).astype(bf16)
    for d in (1, 3, 2):
        second_b[d] = copies.send(tb.at[step(me, "z", d)], r2b.at[d - 1], zs[d])
    for d in (1, 3, 2):
        second_a[d].wait_recv()
        second_b[d].wait_recv()
    ua = ta[y].astype(f32) + three(r2a)
    ub = tb[z].astype(f32) + three(r2b)
    u[:, low] = ua.astype(bf16)
    u[:, high] = ub.astype(bf16)
    kv_last = copies.send(u.at[1 - xh], r3, across)

    branches.complete()
    kv_last.wait_recv()
    grad_kv = u[xh].astype(f32) + r3[...].astype(f32)
    keep_head(HEADS, revert(grad_kv[:, :HD]))
    keep_head(HEADS + 1, grad_kv[:, HD:])
    gp_moves = [
        copies.send(gp.at[step(me, "y", m[0]) * 2 + step(me, "c", m[1])], gp_all.at[y, c], group[m])
        for m in near_moves
    ]
    gp_all[y, c] = gp[y * 2 + c]
    back = pl.ds(front, 2 * HD)
    part[...] = (partial + nt(gp_flat[:, back], w_qkv[:, back])).astype(bf16)
    swap = copies.send(part, part_other, other)
    load_act.wait()
    for copy in gp_moves:
        copy.wait_recv()
    q_terms[pl.ds(0, HD), :] = tn(
        gp_all[...].reshape(GROUP * TOK, HD), act_all[...].reshape(GROUP * TOK, D)
    ).astype(bf16)

    q_one = {d: copies.send(q_terms.at[pl.ds(0, HD), z_cols(d)], q_first.at[d - 1, pl.ds(0, HD)], zs[d]) for d in (1, 3, 2)}
    branches.wait()
    for copy in al_moves:
        copy.wait_recv()
    q_terms[pl.ds(HD, HD), :] = tn(
        al_all[...].reshape(GROUP * TOK, HD), gb_all[...].reshape(GROUP * TOK, D)
    ).astype(bf16)
    q_two = {d: copies.send(q_terms.at[pl.ds(HD, HD), z_cols(d)], q_first.at[d - 1, pl.ds(HD, HD)], zs[d]) for d in (1, 3, 2)}

    swap.wait_recv()
    grad_act = part[...].astype(f32) + part_other[...].astype(f32)
    small[pl.ds(0, 1), :] = jnp.sum(grad_act * normed[...], axis=0, keepdims=True)
    small_one = {d: copies.send(small, e1.at[d - 1], zs[d]) for d in (1, 3, 2)}
    grad_normed = grad_act * gain[...]
    inner = jnp.mean(grad_normed * normed[...], axis=-1, keepdims=True)
    in_grad[...] = (grad_resid[...] + inverse[...] * (grad_normed - normed[...] * inner)).astype(bf16)

    for d in (1, 3, 2):
        small_one[d].wait_recv()
    f1[...] = small[...] + three(e1)
    small_two = {m: copies.send(f1, e2.at[k], near[m]) for k, m in enumerate(near_moves)}
    def send_mid(i, total, mid_ref, in_ref):
        turned = total.T.astype(bf16)
        for yi in range(4):
            for xi in range(2):
                rows = 96 * yi + 48 * xi
                mid_ref[yi, xi] = turned[rows : rows + 48]
        send_second(i, lambda yi, xi: mid_ref.at[yi, xi], in_ref)
        in_ref[y, xh] = mid_ref[y, xh]

    for i in range(2):
        load_own[i].wait()
        for d in (1, 3, 2):
            first[i, d].wait_recv()
        send_mid(i + 1, own[i][...].astype(f32) + three(first_in[i]), mid[i], second_in[i + 1])
    for d in (1, 3, 2):
        q_one[d].wait_recv()
        q_two[d].wait_recv()
    send_mid(3, q_terms[:, z_cols(0)].astype(f32) + three(q_first), q_mid, q_second)

    for m in near_moves:
        small_two[m].wait_recv()
    f2[...] = f1[...]
    for k in range(len(near_moves)):
        f2[...] = f2[...] + e2[k]
    small_three = copies.send(f2, e3, partner)
    keep, give = pl.ds(pl.multiple_of(24 * c, 8), 24), pl.ds(pl.multiple_of(24 * (1 - c), 8), 24)
    third = []
    all_summed = [*summed, q_summed]
    all_second = [*second_in, q_second]
    all_third = [*third_in, q_third]
    for i in range(4):
        for m in near_moves:
            second[i, m].wait_recv()
        all_summed[i][...] = all_second[i][:, 0].astype(f32) + all_second[i][:, 1].astype(f32)
        third.append(copies.send(all_summed[i].at[:, give], all_third[i], partner))
    for i, outs in enumerate(((sum_gate,), (sum_up,), (sum_down,), (sum_qkv, sum_out))):
        third[i].wait_recv()
        for yi in range(4):
            mine_sum, their_sum = all_summed[i][yi, keep], all_third[i][yi]
            pair = (jnp.where(c == 0, mine_sum, their_sum), jnp.where(c == 0, their_sum, mine_sum))
            for e in range(2):
                k = 2 * yi + e
                if i < 3:
                    outs[0][:, pl.ds(k * UNITS, UNITS)] = pair[e]
                else:
                    outs[0][:, pl.ds(k * HD, HD)] = pair[e][:, :HD]
                    if k < HEADS:
                        outs[1][:, pl.ds(k * HD, HD)] = pair[e][:, HD:]
    small_three.wait_recv()
    small_out[...] = f2[...] + e3[...]
    down_swap.wait_recv()
    layer_out[...] = (
        resid[...] + (down_part[...].astype(f32) + down_other[...].astype(f32))
    ).astype(bf16)
    copies.finish()


def back(*arrays):
    half = TOK // 2
    wide = 2 * HD
    return pl.pallas_call(
        back_kernel,
        out_shape=[
            jax.ShapeDtypeStruct((TOK, D), bf16),
            jax.ShapeDtypeStruct((TOK, D), bf16),
            *[jax.ShapeDtypeStruct((24, FF // 2), f32)] * 3,
            jax.ShapeDtypeStruct((24, (HEADS + 2) * HD), f32),
            jax.ShapeDtypeStruct((24, HEADS * HD), f32),
            jax.ShapeDtypeStruct((8, D), f32),
        ],
        in_specs=[VMEM] * 17 + [ANY] * 5,
        out_specs=[VMEM] * 8,
        scratch_shapes=[
            pltpu.VMEM((NQ, HD), bf16),
            pltpu.VMEM((NQ, HD), bf16),
            pltpu.VMEM((HD, NQ), f32),
            pltpu.VMEM((4, 4, 2, 2, TOK, wide), bf16),
            pltpu.VMEM((4, 4, 2, TOK, wide), bf16),
            pltpu.VMEM((4, 4, 2, TOK, wide), bf16),
            pltpu.VMEM((3, 4, 2, half, wide), bf16),
            pltpu.VMEM((3, 4, 2, half, wide), bf16),
            pltpu.VMEM((4, 2, half, wide), bf16),
            pltpu.VMEM((4, 2, half, wide), bf16),
            pltpu.VMEM((3, 2, half, wide), bf16),
            pltpu.VMEM((3, 2, half, wide), bf16),
            pltpu.VMEM((2, TOK, wide), bf16),
            pltpu.VMEM((TOK, wide), bf16),
            pltpu.VMEM((D, (HEADS + 2) * HD), bf16),
            pltpu.VMEM((4, 2, TOK, D), bf16),
            pltpu.VMEM((4, 2, TOK, D), bf16),
            pltpu.VMEM((HEADS, TOK, HD), bf16),
            pltpu.VMEM((4, 2, TOK, HD), bf16),
            pltpu.VMEM((HEADS + 2, TOK, HD), bf16),
            pltpu.VMEM((TOK, (HEADS + 2) * HD), bf16),
            pltpu.VMEM((4, 2, TOK, HD), bf16),
            pltpu.VMEM((TOK, D), bf16),
            pltpu.VMEM((TOK, D), bf16),
            pltpu.VMEM((8, D), f32),
            pltpu.VMEM((3, 8, D), f32),
            pltpu.VMEM((7, 8, D), f32),
            pltpu.VMEM((8, D), f32),
            pltpu.VMEM((8, D), f32),
            pltpu.VMEM((8, D), f32),
            *[pltpu.VMEM((UNITS, 384), bf16)] * 2,
            *[pltpu.VMEM((3, UNITS, 384), bf16)] * 2,
            *[pltpu.VMEM((4, 2, 48, UNITS), bf16)] * 2,
            *[pltpu.VMEM((4, 2, 48, UNITS), bf16)] * 3,
            *[pltpu.VMEM((4, 48, UNITS), f32)] * 3,
            *[pltpu.VMEM((4, 24, UNITS), f32)] * 3,
            pltpu.VMEM((wide, D), bf16),
            pltpu.VMEM((3, wide, 384), bf16),
            pltpu.VMEM((4, 2, 48, wide), bf16),
            pltpu.VMEM((4, 2, 48, wide), bf16),
            pltpu.VMEM((4, 48, wide), f32),
            pltpu.VMEM((4, 24, wide), f32),
            pltpu.VMEM((TOK, D), bf16),
            pltpu.VMEM((3, TOK, D), bf16),
            pltpu.VMEM((TOK, D), bf16),
            pltpu.VMEM((TOK, D), bf16),
            *sems(140),
            pltpu.SemaphoreType.DMA((9,)),
        ],
        compiler_params=params(9, 62),
    )(*arrays)


def row_starts(lengths, token_ids):
    ends = jnp.cumsum(lengths)
    before = ends[None, :] <= token_ids[:, None]
    return jnp.sum(jnp.where(before, lengths[None, :], 0), axis=1)


def rope_tables(positions):
    half = HD // 2
    freqs = rope_base ** (-2.0 * jnp.arange(half, dtype=f32) / HD)
    angles = positions.astype(f32)[:, None] * freqs[None, :]
    cosine, sine = jnp.cos(angles), jnp.sin(angles)
    return jnp.concatenate([cosine, cosine], 1), jnp.concatenate([-sine, sine], 1)


def rotate(values, cosine, sine):
    heads = []
    for h in range(values.shape[1] // HD):
        one = values[:, h * HD : (h + 1) * HD]
        swapped = jnp.concatenate([one[:, HD // 2 :], one[:, : HD // 2]], axis=1)
        heads.append(one * cosine + swapped * sine)
    return jnp.concatenate(heads, axis=1)


def normalize(values):
    inverse = lax.rsqrt(jnp.mean(values * values, axis=-1) + rms_eps)
    return (values * inverse[:, None], inverse)


def shards(
    layer_in, lengths, norm_attn, w_qkv, qkv_bias, w_out, norm_mlp, w_gate, w_up, w_down, out_grad
):
    shard = lax.axis_index(WIDE)
    member = lax.axis_index(("y", "c"))
    own_ids = shard * TOK + jnp.arange(TOK, dtype=jnp.int32)
    seq_starts = row_starts(lengths, own_ids)
    cosine, sine = rope_tables(own_ids - seq_starts)
    start = jnp.tile(seq_starts, HEADS)[None]
    ids = jnp.tile(own_ids, HEADS)[None]
    gate_w = lax.dynamic_slice(w_gate, (0, member * UNITS), (D, UNITS))
    up_w = lax.dynamic_slice(w_up, (0, member * UNITS), (D, UNITS))

    input_f32 = layer_in.astype(f32)
    normed_attn, inverse_attn = normalize(input_f32)
    act_attn = (normed_attn * norm_attn).astype(bf16)
    projected = nn(act_attn, w_qkv) + qkv_bias[0]
    turned = rotate(projected[:, : (HEADS + 1) * HD], cosine, sine).astype(bf16)
    queries = turned[:, : HEADS * HD]
    kv_own = jnp.concatenate(
        [turned[:, HEADS * HD :], projected[:, (HEADS + 1) * HD :].astype(bf16)], axis=1
    )
    kv, attn_low, exact, lse, out_grad_all, act_attn_all = attend(
        kv_own, queries, start, ids, out_grad, act_attn
    )
    resid, grad_resid, gain_terms, up_terms, down_terms, gate_sum, down_sum = feed_forward(
        attn_low, w_out, layer_in, norm_mlp[None], gate_w, up_w, out_grad, out_grad_all, w_down
    )
    in_grad, layer_out, sum_gate, sum_up, sum_down, sum_qkv, sum_out, small = back(
        queries, kv, exact, start, ids, lse, grad_resid, w_out, attn_low, cosine, sine, normed_attn,
        inverse_attn[:, None], norm_attn[None], resid, gain_terms, gate_sum,
        w_qkv, act_attn_all, up_terms, down_terms, down_sum,
    )
    norms = lax.dynamic_slice(small, (0, shard * 24), (2, 24))
    bias = lax.dynamic_slice(
        small[2, : (HEADS + 2) * HD].reshape(HEADS + 2, HD), (0, shard * 2), (HEADS + 2, 2)
    )
    return (
        layer_out,
        in_grad,
        norms[0],
        sum_qkv,
        bias[None, : HEADS + 1],
        bias[HEADS + 1 :],
        sum_out.T,
        norms[1],
        sum_gate,
        sum_up,
        sum_down.T,
    )


def solution(mesh):
    torus = Mesh(mesh.devices.reshape(4, 4, 2, 2, 2), AXES)
    in_specs = (
        P(WIDE, None),
        P(),
        P(),
        P(None, "n"),
        P("n", None),
        P("n", None),
        P(),
        P(None, "n"),
        P(None, "n"),
        P("n", None),
        P(WIDE, None),
    )
    out_specs = (
        P(WIDE, None),
        P(WIDE, None),
        P(WIDE),
        P(WIDE, "n"),
        P("n", None, WIDE),
        P("n", WIDE),
        P("n", WIDE),
        P(WIDE),
        P(WIDE, "n"),
        P(WIDE, "n"),
        P("n", WIDE),
    )
    return jax.shard_map(
        shards, mesh=torus, in_specs=in_specs, out_specs=out_specs, check_vma=False
    )
```

```python
import functools
import math

import jax
import jax.numpy as jnp
from jax import lax
from jax.experimental import pallas as pl
from jax.experimental.pallas import tpu as pltpu
from jax.sharding import Mesh
from jax.sharding import PartitionSpec as P

HD = 128
QH = 12
KVH = 2
HEADS = QH // KVH
D = 1536
FF = 8960
TOK = 128
TOKENS = 8192
NQ = HEADS * TOK
GROUP = 8
UNITS = FF // 2 // GROUP
WINDOW = 768

AXES = ("z", "y", "xh", "c", "n")
SIZE = {"z": 4, "y": 4, "xh": 2, "c": 2, "n": 2}
WIDE = ("z", "y", "xh", "c")
MESH = pl.DeviceIdType.MESH

rms_eps = 1e-06
rope_base = 10000.0
big_negative = -1e30
SCALE = HD ** (-0.5)
SCALE_LOG2 = SCALE * math.log2(math.e)
KEY_BLOCK = 512
BLOCK_SHARDS = KEY_BLOCK // TOK
Q_CHUNK = 256

bf16 = jnp.bfloat16
f32 = jnp.float32
VMEM = pl.BlockSpec(memory_space=pltpu.VMEM)
SMEM = pl.BlockSpec(memory_space=pltpu.SMEM)
ANY = pl.BlockSpec(memory_space=pl.ANY)


def nn(a, b):
    return lax.dot_general(a, b, (((1,), (0,)), ((), ())), preferred_element_type=f32)


def nt(a, b):
    return lax.dot_general(a, b, (((1,), (1,)), ((), ())), preferred_element_type=f32)


def tn(a, b):
    return lax.dot_general(a, b, (((0,), (0,)), ((), ())), preferred_element_type=f32)


def here():
    return {a: lax.axis_index(a) for a in AXES}


def step(me, axis, by):
    return lax.rem(me[axis] + by, SIZE[axis])


def at(me, **moved):
    return tuple(step(me, a, moved[a]) if a in moved else me[a] for a in AXES)


def greet(peers):
    barrier = pltpu.get_barrier_semaphore()
    for p in peers:
        pl.semaphore_signal(barrier, inc=1, device_id=p, device_id_type=MESH)
    pl.semaphore_wait(barrier, len(peers))


class Copies:
    def __init__(self, send_sems, recv_sems):
        self.send_sems, self.recv_sems, self.used, self.started = send_sems, recv_sems, 0, []

    def make(self, src, dst, target):
        k = self.used
        self.used += 1
        return pltpu.make_async_remote_copy(
            src_ref=src,
            dst_ref=dst,
            send_sem=self.send_sems.at[k],
            recv_sem=self.recv_sems.at[k],
            device_id=target,
            device_id_type=MESH,
        )

    def send(self, src, dst, target):
        copy = self.make(src, dst, target)
        copy.start()
        self.started.append(copy)
        return copy

    def finish(self):
        for copy in self.started:
            copy.wait_send()


def sems(count):
    return [pltpu.SemaphoreType.DMA((count,)), pltpu.SemaphoreType.DMA((count,))]


def params(ident, mib=60):
    return pltpu.CompilerParams(
        collective_id=ident, has_side_effects=True, vmem_limit_bytes=mib * 2**20
    )


def three(ref):
    return ref[0].astype(f32) + ref[1].astype(f32) + ref[2].astype(f32)


def heads_in(ref, scratch):
    for h in range(HEADS):
        scratch[pl.ds(h * TOK, TOK), :] = ref[:, pl.ds(h * HD, HD)]


def shard_of(me):
    return ((me["z"] * 4 + me["y"]) * 2 + me["xh"]) * 2 + me["c"]


class Rows:
    def __init__(self, me, copies, source, slots, split=True):
        self.me, self.copies, self.slots = me, copies, slots
        half = TOK // 2 if split else TOK
        n = me["n"] if split else 0
        self.mine = pl.ds(pl.multiple_of(half * n, half), half)
        self.theirs = pl.ds(pl.multiple_of(half * (1 - n), half), half)
        self.split = split
        y, c = me["y"], me["c"]
        own = slots.at[y, c]
        self.far = {
            d: copies.send(source.at[self.mine], own.at[self.mine], at(me, y=d)) for d in (1, 3, 2)
        }
        self.near = [copies.send(source, own, at(me, c=1))]
        self.across = {}

    def slot(self, d, rows):
        return self.slots.at[lax.rem(self.me["y"] + (4 - d), 4), self.me["c"], rows]

    def pass_on(self):
        for d in (1, 3, 2):
            self.far[d].wait_recv()
            got = self.slot(d, self.mine)
            if self.split:
                self.across[d] = self.copies.send(got, got, at(self.me, n=1))
            self.near.append(self.copies.send(got, got, at(self.me, c=1)))

    def complete(self):
        for d in (1, 3, 2):
            self.across[d].wait_recv()
            got = self.slot(d, self.theirs)
            self.near.append(self.copies.send(got, got, at(self.me, c=1)))

    def wait(self):
        for copy in self.near:
            copy.wait_recv()


def attend_kernel(
    x, q_in, start, ids, og, kv, o, exact, lse, og_all,
    q, top, total, acc, low_acc, send_sems, recv_sems, local_sems,
):
    me = here()
    z, y, xh, c = me["z"], me["y"], me["xh"], me["c"]
    partner, across = at(me, c=1), at(me, xh=1)
    ys = {d: at(me, y=d) for d in (1, 2, 3)}
    zs = {d: at(me, z=d) for d in (1, 2, 3)}
    kv[z, y, xh, c] = x[...]
    greet([partner, across, *ys.values(), *zs.values()])
    copies = Copies(send_sems, recv_sems)
    mine = kv.at[z, y, xh, c]
    first = copies.send(mine, mine, across)
    to_core = [copies.send(mine, mine, partner)]
    heads_in(q_in, q)
    top[...] = jnp.full_like(top, big_negative)
    total[...] = jnp.zeros_like(total)
    acc[...] = jnp.zeros_like(acc)
    low_acc[...] = jnp.zeros_like(low_acc)
    first.wait_recv()
    theirs = kv.at[z, y, 1 - xh, c]
    to_core.append(copies.send(theirs, theirs, partner))
    half = TOK // 2
    low, high = pl.ds(0, half), pl.ds(half, half)

    def slot(zi, yi, rows):
        return kv.at[zi, yi, :, c, rows]

    first_low, first_high = {}, {}
    for d in (1, 3, 2):
        first_low[d] = copies.send(slot(z, y, low), slot(z, y, low), ys[d])
        first_high[d] = copies.send(slot(z, y, high), slot(z, y, high), zs[d])
    second_low, second_high = {}, {}
    for e in (0, 1, 3, 2):
        yi, zi = lax.rem(y + (4 - e), 4), lax.rem(z + (4 - e), 4)
        if e:
            first_low[e].wait_recv()
            to_core.append(copies.send(slot(z, yi, low), slot(z, yi, low), partner))
            first_high[e].wait_recv()
            to_core.append(copies.send(slot(zi, y, high), slot(zi, y, high), partner))
        for d in (1, 3, 2):
            second_low[e, d] = copies.send(slot(z, yi, low), slot(z, yi, low), zs[d])
            second_high[e, d] = copies.send(slot(zi, y, high), slot(zi, y, high), ys[d])
    local = pltpu.make_async_copy(og, og_all.at[y, c], local_sems.at[0])
    local.start()
    gathers = [Rows(me, copies, og, og_all, split=False)]
    for e in (0, 1, 3, 2):
        for d in (1, 3, 2):
            yi, zi = lax.rem(y + (4 - e), 4), lax.rem(z + (4 - e), 4)
            yd, zd = lax.rem(y + (4 - d), 4), lax.rem(z + (4 - d), 4)
            second_low[e, d].wait_recv()
            to_core.append(copies.send(slot(zd, yi, low), slot(zd, yi, low), partner))
            second_high[e, d].wait_recv()
            to_core.append(copies.send(slot(zi, yd, high), slot(zi, yd, high), partner))
    for copy in to_core:
        copy.wait_recv()

    last = shard_of(me) // BLOCK_SHARDS

    def block(index, masked):
        zi, yi = index // 4, lax.rem(index, 4)
        shape = (KEY_BLOCK, HD)
        keys = kv[zi, yi, :, :, :, pl.ds(0, HD)].reshape(shape)
        values = kv[zi, yi, :, :, :, pl.ds(HD, HD)].reshape(shape).T
        for chunk in range(NQ // Q_CHUNK):
            cs = pl.ds(chunk * Q_CHUNK, Q_CHUNK)
            scores = nt(keys, q[cs, :]) * SCALE_LOG2
            if masked:
                key_ids = index * KEY_BLOCK + lax.broadcasted_iota(jnp.int32, (KEY_BLOCK, Q_CHUNK), 0)
                allowed = (key_ids >= start[:, cs]) & (key_ids <= ids[:, cs])
                scores = jnp.where(allowed, scores, big_negative)
            old = top[:, cs]
            new = jnp.maximum(old, jnp.max(scores, axis=0, keepdims=True))
            probs = jnp.exp2(scores - new)
            if masked:
                probs = jnp.where(allowed, probs, 0.0)
            fade = jnp.exp2(old - new)
            top[:, cs] = new
            total[:, cs] = total[:, cs] * fade + jnp.sum(probs, axis=0, keepdims=True)
            upper = probs.astype(bf16)
            rest = (probs - upper.astype(f32)).astype(bf16)
            acc[:, cs] = acc[:, cs] * fade + nn(values, upper)
            low_acc[:, cs] = low_acc[:, cs] * fade + nn(values, rest)

    middle = (last + 1) // 2

    @pl.when(last > 0)
    def _():
        block(0, True)

    @pl.loop(1, middle)
    def _(index):
        block(index, False)

    for rows in gathers:
        rows.pass_on()

    @pl.loop(jnp.maximum(middle, 1), last)
    def _(index):
        block(index, False)

    kept = start[...] < last * KEY_BLOCK
    top[...] = jnp.where(kept, top[...], big_negative)
    kept = kept.astype(f32)
    total[...] = total[...] * kept
    acc[...] = acc[...] * kept
    low_acc[...] = low_acc[...] * kept
    block(last, True)
    inverse = 1.0 / total[...]
    rows = acc[...] * inverse
    exact[...] = rows + low_acc[...] * inverse
    rows = rows.T.astype(bf16)
    for h in range(HEADS):
        o[:, pl.ds(h * HD, HD)] = rows[h * TOK : (h + 1) * TOK]
    lse[...] = top[...] + jnp.log2(total[...])
    for rows in gathers:
        rows.wait()
    local.wait()
    copies.finish()


def attend(*arrays):
    slots = jax.ShapeDtypeStruct((4, 2, TOK, D), bf16)
    return pl.pallas_call(
        attend_kernel,
        out_shape=(
            jax.ShapeDtypeStruct((4, 4, 2, 2, TOK, 2 * HD), bf16),
            jax.ShapeDtypeStruct((TOK, HEADS * HD), bf16),
            jax.ShapeDtypeStruct((HD, NQ), f32),
            jax.ShapeDtypeStruct((1, NQ), f32),
            slots,
        ),
        in_specs=[VMEM] * 5,
        out_specs=(VMEM,) * 4 + (ANY,),
        scratch_shapes=[
            pltpu.VMEM((NQ, HD), bf16),
            pltpu.VMEM((1, NQ), f32),
            pltpu.VMEM((1, NQ), f32),
            pltpu.VMEM((HD, NQ), f32),
            pltpu.VMEM((HD, NQ), f32),
            *sems(110),
            pltpu.SemaphoreType.DMA((1,)),
        ],
        compiler_params=params(1),
    )(*arrays)


def mlp_kernel(*refs):
    attn_low, w_out, x, gain, og, aa, og_hbm, w_gate_hbm, w_up_hbm, w_down_hbm = refs[:10]
    resid, grad_resid, gain_terms, up_terms, down_terms, gate_sum, down_sum, aa_all = refs[10:18]
    pa, pb, wd, og_all, act_all, grad_hidden, hidden, ggp, gup, bk, dn, bk_core, dn_core, bk_sent, bk_in = refs[18:33]
    nb, rn, gate_terms, gate_in, gate_w, up_w, wide_gate, wide_up, send_sems, recv_sems, local_sems = refs[33:]
    me = here()
    z, y, c = me["z"], me["y"], me["c"]
    partner, other = at(me, c=1), at(me, n=1)
    ys = {d: at(me, y=d) for d in (1, 2, 3)}
    zs = {d: at(me, z=d) for d in (1, 2, 3)}
    greet([partner, other, *ys.values(), *zs.values()])
    copies = Copies(send_sems, recv_sems)
    units = pl.ds(pl.multiple_of((y * 2 + c) * UNITS, 16), UNITS)
    load_down = pltpu.make_async_copy(w_down_hbm.at[units], wd, local_sems.at[0])
    load_down.start()
    load_og = pltpu.make_async_copy(og_hbm, og_all, local_sems.at[1])
    load_og.start()
    first = (y * 2 + c) * UNITS
    tile = jnp.minimum(first // 128, FF // 2 // 128 - WINDOW // 128)
    window = pl.ds(pl.multiple_of(tile * 128, 128), WINDOW)
    load_wide = []
    for i, (whole, part) in enumerate(((w_gate_hbm, wide_gate), (w_up_hbm, wide_up))):
        load_wide.append(pltpu.make_async_copy(whole.at[:, window], part, local_sems.at[2 + i]))
        load_wide[-1].start()
    keep_aa = pltpu.make_async_copy(aa, aa_all.at[y, c], local_sems.at[4])
    keep_aa.start()
    pa[...] = nn(attn_low[...], w_out[...]).astype(bf16)
    swap = copies.send(pa, pb, other)
    aa_rows = Rows(me, copies, aa, aa_all)
    load_down.wait()
    load_og.wait()
    pair = (2 * TOK, D)
    for yi in range(4):
        grad_hidden[yi] = nt(og_all[yi].reshape(pair), wd[...])
    turn = lax.rem(WINDOW - (first - tile * 128), WINDOW)
    for copy, part, weights in ((load_wide[0], wide_gate, gate_w), (load_wide[1], wide_up, up_w)):
        copy.wait()

        @pl.loop(0, D // 128)
        def _(index, part=part, weights=weights):
            rows = pl.ds(pl.multiple_of(index * 128, 128), 128)
            turned = pltpu.roll(part[rows, :].astype(f32), turn, 1)
            weights[rows, :] = turned[:, :UNITS].astype(bf16)

    swap.wait_recv()
    total = x[...].astype(f32) + (pa[...].astype(f32) + pb[...].astype(f32))
    resid[...] = total
    inverse = lax.rsqrt(jnp.mean(total * total, axis=-1, keepdims=True) + rms_eps)
    act_all[y, c] = (total * inverse * gain[...]).astype(bf16)

    own = act_all.at[y, c]
    far = {d: copies.send(own, own, ys[d]) for d in (1, 3)}
    to_core = {0: [copies.send(own, own, partner)]}
    bk_cores, dn_cores, bk_moves = {}, {}, {}

    def block(d, beside=None):
        yi = step(me, "y", d)
        rows = act_all[yi].reshape(pair)
        gate = nn(rows, gate_w[...])
        up = nn(rows, up_w[...])
        sigmoid = 1.0 / (1.0 + jnp.exp(-gate))
        silu = gate * sigmoid
        grads = grad_hidden[yi]
        hidden[yi] = (silu * up).astype(bf16)
        ggp[yi] = (grads * up * (sigmoid * (1.0 + gate * (1.0 - sigmoid)))).astype(bf16)
        gup[yi] = (grads * silu).astype(bf16)
        if beside is not None:
            pass_block(beside)
        both = nt(ggp[yi], gate_w[...]) + nt(gup[yi], up_w[...])
        bk[yi] = both.astype(bf16).reshape(2, TOK, D)
        bk_cores[d] = copies.send(bk.at[yi, 1 - c], bk_core.at[yi], partner)
        dn[yi] = nn(hidden[yi], wd[...]).astype(bf16).reshape(2, TOK, D)
        dn_cores[d] = copies.send(dn.at[yi, 1 - c], dn_core.at[yi], partner)

    half = TOK // 2
    low, high = pl.ds(0, half), pl.ds(half, half)

    def pass_block(d):
        yi = step(me, "y", d)
        bk_cores[d].wait_recv()
        for k, rows in enumerate((low, high)):
            bk_sent[yi, rows] = (
                bk[yi, c, rows].astype(f32) + bk_core[yi, rows].astype(f32)
            ).astype(bf16)
            if d:
                bk_moves[d, k] = copies.send(
                    bk_sent.at[yi, rows], bk_in.at[d - 1, rows], ys[d]
                )

    def sum_down(d):
        yi = step(me, "y", d)
        dn_cores[d].wait_recv()
        down_sum[yi] = (dn[yi, c].astype(f32) + dn_core[yi].astype(f32)).astype(bf16)

    aa_rows.pass_on()
    to_core[0][0].wait_recv()
    block(0)
    relay = {}
    for d, rows in ((1, low), (3, high)):
        far[d].wait_recv()
        yi = lax.rem(y + (4 - d), 4)
        got = act_all.at[yi, c]
        relay[d] = copies.send(got.at[rows], got.at[rows], ys[d])
        to_core[4 - d] = [copies.send(got, got, partner)]
    to_core[3][0].wait_recv()
    block(3, 0)
    to_core[2] = []
    for d, rows in ((1, low), (3, high)):
        relay[d].wait_recv()
        got = act_all.at[step(me, "y", 2), c, rows]
        to_core[2].append(copies.send(got, got, partner))
    to_core[1][0].wait_recv()
    block(1, 3)
    for copy in to_core[2]:
        copy.wait_recv()
    block(2, 1)

    aa_rows.complete()
    everything = (GROUP * TOK, D)
    all_units = (GROUP * TOK, UNITS)
    gate_terms[...] = tn(ggp[...].reshape(all_units), act_all[...].reshape(everything)).astype(bf16)

    def z_cols(d):
        return pl.ds(pl.multiple_of(step(me, "z", d) * 384, 384), 384)

    gate_moves = {
        d: copies.send(gate_terms.at[:, z_cols(d)], gate_in.at[d - 1], zs[d]) for d in (1, 3, 2)
    }
    pass_block(2)
    up_terms[...] = tn(gup[...].reshape(all_units), act_all[...].reshape(everything)).astype(bf16)
    swaps_back = []
    for k, rows in enumerate((low, high)):
        back = bk_sent[y, rows].astype(f32)
        for d in (1, 3, 2):
            bk_moves[d, k].wait_recv()
            back = back + bk_in[d - 1, rows].astype(f32)
        nb[rows] = back.astype(bf16)
        swaps_back.append(copies.send(nb.at[rows], rn.at[rows], other))
    down_terms[...] = tn(hidden[...].reshape(all_units), og_all[...].reshape(everything)).astype(bf16)
    for d in range(4):
        sum_down(d)
    for copy in swaps_back:
        copy.wait_recv()
    grad_act = nb[...].astype(f32) + rn[...].astype(f32)
    normed = resid[...] * inverse
    gain_terms[...] = jnp.sum(grad_act * normed, axis=0, keepdims=True)
    grad_normed = grad_act * gain[...]
    inner = jnp.mean(grad_normed * normed, axis=-1, keepdims=True)
    grad_resid[...] = og[...].astype(f32) + inverse * (grad_normed - normed * inner)
    for d in (1, 3, 2):
        gate_moves[d].wait_recv()
    gate_sum[...] = (gate_terms[:, z_cols(0)].astype(f32) + three(gate_in)).T.astype(bf16)
    aa_rows.wait()
    keep_aa.wait()
    copies.finish()


def feed_forward(*arrays):
    rows = pltpu.VMEM((TOK, D), bf16)
    return pl.pallas_call(
        mlp_kernel,
        out_shape=[
            jax.ShapeDtypeStruct((TOK, D), f32),
            jax.ShapeDtypeStruct((TOK, D), f32),
            jax.ShapeDtypeStruct((1, D), f32),
            jax.ShapeDtypeStruct((UNITS, D), bf16),
            jax.ShapeDtypeStruct((UNITS, D), bf16),
            jax.ShapeDtypeStruct((D // 4, UNITS), bf16),
            jax.ShapeDtypeStruct((4, TOK, D), bf16),
            jax.ShapeDtypeStruct((4, 2, TOK, D), bf16),
        ],
        in_specs=[VMEM] * 6 + [ANY] * 4,
        out_specs=[VMEM] * 7 + [ANY],
        scratch_shapes=[
            rows,
            rows,
            pltpu.VMEM((UNITS, D), bf16),
            pltpu.VMEM((4, 2, TOK, D), bf16),
            pltpu.VMEM((4, 2, TOK, D), bf16),
            pltpu.VMEM((4, 2 * TOK, UNITS), f32),
            *[pltpu.VMEM((4, 2 * TOK, UNITS), bf16)] * 3,
            *[pltpu.VMEM((4, 2, TOK, D), bf16)] * 2,
            *[pltpu.VMEM((4, TOK, D), bf16)] * 3,
            pltpu.VMEM((3, TOK, D), bf16),
            rows,
            rows,
            pltpu.VMEM((UNITS, D), bf16),
            pltpu.VMEM((3, UNITS, D // 4), bf16),
            *[pltpu.VMEM((D, UNITS), bf16)] * 2,
            *[pltpu.VMEM((D, WINDOW), bf16)] * 2,
            *sems(60),
            pltpu.SemaphoreType.DMA((5,)),
        ],
        compiler_params=params(2),
    )(*arrays)


def back_kernel(*refs):
    (q_in, kv, exact, start, ids, lse, grad_resid, w_out, attn_low, cosine, sine, normed, inverse) = refs[:13]
    gain, resid, mlp_gain_terms, gate_sum, w_qkv_hbm, act_hbm, *terms, down_terms = refs[13:22]
    in_grad, layer_out, sum_gate, sum_up, sum_down, sum_qkv, sum_out, small_out = refs[22:30]
    (q, g, acc, dkv, cb, s, r1a, r1b, ta, tb, r2a, r2b, u, r3, w_qkv, act_all, gb_all, al_heads, al_all) = refs[30:49]
    gp, gp_flat, gp_all, part, part_other, small, e1, e2, e3, f1, f2 = refs[49:60]
    own, first_in, mid = refs[60:62], refs[62:64], refs[64:66]
    second_in, summed, third_in = (refs[66 + 3 * k : 69 + 3 * k] for k in range(3))
    q_terms, q_first, q_mid, q_second, q_summed, q_third = refs[75:81]
    down_own, down_in, down_part, down_other, send_sems, recv_sems, local_sems = refs[81:]

    me = here()
    z, y, xh, c, n = (me[a] for a in AXES)
    partner, across, other = at(me, c=1), at(me, xh=1), at(me, n=1)
    ys = {d: at(me, y=d) for d in (1, 2, 3)}
    zs = {d: at(me, z=d) for d in (1, 2, 3)}
    near_moves = [(d, e) for d in (1, 3, 2, 0) for e in (0, 1) if d or e]
    near = {m: at(me, y=m[0], xh=m[1]) for m in near_moves}
    group = {m: at(me, y=m[0], c=m[1]) for m in near_moves}
    greet([other, *zs.values(), *near.values(), *(group[m] for m in near_moves if m[1])])
    copies = Copies(send_sems, recv_sems)
    half = TOK // 2
    low, high = pl.ds(0, half), pl.ds(half, half)

    local = []

    def load(src, dst):
        copy = pltpu.make_async_copy(src, dst, local_sems.at[len(local)])
        copy.start()
        local.append(copy)
        return copy

    def z_cols(d):
        return pl.ds(pl.multiple_of(step(me, "z", d) * 384, 384), 384)

    second = {}

    def send_second(i, source, in_ref):
        for m in near_moves:
            second[i, m] = copies.send(
                source(step(me, "y", m[0]), step(me, "xh", m[1])), in_ref.at[y, xh], near[m]
            )

    def strip(yi, xi):
        return pl.ds(pl.multiple_of(96 * yi + 48 * xi, 48), 48)

    def send_mid(i, total, mid_ref, in_ref):
        turned = total.T.astype(bf16)
        for yi in range(4):
            for xi in range(2):
                rows = 96 * yi + 48 * xi
                mid_ref[yi, xi] = turned[rows : rows + 48]
        send_second(i, lambda yi, xi: mid_ref.at[yi, xi], in_ref)
        in_ref[y, xh] = mid_ref[y, xh]

    keep, give = pl.ds(pl.multiple_of(24 * c, 8), 24), pl.ds(pl.multiple_of(24 * (1 - c), 8), 24)
    third = {}
    all_summed = [*summed, q_summed]
    all_second = [*second_in, q_second]
    all_third = [*third_in, q_third]
    outs = ((sum_gate,), (sum_up,), (sum_down,), (sum_qkv, sum_out))

    def collect(i):
        for m in near_moves:
            second[i, m].wait_recv()
        all_summed[i][...] = all_second[i][:, 0].astype(f32) + all_second[i][:, 1].astype(f32)
        third[i] = copies.send(all_summed[i].at[:, give], all_third[i], partner)

    def deliver(i):
        third[i].wait_recv()
        for yi in range(4):
            mine_sum, their_sum = all_summed[i][yi, keep], all_third[i][yi]
            pair = (jnp.where(c == 0, mine_sum, their_sum), jnp.where(c == 0, their_sum, mine_sum))
            for e in range(2):
                k = 2 * yi + e
                if i < 3:
                    outs[i][0][:, pl.ds(k * UNITS, UNITS)] = pair[e]
                else:
                    outs[i][0][:, pl.ds(k * HD, HD)] = pair[e][:, :HD]
                    if k < HEADS:
                        outs[i][1][:, pl.ds(k * HD, HD)] = pair[e][:, HD:]

    send_second(0, lambda yi, xi: gate_sum.at[strip(yi, xi)], second_in[0])
    second_in[0][y, xh] = gate_sum[strip(y, xh), :]
    first = {}

    def send_first(i, d):
        first[i, d] = copies.send(terms[i].at[:, z_cols(d)], first_in[i].at[d - 1], zs[d])

    for d in (1, 3, 2):
        send_first(0, d)

    gb_all[y, c] = grad_resid[...].astype(bf16)
    branch = gb_all[y, c]
    branches = Rows(me, copies, gb_all.at[y, c], gb_all)
    load_down = load(down_terms.at[y], down_own)
    for h in range(HEADS):
        al_heads[h] = attn_low[:, pl.ds(h * HD, HD)]

    def head_of(d, e):
        taker = step(me, "y", d) * 2 + step(me, "c", e)
        return jnp.where(taker < HEADS, taker, 0)

    al_moves = [
        copies.send(al_heads.at[head_of(*m)], al_all.at[y, c], group[m]) for m in near_moves
    ]
    al_all[y, c] = al_heads[head_of(0, 0)]
    load_w = load(w_qkv_hbm, w_qkv)
    load_act = load(act_hbm, act_all)
    load_own = [load(terms[i].at[:, z_cols(0)], own[i]) for i in range(2)]

    heads_in(q_in, q)
    grads_in = nt(branch, w_out[...]).astype(bf16)
    for h in range(HEADS):
        g[pl.ds(h * TOK, TOK), :] = grads_in[:, h * HD : (h + 1) * HD]
    balance = jnp.sum(g[...].astype(f32).T * exact[...], axis=0, keepdims=True)
    acc[...] = jnp.zeros_like(acc)
    last = shard_of(me) // BLOCK_SHARDS
    log_total = lse[...]
    earlier = jnp.where(start[...] < last * KEY_BLOCK, log_total, -big_negative)

    def block(index, masked, shift):
        zi, yi = index // 4, lax.rem(index, 4)
        shape = (2, 2, TOK, HD)
        keys = kv[zi, yi, :, :, :, pl.ds(0, HD)].reshape(KEY_BLOCK, HD)
        values = kv[zi, yi, :, :, :, pl.ds(HD, HD)].reshape(KEY_BLOCK, HD)
        keys_t = keys.T
        dk = jnp.zeros((KEY_BLOCK, HD), f32)
        dv = jnp.zeros((KEY_BLOCK, HD), f32)
        for chunk in range(NQ // Q_CHUNK):
            cs = pl.ds(chunk * Q_CHUNK, Q_CHUNK)
            piece = slice(chunk * Q_CHUNK, (chunk + 1) * Q_CHUNK)
            qc, gc = q[cs, :], g[cs, :]
            probs = jnp.exp2(nt(keys, qc) * SCALE_LOG2 - shift[:, piece])
            if masked:
                key_ids = index * KEY_BLOCK + lax.broadcasted_iota(jnp.int32, (KEY_BLOCK, Q_CHUNK), 0)
                allowed = (key_ids >= start[:, cs]) & (key_ids <= ids[:, cs])
                probs = jnp.where(allowed, probs, 0.0)
            grads = (probs * (nt(values, gc) - balance[:, piece])).astype(bf16)
            dv = dv + nn(probs.astype(bf16), gc)
            dk = dk + nn(grads, qc)
            acc[:, cs] = acc[:, cs] + nn(keys_t, grads)
        dkv[zi, yi, :, :, :, pl.ds(0, HD)] = (dk * SCALE).astype(bf16).reshape(shape)
        dkv[zi, yi, :, :, :, pl.ds(HD, HD)] = dv.astype(bf16).reshape(shape)


    def segment(zi):
        @pl.loop(0, 4)
        def _(yi):
            index = 4 * zi + yi
            edge = (index == 0) | (index == last)

            @pl.when(edge & (index <= last))
            def _():
                block(index, True, jnp.where(index == last, log_total, earlier))

            @pl.when((index < last) & jnp.logical_not(edge))
            def _():
                block(index, False, earlier)

            @pl.when(index > last)
            def _():
                dkv[zi, yi] = jnp.zeros((2, 2, TOK, 2 * HD), bf16)

    kv_cores, first_a, first_b, second_a, second_b = {}, {}, {}, {}, {}

    def to_partner(d):
        zi = step(me, "z", d)
        kv_cores[d] = copies.send(dkv.at[zi, :, :, 1 - c], cb.at[zi], partner)

    def settle(d):
        zi = step(me, "z", d)
        kv_cores[d].wait_recv()
        s[zi] = (dkv[zi, :, :, c].astype(f32) + cb[zi].astype(f32)).astype(bf16)
        if d:
            first_a[d] = copies.send(s.at[zi, :, :, low], r1a.at[d - 1], zs[d])
        for e in (1, 3, 2):
            first_b[d, e] = copies.send(
                s.at[zi, step(me, "y", e), :, high], r1b.at[e - 1, zi], ys[e]
            )

    segment(step(me, "z", 1))
    to_partner(1)
    segment(step(me, "z", 2))
    to_partner(2)
    settle(1)
    segment(step(me, "z", 3))
    to_partner(3)
    settle(2)
    branches.pass_on()
    segment(z)
    to_partner(0)
    settle(3)
    turned_back = (acc[...] * SCALE).T

    def revert(rows):
        return rows * cosine[...] - pltpu.roll(rows, HD // 2, 1) * sine[...]

    def keep_head(h, rows):
        low_rows = rows.astype(bf16)
        gp[h] = low_rows
        gp_flat[:, pl.ds(h * HD, HD)] = low_rows
        small[pl.ds(2, 1), pl.ds(h * HD, HD)] = jnp.sum(low_rows.astype(f32), axis=0, keepdims=True)

    small[...] = jnp.zeros_like(small)
    small[pl.ds(1, 1), :] = mlp_gain_terms[...]
    for h in range(HEADS):
        keep_head(h, revert(turned_back[h * TOK : (h + 1) * TOK]))
    load_w.wait()
    front = HEADS * HD
    partial = nt(gp_flat[:, pl.ds(0, front)], w_qkv[:, pl.ds(0, front)])

    settle(0)
    for d in (1, 3, 2):
        first_a[d].wait_recv()
    ta[...] = (s[z, :, :, low].astype(f32) + three(r1a)).astype(bf16)
    for d in (1, 3, 2):
        second_a[d] = copies.send(ta.at[step(me, "y", d)], r2a.at[d - 1], ys[d])
    for copy in first_b.values():
        copy.wait_recv()
    tb[...] = (s[:, y, :, high].astype(f32) + three(r1b)).astype(bf16)
    for d in (1, 3, 2):
        second_b[d] = copies.send(tb.at[step(me, "z", d)], r2b.at[d - 1], zs[d])
    for d in (1, 3, 2):
        send_first(1, d)
    for i in (0,):
        load_own[i].wait()
        for d in (1, 3, 2):
            first[i, d].wait_recv()
        send_mid(i + 1, own[i][...].astype(f32) + three(first_in[i]), mid[i], second_in[i + 1])
    down_moves = {}

    def send_down(d):
        down_moves[d] = copies.send(down_terms.at[step(me, "y", d)], down_in.at[d - 1], ys[d])

    send_down(1)
    send_down(3)
    for d in (1, 3, 2):
        second_a[d].wait_recv()
        second_b[d].wait_recv()
    ua = ta[y].astype(f32) + three(r2a)
    ub = tb[z].astype(f32) + three(r2b)
    u[:, low] = ua.astype(bf16)
    u[:, high] = ub.astype(bf16)
    kv_last = copies.send(u.at[1 - xh], r3, across)
    kv_last.wait_recv()
    grad_kv = u[xh].astype(f32) + r3[...].astype(f32)
    keep_head(HEADS, revert(grad_kv[:, :HD]))
    keep_head(HEADS + 1, grad_kv[:, HD:])
    gp_moves = [
        copies.send(gp.at[step(me, "y", m[0]) * 2 + step(me, "c", m[1])], gp_all.at[y, c], group[m])
        for m in near_moves
    ]
    gp_all[y, c] = gp[y * 2 + c]
    send_down(2)
    back = pl.ds(front, 2 * HD)
    part[...] = (partial + nt(gp_flat[:, back], w_qkv[:, back])).astype(bf16)
    swap = copies.send(part, part_other, other)
    collect(0)
    branches.complete()
    load_act.wait()
    for copy in gp_moves:
        copy.wait_recv()
    q_terms[pl.ds(0, HD), :] = tn(
        gp_all[...].reshape(GROUP * TOK, HD), act_all[...].reshape(GROUP * TOK, D)
    ).astype(bf16)

    q_one = {d: copies.send(q_terms.at[pl.ds(0, HD), z_cols(d)], q_first.at[d - 1, pl.ds(0, HD)], zs[d]) for d in (1, 3, 2)}
    branches.wait()
    for copy in al_moves:
        copy.wait_recv()
    q_terms[pl.ds(HD, HD), :] = tn(
        al_all[...].reshape(GROUP * TOK, HD), gb_all[...].reshape(GROUP * TOK, D)
    ).astype(bf16)
    q_two = {d: copies.send(q_terms.at[pl.ds(HD, HD), z_cols(d)], q_first.at[d - 1, pl.ds(HD, HD)], zs[d]) for d in (1, 3, 2)}

    load_down.wait()
    mlp_out = down_own[...].astype(f32)
    for d in (1, 3, 2):
        down_moves[d].wait_recv()
        mlp_out = mlp_out + down_in[d - 1].astype(f32)
    down_part[...] = mlp_out.astype(bf16)
    down_swap = copies.send(down_part, down_other, other)
    swap.wait_recv()
    grad_act = part[...].astype(f32) + part_other[...].astype(f32)
    small[pl.ds(0, 1), :] = jnp.sum(grad_act * normed[...], axis=0, keepdims=True)
    small_one = {d: copies.send(small, e1.at[d - 1], zs[d]) for d in (1, 3, 2)}
    grad_normed = grad_act * gain[...]
    inner = jnp.mean(grad_normed * normed[...], axis=-1, keepdims=True)
    in_grad[...] = (grad_resid[...] + inverse[...] * (grad_normed - normed[...] * inner)).astype(bf16)

    load_own[1].wait()
    for d in (1, 3, 2):
        first[1, d].wait_recv()
    send_mid(2, own[1][...].astype(f32) + three(first_in[1]), mid[1], second_in[2])
    for d in (1, 3, 2):
        q_one[d].wait_recv()
        q_two[d].wait_recv()
    send_mid(3, q_terms[:, z_cols(0)].astype(f32) + three(q_first), q_mid, q_second)
    for d in (1, 3, 2):
        small_one[d].wait_recv()
    f1[...] = small[...] + three(e1)
    small_two = {m: copies.send(f1, e2.at[k], near[m]) for k, m in enumerate(near_moves)}
    collect(1)
    deliver(0)
    deliver(1)
    collect(2)
    collect(3)
    for m in near_moves:
        small_two[m].wait_recv()
    f2[...] = f1[...]
    for k in range(len(near_moves)):
        f2[...] = f2[...] + e2[k]
    small_three = copies.send(f2, e3, partner)
    deliver(2)
    deliver(3)
    small_three.wait_recv()
    small_out[...] = f2[...] + e3[...]
    down_swap.wait_recv()
    layer_out[...] = (
        resid[...] + (down_part[...].astype(f32) + down_other[...].astype(f32))
    ).astype(bf16)
    copies.finish()


def back(*arrays):
    half = TOK // 2
    wide = 2 * HD
    return pl.pallas_call(
        back_kernel,
        out_shape=[
            jax.ShapeDtypeStruct((TOK, D), bf16),
            jax.ShapeDtypeStruct((TOK, D), bf16),
            *[jax.ShapeDtypeStruct((24, FF // 2), f32)] * 3,
            jax.ShapeDtypeStruct((24, (HEADS + 2) * HD), f32),
            jax.ShapeDtypeStruct((24, HEADS * HD), f32),
            jax.ShapeDtypeStruct((8, D), f32),
        ],
        in_specs=[VMEM] * 17 + [ANY] * 5,
        out_specs=[VMEM] * 8,
        scratch_shapes=[
            pltpu.VMEM((NQ, HD), bf16),
            pltpu.VMEM((NQ, HD), bf16),
            pltpu.VMEM((HD, NQ), f32),
            pltpu.VMEM((4, 4, 2, 2, TOK, wide), bf16),
            pltpu.VMEM((4, 4, 2, TOK, wide), bf16),
            pltpu.VMEM((4, 4, 2, TOK, wide), bf16),
            pltpu.VMEM((3, 4, 2, half, wide), bf16),
            pltpu.VMEM((3, 4, 2, half, wide), bf16),
            pltpu.VMEM((4, 2, half, wide), bf16),
            pltpu.VMEM((4, 2, half, wide), bf16),
            pltpu.VMEM((3, 2, half, wide), bf16),
            pltpu.VMEM((3, 2, half, wide), bf16),
            pltpu.VMEM((2, TOK, wide), bf16),
            pltpu.VMEM((TOK, wide), bf16),
            pltpu.VMEM((D, (HEADS + 2) * HD), bf16),
            pltpu.VMEM((4, 2, TOK, D), bf16),
            pltpu.VMEM((4, 2, TOK, D), bf16),
            pltpu.VMEM((HEADS, TOK, HD), bf16),
            pltpu.VMEM((4, 2, TOK, HD), bf16),
            pltpu.VMEM((HEADS + 2, TOK, HD), bf16),
            pltpu.VMEM((TOK, (HEADS + 2) * HD), bf16),
            pltpu.VMEM((4, 2, TOK, HD), bf16),
            pltpu.VMEM((TOK, D), bf16),
            pltpu.VMEM((TOK, D), bf16),
            pltpu.VMEM((8, D), f32),
            pltpu.VMEM((3, 8, D), f32),
            pltpu.VMEM((7, 8, D), f32),
            pltpu.VMEM((8, D), f32),
            pltpu.VMEM((8, D), f32),
            pltpu.VMEM((8, D), f32),
            *[pltpu.VMEM((UNITS, 384), bf16)] * 2,
            *[pltpu.VMEM((3, UNITS, 384), bf16)] * 2,
            *[pltpu.VMEM((4, 2, 48, UNITS), bf16)] * 2,
            *[pltpu.VMEM((4, 2, 48, UNITS), bf16)] * 3,
            *[pltpu.VMEM((4, 48, UNITS), f32)] * 3,
            *[pltpu.VMEM((4, 24, UNITS), f32)] * 3,
            pltpu.VMEM((wide, D), bf16),
            pltpu.VMEM((3, wide, 384), bf16),
            pltpu.VMEM((4, 2, 48, wide), bf16),
            pltpu.VMEM((4, 2, 48, wide), bf16),
            pltpu.VMEM((4, 48, wide), f32),
            pltpu.VMEM((4, 24, wide), f32),
            pltpu.VMEM((TOK, D), bf16),
            pltpu.VMEM((3, TOK, D), bf16),
            pltpu.VMEM((TOK, D), bf16),
            pltpu.VMEM((TOK, D), bf16),
            *sems(150),
            pltpu.SemaphoreType.DMA((9,)),
        ],
        compiler_params=params(9, 62),
    )(*arrays)


def results_kernel(
    layer, grad, gate, up, down, qkv, out, small,
    layer_out, in_grad, norm_attn, norm_mlp, sum_qkv, bias, value_bias, sum_out, sum_gate, sum_up, sum_down,
):
    shard = shard_of(here())
    layer_out[...] = layer[...]
    in_grad[...] = grad[...]
    sum_qkv[...] = qkv[...]
    sum_gate[...] = gate[...]
    sum_up[...] = up[...]
    sum_out[...] = out[...].T
    sum_down[...] = down[...].T
    turned = pltpu.roll(small[...], lax.rem(D - 24 * shard, D), 1)
    norm_attn[...] = turned[0:1, :24]
    norm_mlp[...] = turned[1:2, :24]
    heads = jnp.concatenate([small[2:3, h * HD : (h + 1) * HD] for h in range(HEADS + 2)], axis=0)
    heads = pltpu.roll(heads, lax.rem(HD - 2 * shard, HD), 1)
    bias[0] = heads[: HEADS + 1, :2]
    value_bias[...] = heads[HEADS + 1 :, :2]


def results(*arrays):
    return pl.pallas_call(
        results_kernel,
        out_shape=[
            jax.ShapeDtypeStruct((TOK, D), bf16),
            jax.ShapeDtypeStruct((TOK, D), bf16),
            jax.ShapeDtypeStruct((1, 24), f32),
            jax.ShapeDtypeStruct((1, 24), f32),
            jax.ShapeDtypeStruct((24, (HEADS + 2) * HD), f32),
            jax.ShapeDtypeStruct((1, HEADS + 1, 2), f32),
            jax.ShapeDtypeStruct((1, 2), f32),
            jax.ShapeDtypeStruct((HEADS * HD, 24), f32),
            jax.ShapeDtypeStruct((24, FF // 2), f32),
            jax.ShapeDtypeStruct((24, FF // 2), f32),
            jax.ShapeDtypeStruct((FF // 2, 24), f32),
        ],
        in_specs=[VMEM] * 8,
        out_specs=[VMEM] * 11,
        compiler_params=pltpu.CompilerParams(vmem_limit_bytes=40 * 2**20),
    )(*arrays)


def row_starts(lengths, token_ids):
    ends = jnp.cumsum(lengths)
    before = ends[None, :] <= token_ids[:, None]
    return jnp.sum(jnp.where(before, lengths[None, :], 0), axis=1)


def rope_tables(positions):
    half = HD // 2
    freqs = rope_base ** (-2.0 * jnp.arange(half, dtype=f32) / HD)
    angles = positions.astype(f32)[:, None] * freqs[None, :]
    cosine, sine = jnp.cos(angles), jnp.sin(angles)
    return jnp.concatenate([cosine, cosine], 1), jnp.concatenate([-sine, sine], 1)


def rotate(values, cosine, sine):
    heads = []
    for h in range(values.shape[1] // HD):
        one = values[:, h * HD : (h + 1) * HD]
        swapped = jnp.concatenate([one[:, HD // 2 :], one[:, : HD // 2]], axis=1)
        heads.append(one * cosine + swapped * sine)
    return jnp.concatenate(heads, axis=1)


def normalize(values):
    inverse = lax.rsqrt(jnp.mean(values * values, axis=-1) + rms_eps)
    return (values * inverse[:, None], inverse)


def shards(
    layer_in, lengths, norm_attn, w_qkv, qkv_bias, w_out, norm_mlp, w_gate, w_up, w_down, out_grad
):
    shard = lax.axis_index(WIDE)
    own_ids = shard * TOK + jnp.arange(TOK, dtype=jnp.int32)
    seq_starts = row_starts(lengths, own_ids)
    cosine, sine = rope_tables(own_ids - seq_starts)
    start = jnp.tile(seq_starts, HEADS)[None]
    ids = jnp.tile(own_ids, HEADS)[None]
    input_f32 = layer_in.astype(f32)
    normed_attn, inverse_attn = normalize(input_f32)
    act_attn = (normed_attn * norm_attn).astype(bf16)
    projected = nn(act_attn, w_qkv) + qkv_bias[0]
    turned = rotate(projected[:, : (HEADS + 1) * HD], cosine, sine).astype(bf16)
    queries = turned[:, : HEADS * HD]
    kv_own = jnp.concatenate(
        [turned[:, HEADS * HD :], projected[:, (HEADS + 1) * HD :].astype(bf16)], axis=1
    )
    kv, attn_low, exact, lse, out_grad_all = attend(kv_own, queries, start, ids, out_grad)
    resid, grad_resid, gain_terms, up_terms, down_terms, gate_sum, down_sum, act_attn_all = feed_forward(
        attn_low, w_out, layer_in, norm_mlp[None], out_grad, act_attn, out_grad_all, w_gate, w_up, w_down
    )
    in_grad, layer_out, sum_gate, sum_up, sum_down, sum_qkv, sum_out, small = back(
        queries, kv, exact, start, ids, lse, grad_resid, w_out, attn_low, cosine, sine, normed_attn,
        inverse_attn[:, None], norm_attn[None], resid, gain_terms, gate_sum,
        w_qkv, act_attn_all, up_terms, down_terms, down_sum,
    )
    layer_out, in_grad, sum_norm_attn, sum_norm_mlp, *rest = results(
        layer_out, in_grad, sum_gate, sum_up, sum_down, sum_qkv, sum_out, small
    )
    sum_qkv, bias, value_bias, sum_out, sum_gate, sum_up, sum_down = rest
    return (
        layer_out,
        in_grad,
        sum_norm_attn[0],
        sum_qkv,
        bias,
        value_bias,
        sum_out,
        sum_norm_mlp[0],
        sum_gate,
        sum_up,
        sum_down,
    )


def solution(mesh):
    torus = Mesh(mesh.devices.reshape(4, 4, 2, 2, 2), AXES)
    in_specs = (
        P(WIDE, None),
        P(),
        P(),
        P(None, "n"),
        P("n", None),
        P("n", None),
        P(),
        P(None, "n"),
        P(None, "n"),
        P("n", None),
        P(WIDE, None),
    )
    out_specs = (
        P(WIDE, None),
        P(WIDE, None),
        P(WIDE),
        P(WIDE, "n"),
        P("n", None, WIDE),
        P("n", WIDE),
        P("n", WIDE),
        P(WIDE),
        P(WIDE, "n"),
        P(WIDE, "n"),
        P("n", WIDE),
    )
    return jax.shard_map(
        shards, mesh=torus, in_specs=in_specs, out_specs=out_specs, check_vma=False
    )
```

```python
import functools
import math

import jax
import jax.numpy as jnp
from jax import lax
from jax.experimental import pallas as pl
from jax.experimental.pallas import tpu as pltpu
from jax.sharding import Mesh
from jax.sharding import PartitionSpec as P

HD = 128
QH = 12
KVH = 2
HEADS = QH // KVH
D = 1536
FF = 8960
TOK = 128
TOKENS = 8192
NQ = HEADS * TOK
GROUP = 8
UNITS = FF // 2 // GROUP
WINDOW = 768

AXES = ("z", "y", "xh", "c", "n")
SIZE = {"z": 4, "y": 4, "xh": 2, "c": 2, "n": 2}
WIDE = ("z", "y", "xh", "c")
MESH = pl.DeviceIdType.MESH

rms_eps = 1e-06
rope_base = 10000.0
big_negative = -1e30
SCALE = HD ** (-0.5)
SCALE_LOG2 = SCALE * math.log2(math.e)
KEY_BLOCK = 512
BLOCK_SHARDS = KEY_BLOCK // TOK
Q_CHUNK = 256

bf16 = jnp.bfloat16
f32 = jnp.float32
VMEM = pl.BlockSpec(memory_space=pltpu.VMEM)
SMEM = pl.BlockSpec(memory_space=pltpu.SMEM)
ANY = pl.BlockSpec(memory_space=pl.ANY)


def nn(a, b):
    return lax.dot_general(a, b, (((1,), (0,)), ((), ())), preferred_element_type=f32)


def nt(a, b):
    return lax.dot_general(a, b, (((1,), (1,)), ((), ())), preferred_element_type=f32)


def tn(a, b):
    return lax.dot_general(a, b, (((0,), (0,)), ((), ())), preferred_element_type=f32)


def here():
    return {a: lax.axis_index(a) for a in AXES}


def step(me, axis, by):
    return lax.rem(me[axis] + by, SIZE[axis])


def at(me, **moved):
    return tuple(step(me, a, moved[a]) if a in moved else me[a] for a in AXES)


def hail(peers):
    barrier = pltpu.get_barrier_semaphore()
    for p in peers:
        pl.semaphore_signal(barrier, inc=1, device_id=p, device_id_type=MESH)
    return lambda: pl.semaphore_wait(barrier, len(peers))


def greet(peers):
    hail(peers)()


class Copies:
    def __init__(self, send_sems, recv_sems):
        self.send_sems, self.recv_sems, self.used, self.started = send_sems, recv_sems, 0, []

    def make(self, src, dst, target):
        self.used += 1
        return self.numbered(self.used - 1, src, dst, target)

    def numbered(self, k, src, dst, target):
        return pltpu.make_async_remote_copy(
            src_ref=src,
            dst_ref=dst,
            send_sem=self.send_sems.at[k],
            recv_sem=self.recv_sems.at[k],
            device_id=target,
            device_id_type=MESH,
        )

    def send(self, src, dst, target):
        copy = self.make(src, dst, target)
        copy.start()
        self.started.append(copy)
        return copy

    def finish(self):
        for copy in self.started:
            copy.wait_send()


def sems(count):
    return [pltpu.SemaphoreType.DMA((count,)), pltpu.SemaphoreType.DMA((count,))]


def params(ident, mib=60):
    return pltpu.CompilerParams(
        collective_id=ident, has_side_effects=True, vmem_limit_bytes=mib * 2**20
    )


def three(ref):
    return ref[0].astype(f32) + ref[1].astype(f32) + ref[2].astype(f32)


def shard_of(me):
    return ((me["z"] * 4 + me["y"]) * 2 + me["xh"]) * 2 + me["c"]


class Rows:
    def __init__(self, me, copies, source, slots):
        self.me, self.copies, self.source, self.slots = me, copies, source, slots
        half = TOK // 2
        n = me["n"]
        self.mine = pl.ds(pl.multiple_of(half * n, half), half)
        self.theirs = pl.ds(pl.multiple_of(half * (1 - n), half), half)
        self.own = slots.at[me["y"], me["c"]]
        self.near = [copies.send(source, self.own, at(me, c=1))]
        self.far, self.across = {}, {}

    def slot(self, d, rows):
        return self.slots.at[lax.rem(self.me["y"] + (4 - d), 4), self.me["c"], rows]

    def start(self, *steps):
        for d in steps:
            self.far[d] = self.copies.send(
                self.source.at[self.mine], self.own.at[self.mine], at(self.me, y=d)
            )

    def pass_on(self, *steps):
        for d in steps:
            self.far[d].wait_recv()
            got = self.slot(d, self.mine)
            self.across[d] = self.copies.send(got, got, at(self.me, n=1))
            self.near.append(self.copies.send(got, got, at(self.me, c=1)))

    def complete(self, *steps):
        for d in steps:
            self.across[d].wait_recv()
            got = self.slot(d, self.theirs)
            self.near.append(self.copies.send(got, got, at(self.me, c=1)))

    def wait(self):
        for copy in self.near:
            copy.wait_recv()


def attend_kernel(
    x, gains, w_qkv, bias, cosine, sine, start, ids, og, kv, q, act, o, exact, lse, og_all,
    stats, acc, low_acc, stats_in, acc_in, low_in, send_sems, recv_sems, local_sems,
):
    me = here()
    z, y, xh, c = me["z"], me["y"], me["xh"], me["c"]
    partner, across, other = at(me, c=1), at(me, xh=1), at(me, n=1)
    ys = {d: at(me, y=d) for d in (1, 2, 3)}
    zs = {d: at(me, z=d) for d in (1, 2, 3)}
    everyone_in = hail([partner, across, other, *ys.values(), *zs.values()])
    rows = x[...].astype(f32)
    inverse = lax.rsqrt(jnp.mean(rows * rows, axis=-1, keepdims=True) + rms_eps)
    act[...] = (rows * inverse * gains[0:1]).astype(bf16)
    front = HEADS * HD

    def turn(values):
        return values * cosine[...] + pltpu.roll(values, HD // 2, 1) * sine[...]

    back = nn(act[...], w_qkv[:, front:]) + bias[:, front:]
    mine = kv.at[z, y, xh]
    mine[:, pl.ds(0, HD)] = turn(back[:, :HD]).astype(bf16)
    mine[:, pl.ds(HD, HD)] = back[:, HD:].astype(bf16)
    everyone_in()
    copies = Copies(send_sems, recv_sems)
    first = copies.send(mine, mine, across)
    ahead = nn(act[...], w_qkv[:, :front]) + bias[:, :front]
    for h in range(HEADS):
        head = turn(ahead[:, h * HD : (h + 1) * HD]).astype(bf16)
        q[c, pl.ds(h * TOK, TOK), :] = head
    share_q = copies.send(q.at[c], q.at[c], partner)
    rows_of_og = Rows(me, copies, og, og_all)
    rows_of_og.start(1, 3)
    local = pltpu.make_async_copy(og, og_all.at[y, c], local_sems.at[0])
    local.start()
    stats[:, 0:1, :] = jnp.full((2, 1, NQ), big_negative, f32)
    stats[:, 1:8, :] = jnp.zeros((2, 7, NQ), f32)
    acc[...] = jnp.zeros_like(acc)
    low_acc[...] = jnp.zeros_like(low_acc)
    last = shard_of(me) // BLOCK_SHARDS
    kept = start[...] < last * KEY_BLOCK
    half = TOK // 2
    keys_here = 2 * half

    def take(parts, masked):
        def both(columns):
            return jnp.concatenate(
                [
                    kv[zi, yi, :, pl.ds(pl.multiple_of(half * k, half), half), columns].reshape(
                        keys_here, HD
                    )
                    for zi, yi, k in parts
                ],
                axis=0,
            )

        keys, values = both(pl.ds(0, HD)), both(pl.ds(HD, HD)).T
        for chunk in range(2 * NQ // Q_CHUNK):
            core, cs = divmod(chunk * Q_CHUNK, NQ)
            cs = pl.ds(cs, Q_CHUNK)
            here_cols = slice(chunk * Q_CHUNK, (chunk + 1) * Q_CHUNK)
            scores = nt(keys, q[core, cs, :]) * SCALE_LOG2
            if masked:
                ((zi, yi, k),) = parts
                place = lax.broadcasted_iota(jnp.int32, (keys_here, Q_CHUNK), 0)
                first_key = (4 * zi + yi) * KEY_BLOCK + c * TOK + half * k
                key_ids = first_key + place + place // half * (2 * TOK - half)
                allowed = (key_ids >= start[:, here_cols]) & (key_ids <= ids[:, here_cols])
                scores = jnp.where(allowed, scores, big_negative)
            old = stats[core, 0:1, cs]
            new = jnp.maximum(old, jnp.max(scores, axis=0, keepdims=True))
            if masked:
                probs = jnp.where(allowed, jnp.exp2(scores - new), 0.0)
            else:
                taken = kept[:, here_cols]
                new = jnp.where(taken, new, old)
                probs = jnp.exp2(scores - jnp.where(taken, new, -big_negative))
            fade = jnp.exp2(old - new)
            stats[core, 0:1, cs] = new
            stats[core, 1:2, cs] = stats[core, 1:2, cs] * fade + jnp.sum(probs, axis=0, keepdims=True)
            upper = probs.astype(bf16)
            rest = (probs - upper.astype(f32)).astype(bf16)
            acc[core, :, cs] = acc[core, :, cs] * fade + nn(values, upper)
            low_acc[core, :, cs] = low_acc[core, :, cs] * fade + nn(values, rest)

    def pair(za, ya, zb, yb):
        a, b = 4 * za + ya, 4 * zb + yb
        inner = (jnp.minimum(a, b) > 0) & (jnp.maximum(a, b) < last)

        @pl.when(inner)
        def _():
            take([(za, ya, 0), (zb, yb, 1)], False)

        @pl.when(jnp.logical_not(inner))
        def _():
            @pl.loop(0, 2)
            def _(k):
                zi, yi = jnp.where(k == 0, za, zb), jnp.where(k == 0, ya, yb)
                index = 4 * zi + yi
                edge = (index == 0) | (index == last)

                @pl.when(edge & (index <= last))
                def _():
                    take([(zi, yi, k)], True)

                @pl.when((index < last) & jnp.logical_not(edge))
                def _():
                    take([(zi, yi, k)], False)

    first.wait_recv()
    low, high = pl.ds(0, half), pl.ds(half, half)

    def slot(zi, yi, rows):
        return kv.at[zi, yi, :, rows]

    def before(axis, d):
        return lax.rem(me[axis] + (4 - d), 4)

    first_low, first_high = {}, {}
    for d in (1, 3, 2):
        first_low[d] = copies.send(slot(z, y, low), slot(z, y, low), ys[d])
        first_high[d] = copies.send(slot(z, y, high), slot(z, y, high), zs[d])
    share_q.wait_recv()

    pair(z, y, z, y)
    second_from = copies.used
    copies.used += 24
    for i, e in enumerate((0, 1, 3, 2)):
        yi, zi = before("y", e), before("z", e)
        if e:
            first_low[e].wait_recv()
            first_high[e].wait_recv()
        for j, d in enumerate((1, 3, 2)):
            k = second_from + 2 * (3 * i + j)
            for copy in (
                copies.numbered(k, slot(z, yi, low), slot(z, yi, low), zs[d]),
                copies.numbered(k + 1, slot(zi, y, high), slot(zi, y, high), ys[d]),
            ):
                copy.start()
                copies.started.append(copy)
    rows_of_og.start(2)
    rows_of_og.pass_on(1, 3)

    @pl.loop(1, 4)
    def _(e):
        pair(z, before("y", e), before("z", e), y)

    def places(k):
        i, j = k // 3, lax.rem(k, 3)
        e = jnp.where(i < 2, i, 5 - i)
        d = jnp.where(j < 2, 1 + 2 * j, 2)
        return before("z", d), before("y", e), before("z", e), before("y", d)

    def arrive(k):
        za, ya, zb, yb = places(k)
        one, two = slot(za, ya, low), slot(zb, yb, high)
        copies.numbered(second_from + 2 * k, one, one, zs[1]).wait_recv()
        copies.numbered(second_from + 2 * k + 1, two, two, ys[1]).wait_recv()
        pair(za, ya, zb, yb)

    pl.loop(0, 8)(arrive)
    rows_of_og.pass_on(2)
    pl.loop(8, 12)(arrive)
    merge = [
        copies.send(stats.at[1 - c], stats_in, partner),
        copies.send(acc.at[1 - c], acc_in, partner),
        copies.send(low_acc.at[1 - c], low_in, partner),
    ]
    rows_of_og.complete(1, 3, 2)
    for copy in merge:
        copy.wait_recv()
    own_top, in_top = stats[c, 0:1, :], stats_in[0:1, :]
    top = jnp.maximum(own_top, in_top)
    own_part, in_part = jnp.exp2(own_top - top), jnp.exp2(in_top - top)
    total = stats[c, 1:2, :] * own_part + stats_in[1:2, :] * in_part
    inverse = 1.0 / total
    own_part, in_part = own_part * inverse, in_part * inverse
    rows = acc[c] * own_part + acc_in[...] * in_part
    exact[...] = rows + (low_acc[c] * own_part + low_in[...] * in_part)
    rows = rows.T.astype(bf16)
    for h in range(HEADS):
        o[:, pl.ds(h * HD, HD)] = rows[h * TOK : (h + 1) * TOK]
    lse[...] = top + jnp.log2(total)
    rows_of_og.wait()
    local.wait()
    copies.finish()


def attend(*arrays):
    slots = jax.ShapeDtypeStruct((4, 2, TOK, D), bf16)
    return pl.pallas_call(
        attend_kernel,
        out_shape=(
            jax.ShapeDtypeStruct((4, 4, 2, TOK, 2 * HD), bf16),
            jax.ShapeDtypeStruct((2, NQ, HD), bf16),
            jax.ShapeDtypeStruct((TOK, D), bf16),
            jax.ShapeDtypeStruct((TOK, HEADS * HD), bf16),
            jax.ShapeDtypeStruct((HD, NQ), f32),
            jax.ShapeDtypeStruct((1, NQ), f32),
            slots,
        ),
        in_specs=[VMEM] * 9,
        out_specs=(VMEM,) * 6 + (ANY,),
        scratch_shapes=[
            pltpu.VMEM((2, 8, NQ), f32),
            pltpu.VMEM((2, HD, NQ), f32),
            pltpu.VMEM((2, HD, NQ), f32),
            pltpu.VMEM((8, NQ), f32),
            pltpu.VMEM((HD, NQ), f32),
            pltpu.VMEM((HD, NQ), f32),
            *sems(110),
            pltpu.SemaphoreType.DMA((1,)),
        ],
        compiler_params=params(1),
    )(*arrays)


def mlp_kernel(*refs):
    attn_low, w_out, x, gains, og, aa, og_hbm, w_gate_hbm, w_up_hbm, w_down_hbm = refs[:10]
    resid, grad_resid, gain_terms, up_terms, down_terms, gate_sum, down_sum, aa_all = refs[10:18]
    pa, pb, wd, og_all, act_all, grad_hidden, hidden, ggp, gup, bk, dn, bk_core, dn_core, bk_sent, bk_in = refs[18:33]
    nb, rn, gate_terms, gate_in, gate_w, up_w, wide_gate, wide_up, send_sems, recv_sems, local_sems = refs[33:]
    me = here()
    z, y, c = me["z"], me["y"], me["c"]
    partner, other = at(me, c=1), at(me, n=1)
    ys = {d: at(me, y=d) for d in (1, 2, 3)}
    zs = {d: at(me, z=d) for d in (1, 2, 3)}
    greet([partner, other, *ys.values(), *zs.values()])
    copies = Copies(send_sems, recv_sems)
    units = pl.ds(pl.multiple_of((y * 2 + c) * UNITS, 16), UNITS)
    load_down = pltpu.make_async_copy(w_down_hbm.at[units], wd, local_sems.at[0])
    load_down.start()
    load_og = pltpu.make_async_copy(og_hbm, og_all, local_sems.at[1])
    load_og.start()
    first = (y * 2 + c) * UNITS
    tile = jnp.minimum(first // 128, FF // 2 // 128 - WINDOW // 128)
    window = pl.ds(pl.multiple_of(tile * 128, 128), WINDOW)
    load_wide = []
    for i, (whole, part) in enumerate(((w_gate_hbm, wide_gate), (w_up_hbm, wide_up))):
        load_wide.append(pltpu.make_async_copy(whole.at[:, window], part, local_sems.at[2 + i]))
        load_wide[-1].start()
    keep_aa = pltpu.make_async_copy(aa, aa_all.at[y, c], local_sems.at[4])
    keep_aa.start()
    pa[...] = nn(attn_low[...], w_out[...]).astype(bf16)
    swap = copies.send(pa, pb, other)
    aa_rows = Rows(me, copies, aa, aa_all)
    aa_rows.start(1, 3, 2)
    load_down.wait()
    load_og.wait()
    pair = (2 * TOK, D)
    for yi in range(4):
        grad_hidden[yi] = nt(og_all[yi].reshape(pair), wd[...])
    turn = lax.rem(WINDOW - (first - tile * 128), WINDOW)
    for copy, part, weights in ((load_wide[0], wide_gate, gate_w), (load_wide[1], wide_up, up_w)):
        copy.wait()

        @pl.loop(0, D // 128)
        def _(index, part=part, weights=weights):
            rows = pl.ds(pl.multiple_of(index * 128, 128), 128)
            turned = pltpu.roll(part[rows, :].astype(f32), turn, 1)
            weights[rows, :] = turned[:, :UNITS].astype(bf16)

    swap.wait_recv()
    gain = gains[1:2]
    total = x[...].astype(f32) + (pa[...].astype(f32) + pb[...].astype(f32))
    resid[...] = total
    inverse = lax.rsqrt(jnp.mean(total * total, axis=-1, keepdims=True) + rms_eps)
    act_all[y, c] = (total * inverse * gain).astype(bf16)

    own = act_all.at[y, c]
    far = {d: copies.send(own, own, ys[d]) for d in (1, 3)}
    to_core = {0: [copies.send(own, own, partner)]}
    bk_cores, dn_cores, bk_moves = {}, {}, {}

    def block(d, beside=None):
        yi = step(me, "y", d)
        rows = act_all[yi].reshape(pair)
        gate = nn(rows, gate_w[...])
        up = nn(rows, up_w[...])
        sigmoid = 1.0 / (1.0 + jnp.exp(-gate))
        silu = gate * sigmoid
        grads = grad_hidden[yi]
        hidden[yi] = (silu * up).astype(bf16)
        ggp[yi] = (grads * up * (sigmoid * (1.0 + gate * (1.0 - sigmoid)))).astype(bf16)
        gup[yi] = (grads * silu).astype(bf16)
        if beside is not None:
            pass_block(beside)
        both = nt(ggp[yi], gate_w[...]) + nt(gup[yi], up_w[...])
        bk[yi] = both.astype(bf16).reshape(2, TOK, D)
        bk_cores[d] = copies.send(bk.at[yi, 1 - c], bk_core.at[yi], partner)
        dn[yi] = nn(hidden[yi], wd[...]).astype(bf16).reshape(2, TOK, D)
        dn_cores[d] = copies.send(dn.at[yi, 1 - c], dn_core.at[yi], partner)

    half = TOK // 2
    low, high = pl.ds(0, half), pl.ds(half, half)

    def pass_block(d):
        yi = step(me, "y", d)
        bk_cores[d].wait_recv()
        for k, rows in enumerate((low, high)):
            bk_sent[yi, rows] = (
                bk[yi, c, rows].astype(f32) + bk_core[yi, rows].astype(f32)
            ).astype(bf16)
            if d:
                bk_moves[d, k] = copies.send(
                    bk_sent.at[yi, rows], bk_in.at[d - 1, rows], ys[d]
                )

    def sum_down(d):
        yi = step(me, "y", d)
        dn_cores[d].wait_recv()
        down_sum[yi] = (dn[yi, c].astype(f32) + dn_core[yi].astype(f32)).astype(bf16)

    aa_rows.pass_on(1, 3, 2)
    to_core[0][0].wait_recv()
    block(0)
    relay = {}
    for d, rows in ((1, low), (3, high)):
        far[d].wait_recv()
        yi = lax.rem(y + (4 - d), 4)
        got = act_all.at[yi, c]
        relay[d] = copies.send(got.at[rows], got.at[rows], ys[d])
        to_core[4 - d] = [copies.send(got, got, partner)]
    to_core[3][0].wait_recv()
    block(3, 0)
    to_core[2] = []
    for d, rows in ((1, low), (3, high)):
        relay[d].wait_recv()
        got = act_all.at[step(me, "y", 2), c, rows]
        to_core[2].append(copies.send(got, got, partner))
    to_core[1][0].wait_recv()
    block(1, 3)
    for copy in to_core[2]:
        copy.wait_recv()
    block(2, 1)

    aa_rows.complete(1, 3, 2)
    everything = (GROUP * TOK, D)
    all_units = (GROUP * TOK, UNITS)
    gate_terms[...] = tn(ggp[...].reshape(all_units), act_all[...].reshape(everything)).astype(bf16)

    def z_cols(d):
        return pl.ds(pl.multiple_of(step(me, "z", d) * 384, 384), 384)

    gate_moves = {
        d: copies.send(gate_terms.at[:, z_cols(d)], gate_in.at[d - 1], zs[d]) for d in (1, 3, 2)
    }
    pass_block(2)
    up_terms[...] = tn(gup[...].reshape(all_units), act_all[...].reshape(everything)).astype(bf16)
    swaps_back = []
    for k, rows in enumerate((low, high)):
        back = bk_sent[y, rows].astype(f32)
        for d in (1, 3, 2):
            bk_moves[d, k].wait_recv()
            back = back + bk_in[d - 1, rows].astype(f32)
        nb[rows] = back.astype(bf16)
        swaps_back.append(copies.send(nb.at[rows], rn.at[rows], other))
    down_terms[...] = tn(hidden[...].reshape(all_units), og_all[...].reshape(everything)).astype(bf16)
    for d in range(4):
        sum_down(d)
    for copy in swaps_back:
        copy.wait_recv()
    grad_act = nb[...].astype(f32) + rn[...].astype(f32)
    normed = resid[...] * inverse
    gain_terms[...] = jnp.sum(grad_act * normed, axis=0, keepdims=True)
    grad_normed = grad_act * gain
    inner = jnp.mean(grad_normed * normed, axis=-1, keepdims=True)
    grad_resid[...] = og[...].astype(f32) + inverse * (grad_normed - normed * inner)
    for d in (1, 3, 2):
        gate_moves[d].wait_recv()
    gate_sum[...] = (gate_terms[:, z_cols(0)].astype(f32) + three(gate_in)).T.astype(bf16)
    aa_rows.wait()
    keep_aa.wait()
    copies.finish()


def feed_forward(*arrays):
    rows = pltpu.VMEM((TOK, D), bf16)
    return pl.pallas_call(
        mlp_kernel,
        out_shape=[
            jax.ShapeDtypeStruct((TOK, D), f32),
            jax.ShapeDtypeStruct((TOK, D), f32),
            jax.ShapeDtypeStruct((1, D), f32),
            jax.ShapeDtypeStruct((UNITS, D), bf16),
            jax.ShapeDtypeStruct((UNITS, D), bf16),
            jax.ShapeDtypeStruct((D // 4, UNITS), bf16),
            jax.ShapeDtypeStruct((4, TOK, D), bf16),
            jax.ShapeDtypeStruct((4, 2, TOK, D), bf16),
        ],
        in_specs=[VMEM] * 6 + [ANY] * 4,
        out_specs=[VMEM] * 7 + [ANY],
        scratch_shapes=[
            rows,
            rows,
            pltpu.VMEM((UNITS, D), bf16),
            pltpu.VMEM((4, 2, TOK, D), bf16),
            pltpu.VMEM((4, 2, TOK, D), bf16),
            pltpu.VMEM((4, 2 * TOK, UNITS), f32),
            *[pltpu.VMEM((4, 2 * TOK, UNITS), bf16)] * 3,
            *[pltpu.VMEM((4, 2, TOK, D), bf16)] * 2,
            *[pltpu.VMEM((4, TOK, D), bf16)] * 3,
            pltpu.VMEM((3, TOK, D), bf16),
            rows,
            rows,
            pltpu.VMEM((UNITS, D), bf16),
            pltpu.VMEM((3, UNITS, D // 4), bf16),
            *[pltpu.VMEM((D, UNITS), bf16)] * 2,
            *[pltpu.VMEM((D, WINDOW), bf16)] * 2,
            *sems(60),
            pltpu.SemaphoreType.DMA((5,)),
        ],
        compiler_params=params(2),
    )(*arrays)


def back_kernel(*refs):
    (q, kv, exact, start, ids, lse, grad_resid, w_out, attn_low, cosine, sine, x, gains) = refs[:13]
    resid, mlp_gain_terms, gate_sum, w_qkv_hbm, act_hbm, *terms, down_terms = refs[13:21]
    in_grad, layer_out, sum_gate, sum_up, sum_down, sum_qkv, sum_out, small_out = refs[21:29]
    (g, stats, acc, acc_in, dkv, r1a, r1b, ta, tb, r2a, r2b, u, r3, w_qkv, act_all, gb_all, al_heads, al_all) = refs[29:47]
    gp, gp_flat, gp_all, part, part_other, small, e1, e2, e3, f1, f2 = refs[47:58]
    own, first_in, mid = refs[58:60], refs[60:62], refs[62:64]
    second_in, summed, third_in = (refs[64 + 3 * k : 67 + 3 * k] for k in range(3))
    q_terms, q_first, q_mid, q_second, q_summed, q_third = refs[73:79]
    down_own, down_in, down_part, down_other, send_sems, recv_sems, local_sems = refs[79:]

    me = here()
    z, y, xh, c, n = (me[a] for a in AXES)
    partner, across, other = at(me, c=1), at(me, xh=1), at(me, n=1)
    ys = {d: at(me, y=d) for d in (1, 2, 3)}
    zs = {d: at(me, z=d) for d in (1, 2, 3)}
    near_moves = [(d, e) for d in (1, 3, 2, 0) for e in (0, 1) if d or e]
    near = {m: at(me, y=m[0], xh=m[1]) for m in near_moves}
    group = {m: at(me, y=m[0], c=m[1]) for m in near_moves}
    greet([other, *zs.values(), *near.values(), *(group[m] for m in near_moves if m[1])])
    copies = Copies(send_sems, recv_sems)
    half = TOK // 2
    low, high = pl.ds(0, half), pl.ds(half, half)
    gb_all[y, c] = grad_resid[...].astype(bf16)
    grads_in = nt(gb_all[y, c], w_out[...]).astype(bf16)
    for h in range(HEADS):
        g[c, pl.ds(h * TOK, TOK), :] = grads_in[:, h * HD : (h + 1) * HD]
    stats[c, 0:1, :] = lse[...]
    stats[c, 1:2, :] = jnp.sum(g[c].astype(f32).T * exact[...], axis=0, keepdims=True)
    stats[c, 2:8, :] = jnp.zeros((6, NQ), f32)
    shared = [copies.send(g.at[c], g.at[c], partner), copies.send(stats.at[c], stats.at[c], partner)]

    local = []

    def load(src, dst):
        copy = pltpu.make_async_copy(src, dst, local_sems.at[len(local)])
        copy.start()
        local.append(copy)
        return copy

    def z_cols(d):
        return pl.ds(pl.multiple_of(step(me, "z", d) * 384, 384), 384)

    second = {}

    def send_second(i, source, in_ref):
        for m in near_moves:
            second[i, m] = copies.send(
                source(step(me, "y", m[0]), step(me, "xh", m[1])), in_ref.at[y, xh], near[m]
            )

    def strip(yi, xi):
        return pl.ds(pl.multiple_of(96 * yi + 48 * xi, 48), 48)

    def send_mid(i, total, mid_ref, in_ref):
        turned = total.T.astype(bf16)
        for yi in range(4):
            for xi in range(2):
                rows = 96 * yi + 48 * xi
                mid_ref[yi, xi] = turned[rows : rows + 48]
        send_second(i, lambda yi, xi: mid_ref.at[yi, xi], in_ref)
        in_ref[y, xh] = mid_ref[y, xh]

    keep, give = pl.ds(pl.multiple_of(24 * c, 8), 24), pl.ds(pl.multiple_of(24 * (1 - c), 8), 24)
    third = {}
    all_summed = [*summed, q_summed]
    all_second = [*second_in, q_second]
    all_third = [*third_in, q_third]
    outs = ((sum_gate,), (sum_up,), (sum_down,), (sum_qkv, sum_out))

    def collect(i):
        for m in near_moves:
            second[i, m].wait_recv()
        all_summed[i][...] = all_second[i][:, 0].astype(f32) + all_second[i][:, 1].astype(f32)
        third[i] = copies.send(all_summed[i].at[:, give], all_third[i], partner)

    def deliver(i):
        third[i].wait_recv()
        for yi in range(4):
            mine_sum, their_sum = all_summed[i][yi, keep], all_third[i][yi]
            pair = (jnp.where(c == 0, mine_sum, their_sum), jnp.where(c == 0, their_sum, mine_sum))
            for e in range(2):
                k = 2 * yi + e
                if i < 3:
                    outs[i][0][:, pl.ds(k * UNITS, UNITS)] = pair[e]
                else:
                    outs[i][0][:, pl.ds(k * HD, HD)] = pair[e][:, :HD]
                    if k < HEADS:
                        outs[i][1][:, pl.ds(k * HD, HD)] = pair[e][:, HD:]

    send_second(0, lambda yi, xi: gate_sum.at[strip(yi, xi)], second_in[0])
    second_in[0][y, xh] = gate_sum[strip(y, xh), :]
    first = {}

    def send_first(i, d):
        first[i, d] = copies.send(terms[i].at[:, z_cols(d)], first_in[i].at[d - 1], zs[d])

    for d in (1, 3, 2):
        send_first(0, d)

    branches = Rows(me, copies, gb_all.at[y, c], gb_all)
    branches.start(1, 3, 2)
    load_down = load(down_terms.at[y], down_own)
    for h in range(HEADS):
        al_heads[h] = attn_low[:, pl.ds(h * HD, HD)]

    def head_of(d, e):
        taker = step(me, "y", d) * 2 + step(me, "c", e)
        return jnp.where(taker < HEADS, taker, 0)

    al_moves = [
        copies.send(al_heads.at[head_of(*m)], al_all.at[y, c], group[m]) for m in near_moves
    ]
    al_all[y, c] = al_heads[head_of(0, 0)]
    load_w = load(w_qkv_hbm, w_qkv)
    load_act = load(act_hbm, act_all)
    load_own = [load(terms[i].at[:, z_cols(0)], own[i]) for i in range(2)]

    for copy in shared:
        copy.wait_recv()
    acc[...] = jnp.zeros_like(acc)
    last = shard_of(me) // BLOCK_SHARDS

    def of_both(row):
        return jnp.concatenate([stats[0, row : row + 1, :], stats[1, row : row + 1, :]], axis=1)

    log_total, balance = of_both(0), of_both(1)
    earlier = jnp.where(start[...] < last * KEY_BLOCK, log_total, -big_negative)
    keys_here = 2 * TOK

    def block(index, masked, shift):
        zi, yi = index // 4, lax.rem(index, 4)
        keys = kv[zi, yi, :, :, pl.ds(0, HD)].reshape(keys_here, HD)
        values = kv[zi, yi, :, :, pl.ds(HD, HD)].reshape(keys_here, HD)
        keys_t = keys.T
        dk = jnp.zeros((keys_here, HD), f32)
        dv = jnp.zeros((keys_here, HD), f32)
        for chunk in range(2 * NQ // Q_CHUNK):
            core, cs = divmod(chunk * Q_CHUNK, NQ)
            cs = pl.ds(cs, Q_CHUNK)
            piece = slice(chunk * Q_CHUNK, (chunk + 1) * Q_CHUNK)
            qc, gc = q[core, cs, :], g[core, cs, :]
            probs = jnp.exp2(nt(keys, qc) * SCALE_LOG2 - shift[:, piece])
            if masked:
                place = lax.broadcasted_iota(jnp.int32, (keys_here, Q_CHUNK), 0)
                key_ids = index * KEY_BLOCK + c * TOK + place + place // TOK * TOK
                allowed = (key_ids >= start[:, piece]) & (key_ids <= ids[:, piece])
                probs = jnp.where(allowed, probs, 0.0)
            grads = (probs * (nt(values, gc) - balance[:, piece])).astype(bf16)
            dv = dv + nn(probs.astype(bf16), gc)
            dk = dk + nn(grads, qc)
            acc[core, :, cs] = acc[core, :, cs] + nn(keys_t, grads)
        dkv[zi, yi, :, :, pl.ds(0, HD)] = (dk * SCALE).astype(bf16).reshape(2, TOK, HD)
        dkv[zi, yi, :, :, pl.ds(HD, HD)] = dv.astype(bf16).reshape(2, TOK, HD)

    def segment(zi):
        @pl.loop(0, 4)
        def _(yi):
            index = 4 * zi + yi
            edge = (index == 0) | (index == last)

            @pl.when(edge & (index <= last))
            def _():
                block(index, True, jnp.where(index == last, log_total, earlier))

            @pl.when((index < last) & jnp.logical_not(edge))
            def _():
                block(index, False, earlier)

            @pl.when(index > last)
            def _():
                dkv[zi, yi] = jnp.zeros((2, TOK, 2 * HD), bf16)

    first_a, first_b, second_a, second_b = {}, {}, {}, {}

    def settle(d):
        zi = step(me, "z", d)
        if d:
            first_a[d] = copies.send(dkv.at[zi, :, :, low], r1a.at[d - 1], zs[d])
        for e in (1, 3, 2):
            first_b[d, e] = copies.send(
                dkv.at[zi, step(me, "y", e), :, high], r1b.at[e - 1, zi], ys[e]
            )

    segment(step(me, "z", 1))
    settle(1)
    segment(step(me, "z", 2))
    settle(2)
    segment(step(me, "z", 3))
    settle(3)
    branches.pass_on(1, 3, 2)
    segment(z)
    settle(0)
    queries_back = copies.send(acc.at[1 - c], acc_in, partner)
    for d in (1, 3, 2):
        first_a[d].wait_recv()
    ta[...] = (dkv[z, :, :, low].astype(f32) + three(r1a)).astype(bf16)
    for d in (1, 3, 2):
        second_a[d] = copies.send(ta.at[step(me, "y", d)], r2a.at[d - 1], ys[d])
    for copy in first_b.values():
        copy.wait_recv()
    tb[...] = (dkv[:, y, :, high].astype(f32) + three(r1b)).astype(bf16)
    for d in (1, 3, 2):
        second_b[d] = copies.send(tb.at[step(me, "z", d)], r2b.at[d - 1], zs[d])
    for d in (1, 3, 2):
        send_first(1, d)
    queries_back.wait_recv()
    turned_back = ((acc[c] + acc_in[...]) * SCALE).T

    def revert(rows):
        return rows * cosine[...] - pltpu.roll(rows, HD // 2, 1) * sine[...]

    def keep_head(h, rows):
        low_rows = rows.astype(bf16)
        gp[h] = low_rows
        gp_flat[:, pl.ds(h * HD, HD)] = low_rows
        small[pl.ds(2, 1), pl.ds(h * HD, HD)] = jnp.sum(low_rows.astype(f32), axis=0, keepdims=True)

    small[...] = jnp.zeros_like(small)
    small[pl.ds(1, 1), :] = mlp_gain_terms[...]
    for h in range(HEADS):
        keep_head(h, revert(turned_back[h * TOK : (h + 1) * TOK]))
    load_w.wait()
    front = HEADS * HD
    partial = nt(gp_flat[:, pl.ds(0, front)], w_qkv[:, pl.ds(0, front)])

    for i in (0,):
        load_own[i].wait()
        for d in (1, 3, 2):
            first[i, d].wait_recv()
        send_mid(i + 1, own[i][...].astype(f32) + three(first_in[i]), mid[i], second_in[i + 1])
    down_moves = {}

    def send_down(d):
        down_moves[d] = copies.send(down_terms.at[step(me, "y", d)], down_in.at[d - 1], ys[d])

    send_down(1)
    send_down(3)
    for d in (1, 3, 2):
        second_a[d].wait_recv()
        second_b[d].wait_recv()
    ua = ta[y].astype(f32) + three(r2a)
    ub = tb[z].astype(f32) + three(r2b)
    u[:, low] = ua.astype(bf16)
    u[:, high] = ub.astype(bf16)
    kv_last = copies.send(u.at[1 - xh], r3, across)
    kv_last.wait_recv()
    grad_kv = u[xh].astype(f32) + r3[...].astype(f32)
    keep_head(HEADS, revert(grad_kv[:, :HD]))
    keep_head(HEADS + 1, grad_kv[:, HD:])
    gp_moves = [
        copies.send(gp.at[step(me, "y", m[0]) * 2 + step(me, "c", m[1])], gp_all.at[y, c], group[m])
        for m in near_moves
    ]
    gp_all[y, c] = gp[y * 2 + c]
    send_down(2)
    back = pl.ds(front, 2 * HD)
    part[...] = (partial + nt(gp_flat[:, back], w_qkv[:, back])).astype(bf16)
    swap = copies.send(part, part_other, other)
    collect(0)
    branches.complete(1, 3, 2)
    load_act.wait()
    for copy in gp_moves:
        copy.wait_recv()
    q_terms[pl.ds(0, HD), :] = tn(
        gp_all[...].reshape(GROUP * TOK, HD), act_all[...].reshape(GROUP * TOK, D)
    ).astype(bf16)

    q_one = {d: copies.send(q_terms.at[pl.ds(0, HD), z_cols(d)], q_first.at[d - 1, pl.ds(0, HD)], zs[d]) for d in (1, 3, 2)}
    branches.wait()
    for copy in al_moves:
        copy.wait_recv()
    q_terms[pl.ds(HD, HD), :] = tn(
        al_all[...].reshape(GROUP * TOK, HD), gb_all[...].reshape(GROUP * TOK, D)
    ).astype(bf16)
    q_two = {d: copies.send(q_terms.at[pl.ds(HD, HD), z_cols(d)], q_first.at[d - 1, pl.ds(HD, HD)], zs[d]) for d in (1, 3, 2)}

    load_down.wait()
    mlp_out = down_own[...].astype(f32)
    for d in (1, 3, 2):
        down_moves[d].wait_recv()
        mlp_out = mlp_out + down_in[d - 1].astype(f32)
    down_part[...] = mlp_out.astype(bf16)
    down_swap = copies.send(down_part, down_other, other)
    swap.wait_recv()
    grad_act = part[...].astype(f32) + part_other[...].astype(f32)
    rows = x[...].astype(f32)
    inverse = lax.rsqrt(jnp.mean(rows * rows, axis=-1, keepdims=True) + rms_eps)
    normed = rows * inverse
    small[pl.ds(0, 1), :] = jnp.sum(grad_act * normed, axis=0, keepdims=True)
    small_one = {d: copies.send(small, e1.at[d - 1], zs[d]) for d in (1, 3, 2)}
    grad_normed = grad_act * gains[0:1]
    inner = jnp.mean(grad_normed * normed, axis=-1, keepdims=True)
    in_grad[...] = (grad_resid[...] + inverse * (grad_normed - normed * inner)).astype(bf16)

    load_own[1].wait()
    for d in (1, 3, 2):
        first[1, d].wait_recv()
    send_mid(2, own[1][...].astype(f32) + three(first_in[1]), mid[1], second_in[2])
    for d in (1, 3, 2):
        q_one[d].wait_recv()
        q_two[d].wait_recv()
    send_mid(3, q_terms[:, z_cols(0)].astype(f32) + three(q_first), q_mid, q_second)
    for d in (1, 3, 2):
        small_one[d].wait_recv()
    f1[...] = small[...] + three(e1)
    small_two = {m: copies.send(f1, e2.at[k], near[m]) for k, m in enumerate(near_moves)}
    collect(1)
    deliver(0)
    deliver(1)
    collect(2)
    collect(3)
    for m in near_moves:
        small_two[m].wait_recv()
    f2[...] = f1[...]
    for k in range(len(near_moves)):
        f2[...] = f2[...] + e2[k]
    small_three = copies.send(f2, e3, partner)
    deliver(2)
    deliver(3)
    small_three.wait_recv()
    small_out[...] = f2[...] + e3[...]
    down_swap.wait_recv()
    layer_out[...] = (
        resid[...] + (down_part[...].astype(f32) + down_other[...].astype(f32))
    ).astype(bf16)
    copies.finish()


def back(*arrays):
    half = TOK // 2
    wide = 2 * HD
    return pl.pallas_call(
        back_kernel,
        out_shape=[
            jax.ShapeDtypeStruct((TOK, D), bf16),
            jax.ShapeDtypeStruct((TOK, D), bf16),
            *[jax.ShapeDtypeStruct((24, FF // 2), f32)] * 3,
            jax.ShapeDtypeStruct((24, (HEADS + 2) * HD), f32),
            jax.ShapeDtypeStruct((24, HEADS * HD), f32),
            jax.ShapeDtypeStruct((8, D), f32),
        ],
        in_specs=[VMEM] * 16 + [ANY] * 5,
        out_specs=[VMEM] * 8,
        scratch_shapes=[
            pltpu.VMEM((2, NQ, HD), bf16),
            pltpu.VMEM((2, 8, NQ), f32),
            pltpu.VMEM((2, HD, NQ), f32),
            pltpu.VMEM((HD, NQ), f32),
            pltpu.VMEM((4, 4, 2, TOK, wide), bf16),
            pltpu.VMEM((3, 4, 2, half, wide), bf16),
            pltpu.VMEM((3, 4, 2, half, wide), bf16),
            pltpu.VMEM((4, 2, half, wide), bf16),
            pltpu.VMEM((4, 2, half, wide), bf16),
            pltpu.VMEM((3, 2, half, wide), bf16),
            pltpu.VMEM((3, 2, half, wide), bf16),
            pltpu.VMEM((2, TOK, wide), bf16),
            pltpu.VMEM((TOK, wide), bf16),
            pltpu.VMEM((D, (HEADS + 2) * HD), bf16),
            pltpu.VMEM((4, 2, TOK, D), bf16),
            pltpu.VMEM((4, 2, TOK, D), bf16),
            pltpu.VMEM((HEADS, TOK, HD), bf16),
            pltpu.VMEM((4, 2, TOK, HD), bf16),
            pltpu.VMEM((HEADS + 2, TOK, HD), bf16),
            pltpu.VMEM((TOK, (HEADS + 2) * HD), bf16),
            pltpu.VMEM((4, 2, TOK, HD), bf16),
            pltpu.VMEM((TOK, D), bf16),
            pltpu.VMEM((TOK, D), bf16),
            pltpu.VMEM((8, D), f32),
            pltpu.VMEM((3, 8, D), f32),
            pltpu.VMEM((7, 8, D), f32),
            pltpu.VMEM((8, D), f32),
            pltpu.VMEM((8, D), f32),
            pltpu.VMEM((8, D), f32),
            *[pltpu.VMEM((UNITS, 384), bf16)] * 2,
            *[pltpu.VMEM((3, UNITS, 384), bf16)] * 2,
            *[pltpu.VMEM((4, 2, 48, UNITS), bf16)] * 2,
            *[pltpu.VMEM((4, 2, 48, UNITS), bf16)] * 3,
            *[pltpu.VMEM((4, 48, UNITS), f32)] * 3,
            *[pltpu.VMEM((4, 24, UNITS), f32)] * 3,
            pltpu.VMEM((wide, D), bf16),
            pltpu.VMEM((3, wide, 384), bf16),
            pltpu.VMEM((4, 2, 48, wide), bf16),
            pltpu.VMEM((4, 2, 48, wide), bf16),
            pltpu.VMEM((4, 48, wide), f32),
            pltpu.VMEM((4, 24, wide), f32),
            pltpu.VMEM((TOK, D), bf16),
            pltpu.VMEM((3, TOK, D), bf16),
            pltpu.VMEM((TOK, D), bf16),
            pltpu.VMEM((TOK, D), bf16),
            *sems(150),
            pltpu.SemaphoreType.DMA((9,)),
        ],
        compiler_params=params(9, 62),
    )(*arrays)


def results_kernel(*refs):
    wholes, small, copied = refs[:7], refs[7], refs[8:15]
    norm_attn, norm_mlp, bias, value_bias, sems = refs[15:]
    shard = shard_of(here())
    moves = [
        pltpu.make_async_copy(a, b, sems.at[k]) for k, (a, b) in enumerate(zip(wholes, copied))
    ]
    for move in moves:
        move.start()
    turned = pltpu.roll(small[...], lax.rem(D - 24 * shard, D), 1)
    norm_attn[...] = turned[0:1, :24]
    norm_mlp[...] = turned[1:2, :24]
    heads = jnp.concatenate([small[2:3, h * HD : (h + 1) * HD] for h in range(HEADS + 2)], axis=0)
    heads = pltpu.roll(heads, lax.rem(HD - 2 * shard, HD), 1)
    bias[0] = heads[: HEADS + 1, :2].T
    value_bias[...] = heads[HEADS + 1 :, :2]
    for move in moves:
        move.wait()


def results(*arrays):
    *wholes, small = arrays
    return pl.pallas_call(
        results_kernel,
        out_shape=[
            *[jax.ShapeDtypeStruct(a.shape, a.dtype) for a in wholes],
            jax.ShapeDtypeStruct((1, 24), f32),
            jax.ShapeDtypeStruct((1, 24), f32),
            jax.ShapeDtypeStruct((1, 2, HEADS + 1), f32),
            jax.ShapeDtypeStruct((1, 2), f32),
        ],
        in_specs=[ANY] * 7 + [VMEM],
        out_specs=[VMEM] * 11,
        scratch_shapes=[pltpu.SemaphoreType.DMA((7,))],
    )(*wholes, small)


def row_starts(lengths, token_ids):
    ends = jnp.cumsum(lengths)
    before = ends[None, :] <= token_ids[:, None]
    return jnp.sum(jnp.where(before, lengths[None, :], 0), axis=1)


def rope_tables(positions):
    half = HD // 2
    freqs = rope_base ** (-2.0 * jnp.arange(half, dtype=f32) / HD)
    angles = positions.astype(f32)[:, None] * freqs[None, :]
    cosine, sine = jnp.cos(angles), jnp.sin(angles)
    return jnp.concatenate([cosine, cosine], 1), jnp.concatenate([-sine, sine], 1)


def shards(
    layer_in, lengths, norm_attn, w_qkv, qkv_bias, w_out, norm_mlp, w_gate, w_up, w_down, out_grad
):
    shard = lax.axis_index(WIDE)
    chip_ids = shard // 2 * (2 * TOK) + jnp.arange(2 * TOK, dtype=jnp.int32)
    chip_starts = row_starts(lengths, chip_ids)
    own = lax.rem(shard, 2) * TOK
    cosine, sine = rope_tables(lax.dynamic_slice(chip_ids - chip_starts, (own,), (TOK,)))

    def by_head(row):
        return jnp.broadcast_to(row.reshape(2, 1, TOK), (2, HEADS, TOK)).reshape(1, 2 * NQ)

    start, ids = by_head(chip_starts), by_head(chip_ids)
    gains = jnp.stack([norm_attn, norm_mlp])
    kv, queries, act_attn, attn_low, exact, lse, out_grad_all = attend(
        layer_in, gains, w_qkv, qkv_bias, cosine, sine, start, ids, out_grad
    )
    resid, grad_resid, gain_terms, up_terms, down_terms, gate_sum, down_sum, act_attn_all = feed_forward(
        attn_low, w_out, layer_in, gains, out_grad, act_attn, out_grad_all, w_gate, w_up, w_down
    )
    sums = back(
        queries, kv, exact, start, ids, lse, grad_resid, w_out, attn_low, cosine, sine, layer_in,
        gains, resid, gain_terms, gate_sum,
        w_qkv, act_attn_all, up_terms, down_terms, down_sum,
    )
    in_grad, layer_out, sum_gate, sum_up, sum_down, sum_qkv, sum_out, *rest = results(*sums)
    sum_norm_attn, sum_norm_mlp, bias, value_bias = rest
    return (
        layer_out,
        in_grad,
        sum_norm_attn[0],
        sum_qkv,
        bias.swapaxes(1, 2),
        value_bias,
        sum_out.T,
        sum_norm_mlp[0],
        sum_gate,
        sum_up,
        sum_down.T,
    )


def solution(mesh):
    torus = Mesh(mesh.devices.reshape(4, 4, 2, 2, 2), AXES)
    in_specs = (
        P(WIDE, None),
        P(),
        P(),
        P(None, "n"),
        P("n", None),
        P("n", None),
        P(),
        P(None, "n"),
        P(None, "n"),
        P("n", None),
        P(WIDE, None),
    )
    out_specs = (
        P(WIDE, None),
        P(WIDE, None),
        P(WIDE),
        P(WIDE, "n"),
        P("n", None, WIDE),
        P("n", WIDE),
        P("n", WIDE),
        P(WIDE),
        P(WIDE, "n"),
        P(WIDE, "n"),
        P("n", WIDE),
    )
    return jax.shard_map(
        shards, mesh=torus, in_specs=in_specs, out_specs=out_specs, check_vma=False
    )
```

```python
import functools
import math

import jax
import jax.numpy as jnp
import numpy as np
from jax import lax
from jax.experimental import pallas as pl
from jax.experimental.pallas import tpu as pltpu
from jax.sharding import Mesh
from jax.sharding import PartitionSpec as P

HD = 128
QH = 12
KVH = 2
HEADS = QH // KVH
D = 1536
FF = 8960
TOK = 128
TOKENS = 8192
SEQS = 4
NQ = HEADS * TOK
GROUP = 8
UNITS = FF // 2 // GROUP
WINDOW = 768
COLUMNS = 640

AXES = ("z", "y", "xh", "c", "n")
SIZE = {"z": 4, "y": 4, "xh": 2, "c": 2, "n": 2}
WIDE = ("z", "y", "xh", "c")
MESH = pl.DeviceIdType.MESH

rms_eps = 1e-06
rope_base = 10000.0
big_negative = -1e30
SCALE = HD ** (-0.5)
SCALE_LOG2 = SCALE * math.log2(math.e)
KEY_BLOCK = 512
BLOCK_SHARDS = KEY_BLOCK // TOK
Q_CHUNK = 256

bf16 = jnp.bfloat16
f32 = jnp.float32
VMEM = pl.BlockSpec(memory_space=pltpu.VMEM)
SMEM = pl.BlockSpec(memory_space=pltpu.SMEM)
ANY = pl.BlockSpec(memory_space=pl.ANY)


def nn(a, b):
    return lax.dot_general(a, b, (((1,), (0,)), ((), ())), preferred_element_type=f32)


def nt(a, b):
    return lax.dot_general(a, b, (((1,), (1,)), ((), ())), preferred_element_type=f32)


def tn(a, b):
    return lax.dot_general(a, b, (((0,), (0,)), ((), ())), preferred_element_type=f32)


def here():
    return {a: lax.axis_index(a) for a in AXES}


def step(me, axis, by):
    return lax.rem(me[axis] + by, SIZE[axis])


def at(me, **moved):
    return tuple(step(me, a, moved[a]) if a in moved else me[a] for a in AXES)


def sequence_starts(ids, lengths):
    starts, end = jnp.zeros_like(ids), 0
    for s in range(SEQS):
        end = end + lengths[s]
        starts = starts + jnp.where(ids >= end, lengths[s], 0)
    return starts


def token_rows(me, lengths):
    column = lax.broadcasted_iota(jnp.int32, (1, 2 * NQ), 1)
    ids = shard_of(me) // 2 * (2 * TOK) + column // NQ * TOK + column % TOK
    return ids, sequence_starts(ids, lengths)


def hail(peers):
    barrier = pltpu.get_barrier_semaphore()
    for p in peers:
        pl.semaphore_signal(barrier, inc=1, device_id=p, device_id_type=MESH)
    return lambda: pl.semaphore_wait(barrier, len(peers))


def greet(peers):
    hail(peers)()


class Copies:
    def __init__(self, send_sems, recv_sems):
        self.send_sems, self.recv_sems, self.used, self.started = send_sems, recv_sems, 0, []

    def make(self, src, dst, target):
        self.used += 1
        return self.numbered(self.used - 1, src, dst, target)

    def numbered(self, k, src, dst, target):
        return pltpu.make_async_remote_copy(
            src_ref=src,
            dst_ref=dst,
            send_sem=self.send_sems.at[k],
            recv_sem=self.recv_sems.at[k],
            device_id=target,
            device_id_type=MESH,
        )

    def send(self, src, dst, target):
        copy = self.make(src, dst, target)
        copy.start()
        self.started.append(copy)
        return copy

    def finish(self):
        for copy in self.started:
            copy.wait_send()


def sems(count):
    return [pltpu.SemaphoreType.DMA((count,)), pltpu.SemaphoreType.DMA((count,))]


def params(ident, mib=60):
    return pltpu.CompilerParams(
        collective_id=ident, has_side_effects=True, vmem_limit_bytes=mib * 2**20
    )


def whole_tiles(values):
    pad = jnp.zeros((values.shape[0], COLUMNS - values.shape[1]), values.dtype)
    return jnp.concatenate([values, pad], axis=1)


def three(ref):
    return ref[0].astype(f32) + ref[1].astype(f32) + ref[2].astype(f32)


def shard_of(me):
    return ((me["z"] * 4 + me["y"]) * 2 + me["xh"]) * 2 + me["c"]


class Rows:
    def __init__(self, me, copies, source, slots):
        self.me, self.copies, self.source, self.slots = me, copies, source, slots
        half = TOK // 2
        n = me["n"]
        self.mine = pl.ds(pl.multiple_of(half * n, half), half)
        self.theirs = pl.ds(pl.multiple_of(half * (1 - n), half), half)
        self.own = slots.at[me["y"], me["c"]]
        self.near = [copies.send(source, self.own, at(me, c=1))]
        self.far, self.across = {}, {}

    def slot(self, d, rows):
        return self.slots.at[lax.rem(self.me["y"] + (4 - d), 4), self.me["c"], rows]

    def start(self, *steps):
        for d in steps:
            self.far[d] = self.copies.send(
                self.source.at[self.mine], self.own.at[self.mine], at(self.me, y=d)
            )

    def pass_on(self, *steps):
        for d in steps:
            self.far[d].wait_recv()
            got = self.slot(d, self.mine)
            self.across[d] = self.copies.send(got, got, at(self.me, n=1))
            self.near.append(self.copies.send(got, got, at(self.me, c=1)))

    def complete(self, *steps):
        for d in steps:
            self.across[d].wait_recv()
            got = self.slot(d, self.theirs)
            self.near.append(self.copies.send(got, got, at(self.me, c=1)))

    def wait(self):
        for copy in self.near:
            copy.wait_recv()


def attend_kernel(
    lengths, x, gain, bias, freqs, og, w_qkv_hbm, kv, q, act, o, exact, lse, cosine, sine, og_all,
    stats, acc, low_acc, stats_in, acc_in, low_in, w_qkv, send_sems, recv_sems, local_sems,
):
    me = here()
    load_w = pltpu.make_async_copy(w_qkv_hbm, w_qkv, local_sems.at[1])
    load_w.start()
    ids, start = token_rows(me, lengths)
    z, y, xh, c = me["z"], me["y"], me["xh"], me["c"]
    partner, across, other = at(me, c=1), at(me, xh=1), at(me, n=1)
    ys = {d: at(me, y=d) for d in (1, 2, 3)}
    zs = {d: at(me, z=d) for d in (1, 2, 3)}
    everyone_in = hail([partner, across, other, *ys.values(), *zs.values()])
    rows = x[...].astype(f32)
    inverse = lax.rsqrt(jnp.mean(rows * rows, axis=-1, keepdims=True) + rms_eps)
    act[...] = (rows * inverse * gain[...].reshape(1, D)).astype(bf16)
    token = shard_of(me) * TOK + lax.broadcasted_iota(jnp.int32, (TOK, 1), 0)
    angles = (token - sequence_starts(token, lengths)).astype(f32) * freqs[...]
    cosine[...] = jnp.cos(angles)
    turned = jnp.sin(angles)
    first_half = lax.broadcasted_iota(jnp.int32, (TOK, HD), 1) < HD // 2
    sine[...] = jnp.where(first_half, -turned, turned)
    front = HEADS * HD

    def turn(values):
        return values * cosine[...] + pltpu.roll(values, HD // 2, 1) * sine[...]

    load_w.wait()
    back = nn(act[...], w_qkv[:, front:]) + bias[:, front:]
    mine = kv.at[z, y, xh]
    mine[:, pl.ds(0, HD)] = turn(back[:, :HD]).astype(bf16)
    mine[:, pl.ds(HD, HD)] = back[:, HD:].astype(bf16)
    everyone_in()
    copies = Copies(send_sems, recv_sems)
    first = copies.send(mine, mine, across)
    ahead = nn(act[...], w_qkv[:, :front]) + bias[:, :front]
    for h in range(HEADS):
        head = turn(ahead[:, h * HD : (h + 1) * HD]).astype(bf16)
        q[c, pl.ds(h * TOK, TOK), :] = head
    share_q = copies.send(q.at[c], q.at[c], partner)
    rows_of_og = Rows(me, copies, og, og_all)
    rows_of_og.start(1, 3)
    local = pltpu.make_async_copy(og, og_all.at[y, c], local_sems.at[0])
    local.start()
    stats[:, 0:1, :] = jnp.full((2, 1, NQ), big_negative, f32)
    stats[:, 1:8, :] = jnp.zeros((2, 7, NQ), f32)
    acc[...] = jnp.zeros_like(acc)
    low_acc[...] = jnp.zeros_like(low_acc)
    last = shard_of(me) // BLOCK_SHARDS
    kept = start < last * KEY_BLOCK
    half = TOK // 2
    keys_here = 2 * half

    def take(parts, masked):
        def both(columns):
            return jnp.concatenate(
                [
                    kv[zi, yi, :, pl.ds(pl.multiple_of(half * k, half), half), columns].reshape(
                        keys_here, HD
                    )
                    for zi, yi, k in parts
                ],
                axis=0,
            )

        keys, values = both(pl.ds(0, HD)), both(pl.ds(HD, HD)).T
        for chunk in range(2 * NQ // Q_CHUNK):
            core, cs = divmod(chunk * Q_CHUNK, NQ)
            cs = pl.ds(cs, Q_CHUNK)
            here_cols = slice(chunk * Q_CHUNK, (chunk + 1) * Q_CHUNK)
            scores = nt(keys, q[core, cs, :]) * SCALE_LOG2
            if masked:
                ((zi, yi, k),) = parts
                place = lax.broadcasted_iota(jnp.int32, (keys_here, Q_CHUNK), 0)
                first_key = (4 * zi + yi) * KEY_BLOCK + c * TOK + half * k
                key_ids = first_key + place + place // half * (2 * TOK - half)
                allowed = (key_ids >= start[:, here_cols]) & (key_ids <= ids[:, here_cols])
                scores = jnp.where(allowed, scores, big_negative)
            old = stats[core, 0:1, cs]
            new = jnp.maximum(old, jnp.max(scores, axis=0, keepdims=True))
            if masked:
                probs = jnp.where(allowed, jnp.exp2(scores - new), 0.0)
            else:
                taken = kept[:, here_cols]
                new = jnp.where(taken, new, old)
                probs = jnp.exp2(scores - jnp.where(taken, new, -big_negative))
            fade = jnp.exp2(old - new)
            stats[core, 0:1, cs] = new
            stats[core, 1:2, cs] = stats[core, 1:2, cs] * fade + jnp.sum(probs, axis=0, keepdims=True)
            upper = probs.astype(bf16)
            rest = (probs - upper.astype(f32)).astype(bf16)
            acc[core, :, cs] = acc[core, :, cs] * fade + nn(values, upper)
            low_acc[core, :, cs] = low_acc[core, :, cs] * fade + nn(values, rest)

    def pair(za, ya, zb, yb):
        a, b = 4 * za + ya, 4 * zb + yb
        inner = (jnp.minimum(a, b) > 0) & (jnp.maximum(a, b) < last)

        @pl.when(inner)
        def _():
            take([(za, ya, 0), (zb, yb, 1)], False)

        @pl.when(jnp.logical_not(inner))
        def _():
            @pl.loop(0, 2)
            def _(k):
                zi, yi = jnp.where(k == 0, za, zb), jnp.where(k == 0, ya, yb)
                index = 4 * zi + yi
                edge = (index == 0) | (index == last)

                @pl.when(edge & (index <= last))
                def _():
                    take([(zi, yi, k)], True)

                @pl.when((index < last) & jnp.logical_not(edge))
                def _():
                    take([(zi, yi, k)], False)

    first.wait_recv()
    low, high = pl.ds(0, half), pl.ds(half, half)

    def slot(zi, yi, rows):
        return kv.at[zi, yi, :, rows]

    def before(axis, d):
        return lax.rem(me[axis] + (4 - d), 4)

    first_low, first_high = {}, {}
    for d in (1, 3, 2):
        first_low[d] = copies.send(slot(z, y, low), slot(z, y, low), ys[d])
        first_high[d] = copies.send(slot(z, y, high), slot(z, y, high), zs[d])
    share_q.wait_recv()

    pair(z, y, z, y)
    second_from = copies.used
    copies.used += 24
    for i, e in enumerate((0, 1, 3, 2)):
        yi, zi = before("y", e), before("z", e)
        if e:
            first_low[e].wait_recv()
            first_high[e].wait_recv()
        for j, d in enumerate((1, 3, 2)):
            k = second_from + 2 * (3 * i + j)
            for copy in (
                copies.numbered(k, slot(z, yi, low), slot(z, yi, low), zs[d]),
                copies.numbered(k + 1, slot(zi, y, high), slot(zi, y, high), ys[d]),
            ):
                copy.start()
                copies.started.append(copy)
    rows_of_og.start(2)
    rows_of_og.pass_on(1, 3)

    @pl.loop(1, 4)
    def _(e):
        pair(z, before("y", e), before("z", e), y)

    def places(k):
        i, j = k // 3, lax.rem(k, 3)
        e = jnp.where(i < 2, i, 5 - i)
        d = jnp.where(j < 2, 1 + 2 * j, 2)
        return before("z", d), before("y", e), before("z", e), before("y", d)

    def arrive(k):
        za, ya, zb, yb = places(k)
        one, two = slot(za, ya, low), slot(zb, yb, high)
        copies.numbered(second_from + 2 * k, one, one, zs[1]).wait_recv()
        copies.numbered(second_from + 2 * k + 1, two, two, ys[1]).wait_recv()
        pair(za, ya, zb, yb)

    pl.loop(0, 8)(arrive)
    rows_of_og.pass_on(2)
    pl.loop(8, 12)(arrive)
    merge = [
        copies.send(stats.at[1 - c], stats_in, partner),
        copies.send(acc.at[1 - c], acc_in, partner),
        copies.send(low_acc.at[1 - c], low_in, partner),
    ]
    rows_of_og.complete(1, 3, 2)
    for copy in merge:
        copy.wait_recv()
    own_top, in_top = stats[c, 0:1, :], stats_in[0:1, :]
    top = jnp.maximum(own_top, in_top)
    own_part, in_part = jnp.exp2(own_top - top), jnp.exp2(in_top - top)
    total = stats[c, 1:2, :] * own_part + stats_in[1:2, :] * in_part
    inverse = 1.0 / total
    own_part, in_part = own_part * inverse, in_part * inverse
    rows = acc[c] * own_part + acc_in[...] * in_part
    exact[...] = rows + (low_acc[c] * own_part + low_in[...] * in_part)
    rows = rows.T.astype(bf16)
    for h in range(HEADS):
        o[:, pl.ds(h * HD, HD)] = rows[h * TOK : (h + 1) * TOK]
    lse[...] = top + jnp.log2(total)
    rows_of_og.wait()
    local.wait()
    copies.finish()


def attend(*arrays):
    slots = jax.ShapeDtypeStruct((4, 2, TOK, D), bf16)
    return pl.pallas_call(
        attend_kernel,
        out_shape=(
            jax.ShapeDtypeStruct((4, 4, 2, TOK, 2 * HD), bf16),
            jax.ShapeDtypeStruct((2, NQ, HD), bf16),
            jax.ShapeDtypeStruct((TOK, D), bf16),
            jax.ShapeDtypeStruct((TOK, HEADS * HD), bf16),
            jax.ShapeDtypeStruct((HD, NQ), f32),
            jax.ShapeDtypeStruct((1, NQ), f32),
            jax.ShapeDtypeStruct((TOK, HD), f32),
            jax.ShapeDtypeStruct((TOK, HD), f32),
            slots,
        ),
        in_specs=[SMEM] + [VMEM] * 5 + [ANY],
        out_specs=(VMEM,) * 8 + (ANY,),
        scratch_shapes=[
            pltpu.VMEM((2, 8, NQ), f32),
            pltpu.VMEM((2, HD, NQ), f32),
            pltpu.VMEM((2, HD, NQ), f32),
            pltpu.VMEM((8, NQ), f32),
            pltpu.VMEM((HD, NQ), f32),
            pltpu.VMEM((HD, NQ), f32),
            pltpu.VMEM((D, (HEADS + 2) * HD), bf16),
            *sems(110),
            pltpu.SemaphoreType.DMA((2,)),
        ],
        compiler_params=params(1),
    )(*arrays)


def mlp_kernel(*refs):
    attn_low, x, gain, og, aa, w_out_hbm, og_hbm, w_gate_hbm, w_up_hbm, w_down_hbm = refs[:10]
    resid, grad_resid, grads, gain_terms, gate_sum, down_near, down_far, up_hbm, down_hbm, aa_all = refs[10:20]
    pa, pb, wd, og_all, act_all, grad_hidden, hidden, ggp, gup, bk, dn, bk_core, dn_core, bk_sent, bk_in = refs[20:35]
    nb, rn, gate_terms, gate_in, gate_w, up_w, wide_gate, wide_up, up_terms, down_terms = refs[35:45]
    down_sum, dn_in, w_out, send_sems, recv_sems, local_sems = refs[45:]
    me = here()
    z, y, c = me["z"], me["y"], me["c"]
    partner, other = at(me, c=1), at(me, n=1)
    ys = {d: at(me, y=d) for d in (1, 2, 3)}
    zs = {d: at(me, z=d) for d in (1, 2, 3)}
    everyone_in = hail([partner, other, *ys.values(), *zs.values()])
    load_out = pltpu.make_async_copy(w_out_hbm, w_out, local_sems.at[7])
    load_out.start()
    units = pl.ds(pl.multiple_of((y * 2 + c) * UNITS, 16), UNITS)
    load_down = pltpu.make_async_copy(w_down_hbm.at[units], wd, local_sems.at[0])
    load_down.start()
    load_og = pltpu.make_async_copy(og_hbm, og_all, local_sems.at[1])
    load_og.start()
    first = (y * 2 + c) * UNITS
    tile = jnp.minimum(first // 128, FF // 2 // 128 - WINDOW // 128)
    window = pl.ds(pl.multiple_of(tile * 128, 128), WINDOW)
    load_wide = []
    for i, (whole, part) in enumerate(((w_gate_hbm, wide_gate), (w_up_hbm, wide_up))):
        load_wide.append(pltpu.make_async_copy(whole.at[:, window], part, local_sems.at[2 + i]))
        load_wide[-1].start()
    keep_aa = pltpu.make_async_copy(aa, aa_all.at[y, c], local_sems.at[4])
    keep_aa.start()
    load_out.wait()
    pa[...] = nn(attn_low[...], w_out[...]).astype(bf16)
    everyone_in()
    copies = Copies(send_sems, recv_sems)
    half = TOK // 2
    halves = (pl.ds(0, half), pl.ds(half, half))
    swaps = [copies.send(pa.at[rows], pb.at[rows], other) for rows in halves]
    aa_rows = Rows(me, copies, aa, aa_all)
    aa_rows.start(1, 3, 2)
    load_down.wait()
    load_og.wait()
    pair = (2 * TOK, D)
    for yi in range(4):
        grad_hidden[yi] = nt(og_all[yi].reshape(pair), wd[...])
    turn = lax.rem(WINDOW - (first - tile * 128), WINDOW)
    for copy, part, weights in ((load_wide[0], wide_gate, gate_w), (load_wide[1], wide_up, up_w)):
        copy.wait()

        @pl.loop(0, D // 128)
        def _(index, part=part, weights=weights):
            rows = pl.ds(pl.multiple_of(index * 128, 128), 128)
            turned = pltpu.roll(part[rows, :].astype(f32), turn, 1)
            weights[rows, :] = turned[:, :UNITS].astype(bf16)

    gain = gain[...].reshape(1, D)

    def inverse_of(rows):
        return lax.rsqrt(jnp.mean(rows * rows, axis=-1, keepdims=True) + rms_eps)

    own = act_all.at[y, c]
    far, to_core = {}, {0: [], 1: [], 2: [], 3: []}
    for k, rows in enumerate(halves):
        swaps[k].wait_recv()
        total = x[rows, :].astype(f32) + (pa[rows, :].astype(f32) + pb[rows, :].astype(f32))
        resid[rows, :] = total
        act_all[y, c, rows] = (total * inverse_of(total) * gain).astype(bf16)
        to_core[0].append(copies.send(own.at[rows], own.at[rows], partner))
        for d in (1, 3):
            far[d, k] = copies.send(own.at[rows], own.at[rows], ys[d])
    bk_cores, dn_cores, bk_moves = {}, {}, {}

    def block(d, beside=None):
        yi = step(me, "y", d)
        rows = act_all[yi].reshape(pair)
        gate = nn(rows, gate_w[...])
        up = nn(rows, up_w[...])
        sigmoid = 1.0 / (1.0 + jnp.exp(-gate))
        silu = gate * sigmoid
        grads = grad_hidden[yi]
        hidden[yi] = (silu * up).astype(bf16)
        ggp[yi] = (grads * up * (sigmoid * (1.0 + gate * (1.0 - sigmoid)))).astype(bf16)
        gup[yi] = (grads * silu).astype(bf16)
        if beside is not None:
            pass_block(beside)
        both = nt(ggp[yi], gate_w[...]) + nt(gup[yi], up_w[...])
        bk[yi] = both.astype(bf16).reshape(2, TOK, D)
        bk_cores[d] = copies.send(bk.at[yi, 1 - c], bk_core.at[yi], partner)
    low, high = halves

    def pass_block(d):
        yi = step(me, "y", d)
        bk_cores[d].wait_recv()
        for k, rows in enumerate((low, high)):
            bk_sent[yi, rows] = (
                bk[yi, c, rows].astype(f32) + bk_core[yi, rows].astype(f32)
            ).astype(bf16)
            if d:
                bk_moves[d, k] = copies.send(
                    bk_sent.at[yi, rows], bk_in.at[d - 1, rows], ys[d]
                )

    def down_block(d):
        yi = step(me, "y", d)
        dn[yi] = nn(hidden[yi], wd[...]).astype(bf16).reshape(2, TOK, D)
        dn_cores[d] = copies.send(dn.at[yi, 1 - c], dn_core.at[yi], partner)

    def sum_down(d):
        yi = step(me, "y", d)
        dn_cores[d].wait_recv()
        down_sum[yi] = (dn[yi, c].astype(f32) + dn_core[yi].astype(f32)).astype(bf16)

    for copy in to_core[0]:
        copy.wait_recv()
    block(0)
    aa_rows.pass_on(1, 3, 2)
    relay = {}
    for k, rows in enumerate(halves):
        for d in (1, 3):
            far[d, k].wait_recv()
            got = act_all.at[lax.rem(y + (4 - d), 4), c, rows]
            to_core[4 - d].append(copies.send(got, got, partner))
            if d == 1 + 2 * k:
                relay[d] = copies.send(got, got, ys[d])
    for copy in to_core[3]:
        copy.wait_recv()
    block(3, 0)
    for d, rows in ((1, low), (3, high)):
        relay[d].wait_recv()
        got = act_all.at[step(me, "y", 2), c, rows]
        to_core[2].append(copies.send(got, got, partner))
    for copy in to_core[1]:
        copy.wait_recv()
    block(1, 3)
    for copy in to_core[2]:
        copy.wait_recv()
    block(2, 1)

    aa_rows.complete(1, 3, 2)
    everything = (GROUP * TOK, D)
    all_units = (GROUP * TOK, UNITS)
    gate_terms[...] = tn(ggp[...].reshape(all_units), act_all[...].reshape(everything)).astype(bf16)

    def z_cols(d):
        return pl.ds(pl.multiple_of(step(me, "z", d) * 384, 384), 384)

    gate_moves = {
        d: copies.send(gate_terms.at[:, z_cols(d)], gate_in.at[d - 1], zs[d]) for d in (1, 3, 2)
    }
    pass_block(2)
    for d in (1, 3, 2, 0):
        down_block(d)
    up_terms[...] = tn(gup[...].reshape(all_units), act_all[...].reshape(everything)).astype(bf16)
    keep_up = pltpu.make_async_copy(up_terms, up_hbm, local_sems.at[5])
    keep_up.start()
    for d in range(4):
        sum_down(d)
    swaps_back = []
    for k, rows in enumerate((low, high)):
        back = bk_sent[y, rows].astype(f32)
        for d in (1, 3, 2):
            bk_moves[d, k].wait_recv()
            back = back + bk_in[d - 1, rows].astype(f32)
        nb[rows] = back.astype(bf16)
        swaps_back.append(copies.send(nb.at[rows], rn.at[rows], other))
    dn_moves = {
        d: copies.send(down_sum.at[step(me, "y", d)], dn_in.at[d // 2], ys[d]) for d in (1, 3)
    }
    down_far[...] = down_sum[step(me, "y", 2)]
    for zi in range(4):
        columns = og_all[:, :, :, pl.ds(384 * zi, 384)].reshape(GROUP * TOK, 384)
        sums = whole_tiles(tn(columns, hidden[...].reshape(all_units)).astype(bf16))
        down_terms[zi] = sums.reshape(4, 2, 48, COLUMNS)
    keep_down = pltpu.make_async_copy(down_terms, down_hbm, local_sems.at[6])
    keep_down.start()
    for copy in swaps_back:
        copy.wait_recv()
    grad_act = nb[...].astype(f32) + rn[...].astype(f32)
    inverse = inverse_of(resid[...])
    normed = resid[...] * inverse
    gain_terms[...] = jnp.sum(grad_act * normed, axis=0, keepdims=True)
    grad_normed = grad_act * gain
    inner = jnp.mean(grad_normed * normed, axis=-1, keepdims=True)
    grad_resid[...] = og[...].astype(f32) + inverse * (grad_normed - normed * inner)
    grads[...] = nt(grad_resid[...].astype(bf16), w_out[...]).astype(bf16)
    for d in (1, 3, 2):
        gate_moves[d].wait_recv()
    gate_sum[...] = whole_tiles((gate_terms[:, z_cols(0)].astype(f32) + three(gate_in)).T.astype(bf16))
    total = down_sum[y].astype(f32)
    for d in (1, 3):
        dn_moves[d].wait_recv()
        total = total + dn_in[d // 2].astype(f32)
    down_near[...] = total
    keep_up.wait()
    keep_down.wait()
    aa_rows.wait()
    keep_aa.wait()
    copies.finish()


def feed_forward(*arrays):
    rows = pltpu.VMEM((TOK, D), bf16)
    return pl.pallas_call(
        mlp_kernel,
        out_shape=[
            jax.ShapeDtypeStruct((TOK, D), f32),
            jax.ShapeDtypeStruct((TOK, D), f32),
            jax.ShapeDtypeStruct((TOK, HEADS * HD), bf16),
            jax.ShapeDtypeStruct((1, D), f32),
            jax.ShapeDtypeStruct((D // 4, COLUMNS), bf16),
            jax.ShapeDtypeStruct((TOK, D), f32),
            jax.ShapeDtypeStruct((TOK, D), bf16),
            jax.ShapeDtypeStruct((UNITS, D), bf16),
            jax.ShapeDtypeStruct((4, 4, 2, 48, COLUMNS), bf16),
            jax.ShapeDtypeStruct((4, 2, TOK, D), bf16),
        ],
        in_specs=[VMEM] * 5 + [ANY] * 5,
        out_specs=[VMEM] * 7 + [ANY] * 3,
        scratch_shapes=[
            rows,
            rows,
            pltpu.VMEM((UNITS, D), bf16),
            pltpu.VMEM((4, 2, TOK, D), bf16),
            pltpu.VMEM((4, 2, TOK, D), bf16),
            pltpu.VMEM((4, 2 * TOK, UNITS), f32),
            *[pltpu.VMEM((4, 2 * TOK, UNITS), bf16)] * 3,
            *[pltpu.VMEM((4, 2, TOK, D), bf16)] * 2,
            *[pltpu.VMEM((4, TOK, D), bf16)] * 3,
            pltpu.VMEM((3, TOK, D), bf16),
            rows,
            rows,
            pltpu.VMEM((UNITS, D), bf16),
            pltpu.VMEM((3, UNITS, D // 4), bf16),
            *[pltpu.VMEM((D, UNITS), bf16)] * 2,
            *[pltpu.VMEM((D, WINDOW), bf16)] * 2,
            pltpu.VMEM((UNITS, D), bf16),
            pltpu.VMEM((4, 4, 2, 48, COLUMNS), bf16),
            pltpu.VMEM((4, TOK, D), bf16),
            pltpu.VMEM((2, TOK, D), bf16),
            pltpu.VMEM((HEADS * HD, D), bf16),
            *sems(70),
            pltpu.SemaphoreType.DMA((8,)),
        ],
        compiler_params=params(2),
    )(*arrays)


def back_kernel(*refs):
    lengths, lse, grad_resid, grads_in, attn_low, cosine, sine, x, gain, mlp_gain_terms, gate_sum, down_far = refs[:12]
    q_hbm, kv_hbm, exact_hbm, resid_hbm, near_hbm, w_qkv_hbm, act_hbm, up_terms, wd_terms = refs[12:21]
    in_grad, layer_out, sum_gate, sum_up, sum_down, sum_qkv, sum_out, small_out = refs[21:29]
    (g, stats, acc, acc_in, dkv, r1a, r1b, ta, tb, r2a, r2b, u, r3, w_qkv, act_all, gb_all, al_heads, al_all) = refs[29:47]
    gp, gp_flat, gp_all, part, part_other, small, e1, e2, e3, f1, f2 = refs[47:58]
    up_own, up_in, up_mid, wd_own, wd_across, wd_sum, wd_in, wd_mid, wd_second = refs[58:67]
    gate_second, up_second = refs[67:69]
    summed, third_in = refs[69:72], refs[72:75]
    q_terms, q_first, q_mid, q_second, q_summed, q_third = refs[75:81]
    down_in, down_part, down_other, q, kv, exact, resid, down_near, send_sems, recv_sems, local_sems = refs[81:]

    me = here()
    ids, start = token_rows(me, lengths)
    z, y, xh, c, n = (me[a] for a in AXES)
    partner, across, other = at(me, c=1), at(me, xh=1), at(me, n=1)
    ys = {d: at(me, y=d) for d in (1, 2, 3)}
    zs = {d: at(me, z=d) for d in (1, 2, 3)}
    near_moves = [(d, e) for d in (1, 3, 2, 0) for e in (0, 1) if d or e]
    near = {m: at(me, y=m[0], xh=m[1]) for m in near_moves}
    group = {m: at(me, y=m[0], c=m[1]) for m in near_moves}
    everyone_in = hail([other, *zs.values(), *near.values(), *(group[m] for m in near_moves if m[1])])
    local = []

    def load(src, dst):
        copy = pltpu.make_async_copy(src, dst, local_sems.at[len(local)])
        copy.start()
        local.append(copy)
        return copy

    loads = [load(exact_hbm, exact), load(q_hbm, q), load(kv_hbm, kv)]
    load_resid, load_near = load(resid_hbm, resid), load(near_hbm, down_near)
    half = TOK // 2
    low, high = pl.ds(0, half), pl.ds(half, half)
    gb_all[y, c] = grad_resid[...].astype(bf16)
    for h in range(HEADS):
        g[c, pl.ds(h * TOK, TOK), :] = grads_in[:, h * HD : (h + 1) * HD]
    loads[0].wait()
    stats[c, 0:1, :] = lse[...]
    stats[c, 1:2, :] = jnp.sum(g[c].astype(f32).T * exact[...], axis=0, keepdims=True)
    stats[c, 2:8, :] = jnp.zeros((6, NQ), f32)
    everyone_in()
    copies = Copies(send_sems, recv_sems)
    shared = [copies.send(g.at[c], g.at[c], partner), copies.send(stats.at[c], stats.at[c], partner)]

    def z_cols(d):
        return pl.ds(pl.multiple_of(step(me, "z", d) * 384, 384), 384)

    second = {}

    def send_second(i, source, in_ref):
        for m in near_moves:
            second[i, m] = copies.send(
                source(step(me, "y", m[0]), step(me, "xh", m[1])), in_ref.at[y, xh], near[m]
            )

    def strip(yi, xi):
        return pl.ds(pl.multiple_of(96 * yi + 48 * xi, 48), 48)

    def send_mid(i, total, mid_ref, in_ref):
        turned = total.T.astype(bf16)
        if turned.shape[1] == UNITS:
            turned = whole_tiles(turned)
        for yi in range(4):
            for xi in range(2):
                rows = 96 * yi + 48 * xi
                mid_ref[yi, xi] = turned[rows : rows + 48]
        send_second(i, lambda yi, xi: mid_ref.at[yi, xi], in_ref)
        in_ref[y, xh] = mid_ref[y, xh]

    keep, give = pl.ds(pl.multiple_of(24 * c, 8), 24), pl.ds(pl.multiple_of(24 * (1 - c), 8), 24)
    third = {}
    all_summed = [*summed, q_summed]
    all_second = [gate_second, up_second, None, q_second]
    all_third = [*third_in, q_third]
    outs = ((sum_gate,), (sum_up,), (sum_down,), (sum_qkv, sum_out))

    def collect(i):
        if i == 2:
            for d in (1, 3, 2):
                second[2, d].wait_recv()
            summed[2][...] = wd_second[...].astype(f32)
        else:
            for m in near_moves:
                second[i, m].wait_recv()
            all_summed[i][...] = all_second[i][:, 0].astype(f32) + all_second[i][:, 1].astype(f32)
        third[i] = copies.send(all_summed[i].at[:, give], all_third[i], partner)

    def deliver(i):
        third[i].wait_recv()
        for yi in range(4):
            mine_sum, their_sum = all_summed[i][yi, keep], all_third[i][yi]
            pair = (jnp.where(c == 0, mine_sum, their_sum), jnp.where(c == 0, their_sum, mine_sum))
            for e in range(2):
                k = 2 * yi + e
                if i < 3:
                    outs[i][0][:, pl.ds(k * UNITS, UNITS)] = pair[e][:, :UNITS]
                else:
                    outs[i][0][:, pl.ds(k * HD, HD)] = pair[e][:, :HD]
                    if k < HEADS:
                        outs[i][1][:, pl.ds(k * HD, HD)] = pair[e][:, HD:]

    send_second(0, lambda yi, xi: gate_sum.at[strip(yi, xi)], gate_second)
    gate_second[y, xh] = gate_sum[strip(y, xh), :]
    first = {}
    for d in (1, 3, 2):
        first[d] = copies.send(up_terms.at[:, z_cols(d)], up_in.at[d - 1], zs[d])
    wd_move = copies.send(wd_terms.at[:, :, 1 - xh], wd_across, across)

    branches = Rows(me, copies, gb_all.at[y, c], gb_all)
    branches.start(1, 3, 2)
    for h in range(HEADS):
        al_heads[h] = attn_low[:, pl.ds(h * HD, HD)]

    def head_of(d, e):
        taker = step(me, "y", d) * 2 + step(me, "c", e)
        return jnp.where(taker < HEADS, taker, 0)

    al_moves = [
        copies.send(al_heads.at[head_of(*m)], al_all.at[y, c], group[m]) for m in near_moves
    ]
    al_all[y, c] = al_heads[head_of(0, 0)]
    load_w = load(w_qkv_hbm, w_qkv)
    load_act = load(act_hbm, act_all)
    load_up = load(up_terms.at[:, z_cols(0)], up_own)
    load_wd = load(wd_terms.at[:, :, xh], wd_own)

    for copy in shared:
        copy.wait_recv()
    for copy in loads[1:]:
        copy.wait()
    acc[...] = jnp.zeros_like(acc)
    last = shard_of(me) // BLOCK_SHARDS

    def of_both(row):
        return jnp.concatenate([stats[0, row : row + 1, :], stats[1, row : row + 1, :]], axis=1)

    log_total, balance = of_both(0), of_both(1)
    earlier = jnp.where(start < last * KEY_BLOCK, log_total, -big_negative)
    keys_here = 2 * TOK

    def block(index, masked, shift):
        zi, yi = index // 4, lax.rem(index, 4)
        keys = kv[zi, yi, :, :, pl.ds(0, HD)].reshape(keys_here, HD)
        values = kv[zi, yi, :, :, pl.ds(HD, HD)].reshape(keys_here, HD)
        keys_t = keys.T
        dk = jnp.zeros((keys_here, HD), f32)
        dv = jnp.zeros((keys_here, HD), f32)
        for chunk in range(2 * NQ // Q_CHUNK):
            core, cs = divmod(chunk * Q_CHUNK, NQ)
            cs = pl.ds(cs, Q_CHUNK)
            piece = slice(chunk * Q_CHUNK, (chunk + 1) * Q_CHUNK)
            qc, gc = q[core, cs, :], g[core, cs, :]
            probs = jnp.exp2(nt(keys, qc) * SCALE_LOG2 - shift[:, piece])
            if masked:
                place = lax.broadcasted_iota(jnp.int32, (keys_here, Q_CHUNK), 0)
                key_ids = index * KEY_BLOCK + c * TOK + place + place // TOK * TOK
                allowed = (key_ids >= start[:, piece]) & (key_ids <= ids[:, piece])
                probs = jnp.where(allowed, probs, 0.0)
            grads = (probs * (nt(values, gc) - balance[:, piece])).astype(bf16)
            dv = dv + nn(probs.astype(bf16), gc)
            dk = dk + nn(grads, qc)
            acc[core, :, cs] = acc[core, :, cs] + nn(keys_t, grads)
        dkv[zi, yi, :, :, pl.ds(0, HD)] = (dk * SCALE).astype(bf16).reshape(2, TOK, HD)
        dkv[zi, yi, :, :, pl.ds(HD, HD)] = dv.astype(bf16).reshape(2, TOK, HD)

    def segment(zi):
        @pl.loop(0, 4)
        def _(yi):
            index = 4 * zi + yi
            edge = (index == 0) | (index == last)

            @pl.when(edge & (index <= last))
            def _():
                block(index, True, jnp.where(index == last, log_total, earlier))

            @pl.when((index < last) & jnp.logical_not(edge))
            def _():
                block(index, False, earlier)

            @pl.when(index > last)
            def _():
                dkv[zi, yi] = jnp.zeros((2, TOK, 2 * HD), bf16)

    first_a, first_b, second_a, second_b = {}, {}, {}, {}

    def settle(d):
        zi = step(me, "z", d)
        if d:
            first_a[d] = copies.send(dkv.at[zi, :, :, low], r1a.at[d - 1], zs[d])
        for e in (1, 3, 2):
            first_b[d, e] = copies.send(
                dkv.at[zi, step(me, "y", e), :, high], r1b.at[e - 1, zi], ys[e]
            )

    segment(step(me, "z", 1))
    settle(1)
    segment(step(me, "z", 2))
    settle(2)
    segment(step(me, "z", 3))
    settle(3)
    branches.pass_on(1, 3, 2)
    segment(z)
    settle(0)
    queries_back = copies.send(acc.at[1 - c], acc_in, partner)
    for d in (1, 3, 2):
        first_a[d].wait_recv()
    ta[...] = (dkv[z, :, :, low].astype(f32) + three(r1a)).astype(bf16)
    for d in (1, 3, 2):
        second_a[d] = copies.send(ta.at[step(me, "y", d)], r2a.at[d - 1], ys[d])
    for copy in first_b.values():
        copy.wait_recv()
    tb[...] = (dkv[:, y, :, high].astype(f32) + three(r1b)).astype(bf16)
    for d in (1, 3, 2):
        second_b[d] = copies.send(tb.at[step(me, "z", d)], r2b.at[d - 1], zs[d])
    branches.complete(1, 3, 2)
    for d in (1, 3, 2):
        second_a[d].wait_recv()
        second_b[d].wait_recv()
    ua = ta[y].astype(f32) + three(r2a)
    ub = tb[z].astype(f32) + three(r2b)
    u[:, low] = ua.astype(bf16)
    u[:, high] = ub.astype(bf16)
    kv_last = copies.send(u.at[1 - xh], r3, across)
    load_wd.wait()
    wd_move.wait_recv()
    for zi in range(4):
        wd_sum[zi] = (wd_own[zi].astype(f32) + wd_across[zi].astype(f32)).astype(bf16)
    wd_first = {d: copies.send(wd_sum.at[step(me, "z", d)], wd_in.at[d - 1], zs[d]) for d in (1, 3, 2)}
    load_up.wait()
    for d in (1, 3, 2):
        first[d].wait_recv()
    send_mid(1, up_own[...].astype(f32) + three(up_in), up_mid, up_second)
    branches.wait()
    for copy in al_moves:
        copy.wait_recv()
    q_terms[pl.ds(HD, HD), :] = tn(
        al_all[...].reshape(GROUP * TOK, HD), gb_all[...].reshape(GROUP * TOK, D)
    ).astype(bf16)
    q_two = {d: copies.send(q_terms.at[pl.ds(HD, HD), z_cols(d)], q_first.at[d - 1, pl.ds(HD, HD)], zs[d]) for d in (1, 3, 2)}

    queries_back.wait_recv()
    turned_back = ((acc[c] + acc_in[...]) * SCALE).T

    def revert(rows):
        return rows * cosine[...] - pltpu.roll(rows, HD // 2, 1) * sine[...]

    def keep_head(h, rows):
        low_rows = rows.astype(bf16)
        gp[h] = low_rows
        gp_flat[:, pl.ds(h * HD, HD)] = low_rows
        small[pl.ds(24 + h, 1), :] = jnp.sum(low_rows.astype(f32), axis=0, keepdims=True)

    def to_small(first_row, row):
        for k in range(D // 128):
            small[pl.ds(first_row + k, 1), :] = row[:, k * 128 : (k + 1) * 128]

    small[...] = jnp.zeros_like(small)
    to_small(12, mlp_gain_terms[...])
    for h in range(HEADS):
        keep_head(h, revert(turned_back[h * TOK : (h + 1) * TOK]))
    load_w.wait()
    front = HEADS * HD
    partial = nt(gp_flat[:, pl.ds(0, front)], w_qkv[:, pl.ds(0, front)])

    kv_last.wait_recv()
    grad_kv = u[xh].astype(f32) + r3[...].astype(f32)
    keep_head(HEADS, revert(grad_kv[:, :HD]))
    keep_head(HEADS + 1, grad_kv[:, HD:])
    gp_moves = [
        copies.send(gp.at[step(me, "y", m[0]) * 2 + step(me, "c", m[1])], gp_all.at[y, c], group[m])
        for m in near_moves
    ]
    gp_all[y, c] = gp[y * 2 + c]
    down_move = copies.send(down_far, down_in, ys[2])
    back = pl.ds(front, 2 * HD)
    part[...] = (partial + nt(gp_flat[:, back], w_qkv[:, back])).astype(bf16)
    swap = copies.send(part, part_other, other)
    collect(0)
    load_act.wait()
    for copy in gp_moves:
        copy.wait_recv()
    q_terms[pl.ds(0, HD), :] = tn(
        gp_all[...].reshape(GROUP * TOK, HD), act_all[...].reshape(GROUP * TOK, D)
    ).astype(bf16)

    q_one = {d: copies.send(q_terms.at[pl.ds(0, HD), z_cols(d)], q_first.at[d - 1, pl.ds(0, HD)], zs[d]) for d in (1, 3, 2)}
    down_move.wait_recv()
    load_near.wait()
    down_part[...] = (down_near[...] + down_in[...].astype(f32)).astype(bf16)
    down_swaps = [copies.send(down_part.at[low], down_other.at[low], other)]
    swap.wait_recv()
    grad_act = part[...].astype(f32) + part_other[...].astype(f32)
    rows = x[...].astype(f32)
    inverse = lax.rsqrt(jnp.mean(rows * rows, axis=-1, keepdims=True) + rms_eps)
    normed = rows * inverse
    to_small(0, jnp.sum(grad_act * normed, axis=0, keepdims=True))
    small_one = {d: copies.send(small, e1.at[d - 1], zs[d]) for d in (1, 3, 2)}
    grad_normed = grad_act * gain[...].reshape(1, D)
    inner = jnp.mean(grad_normed * normed, axis=-1, keepdims=True)
    in_grad[...] = (grad_resid[...] + inverse * (grad_normed - normed * inner)).astype(bf16)

    for d in (1, 3, 2):
        wd_first[d].wait_recv()
    wd_mid[...] = (wd_sum[z].astype(f32) + three(wd_in)).astype(bf16)
    for d in (1, 3, 2):
        second[2, d] = copies.send(wd_mid.at[step(me, "y", d)], wd_second.at[y], ys[d])
    wd_second[y] = wd_mid[y]
    for d in (1, 3, 2):
        q_one[d].wait_recv()
        q_two[d].wait_recv()
    send_mid(3, q_terms[:, z_cols(0)].astype(f32) + three(q_first), q_mid, q_second)
    for d in (1, 3, 2):
        small_one[d].wait_recv()
    f1[...] = small[...] + three(e1)
    small_two = {m: copies.send(f1, e2.at[k], near[m]) for k, m in enumerate(near_moves)}
    down_swaps.append(copies.send(down_part.at[high], down_other.at[high], other))
    collect(1)
    deliver(0)
    deliver(1)
    collect(2)
    collect(3)
    for m in near_moves:
        small_two[m].wait_recv()
    f2[...] = f1[...]
    for k in range(len(near_moves)):
        f2[...] = f2[...] + e2[k]
    small_three = copies.send(f2, e3, partner)
    deliver(2)
    deliver(3)
    small_three.wait_recv()
    small_out[...] = f2[...] + e3[...]
    for copy in down_swaps:
        copy.wait_recv()
    load_resid.wait()
    layer_out[...] = (
        resid[...] + (down_part[...].astype(f32) + down_other[...].astype(f32))
    ).astype(bf16)
    copies.finish()


def back(*arrays):
    half = TOK // 2
    wide = 2 * HD
    return pl.pallas_call(
        back_kernel,
        out_shape=[
            jax.ShapeDtypeStruct((TOK, D), bf16),
            jax.ShapeDtypeStruct((TOK, D), bf16),
            *[jax.ShapeDtypeStruct((24, FF // 2), f32)] * 3,
            jax.ShapeDtypeStruct((24, (HEADS + 2) * HD), f32),
            jax.ShapeDtypeStruct((24, HEADS * HD), f32),
            jax.ShapeDtypeStruct((40, 128), f32),
        ],
        in_specs=[SMEM] + [VMEM] * 11 + [ANY] * 9,
        out_specs=[VMEM] * 8,
        scratch_shapes=[
            pltpu.VMEM((2, NQ, HD), bf16),
            pltpu.VMEM((2, 8, NQ), f32),
            pltpu.VMEM((2, HD, NQ), f32),
            pltpu.VMEM((HD, NQ), f32),
            pltpu.VMEM((4, 4, 2, TOK, wide), bf16),
            pltpu.VMEM((3, 4, 2, half, wide), bf16),
            pltpu.VMEM((3, 4, 2, half, wide), bf16),
            pltpu.VMEM((4, 2, half, wide), bf16),
            pltpu.VMEM((4, 2, half, wide), bf16),
            pltpu.VMEM((3, 2, half, wide), bf16),
            pltpu.VMEM((3, 2, half, wide), bf16),
            pltpu.VMEM((2, TOK, wide), bf16),
            pltpu.VMEM((TOK, wide), bf16),
            pltpu.VMEM((D, (HEADS + 2) * HD), bf16),
            pltpu.VMEM((4, 2, TOK, D), bf16),
            pltpu.VMEM((4, 2, TOK, D), bf16),
            pltpu.VMEM((HEADS, TOK, HD), bf16),
            pltpu.VMEM((4, 2, TOK, HD), bf16),
            pltpu.VMEM((HEADS + 2, TOK, HD), bf16),
            pltpu.VMEM((TOK, (HEADS + 2) * HD), bf16),
            pltpu.VMEM((4, 2, TOK, HD), bf16),
            pltpu.VMEM((TOK, D), bf16),
            pltpu.VMEM((TOK, D), bf16),
            pltpu.VMEM((40, 128), f32),
            pltpu.VMEM((3, 40, 128), f32),
            pltpu.VMEM((7, 40, 128), f32),
            pltpu.VMEM((40, 128), f32),
            pltpu.VMEM((40, 128), f32),
            pltpu.VMEM((40, 128), f32),
            pltpu.VMEM((UNITS, 384), bf16),
            pltpu.VMEM((3, UNITS, 384), bf16),
            pltpu.VMEM((4, 2, 48, COLUMNS), bf16),
            *[pltpu.VMEM((4, 4, 48, COLUMNS), bf16)] * 3,
            pltpu.VMEM((3, 4, 48, COLUMNS), bf16),
            *[pltpu.VMEM((4, 48, COLUMNS), bf16)] * 2,
            *[pltpu.VMEM((4, 2, 48, COLUMNS), bf16)] * 2,
            *[pltpu.VMEM((4, 48, COLUMNS), f32)] * 3,
            *[pltpu.VMEM((4, 24, COLUMNS), f32)] * 3,
            pltpu.VMEM((wide, D), bf16),
            pltpu.VMEM((3, wide, 384), bf16),
            pltpu.VMEM((4, 2, 48, wide), bf16),
            pltpu.VMEM((4, 2, 48, wide), bf16),
            pltpu.VMEM((4, 48, wide), f32),
            pltpu.VMEM((4, 24, wide), f32),
            pltpu.VMEM((TOK, D), bf16),
            pltpu.VMEM((TOK, D), bf16),
            pltpu.VMEM((TOK, D), bf16),
            pltpu.VMEM((2, NQ, HD), bf16),
            pltpu.VMEM((4, 4, 2, TOK, wide), bf16),
            pltpu.VMEM((HD, NQ), f32),
            pltpu.VMEM((TOK, D), f32),
            pltpu.VMEM((TOK, D), f32),
            *sems(150),
            pltpu.SemaphoreType.DMA((12,)),
        ],
        compiler_params=params(9, 62),
    )(*arrays)


def results_kernel(*refs):
    wholes, small, copied = refs[:7], refs[7], refs[8:15]
    norm_attn, norm_mlp, bias, value_bias, sems = refs[15:]
    shard = shard_of(here())
    moves = [
        pltpu.make_async_copy(a, b, sems.at[k]) for k, (a, b) in enumerate(zip(wholes, copied))
    ]
    for move in moves:
        move.start()
    rows = jnp.concatenate(
        [
            jnp.concatenate([small[12 * i + k : 12 * i + k + 1, :] for k in range(12)], axis=1)
            for i in range(2)
        ],
        axis=0,
    )
    turned = pltpu.roll(rows, lax.rem(D - 24 * shard, D), 1)
    norm_attn[...] = turned[0:1, :24]
    norm_mlp[...] = turned[1:2, :24]
    heads = pltpu.roll(small[24 : 24 + HEADS + 2, :], lax.rem(HD - 2 * shard, HD), 1)
    bias[0] = heads[: HEADS + 1, :2].T
    value_bias[...] = heads[HEADS + 1 :, :2]
    for move in moves:
        move.wait()


def results(*arrays):
    *wholes, small = arrays
    return pl.pallas_call(
        results_kernel,
        out_shape=[
            *[jax.ShapeDtypeStruct(a.shape, a.dtype) for a in wholes],
            jax.ShapeDtypeStruct((1, 24), f32),
            jax.ShapeDtypeStruct((1, 24), f32),
            jax.ShapeDtypeStruct((1, 2, HEADS + 1), f32),
            jax.ShapeDtypeStruct((1, 2), f32),
        ],
        in_specs=[ANY] * 7 + [VMEM],
        out_specs=[VMEM] * 11,
        scratch_shapes=[pltpu.SemaphoreType.DMA((7,))],
    )(*wholes, small)


def shards(
    layer_in, lengths, norm_attn, w_qkv, qkv_bias, w_out, norm_mlp, w_gate, w_up, w_down, out_grad
):
    half = HD // 2
    freqs = np.float32(rope_base) ** (-2.0 * np.arange(half, dtype=np.float32) / HD)
    freqs = np.concatenate([freqs, freqs]).astype(np.float32)[None]
    kv, queries, act_attn, attn_low, exact, lse, cosine, sine, out_grad_all = attend(
        lengths, layer_in, norm_attn, qkv_bias, freqs, out_grad, w_qkv
    )
    (
        resid, grad_resid, grads, gain_terms, gate_sum, down_near, down_far,
        up_terms, down_terms, act_attn_all,
    ) = feed_forward(
        attn_low, layer_in, norm_mlp, out_grad, act_attn, w_out, out_grad_all, w_gate, w_up, w_down
    )
    sums = back(
        lengths, lse, grad_resid, grads, attn_low, cosine, sine, layer_in, norm_attn, gain_terms,
        gate_sum, down_far,
        queries, kv, exact, resid, down_near, w_qkv, act_attn_all, up_terms, down_terms,
    )
    in_grad, layer_out, sum_gate, sum_up, sum_down, sum_qkv, sum_out, *rest = results(*sums)
    sum_norm_attn, sum_norm_mlp, bias, value_bias = rest
    return (
        layer_out,
        in_grad,
        sum_norm_attn[0],
        sum_qkv,
        bias.swapaxes(1, 2),
        value_bias,
        sum_out.T,
        sum_norm_mlp[0],
        sum_gate,
        sum_up,
        sum_down.T,
    )


def solution(mesh):
    torus = Mesh(mesh.devices.reshape(4, 4, 2, 2, 2), AXES)
    in_specs = (
        P(WIDE, None),
        P(),
        P(),
        P(None, "n"),
        P("n", None),
        P("n", None),
        P(),
        P(None, "n"),
        P(None, "n"),
        P("n", None),
        P(WIDE, None),
    )
    out_specs = (
        P(WIDE, None),
        P(WIDE, None),
        P(WIDE),
        P(WIDE, "n"),
        P("n", None, WIDE),
        P("n", WIDE),
        P("n", WIDE),
        P(WIDE),
        P(WIDE, "n"),
        P(WIDE, "n"),
        P("n", WIDE),
    )
    return jax.shard_map(
        shards, mesh=torus, in_specs=in_specs, out_specs=out_specs, check_vma=False
    )
```

```python
import functools
import math

import jax
import jax.numpy as jnp
import numpy as np
from jax import lax
from jax.experimental import pallas as pl
from jax.experimental.pallas import tpu as pltpu
from jax.sharding import Mesh
from jax.sharding import PartitionSpec as P

HD = 128
QH = 12
KVH = 2
HEADS = QH // KVH
D = 1536
FF = 8960
TOK = 128
TOKENS = 8192
SEQS = 4
NQ = HEADS * TOK
GROUP = 8
UNITS = FF // 2 // GROUP
WINDOW = 768
COLUMNS = 640

AXES = ("z", "y", "xh", "c", "n")
SIZE = {"z": 4, "y": 4, "xh": 2, "c": 2, "n": 2}
WIDE = ("z", "y", "xh", "c")
MESH = pl.DeviceIdType.MESH

rms_eps = 1e-06
rope_base = 10000.0
big_negative = -1e30
SCALE = HD ** (-0.5)
SCALE_LOG2 = SCALE * math.log2(math.e)
KEY_BLOCK = 512
BLOCK_SHARDS = KEY_BLOCK // TOK
Q_CHUNK = 256

bf16 = jnp.bfloat16
f32 = jnp.float32
VMEM = pl.BlockSpec(memory_space=pltpu.VMEM)
SMEM = pl.BlockSpec(memory_space=pltpu.SMEM)
ANY = pl.BlockSpec(memory_space=pl.ANY)


def nn(a, b):
    return lax.dot_general(a, b, (((1,), (0,)), ((), ())), preferred_element_type=f32)


def nt(a, b):
    return lax.dot_general(a, b, (((1,), (1,)), ((), ())), preferred_element_type=f32)


def tn(a, b):
    return lax.dot_general(a, b, (((0,), (0,)), ((), ())), preferred_element_type=f32)


def here():
    return {a: lax.axis_index(a) for a in AXES}


def step(me, axis, by):
    return lax.rem(me[axis] + by, SIZE[axis])


def at(me, **moved):
    return tuple(step(me, a, moved[a]) if a in moved else me[a] for a in AXES)


def sequence_starts(ids, lengths):
    starts, end = jnp.zeros_like(ids), 0
    for s in range(SEQS):
        end = end + lengths[s]
        starts = starts + jnp.where(ids >= end, lengths[s], 0)
    return starts


def token_rows(me, lengths):
    column = lax.broadcasted_iota(jnp.int32, (1, 2 * NQ), 1)
    ids = shard_of(me) // 2 * (2 * TOK) + column // NQ * TOK + column % TOK
    return ids, sequence_starts(ids, lengths)


def hail(peers):
    barrier = pltpu.get_barrier_semaphore()
    for p in peers:
        pl.semaphore_signal(barrier, inc=1, device_id=p, device_id_type=MESH)
    return lambda: pl.semaphore_wait(barrier, len(peers))


def greet(peers):
    hail(peers)()


class Copies:
    def __init__(self, send_sems, recv_sems):
        self.send_sems, self.recv_sems, self.used, self.started = send_sems, recv_sems, 0, []

    def make(self, src, dst, target):
        self.used += 1
        return self.numbered(self.used - 1, src, dst, target)

    def numbered(self, k, src, dst, target):
        return pltpu.make_async_remote_copy(
            src_ref=src,
            dst_ref=dst,
            send_sem=self.send_sems.at[k],
            recv_sem=self.recv_sems.at[k],
            device_id=target,
            device_id_type=MESH,
        )

    def send(self, src, dst, target):
        copy = self.make(src, dst, target)
        copy.start()
        self.started.append(copy)
        return copy

    def finish(self):
        for copy in self.started:
            copy.wait_send()


class Moves:
    def __init__(self, move_sems):
        self.move_sems, self.started = move_sems, []

    def start(self, src, dst):
        copy = pltpu.make_async_copy(src, dst, self.move_sems.at[len(self.started)])
        copy.start()
        self.started.append(copy)
        return copy

    def finish(self, copies):
        for copy in copies:
            copy.wait()


def sems(count):
    return [pltpu.SemaphoreType.DMA((count,)), pltpu.SemaphoreType.DMA((count,))]


def params(ident, mib=60):
    return pltpu.CompilerParams(
        collective_id=ident, has_side_effects=True, vmem_limit_bytes=mib * 2**20
    )


def whole_tiles(values):
    pad = jnp.zeros((values.shape[0], COLUMNS - values.shape[1]), values.dtype)
    return jnp.concatenate([values, pad], axis=1)


def three(ref):
    return ref[0].astype(f32) + ref[1].astype(f32) + ref[2].astype(f32)


def shard_of(me):
    return ((me["z"] * 4 + me["y"]) * 2 + me["xh"]) * 2 + me["c"]


class Rows:
    def __init__(self, me, copies, source, slots):
        self.me, self.copies, self.source, self.slots = me, copies, source, slots
        half = TOK // 2
        n = me["n"]
        self.mine = pl.ds(pl.multiple_of(half * n, half), half)
        self.theirs = pl.ds(pl.multiple_of(half * (1 - n), half), half)
        self.own = slots.at[me["y"], me["c"]]
        self.near, self.far, self.across = [], {}, {}

    def pair(self):
        self.near.append(self.copies.send(self.source, self.own, at(self.me, c=1)))

    def slot(self, d, rows):
        return self.slots.at[lax.rem(self.me["y"] + (4 - d), 4), self.me["c"], rows]

    def start(self, *steps):
        for d in steps:
            self.far[d] = self.copies.send(
                self.source.at[self.mine], self.own.at[self.mine], at(self.me, y=d)
            )

    def pass_on(self, *steps):
        for d in steps:
            self.far[d].wait_recv()
            got = self.slot(d, self.mine)
            self.across[d] = self.copies.send(got, got, at(self.me, n=1))
            self.near.append(self.copies.send(got, got, at(self.me, c=1)))

    def complete(self, *steps):
        for d in steps:
            self.across[d].wait_recv()
            got = self.slot(d, self.theirs)
            self.near.append(self.copies.send(got, got, at(self.me, c=1)))

    def wait(self):
        for copy in self.near:
            copy.wait_recv()


def attend_kernel(
    lengths, x, gain, bias, freqs, og, w_qkv_hbm, w_out_hbm, w_gate_hbm, w_up_hbm,
    kv_hbm, q_hbm, act_hbm, resid_hbm, exact_hbm, lse_hbm, rope_hbm, gate_hbm, up_hbm, og_all, al_all,
    stats, acc, low_acc, stats_in, acc_in, low_in, w_qkv, w_out, o, pa, pb,
    kv, q, act, resid, exact, lse, rope, gate_w, up_w, wide_gate, wide_up, send_sems, recv_sems, local_sems,
):
    me = here()
    moves, kept_back = Moves(local_sems), []
    load_w = moves.start(w_qkv_hbm, w_qkv)
    ids, start = token_rows(me, lengths)
    z, y, xh, c = me["z"], me["y"], me["xh"], me["c"]
    partner, across, other = at(me, c=1), at(me, xh=1), at(me, n=1)
    ys = {d: at(me, y=d) for d in (1, 2, 3)}
    zs = {d: at(me, z=d) for d in (1, 2, 3)}
    everyone_in = hail([partner, across, other, *ys.values(), *zs.values()])
    rows = x[...].astype(f32)
    inverse = lax.rsqrt(jnp.mean(rows * rows, axis=-1, keepdims=True) + rms_eps)
    act[...] = (rows * inverse * gain[...].reshape(1, D)).astype(bf16)
    token = shard_of(me) * TOK + lax.broadcasted_iota(jnp.int32, (TOK, 1), 0)
    angles = (token - sequence_starts(token, lengths)).astype(f32) * freqs[...]
    cosine = jnp.cos(angles)
    turned = jnp.sin(angles)
    first_half = lax.broadcasted_iota(jnp.int32, (TOK, HD), 1) < HD // 2
    sine = jnp.where(first_half, -turned, turned)
    rope[0], rope[1] = cosine, sine
    kept_back.append(moves.start(rope, rope_hbm))
    front = HEADS * HD

    def turn(values):
        return values * cosine + pltpu.roll(values, HD // 2, 1) * sine

    load_w.wait()
    back = nn(act[...], w_qkv[:, front:]) + bias[:, front:]
    mine = kv.at[z, y, xh]
    mine[:, pl.ds(0, HD)] = turn(back[:, :HD]).astype(bf16)
    mine[:, pl.ds(HD, HD)] = back[:, HD:].astype(bf16)
    everyone_in()
    kept_back.append(moves.start(act, act_hbm))
    load_out = moves.start(w_out_hbm, w_out)
    copies = Copies(send_sems, recv_sems)
    rows_of_og = Rows(me, copies, og, og_all)
    rows_of_og.start(1, 3)
    first = copies.send(mine, mine, across)
    ahead = nn(act[...], w_qkv[:, :front]) + bias[:, :front]
    for h in range(HEADS):
        head = turn(ahead[:, h * HD : (h + 1) * HD]).astype(bf16)
        q[c, pl.ds(h * TOK, TOK), :] = head
    share_q = copies.send(q.at[c], q.at[c], partner)
    rows_of_og.pair()
    kept_back.append(moves.start(og, og_all.at[y, c]))
    stats[:, 0:1, :] = jnp.full((2, 1, NQ), big_negative, f32)
    stats[:, 1:8, :] = jnp.zeros((2, 7, NQ), f32)
    acc[...] = jnp.zeros_like(acc)
    low_acc[...] = jnp.zeros_like(low_acc)
    last = shard_of(me) // BLOCK_SHARDS
    kept = start < last * KEY_BLOCK
    half = TOK // 2
    keys_here = 2 * half

    def take(parts, masked):
        def both(columns):
            return jnp.concatenate(
                [
                    kv[zi, yi, :, pl.ds(pl.multiple_of(half * k, half), half), columns].reshape(
                        keys_here, HD
                    )
                    for zi, yi, k in parts
                ],
                axis=0,
            )

        keys, values = both(pl.ds(0, HD)), both(pl.ds(HD, HD)).T
        for chunk in range(2 * NQ // Q_CHUNK):
            core, cs = divmod(chunk * Q_CHUNK, NQ)
            cs = pl.ds(cs, Q_CHUNK)
            here_cols = slice(chunk * Q_CHUNK, (chunk + 1) * Q_CHUNK)
            scores = nt(keys, q[core, cs, :]) * SCALE_LOG2
            if masked:
                ((zi, yi, k),) = parts
                place = lax.broadcasted_iota(jnp.int32, (keys_here, Q_CHUNK), 0)
                first_key = (4 * zi + yi) * KEY_BLOCK + c * TOK + half * k
                key_ids = first_key + place + place // half * (2 * TOK - half)
                allowed = (key_ids >= start[:, here_cols]) & (key_ids <= ids[:, here_cols])
                scores = jnp.where(allowed, scores, big_negative)
            old = stats[core, 0:1, cs]
            new = jnp.maximum(old, jnp.max(scores, axis=0, keepdims=True))
            if masked:
                probs = jnp.where(allowed, jnp.exp2(scores - new), 0.0)
            else:
                taken = kept[:, here_cols]
                new = jnp.where(taken, new, old)
                probs = jnp.exp2(scores - jnp.where(taken, new, -big_negative))
            fade = jnp.exp2(old - new)
            stats[core, 0:1, cs] = new
            stats[core, 1:2, cs] = stats[core, 1:2, cs] * fade + jnp.sum(probs, axis=0, keepdims=True)
            upper = probs.astype(bf16)
            rest = (probs - upper.astype(f32)).astype(bf16)
            acc[core, :, cs] = acc[core, :, cs] * fade + nn(values, upper)
            low_acc[core, :, cs] = low_acc[core, :, cs] * fade + nn(values, rest)

    def pair(za, ya, zb, yb):
        a, b = 4 * za + ya, 4 * zb + yb
        inner = (jnp.minimum(a, b) > 0) & (jnp.maximum(a, b) < last)

        @pl.when(inner)
        def _():
            take([(za, ya, 0), (zb, yb, 1)], False)

        @pl.when(jnp.logical_not(inner))
        def _():
            @pl.loop(0, 2)
            def _(k):
                zi, yi = jnp.where(k == 0, za, zb), jnp.where(k == 0, ya, yb)
                index = 4 * zi + yi
                edge = (index == 0) | (index == last)

                @pl.when(edge & (index <= last))
                def _():
                    take([(zi, yi, k)], True)

                @pl.when((index < last) & jnp.logical_not(edge))
                def _():
                    take([(zi, yi, k)], False)

    first.wait_recv()
    low, high = pl.ds(0, half), pl.ds(half, half)

    def slot(zi, yi, rows):
        return kv.at[zi, yi, :, rows]

    def before(axis, d):
        return lax.rem(me[axis] + (4 - d), 4)

    first_low, first_high = {}, {}
    for d in (1, 3, 2):
        first_low[d] = copies.send(slot(z, y, low), slot(z, y, low), ys[d])
        first_high[d] = copies.send(slot(z, y, high), slot(z, y, high), zs[d])
    share_q.wait_recv()

    kept_back.append(moves.start(q, q_hbm))
    first_unit = (y * 2 + c) * UNITS
    tile = jnp.minimum(first_unit // 128, FF // 2 // 128 - WINDOW // 128)
    window = pl.ds(pl.multiple_of(tile * 128, 128), WINDOW)
    load_gate = moves.start(w_gate_hbm.at[:, window], wide_gate)
    load_up = moves.start(w_up_hbm.at[:, window], wide_up)
    pair(z, y, z, y)
    second_from = copies.used
    copies.used += 24
    for i, e in enumerate((0, 1, 3, 2)):
        yi, zi = before("y", e), before("z", e)
        if e:
            first_low[e].wait_recv()
            first_high[e].wait_recv()
        for j, d in enumerate((1, 3, 2)):
            k = second_from + 2 * (3 * i + j)
            for copy in (
                copies.numbered(k, slot(z, yi, low), slot(z, yi, low), zs[d]),
                copies.numbered(k + 1, slot(zi, y, high), slot(zi, y, high), ys[d]),
            ):
                copy.start()
                copies.started.append(copy)
    rows_of_og.start(2)
    rows_of_og.pass_on(1, 3)

    @pl.loop(1, 4)
    def _(e):
        pair(z, before("y", e), before("z", e), y)

    def places(k):
        i, j = k // 3, lax.rem(k, 3)
        e = jnp.where(i < 2, i, 5 - i)
        d = jnp.where(j < 2, 1 + 2 * j, 2)
        return before("z", d), before("y", e), before("z", e), before("y", d)

    def arrive(k):
        za, ya, zb, yb = places(k)
        one, two = slot(za, ya, low), slot(zb, yb, high)
        copies.numbered(second_from + 2 * k, one, one, zs[1]).wait_recv()
        copies.numbered(second_from + 2 * k + 1, two, two, ys[1]).wait_recv()
        pair(za, ya, zb, yb)

    pl.loop(0, 8)(arrive)
    rows_of_og.pass_on(2)
    pl.loop(8, 12)(arrive)
    kept_back.append(moves.start(kv, kv_hbm))
    merge = [
        copies.send(stats.at[1 - c], stats_in, partner),
        copies.send(acc.at[1 - c], acc_in, partner),
        copies.send(low_acc.at[1 - c], low_in, partner),
    ]
    rows_of_og.complete(1, 3, 2)
    for copy in merge:
        copy.wait_recv()
    own_top, in_top = stats[c, 0:1, :], stats_in[0:1, :]
    top = jnp.maximum(own_top, in_top)
    own_part, in_part = jnp.exp2(own_top - top), jnp.exp2(in_top - top)
    total = stats[c, 1:2, :] * own_part + stats_in[1:2, :] * in_part
    inverse = 1.0 / total
    own_part, in_part = own_part * inverse, in_part * inverse
    rows = acc[c] * own_part + acc_in[...] * in_part
    exact[...] = rows + (low_acc[c] * own_part + low_in[...] * in_part)
    rows = rows.T.astype(bf16)
    for h in range(HEADS):
        o[:, pl.ds(h * HD, HD)] = rows[h * TOK : (h + 1) * TOK]
    load_out.wait()
    pa[...] = nn(o[...], w_out[...]).astype(bf16)
    swap = copies.send(pa, pb, other)
    own_al = al_all.at[y]
    al_moves = {d: copies.send(o, own_al, ys[d]) for d in (1, 3, 2)}
    kept_back.append(moves.start(o, own_al))
    lse[...] = top + jnp.log2(total)
    kept_back.append(moves.start(lse, lse_hbm))
    kept_back.append(moves.start(exact, exact_hbm))
    shift = lax.rem(WINDOW - (first_unit - tile * 128), WINDOW)
    for load, part, weights, whole in (
        (load_gate, wide_gate, gate_w, gate_hbm),
        (load_up, wide_up, up_w, up_hbm),
    ):
        load.wait()

        @pl.loop(0, D // 128)
        def _(index, part=part, weights=weights):
            rows = pl.ds(pl.multiple_of(index * 128, 128), 128)
            rolled = pltpu.roll(part[rows, :].astype(f32), shift, 1)
            weights[rows, :] = rolled[:, :COLUMNS].astype(bf16)

        kept_back.append(moves.start(weights, whole))
    rows_of_og.wait()
    swap.wait_recv()
    resid[...] = x[...].astype(f32) + (pa[...].astype(f32) + pb[...].astype(f32))
    kept_back.append(moves.start(resid, resid_hbm))
    for copy in al_moves.values():
        copy.wait_recv()
    moves.finish(kept_back)
    copies.finish()


def attend(*arrays):
    state = [
        jax.ShapeDtypeStruct((4, 4, 2, TOK, 2 * HD), bf16),
        jax.ShapeDtypeStruct((2, NQ, HD), bf16),
        jax.ShapeDtypeStruct((TOK, D), bf16),
        jax.ShapeDtypeStruct((TOK, D), f32),
        jax.ShapeDtypeStruct((HD, NQ), f32),
        jax.ShapeDtypeStruct((1, NQ), f32),
        jax.ShapeDtypeStruct((2, TOK, HD), f32),
        jax.ShapeDtypeStruct((D, COLUMNS), bf16),
        jax.ShapeDtypeStruct((D, COLUMNS), bf16),
    ]
    return pl.pallas_call(
        attend_kernel,
        out_shape=[
            *state,
            jax.ShapeDtypeStruct((4, 2, TOK, D), bf16),
            jax.ShapeDtypeStruct((4, TOK, HEADS * HD), bf16),
        ],
        in_specs=[SMEM] + [VMEM] * 5 + [ANY] * 4,
        out_specs=[ANY] * 11,
        scratch_shapes=[
            pltpu.VMEM((2, 8, NQ), f32),
            pltpu.VMEM((2, HD, NQ), f32),
            pltpu.VMEM((2, HD, NQ), f32),
            pltpu.VMEM((8, NQ), f32),
            pltpu.VMEM((HD, NQ), f32),
            pltpu.VMEM((HD, NQ), f32),
            pltpu.VMEM((D, (HEADS + 2) * HD), bf16),
            pltpu.VMEM((HEADS * HD, D), bf16),
            pltpu.VMEM((TOK, HEADS * HD), bf16),
            *[pltpu.VMEM((TOK, D), bf16)] * 2,
            *[pltpu.VMEM(a.shape, a.dtype) for a in state],
            *[pltpu.VMEM((D, WINDOW), bf16)] * 2,
            *sems(52),
            pltpu.SemaphoreType.DMA((15,)),
        ],
        compiler_params=params(1),
    )(*arrays)


def mlp_kernel(*refs):
    resid, gain, og, aa, w_out_hbm, og_hbm, gate_hbm, up_w_hbm, w_down_hbm = refs[:9]
    back_hbm, grads_hbm, gains_hbm, gate_sum_hbm, near_hbm, far_hbm, up_hbm, down_hbm, aa_all = refs[9:18]
    wd, og_all, act_all, grad_hidden, hidden, ggp, gup, bk, dn, bk_core, dn_core, bk_sent, bk_in = refs[18:31]
    nb, rn, gate_terms, gate_in, gate_w, up_w, up_terms, down_terms, down_sum, dn_in, w_out = refs[31:42]
    grad_resid, grads, gain_terms, gate_sum, down_near, send_sems, recv_sems, local_sems = refs[42:]
    me = here()
    z, y, c = me["z"], me["y"], me["c"]
    partner, other = at(me, c=1), at(me, n=1)
    ys = {d: at(me, y=d) for d in (1, 2, 3)}
    zs = {d: at(me, z=d) for d in (1, 2, 3)}
    everyone_in = hail([partner, other, *ys.values(), *zs.values()])
    moves, kept_back = Moves(local_sems), []
    load_gate, load_up = moves.start(gate_hbm, gate_w), moves.start(up_w_hbm, up_w)
    units = pl.ds(pl.multiple_of((y * 2 + c) * UNITS, 16), UNITS)
    load_down, load_og = moves.start(w_down_hbm.at[units], wd), moves.start(og_hbm, og_all)
    load_out = moves.start(w_out_hbm, w_out)
    kept_back.append(moves.start(aa, aa_all.at[y, c]))
    everyone_in()
    copies = Copies(send_sems, recv_sems)
    half = TOK // 2
    halves = (pl.ds(0, half), pl.ds(half, half))
    gain = gain[...].reshape(1, D)

    def inverse_of(rows):
        return lax.rsqrt(jnp.mean(rows * rows, axis=-1, keepdims=True) + rms_eps)

    own = act_all.at[y, c]
    far, to_core = {}, {0: [], 1: [], 2: [], 3: []}
    for rows in halves:
        total = resid[rows, :]
        act_all[y, c, rows] = (total * inverse_of(total) * gain).astype(bf16)
        to_core[0].append(copies.send(own.at[rows], own.at[rows], partner))
        for d in (1, 3):
            far[d, len(to_core[0]) - 1] = copies.send(own.at[rows], own.at[rows], ys[d])
    load_down.wait()
    load_og.wait()
    pair = (2 * TOK, D)

    def hidden_back(d):
        yi = step(me, "y", d)
        grad_hidden[yi] = nt(og_all[yi].reshape(pair), wd[...])

    hidden_back(0)
    load_gate.wait()
    load_up.wait()
    bk_cores, dn_cores, bk_moves = {}, {}, {}

    def block(d, beside=None):
        yi = step(me, "y", d)
        rows = act_all[yi].reshape(pair)
        gate = nn(rows, gate_w[:, :UNITS])
        up = nn(rows, up_w[:, :UNITS])
        sigmoid = 1.0 / (1.0 + jnp.exp(-gate))
        silu = gate * sigmoid
        grads = grad_hidden[yi]
        hidden[yi] = (silu * up).astype(bf16)
        ggp[yi] = (grads * up * (sigmoid * (1.0 + gate * (1.0 - sigmoid)))).astype(bf16)
        gup[yi] = (grads * silu).astype(bf16)
        if beside is not None:
            pass_block(beside)
        both = nt(ggp[yi], gate_w[:, :UNITS]) + nt(gup[yi], up_w[:, :UNITS])
        bk[yi] = both.astype(bf16).reshape(2, TOK, D)
        bk_cores[d] = copies.send(bk.at[yi, 1 - c], bk_core.at[yi], partner)
    low, high = halves

    def pass_block(d):
        yi = step(me, "y", d)
        bk_cores[d].wait_recv()
        for k, rows in enumerate((low, high)):
            bk_sent[yi, rows] = (
                bk[yi, c, rows].astype(f32) + bk_core[yi, rows].astype(f32)
            ).astype(bf16)
            if d:
                bk_moves[d, k] = copies.send(
                    bk_sent.at[yi, rows], bk_in.at[d - 1, rows], ys[d]
                )

    def down_block(d):
        yi = step(me, "y", d)
        dn[yi] = nn(hidden[yi], wd[...]).astype(bf16).reshape(2, TOK, D)
        dn_cores[d] = copies.send(dn.at[yi, 1 - c], dn_core.at[yi], partner)

    def sum_down(d):
        yi = step(me, "y", d)
        dn_cores[d].wait_recv()
        down_sum[yi] = (dn[yi, c].astype(f32) + dn_core[yi].astype(f32)).astype(bf16)

    for copy in to_core[0]:
        copy.wait_recv()
    block(0)
    for d in (3, 1, 2):
        hidden_back(d)
    relay = {}
    for k, rows in enumerate(halves):
        for d in (1, 3):
            far[d, k].wait_recv()
            got = act_all.at[lax.rem(y + (4 - d), 4), c, rows]
            to_core[4 - d].append(copies.send(got, got, partner))
            if d == 1 + 2 * k:
                relay[d] = copies.send(got, got, ys[d])
    aa_rows = Rows(me, copies, aa, aa_all)
    aa_rows.start(1, 3, 2)
    aa_rows.pair()
    for copy in to_core[3]:
        copy.wait_recv()
    block(3, 0)
    for d, rows in ((1, low), (3, high)):
        relay[d].wait_recv()
        got = act_all.at[step(me, "y", 2), c, rows]
        to_core[2].append(copies.send(got, got, partner))
    for copy in to_core[1]:
        copy.wait_recv()
    block(1, 3)
    for copy in to_core[2]:
        copy.wait_recv()
    block(2, 1)

    everything = (GROUP * TOK, D)
    all_units = (GROUP * TOK, UNITS)
    gate_terms[...] = tn(ggp[...].reshape(all_units), act_all[...].reshape(everything)).astype(bf16)

    def z_cols(d):
        return pl.ds(pl.multiple_of(step(me, "z", d) * 384, 384), 384)

    gate_moves = {
        d: copies.send(gate_terms.at[:, z_cols(d)], gate_in.at[d - 1], zs[d]) for d in (1, 3, 2)
    }
    pass_block(2)
    aa_rows.pass_on(1, 3, 2)
    for d in (1, 3, 2, 0):
        down_block(d)
    up_terms[...] = tn(gup[...].reshape(all_units), act_all[...].reshape(everything)).astype(bf16)
    kept_back.append(moves.start(up_terms, up_hbm))
    for d in range(4):
        sum_down(d)
    swaps_back = []
    for k, rows in enumerate((low, high)):
        back = bk_sent[y, rows].astype(f32)
        for d in (1, 3, 2):
            bk_moves[d, k].wait_recv()
            back = back + bk_in[d - 1, rows].astype(f32)
        nb[rows] = back.astype(bf16)
        swaps_back.append(copies.send(nb.at[rows], rn.at[rows], other))
    dn_moves = {
        d: copies.send(down_sum.at[step(me, "y", d)], dn_in.at[d // 2], ys[d]) for d in (1, 3)
    }
    kept_back.append(moves.start(down_sum.at[step(me, "y", 2)], far_hbm))
    for zi in range(4):
        columns = og_all[:, :, :, pl.ds(384 * zi, 384)].reshape(GROUP * TOK, 384)
        sums = whole_tiles(tn(columns, hidden[...].reshape(all_units)).astype(bf16))
        down_terms[zi] = sums.reshape(4, 2, 48, COLUMNS)
    kept_back.append(moves.start(down_terms, down_hbm))
    aa_rows.complete(1, 3, 2)
    for copy in swaps_back:
        copy.wait_recv()
    grad_act = nb[...].astype(f32) + rn[...].astype(f32)
    inverse = inverse_of(resid[...])
    normed = resid[...] * inverse
    gain_terms[...] = jnp.sum(grad_act * normed, axis=0, keepdims=True)
    grad_normed = grad_act * gain
    inner = jnp.mean(grad_normed * normed, axis=-1, keepdims=True)
    grad_resid[...] = og[...].astype(f32) + inverse * (grad_normed - normed * inner)
    load_out.wait()
    grads[...] = nt(grad_resid[...].astype(bf16), w_out[...]).astype(bf16)
    for vmem, hbm in ((grad_resid, back_hbm), (grads, grads_hbm), (gain_terms, gains_hbm)):
        kept_back.append(moves.start(vmem, hbm))
    for d in (1, 3, 2):
        gate_moves[d].wait_recv()
    gate_sum[...] = whole_tiles((gate_terms[:, z_cols(0)].astype(f32) + three(gate_in)).T.astype(bf16))
    kept_back.append(moves.start(gate_sum, gate_sum_hbm))
    total = down_sum[y].astype(f32)
    for d in (1, 3):
        dn_moves[d].wait_recv()
        total = total + dn_in[d // 2].astype(f32)
    down_near[...] = total
    kept_back.append(moves.start(down_near, near_hbm))
    aa_rows.wait()
    moves.finish(kept_back)
    copies.finish()


def feed_forward(*arrays):
    rows = pltpu.VMEM((TOK, D), bf16)
    return pl.pallas_call(
        mlp_kernel,
        out_shape=[
            jax.ShapeDtypeStruct((TOK, D), f32),
            jax.ShapeDtypeStruct((TOK, HEADS * HD), bf16),
            jax.ShapeDtypeStruct((1, D), f32),
            jax.ShapeDtypeStruct((D // 4, COLUMNS), bf16),
            jax.ShapeDtypeStruct((TOK, D), f32),
            jax.ShapeDtypeStruct((TOK, D), bf16),
            jax.ShapeDtypeStruct((UNITS, D), bf16),
            jax.ShapeDtypeStruct((4, 4, 2, 48, COLUMNS), bf16),
            jax.ShapeDtypeStruct((4, 2, TOK, D), bf16),
        ],
        in_specs=[VMEM] * 4 + [ANY] * 5,
        out_specs=[ANY] * 9,
        scratch_shapes=[
            pltpu.VMEM((UNITS, D), bf16),
            pltpu.VMEM((4, 2, TOK, D), bf16),
            pltpu.VMEM((4, 2, TOK, D), bf16),
            pltpu.VMEM((4, 2 * TOK, UNITS), f32),
            *[pltpu.VMEM((4, 2 * TOK, UNITS), bf16)] * 3,
            *[pltpu.VMEM((4, 2, TOK, D), bf16)] * 2,
            *[pltpu.VMEM((4, TOK, D), bf16)] * 3,
            pltpu.VMEM((3, TOK, D), bf16),
            rows,
            rows,
            pltpu.VMEM((UNITS, D), bf16),
            pltpu.VMEM((3, UNITS, D // 4), bf16),
            *[pltpu.VMEM((D, COLUMNS), bf16)] * 2,
            pltpu.VMEM((UNITS, D), bf16),
            pltpu.VMEM((4, 4, 2, 48, COLUMNS), bf16),
            pltpu.VMEM((4, TOK, D), bf16),
            pltpu.VMEM((2, TOK, D), bf16),
            pltpu.VMEM((HEADS * HD, D), bf16),
            pltpu.VMEM((TOK, D), f32),
            pltpu.VMEM((TOK, HEADS * HD), bf16),
            pltpu.VMEM((1, D), f32),
            pltpu.VMEM((D // 4, COLUMNS), bf16),
            pltpu.VMEM((TOK, D), f32),
            *sems(48),
            pltpu.SemaphoreType.DMA((14,)),
        ],
        compiler_params=params(2),
    )(*arrays)


def back_kernel(*refs):
    lengths, lse, grad_resid, grads_in, gain, mlp_gain_terms = refs[:6]
    x_hbm, rope_hbm, gate_sum, down_far, q_hbm, kv_hbm, exact_hbm, resid_hbm, near_hbm = refs[6:15]
    al_hbm, w_qkv_hbm, act_hbm, up_terms, wd_terms = refs[15:20]
    results_hbm = refs[20:28]
    (g, stats, acc, acc_in, dkv, r1a, r1b, ta, tb, r2a, r2b, u, r3, w_qkv, act_all, gbt, gbt_all, al_all) = refs[28:46]
    gp, gp_flat, gp_all, part, part_other, small, e1, e2, e3, f1, f2 = refs[46:57]
    up_own, up_in, up_mid, wd_own, wd_across, wd_sum, wd_in, wd_mid, wd_second = refs[57:66]
    gate_second, up_second = refs[66:68]
    summed, third_in = refs[68:71], refs[71:74]
    q_terms, q_first, q_mid, q_second, q_summed, q_third = refs[74:80]
    down_in, down_part, down_other, q, kv, exact, resid, down_near, o_half, o_core, o_sum, o_in, o_mid, o_across, o_fin, o_third, *refs = refs[80:]
    x, rope, in_grad, layer_out, sum_gate, sum_up, sum_down, sum_qkv, sum_out, small_out, *refs = refs
    send_sems, recv_sems, local_sems = refs

    me = here()
    ids, start = token_rows(me, lengths)
    z, y, xh, c, n = (me[a] for a in AXES)
    partner, across, other = at(me, c=1), at(me, xh=1), at(me, n=1)
    ys = {d: at(me, y=d) for d in (1, 2, 3)}
    zs = {d: at(me, z=d) for d in (1, 2, 3)}
    near_moves = [(d, e) for d in (1, 3, 2, 0) for e in (0, 1) if d or e]
    near = {m: at(me, y=m[0], xh=m[1]) for m in near_moves}
    group = {m: at(me, y=m[0], c=m[1]) for m in near_moves}
    def strip(yi, xi):
        return pl.ds(pl.multiple_of(96 * yi + 48 * xi, 48), 48)

    everyone_in = hail([other, *zs.values(), *near.values(), *(group[m] for m in near_moves if m[1])])
    moves, kept_back = Moves(local_sems), []
    load = moves.start

    def keep_result(k, vmem):
        kept_back.append(moves.start(vmem, results_hbm[k]))

    loads = [load(exact_hbm, exact), load(q_hbm, q), load(kv_hbm, kv)]
    load_resid, load_near = load(resid_hbm, resid), load(near_hbm, down_near)
    load_x, load_rope = load(x_hbm, x), load(rope_hbm, rope)
    load_strip = load(gate_sum.at[strip(y, xh)], gate_second.at[y, xh])
    half = TOK // 2
    low, high = pl.ds(0, half), pl.ds(half, half)
    gbt[...] = grad_resid[...].T.astype(bf16).reshape(4, 4, 96, TOK)
    for h in range(HEADS):
        g[c, pl.ds(h * TOK, TOK), :] = grads_in[:, h * HD : (h + 1) * HD]
    loads[0].wait()
    stats[c, 0:1, :] = lse[...]
    stats[c, 1:2, :] = jnp.sum(g[c].astype(f32).T * exact[...], axis=0, keepdims=True)
    stats[c, 2:8, :] = jnp.zeros((6, NQ), f32)
    everyone_in()
    copies = Copies(send_sems, recv_sems)
    shared = [copies.send(g.at[c], g.at[c], partner), copies.send(stats.at[c], stats.at[c], partner)]

    def z_cols(d):
        return pl.ds(pl.multiple_of(step(me, "z", d) * 384, 384), 384)

    second = {}

    def send_second(i, source, in_ref):
        for m in near_moves:
            second[i, m] = copies.send(
                source(step(me, "y", m[0]), step(me, "xh", m[1])), in_ref.at[y, xh], near[m]
            )

    def send_mid(i, total, mid_ref, in_ref):
        turned = total.T.astype(bf16)
        if turned.shape[1] == UNITS:
            turned = whole_tiles(turned)
        for yi in range(4):
            for xi in range(2):
                rows = 96 * yi + 48 * xi
                mid_ref[yi, xi] = turned[rows : rows + 48]
        send_second(i, lambda yi, xi: mid_ref.at[yi, xi], in_ref)
        in_ref[y, xh] = mid_ref[y, xh]

    keep, give = pl.ds(pl.multiple_of(24 * c, 8), 24), pl.ds(pl.multiple_of(24 * (1 - c), 8), 24)
    third = {}
    all_summed = [*summed, q_summed]
    all_second = [gate_second, up_second, None, q_second]
    all_third = [*third_in, q_third]
    outs = (sum_gate, sum_up, sum_down, sum_qkv)

    def collect(i):
        if i == 2:
            for d in (1, 3, 2):
                second[2, d].wait_recv()
            summed[2][...] = wd_second[...].astype(f32)
        else:
            for m in near_moves:
                second[i, m].wait_recv()
            all_summed[i][...] = all_second[i][:, 0].astype(f32) + all_second[i][:, 1].astype(f32)
        third[i] = copies.send(all_summed[i].at[:, give], all_third[i], partner)

    def deliver(i):
        third[i].wait_recv()
        for yi in range(4):
            mine_sum, their_sum = all_summed[i][yi, keep], all_third[i][yi]
            pair = (jnp.where(c == 0, mine_sum, their_sum), jnp.where(c == 0, their_sum, mine_sum))
            for e in range(2):
                k = 2 * yi + e
                width = UNITS if i < 3 else HD
                outs[i][:, pl.ds(k * width, width)] = pair[e][:, :width]

    send_second(0, lambda yi, xi: gate_sum.at[strip(yi, xi)], gate_second)
    gbt_moves = {
        d: copies.send(gbt.at[:, step(me, "y", d)], gbt_all.at[y], ys[d]) for d in (1, 3, 2)
    }
    gbt_all[y] = gbt[:, y]
    down_move = copies.send(down_far, down_in, ys[2])
    first = {}
    for d in (1, 3, 2):
        first[d] = copies.send(up_terms.at[:, z_cols(d)], up_in.at[d - 1], zs[d])
    wd_move = copies.send(wd_terms.at[:, :, 1 - xh], wd_across, across)

    load_al = load(al_hbm, al_all)
    load_w = load(w_qkv_hbm, w_qkv)
    load_act = load(act_hbm, act_all)
    load_up = load(up_terms.at[:, z_cols(0)], up_own)
    load_wd = load(wd_terms.at[:, :, xh], wd_own)

    for copy in shared:
        copy.wait_recv()
    for copy in loads[1:]:
        copy.wait()
    acc[...] = jnp.zeros_like(acc)
    last = shard_of(me) // BLOCK_SHARDS

    def of_both(row):
        return jnp.concatenate([stats[0, row : row + 1, :], stats[1, row : row + 1, :]], axis=1)

    log_total, balance = of_both(0), of_both(1)
    earlier = jnp.where(start < last * KEY_BLOCK, log_total, -big_negative)
    keys_here = 2 * TOK

    def block(index, masked, shift):
        zi, yi = index // 4, lax.rem(index, 4)
        keys = kv[zi, yi, :, :, pl.ds(0, HD)].reshape(keys_here, HD)
        values = kv[zi, yi, :, :, pl.ds(HD, HD)].reshape(keys_here, HD)
        keys_t = keys.T
        dk = jnp.zeros((keys_here, HD), f32)
        dv = jnp.zeros((keys_here, HD), f32)
        for chunk in range(2 * NQ // Q_CHUNK):
            core, cs = divmod(chunk * Q_CHUNK, NQ)
            cs = pl.ds(cs, Q_CHUNK)
            piece = slice(chunk * Q_CHUNK, (chunk + 1) * Q_CHUNK)
            qc, gc = q[core, cs, :], g[core, cs, :]
            probs = jnp.exp2(nt(keys, qc) * SCALE_LOG2 - shift[:, piece])
            if masked:
                place = lax.broadcasted_iota(jnp.int32, (keys_here, Q_CHUNK), 0)
                key_ids = index * KEY_BLOCK + c * TOK + place + place // TOK * TOK
                allowed = (key_ids >= start[:, piece]) & (key_ids <= ids[:, piece])
                probs = jnp.where(allowed, probs, 0.0)
            grads = (probs * (nt(values, gc) - balance[:, piece])).astype(bf16)
            dv = dv + nn(probs.astype(bf16), gc)
            dk = dk + nn(grads, qc)
            acc[core, :, cs] = acc[core, :, cs] + nn(keys_t, grads)
        dkv[zi, yi, :, :, pl.ds(0, HD)] = (dk * SCALE).astype(bf16).reshape(2, TOK, HD)
        dkv[zi, yi, :, :, pl.ds(HD, HD)] = dv.astype(bf16).reshape(2, TOK, HD)

    def segment(zi):
        @pl.loop(0, 4)
        def _(yi):
            index = 4 * zi + yi
            edge = (index == 0) | (index == last)

            @pl.when(edge & (index <= last))
            def _():
                block(index, True, jnp.where(index == last, log_total, earlier))

            @pl.when((index < last) & jnp.logical_not(edge))
            def _():
                block(index, False, earlier)

            @pl.when(index > last)
            def _():
                dkv[zi, yi] = jnp.zeros((2, TOK, 2 * HD), bf16)

    first_a, first_b, second_a, second_b = {}, {}, {}, {}

    def settle(d):
        zi = step(me, "z", d)
        if d:
            first_a[d] = copies.send(dkv.at[zi, :, :, low], r1a.at[d - 1], zs[d])
        for e in (1, 3, 2):
            first_b[d, e] = copies.send(
                dkv.at[zi, step(me, "y", e), :, high], r1b.at[e - 1, zi], ys[e]
            )

    segment(step(me, "z", 1))
    settle(1)
    segment(step(me, "z", 2))
    settle(2)
    segment(step(me, "z", 3))
    settle(3)
    load_al.wait()
    for d in (1, 3, 2):
        gbt_moves[d].wait_recv()
    every_al = al_all[...].reshape(4 * TOK, HEADS * HD)
    for zi in range(4):
        lhs = jnp.concatenate([gbt_all[yi, zi] for yi in range(4)], axis=1)
        terms = nn(lhs, every_al).astype(bf16)
        o_half[0, zi] = terms[:, : HEADS * HD // 2]
        o_half[1, zi] = terms[:, HEADS * HD // 2 :]
    o_move = copies.send(o_half.at[1 - c], o_core, partner)
    segment(z)
    settle(0)
    queries_back = copies.send(acc.at[1 - c], acc_in, partner)
    down_move.wait_recv()
    load_near.wait()
    down_part[...] = (down_near[...] + down_in[...].astype(f32)).astype(bf16)
    down_swap = copies.send(down_part, down_other, other)
    for d in (1, 3, 2):
        first_a[d].wait_recv()
    ta[...] = (dkv[z, :, :, low].astype(f32) + three(r1a)).astype(bf16)
    for d in (1, 3, 2):
        second_a[d] = copies.send(ta.at[step(me, "y", d)], r2a.at[d - 1], ys[d])
    for copy in first_b.values():
        copy.wait_recv()
    tb[...] = (dkv[:, y, :, high].astype(f32) + three(r1b)).astype(bf16)
    for d in (1, 3, 2):
        second_b[d] = copies.send(tb.at[step(me, "z", d)], r2b.at[d - 1], zs[d])
    for d in (1, 3, 2):
        second_a[d].wait_recv()
        second_b[d].wait_recv()
    ua = ta[y].astype(f32) + three(r2a)
    ub = tb[z].astype(f32) + three(r2b)
    u[:, low] = ua.astype(bf16)
    u[:, high] = ub.astype(bf16)
    kv_last = copies.send(u.at[1 - xh], r3, across)
    load_wd.wait()
    wd_move.wait_recv()
    for zi in range(4):
        wd_sum[zi] = (wd_own[zi].astype(f32) + wd_across[zi].astype(f32)).astype(bf16)
    wd_first = {d: copies.send(wd_sum.at[step(me, "z", d)], wd_in.at[d - 1], zs[d]) for d in (1, 3, 2)}
    o_move.wait_recv()
    o_sum[...] = (o_half[c].astype(f32) + o_core[...].astype(f32)).astype(bf16)
    o_first = {d: copies.send(o_sum.at[step(me, "z", d)], o_in.at[d - 1], zs[d]) for d in (1, 3, 2)}
    queries_back.wait_recv()
    load_rope.wait()
    load_x.wait()
    turned_back = ((acc[c] + acc_in[...]) * SCALE).T

    def revert(rows):
        return rows * rope[0] - pltpu.roll(rows, HD // 2, 1) * rope[1]

    def keep_head(h, rows):
        low_rows = rows.astype(bf16)
        gp[h] = low_rows
        gp_flat[:, pl.ds(h * HD, HD)] = low_rows
        small[pl.ds(24 + h, 1), :] = jnp.sum(low_rows.astype(f32), axis=0, keepdims=True)

    def to_small(first_row, row):
        for k in range(D // 128):
            small[pl.ds(first_row + k, 1), :] = row[:, k * 128 : (k + 1) * 128]

    small[...] = jnp.zeros_like(small)
    to_small(12, mlp_gain_terms[...])
    for h in range(HEADS):
        keep_head(h, revert(turned_back[h * TOK : (h + 1) * TOK]))
    load_w.wait()
    front = HEADS * HD
    partial = nt(gp_flat[:, pl.ds(0, front)], w_qkv[:, pl.ds(0, front)])

    kv_last.wait_recv()
    grad_kv = u[xh].astype(f32) + r3[...].astype(f32)
    keep_head(HEADS, revert(grad_kv[:, :HD]))
    keep_head(HEADS + 1, grad_kv[:, HD:])
    gp_moves = [
        copies.send(gp.at[step(me, "y", m[0]) * 2 + step(me, "c", m[1])], gp_all.at[y, c], group[m])
        for m in near_moves
    ]
    gp_all[y, c] = gp[y * 2 + c]
    back = pl.ds(front, 2 * HD)
    part[...] = (partial + nt(gp_flat[:, back], w_qkv[:, back])).astype(bf16)
    swap = copies.send(part, part_other, other)
    load_up.wait()
    for d in (1, 3, 2):
        first[d].wait_recv()
    send_mid(1, up_own[...].astype(f32) + three(up_in), up_mid, up_second)
    load_strip.wait()
    collect(0)
    load_act.wait()
    for copy in gp_moves:
        copy.wait_recv()
    q_terms[...] = tn(
        gp_all[...].reshape(GROUP * TOK, HD), act_all[...].reshape(GROUP * TOK, D)
    ).astype(bf16)

    q_one = {d: copies.send(q_terms.at[:, z_cols(d)], q_first.at[d - 1], zs[d]) for d in (1, 3, 2)}
    down_swap.wait_recv()
    load_resid.wait()
    layer_out[...] = (
        resid[...] + (down_part[...].astype(f32) + down_other[...].astype(f32))
    ).astype(bf16)
    keep_result(1, layer_out)
    swap.wait_recv()
    grad_act = part[...].astype(f32) + part_other[...].astype(f32)
    rows = x[...].astype(f32)
    inverse = lax.rsqrt(jnp.mean(rows * rows, axis=-1, keepdims=True) + rms_eps)
    normed = rows * inverse
    to_small(0, jnp.sum(grad_act * normed, axis=0, keepdims=True))
    small_one = {d: copies.send(small, e1.at[d - 1], zs[d]) for d in (1, 3, 2)}
    grad_normed = grad_act * gain[...].reshape(1, D)
    inner = jnp.mean(grad_normed * normed, axis=-1, keepdims=True)
    in_grad[...] = (grad_resid[...] + inverse * (grad_normed - normed * inner)).astype(bf16)

    keep_result(0, in_grad)
    for d in (1, 3, 2):
        wd_first[d].wait_recv()
    wd_mid[...] = (wd_sum[z].astype(f32) + three(wd_in)).astype(bf16)
    for d in (1, 3, 2):
        second[2, d] = copies.send(wd_mid.at[step(me, "y", d)], wd_second.at[y], ys[d])
    wd_second[y] = wd_mid[y]
    for d in (1, 3, 2):
        o_first[d].wait_recv()
    o_total = (o_sum[z].astype(f32) + three(o_in)).astype(bf16)
    o_mid[0], o_mid[1] = o_total[:48], o_total[48:]
    o_last = copies.send(o_mid.at[1 - xh], o_across, across)
    for d in (1, 3, 2):
        q_one[d].wait_recv()
    send_mid(3, q_terms[:, z_cols(0)].astype(f32) + three(q_first), q_mid, q_second)
    for d in (1, 3, 2):
        small_one[d].wait_recv()
    f1[...] = small[...] + three(e1)
    small_two = {m: copies.send(f1, e2.at[k], near[m]) for k, m in enumerate(near_moves)}
    o_last.wait_recv()
    o_fin[...] = o_mid[xh].astype(f32) + o_across[...].astype(f32)
    o_end = copies.send(o_fin.at[give], o_third, partner)
    collect(1)
    deliver(0)
    keep_result(2, sum_gate)
    deliver(1)
    keep_result(3, sum_up)
    collect(2)
    collect(3)
    for m in near_moves:
        small_two[m].wait_recv()
    f2[...] = f1[...]
    for k in range(len(near_moves)):
        f2[...] = f2[...] + e2[k]
    small_three = copies.send(f2, e3, partner)
    deliver(2)
    keep_result(4, sum_down)
    deliver(3)
    keep_result(5, sum_qkv)
    o_end.wait_recv()
    o_mine, o_theirs = o_fin[keep], o_third[...]
    sum_out[:, : HEADS * HD // 2] = jnp.where(c == 0, o_mine, o_theirs)
    sum_out[:, HEADS * HD // 2 :] = jnp.where(c == 0, o_theirs, o_mine)
    keep_result(6, sum_out)
    small_three.wait_recv()
    small_out[...] = f2[...] + e3[...]
    keep_result(7, small_out)
    moves.finish(kept_back)
    copies.finish()


def back(*arrays):
    half = TOK // 2
    wide = 2 * HD
    results_of = [
        jax.ShapeDtypeStruct((TOK, D), bf16),
        jax.ShapeDtypeStruct((TOK, D), bf16),
        *[jax.ShapeDtypeStruct((24, FF // 2), f32)] * 3,
        jax.ShapeDtypeStruct((24, (HEADS + 2) * HD), f32),
        jax.ShapeDtypeStruct((24, HEADS * HD), f32),
        jax.ShapeDtypeStruct((40, 128), f32),
    ]
    return pl.pallas_call(
        back_kernel,
        out_shape=results_of,
        in_specs=[SMEM] + [VMEM] * 5 + [ANY] * 14,
        out_specs=[ANY] * 8,
        scratch_shapes=[
            pltpu.VMEM((2, NQ, HD), bf16),
            pltpu.VMEM((2, 8, NQ), f32),
            pltpu.VMEM((2, HD, NQ), f32),
            pltpu.VMEM((HD, NQ), f32),
            pltpu.VMEM((4, 4, 2, TOK, wide), bf16),
            pltpu.VMEM((3, 4, 2, half, wide), bf16),
            pltpu.VMEM((3, 4, 2, half, wide), bf16),
            pltpu.VMEM((4, 2, half, wide), bf16),
            pltpu.VMEM((4, 2, half, wide), bf16),
            pltpu.VMEM((3, 2, half, wide), bf16),
            pltpu.VMEM((3, 2, half, wide), bf16),
            pltpu.VMEM((2, TOK, wide), bf16),
            pltpu.VMEM((TOK, wide), bf16),
            pltpu.VMEM((D, (HEADS + 2) * HD), bf16),
            pltpu.VMEM((4, 2, TOK, D), bf16),
            pltpu.VMEM((4, 4, 96, TOK), bf16),
            pltpu.VMEM((4, 4, 96, TOK), bf16),
            pltpu.VMEM((4, TOK, HEADS * HD), bf16),
            pltpu.VMEM((HEADS + 2, TOK, HD), bf16),
            pltpu.VMEM((TOK, (HEADS + 2) * HD), bf16),
            pltpu.VMEM((4, 2, TOK, HD), bf16),
            pltpu.VMEM((TOK, D), bf16),
            pltpu.VMEM((TOK, D), bf16),
            pltpu.VMEM((40, 128), f32),
            pltpu.VMEM((3, 40, 128), f32),
            pltpu.VMEM((7, 40, 128), f32),
            pltpu.VMEM((40, 128), f32),
            pltpu.VMEM((40, 128), f32),
            pltpu.VMEM((40, 128), f32),
            pltpu.VMEM((UNITS, 384), bf16),
            pltpu.VMEM((3, UNITS, 384), bf16),
            pltpu.VMEM((4, 2, 48, COLUMNS), bf16),
            *[pltpu.VMEM((4, 4, 48, COLUMNS), bf16)] * 3,
            pltpu.VMEM((3, 4, 48, COLUMNS), bf16),
            *[pltpu.VMEM((4, 48, COLUMNS), bf16)] * 2,
            *[pltpu.VMEM((4, 2, 48, COLUMNS), bf16)] * 2,
            *[pltpu.VMEM((4, 48, COLUMNS), f32)] * 3,
            *[pltpu.VMEM((4, 24, COLUMNS), f32)] * 3,
            pltpu.VMEM((HD, D), bf16),
            pltpu.VMEM((3, HD, 384), bf16),
            pltpu.VMEM((4, 2, 48, HD), bf16),
            pltpu.VMEM((4, 2, 48, HD), bf16),
            pltpu.VMEM((4, 48, HD), f32),
            pltpu.VMEM((4, 24, HD), f32),
            pltpu.VMEM((TOK, D), bf16),
            pltpu.VMEM((TOK, D), bf16),
            pltpu.VMEM((TOK, D), bf16),
            pltpu.VMEM((2, NQ, HD), bf16),
            pltpu.VMEM((4, 4, 2, TOK, wide), bf16),
            pltpu.VMEM((HD, NQ), f32),
            pltpu.VMEM((TOK, D), f32),
            pltpu.VMEM((TOK, D), f32),
            pltpu.VMEM((2, 4, 96, HEADS * HD // 2), bf16),
            *[pltpu.VMEM((4, 96, HEADS * HD // 2), bf16)] * 2,
            pltpu.VMEM((3, 96, HEADS * HD // 2), bf16),
            pltpu.VMEM((2, 48, HEADS * HD // 2), bf16),
            pltpu.VMEM((48, HEADS * HD // 2), bf16),
            pltpu.VMEM((48, HEADS * HD // 2), f32),
            pltpu.VMEM((24, HEADS * HD // 2), f32),
            pltpu.VMEM((TOK, D), bf16),
            pltpu.VMEM((2, TOK, HD), f32),
            *[pltpu.VMEM(a.shape, a.dtype) for a in results_of],
            *sems(93),
            pltpu.SemaphoreType.DMA((21,)),
        ],
        compiler_params=params(9, 62),
    )(*arrays)


def results_kernel(*refs):
    wholes, small, copied = refs[:7], refs[7], refs[8:15]
    norm_attn, norm_mlp, bias, value_bias, *held, into, out_of = refs[15:]
    shard = shard_of(here())
    loads, stores = Moves(into), Moves(out_of)
    for a, b in zip(wholes, held):
        loads.start(a, b)
    rows = jnp.concatenate(
        [
            jnp.concatenate([small[12 * i + k : 12 * i + k + 1, :] for k in range(12)], axis=1)
            for i in range(2)
        ],
        axis=0,
    )
    turned = pltpu.roll(rows, lax.rem(D - 24 * shard, D), 1)
    norm_attn[...] = turned[0:1, :24]
    norm_mlp[...] = turned[1:2, :24]
    heads = pltpu.roll(small[24 : 24 + HEADS + 2, :], lax.rem(HD - 2 * shard, HD), 1)
    bias[0] = heads[: HEADS + 1, :2].T
    value_bias[...] = heads[HEADS + 1 :, :2]
    for load, a, b in zip(loads.started, held, copied):
        load.wait()
        stores.start(a, b)
    stores.finish(stores.started)


def results(*arrays):
    *wholes, small = arrays
    return pl.pallas_call(
        results_kernel,
        out_shape=[
            *[jax.ShapeDtypeStruct(a.shape, a.dtype) for a in wholes],
            jax.ShapeDtypeStruct((1, 24), f32),
            jax.ShapeDtypeStruct((1, 24), f32),
            jax.ShapeDtypeStruct((1, 2, HEADS + 1), f32),
            jax.ShapeDtypeStruct((1, 2), f32),
        ],
        in_specs=[ANY] * 7 + [VMEM],
        out_specs=[ANY] * 7 + [VMEM] * 4,
        scratch_shapes=[
            *[pltpu.VMEM(a.shape, a.dtype) for a in wholes],
            *[pltpu.SemaphoreType.DMA((7,))] * 2,
        ],
    )(*wholes, small)


def shards(
    layer_in, lengths, norm_attn, w_qkv, qkv_bias, w_out, norm_mlp, w_gate, w_up, w_down, out_grad
):
    half = HD // 2
    freqs = np.float32(rope_base) ** (-2.0 * np.arange(half, dtype=np.float32) / HD)
    freqs = np.concatenate([freqs, freqs]).astype(np.float32)[None]
    kv, queries, act_attn, resid, exact, lse, rope, gate_w, up_w, out_grad_all, low_all = attend(
        lengths, layer_in, norm_attn, qkv_bias, freqs, out_grad, w_qkv, w_out, w_gate, w_up
    )
    (
        grad_resid, grads, gain_terms, gate_sum, down_near, down_far,
        up_terms, down_terms, act_attn_all,
    ) = feed_forward(
        resid, norm_mlp, out_grad, act_attn, w_out, out_grad_all, gate_w, up_w, w_down
    )
    sums = back(
        lengths, lse, grad_resid, grads, norm_attn, gain_terms, layer_in, rope, gate_sum, down_far,
        queries, kv, exact, resid, down_near, low_all, w_qkv, act_attn_all, up_terms, down_terms,
    )
    in_grad, layer_out, sum_gate, sum_up, sum_down, sum_qkv, sum_out, *rest = results(*sums)
    sum_norm_attn, sum_norm_mlp, bias, value_bias = rest
    return (
        layer_out,
        in_grad,
        sum_norm_attn[0],
        sum_qkv,
        bias.swapaxes(1, 2),
        value_bias,
        sum_out.T,
        sum_norm_mlp[0],
        sum_gate,
        sum_up,
        sum_down.T,
    )


def solution(mesh):
    torus = Mesh(mesh.devices.reshape(4, 4, 2, 2, 2), AXES)
    in_specs = (
        P(WIDE, None),
        P(),
        P(),
        P(None, "n"),
        P("n", None),
        P("n", None),
        P(),
        P(None, "n"),
        P(None, "n"),
        P("n", None),
        P(WIDE, None),
    )
    out_specs = (
        P(WIDE, None),
        P(WIDE, None),
        P(WIDE),
        P(WIDE, "n"),
        P("n", None, WIDE),
        P("n", WIDE),
        P("n", WIDE),
        P(WIDE),
        P(WIDE, "n"),
        P(WIDE, "n"),
        P("n", WIDE),
    )
    return jax.shard_map(
        shards, mesh=torus, in_specs=in_specs, out_specs=out_specs, check_vma=False
    )
```

```python
import functools
import math

import jax
import jax.numpy as jnp
import numpy as np
from jax import lax
from jax.experimental import pallas as pl
from jax.experimental.pallas import tpu as pltpu
from jax.sharding import Mesh
from jax.sharding import PartitionSpec as P

HD = 128
QH = 12
KVH = 2
HEADS = QH // KVH
D = 1536
FF = 8960
TOK = 128
TOKENS = 8192
SEQS = 4
NQ = HEADS * TOK
GROUP = 8
UNITS = FF // 2 // GROUP
WINDOW = 768
COLUMNS = 640

AXES = ("z", "y", "xh", "c", "n")
SIZE = {"z": 4, "y": 4, "xh": 2, "c": 2, "n": 2}
WIDE = ("z", "y", "xh", "c")
MESH = pl.DeviceIdType.MESH

rms_eps = 1e-06
rope_base = 10000.0
big_negative = -1e30
SCALE = HD ** (-0.5)
SCALE_LOG2 = SCALE * math.log2(math.e)
KEY_BLOCK = 512
BLOCK_SHARDS = KEY_BLOCK // TOK
Q_CHUNK = 256

bf16 = jnp.bfloat16
f32 = jnp.float32
VMEM = pl.BlockSpec(memory_space=pltpu.VMEM)
SMEM = pl.BlockSpec(memory_space=pltpu.SMEM)
ANY = pl.BlockSpec(memory_space=pl.ANY)


def nn(a, b):
    return lax.dot_general(a, b, (((1,), (0,)), ((), ())), preferred_element_type=f32)


def nt(a, b):
    return lax.dot_general(a, b, (((1,), (1,)), ((), ())), preferred_element_type=f32)


def tn(a, b):
    return lax.dot_general(a, b, (((0,), (0,)), ((), ())), preferred_element_type=f32)


def here():
    return {a: lax.axis_index(a) for a in AXES}


def step(me, axis, by):
    return lax.rem(me[axis] + by, SIZE[axis])


def at(me, **moved):
    return tuple(step(me, a, moved[a]) if a in moved else me[a] for a in AXES)


def sequence_starts(ids, lengths):
    starts, end = jnp.zeros_like(ids), 0
    for s in range(SEQS):
        end = end + lengths[s]
        starts = starts + jnp.where(ids >= end, lengths[s], 0)
    return starts


def token_rows(me, lengths):
    column = lax.broadcasted_iota(jnp.int32, (1, 2 * NQ), 1)
    ids = shard_of(me) // 2 * (2 * TOK) + column // NQ * TOK + column % TOK
    return ids, sequence_starts(ids, lengths)


def hail(peers):
    barrier = pltpu.get_barrier_semaphore()
    for p in peers:
        pl.semaphore_signal(barrier, inc=1, device_id=p, device_id_type=MESH)
    return lambda: pl.semaphore_wait(barrier, len(peers))


def greet(peers):
    hail(peers)()


class Copies:
    def __init__(self, send_sems, recv_sems):
        self.send_sems, self.recv_sems, self.used, self.started = send_sems, recv_sems, 0, []

    def make(self, src, dst, target):
        self.used += 1
        return self.numbered(self.used - 1, src, dst, target)

    def numbered(self, k, src, dst, target):
        return pltpu.make_async_remote_copy(
            src_ref=src,
            dst_ref=dst,
            send_sem=self.send_sems.at[k],
            recv_sem=self.recv_sems.at[k],
            device_id=target,
            device_id_type=MESH,
        )

    def send(self, src, dst, target):
        copy = self.make(src, dst, target)
        copy.start()
        self.started.append(copy)
        return copy

    def finish(self):
        for copy in self.started:
            copy.wait_send()


class Moves:
    def __init__(self, move_sems):
        self.move_sems, self.started = move_sems, []

    def start(self, src, dst):
        copy = pltpu.make_async_copy(src, dst, self.move_sems.at[len(self.started)])
        copy.start()
        self.started.append(copy)
        return copy

    def finish(self, copies):
        for copy in copies:
            copy.wait()


def sems(count):
    return [pltpu.SemaphoreType.DMA((count,)), pltpu.SemaphoreType.DMA((count,))]


def params(ident, mib=60):
    return pltpu.CompilerParams(
        collective_id=ident, has_side_effects=True, vmem_limit_bytes=mib * 2**20
    )


def whole_tiles(values):
    pad = jnp.zeros((values.shape[0], COLUMNS - values.shape[1]), values.dtype)
    return jnp.concatenate([values, pad], axis=1)


def three(ref):
    return ref[0].astype(f32) + ref[1].astype(f32) + ref[2].astype(f32)


def shard_of(me):
    return ((me["z"] * 4 + me["y"]) * 2 + me["xh"]) * 2 + me["c"]


class Rows:
    def __init__(self, me, copies, source, slots):
        self.me, self.copies, self.source, self.slots = me, copies, source, slots
        half = TOK // 2
        n = me["n"]
        self.mine = pl.ds(pl.multiple_of(half * n, half), half)
        self.theirs = pl.ds(pl.multiple_of(half * (1 - n), half), half)
        self.own = slots.at[me["y"], me["c"]]
        self.near, self.far, self.across = [], {}, {}

    def pair(self):
        self.near.append(self.copies.send(self.source, self.own, at(self.me, c=1)))

    def slot(self, d, rows):
        return self.slots.at[lax.rem(self.me["y"] + (4 - d), 4), self.me["c"], rows]

    def start(self, *steps):
        for d in steps:
            self.far[d] = self.copies.send(
                self.source.at[self.mine], self.own.at[self.mine], at(self.me, y=d)
            )

    def pass_on(self, *steps):
        for d in steps:
            self.far[d].wait_recv()
            got = self.slot(d, self.mine)
            self.across[d] = self.copies.send(got, got, at(self.me, n=1))
            self.near.append(self.copies.send(got, got, at(self.me, c=1)))

    def complete(self, *steps):
        for d in steps:
            self.across[d].wait_recv()
            got = self.slot(d, self.theirs)
            self.near.append(self.copies.send(got, got, at(self.me, c=1)))

    def wait(self):
        for copy in self.near:
            copy.wait_recv()


def attend_kernel(
    lengths, x, gain, bias, freqs, og, w_qkv_hbm, w_out_hbm, w_gate_hbm, w_up_hbm,
    kv_hbm, q_hbm, act_hbm, resid_hbm, exact_hbm, lse_hbm, rope_hbm, gate_hbm, up_hbm, og_all, al_all,
    stats, acc, low_acc, stats_in, acc_in, low_in, w_qkv, w_out, o, pa, pb,
    kv, q, act, resid, exact, lse, rope, gate_w, up_w, wide_gate, wide_up, send_sems, recv_sems, local_sems,
):
    me = here()
    moves, kept_back = Moves(local_sems), []
    load_w = moves.start(w_qkv_hbm, w_qkv)
    ids, start = token_rows(me, lengths)
    z, y, xh, c = me["z"], me["y"], me["xh"], me["c"]
    partner, across, other = at(me, c=1), at(me, xh=1), at(me, n=1)
    ys = {d: at(me, y=d) for d in (1, 2, 3)}
    zs = {d: at(me, z=d) for d in (1, 2, 3)}
    everyone_in = hail([partner, across, other, *ys.values(), *zs.values()])
    rows = x[...].astype(f32)
    inverse = lax.rsqrt(jnp.mean(rows * rows, axis=-1, keepdims=True) + rms_eps)
    act[...] = (rows * inverse * gain[...].reshape(1, D)).astype(bf16)
    token = shard_of(me) * TOK + lax.broadcasted_iota(jnp.int32, (TOK, 1), 0)
    angles = (token - sequence_starts(token, lengths)).astype(f32) * freqs[...]
    cosine = jnp.cos(angles)
    turned = jnp.sin(angles)
    first_half = lax.broadcasted_iota(jnp.int32, (TOK, HD), 1) < HD // 2
    sine = jnp.where(first_half, -turned, turned)
    rope[0], rope[1] = cosine, sine
    kept_back.append(moves.start(rope, rope_hbm))
    front = HEADS * HD

    def turn(values):
        return values * cosine + pltpu.roll(values, HD // 2, 1) * sine

    load_w.wait()
    back = nn(act[...], w_qkv[:, front:]) + bias[:, front:]
    mine = kv.at[z, y, xh]
    mine[:, pl.ds(0, HD)] = turn(back[:, :HD]).astype(bf16)
    mine[:, pl.ds(HD, HD)] = back[:, HD:].astype(bf16)
    everyone_in()
    kept_back.append(moves.start(act, act_hbm))
    load_out = moves.start(w_out_hbm, w_out)
    copies = Copies(send_sems, recv_sems)
    rows_of_og = Rows(me, copies, og, og_all)
    rows_of_og.start(1, 3)
    first = copies.send(mine, mine, across)
    ahead = nn(act[...], w_qkv[:, :front]) + bias[:, :front]
    for h in range(HEADS):
        head = turn(ahead[:, h * HD : (h + 1) * HD]).astype(bf16)
        q[c, pl.ds(h * TOK, TOK), :] = head
    share_q = copies.send(q.at[c], q.at[c], partner)
    rows_of_og.pair()
    kept_back.append(moves.start(og, og_all.at[y, c]))
    stats[:, 0:1, :] = jnp.full((2, 1, NQ), big_negative, f32)
    stats[:, 1:8, :] = jnp.zeros((2, 7, NQ), f32)
    acc[...] = jnp.zeros_like(acc)
    low_acc[...] = jnp.zeros_like(low_acc)
    last = shard_of(me) // BLOCK_SHARDS
    kept = start < last * KEY_BLOCK
    half = TOK // 2
    keys_here = 2 * half

    early = sequence_starts(last * KEY_BLOCK - 1, lengths)

    def take(parts, masked=False, from_first=False):
        def both(columns):
            return jnp.concatenate(
                [
                    kv[zi, yi, :, pl.ds(pl.multiple_of(half * k, half), half), columns].reshape(
                        keys_here, HD
                    )
                    for zi, yi, k in parts
                ],
                axis=0,
            )

        def key_ids(columns):
            place = lax.broadcasted_iota(jnp.int32, (keys_here, columns), 0)
            place = place + place // half * (2 * TOK - half)
            return jnp.concatenate(
                [(4 * zi + yi) * KEY_BLOCK + c * TOK + half * k + place for zi, yi, k in parts], axis=0
            )

        keys, values = both(pl.ds(0, HD)), both(pl.ds(HD, HD)).T
        if from_first:
            barred = jnp.where(key_ids(1) >= early, 0.0, big_negative)
        for chunk in range(2 * NQ // Q_CHUNK):
            core, cs = divmod(chunk * Q_CHUNK, NQ)
            cs = pl.ds(cs, Q_CHUNK)
            here_cols = slice(chunk * Q_CHUNK, (chunk + 1) * Q_CHUNK)
            scores = nt(keys, q[core, cs, :]) * SCALE_LOG2
            if masked:
                which = key_ids(Q_CHUNK)
                allowed = (which >= start[:, here_cols]) & (which <= ids[:, here_cols])
                scores = jnp.where(allowed, scores, big_negative)
            if from_first:
                scores = scores + barred
            old = stats[core, 0:1, cs]
            new = jnp.maximum(old, jnp.max(scores, axis=0, keepdims=True))
            if masked:
                probs = jnp.where(allowed, jnp.exp2(scores - new), 0.0)
            else:
                taken = kept[:, here_cols]
                new = jnp.where(taken, new, old)
                probs = jnp.exp2(scores - jnp.where(taken, new, -big_negative))
            fade = jnp.exp2(old - new)
            stats[core, 0:1, cs] = new
            stats[core, 1:2, cs] = stats[core, 1:2, cs] * fade + jnp.sum(probs, axis=0, keepdims=True)
            upper = probs.astype(bf16)
            rest = (probs - upper.astype(f32)).astype(bf16)
            acc[core, :, cs] = acc[core, :, cs] * fade + nn(values, upper)
            low_acc[core, :, cs] = low_acc[core, :, cs] * fade + nn(values, rest)

    def pair(za, ya, zb, yb):
        a, b = 4 * za + ya, 4 * zb + yb
        spots = [(za, ya, 0), (zb, yb, 1)]
        before_last = jnp.maximum(a, b) < last
        has_first = jnp.minimum(a, b) == 0

        @pl.when(before_last & jnp.logical_not(has_first))
        def _():
            take(spots)

        @pl.when(before_last & has_first)
        def _():
            take(spots, from_first=True)

        @pl.when(jnp.logical_not(before_last))
        def _():
            @pl.loop(0, 2)
            def _(k):
                zi, yi = jnp.where(k == 0, za, zb), jnp.where(k == 0, ya, yb)
                index = 4 * zi + yi
                edge = (index == 0) | (index == last)

                @pl.when(edge & (index <= last))
                def _():
                    take([(zi, yi, k)], masked=True)

                @pl.when((index < last) & jnp.logical_not(edge))
                def _():
                    take([(zi, yi, k)])

    def two_pairs(one, two):
        spots = [(*one[:2], 0), (*one[2:], 1), (*two[:2], 0), (*two[2:], 1)]
        index = [4 * zi + yi for zi, yi, _ in spots]
        least = jnp.minimum(jnp.minimum(index[0], index[1]), jnp.minimum(index[2], index[3]))
        most = jnp.maximum(jnp.maximum(index[0], index[1]), jnp.maximum(index[2], index[3]))
        @pl.when((most < last) & (least > 0))
        def _():
            take(spots)

        @pl.when((most < last) & (least == 0))
        def _():
            take(spots, from_first=True)

        @pl.when(most >= last)
        def _():
            @pl.loop(0, 2)
            def _(i):
                pair(*(jnp.where(i == 0, a, b) for a, b in zip(one, two)))

    first.wait_recv()
    low, high = pl.ds(0, half), pl.ds(half, half)

    def slot(zi, yi, rows):
        return kv.at[zi, yi, :, rows]

    def before(axis, d):
        return lax.rem(me[axis] + (4 - d), 4)

    first_low, first_high = {}, {}
    for d in (1, 3, 2):
        first_low[d] = copies.send(slot(z, y, low), slot(z, y, low), ys[d])
        first_high[d] = copies.send(slot(z, y, high), slot(z, y, high), zs[d])
    share_q.wait_recv()

    kept_back.append(moves.start(q, q_hbm))
    first_unit = (y * 2 + c) * UNITS
    tile = jnp.minimum(first_unit // 128, FF // 2 // 128 - WINDOW // 128)
    window = pl.ds(pl.multiple_of(tile * 128, 128), WINDOW)
    load_gate = moves.start(w_gate_hbm.at[:, window], wide_gate)
    load_up = moves.start(w_up_hbm.at[:, window], wide_up)
    take([(z, y, 0), (z, y, 1)], masked=True)
    second_from = copies.used
    copies.used += 24
    for i, e in enumerate((0, 1, 3, 2)):
        yi, zi = before("y", e), before("z", e)
        if e:
            first_low[e].wait_recv()
            first_high[e].wait_recv()
        for j, d in enumerate((1, 3, 2)):
            k = second_from + 2 * (3 * i + j)
            for copy in (
                copies.numbered(k, slot(z, yi, low), slot(z, yi, low), zs[d]),
                copies.numbered(k + 1, slot(zi, y, high), slot(zi, y, high), ys[d]),
            ):
                copy.start()
                copies.started.append(copy)
    rows_of_og.start(2)
    rows_of_og.pass_on(1, 3)

    @pl.loop(1, 4)
    def _(e):
        pair(z, before("y", e), before("z", e), y)

    def places(k):
        i, j = k // 3, lax.rem(k, 3)
        e = jnp.where(i < 2, i, 5 - i)
        d = jnp.where(j < 2, 1 + 2 * j, 2)
        return before("z", d), before("y", e), before("z", e), before("y", d)

    def arrive(k):
        za, ya, zb, yb = places(k)
        one, two = slot(za, ya, low), slot(zb, yb, high)
        copies.numbered(second_from + 2 * k, one, one, zs[1]).wait_recv()
        copies.numbered(second_from + 2 * k + 1, two, two, ys[1]).wait_recv()

    def two_arrive(i):
        arrive(2 * i)
        arrive(2 * i + 1)
        two_pairs(places(2 * i), places(2 * i + 1))

    pl.loop(0, 4)(two_arrive)
    rows_of_og.pass_on(2)
    pl.loop(4, 6)(two_arrive)
    kept_back.append(moves.start(kv, kv_hbm))
    merge = [
        copies.send(stats.at[1 - c], stats_in, partner),
        copies.send(acc.at[1 - c], acc_in, partner),
        copies.send(low_acc.at[1 - c], low_in, partner),
    ]
    rows_of_og.complete(1, 3, 2)
    for copy in merge:
        copy.wait_recv()
    own_top, in_top = stats[c, 0:1, :], stats_in[0:1, :]
    top = jnp.maximum(own_top, in_top)
    own_part, in_part = jnp.exp2(own_top - top), jnp.exp2(in_top - top)
    total = stats[c, 1:2, :] * own_part + stats_in[1:2, :] * in_part
    inverse = 1.0 / total
    own_part, in_part = own_part * inverse, in_part * inverse
    rows = acc[c] * own_part + acc_in[...] * in_part
    exact[...] = rows + (low_acc[c] * own_part + low_in[...] * in_part)
    rows = rows.T.astype(bf16)
    for h in range(HEADS):
        o[:, pl.ds(h * HD, HD)] = rows[h * TOK : (h + 1) * TOK]
    load_out.wait()
    pa[...] = nn(o[...], w_out[...]).astype(bf16)
    swap = copies.send(pa, pb, other)
    own_al = al_all.at[y]
    al_moves = {d: copies.send(o, own_al, ys[d]) for d in (1, 3, 2)}
    kept_back.append(moves.start(o, own_al))
    lse[...] = top + jnp.log2(total)
    kept_back.append(moves.start(lse, lse_hbm))
    kept_back.append(moves.start(exact, exact_hbm))
    shift = lax.rem(WINDOW - (first_unit - tile * 128), WINDOW)
    for load, part, weights, whole in (
        (load_gate, wide_gate, gate_w, gate_hbm),
        (load_up, wide_up, up_w, up_hbm),
    ):
        load.wait()

        @pl.loop(0, D // 128)
        def _(index, part=part, weights=weights):
            rows = pl.ds(pl.multiple_of(index * 128, 128), 128)
            rolled = pltpu.roll(part[rows, :].astype(f32), shift, 1)
            weights[rows, :] = rolled[:, :COLUMNS].astype(bf16)

        kept_back.append(moves.start(weights, whole))
    rows_of_og.wait()
    swap.wait_recv()
    resid[...] = x[...].astype(f32) + (pa[...].astype(f32) + pb[...].astype(f32))
    kept_back.append(moves.start(resid, resid_hbm))
    for copy in al_moves.values():
        copy.wait_recv()
    moves.finish(kept_back)
    copies.finish()


def attend(*arrays):
    state = [
        jax.ShapeDtypeStruct((4, 4, 2, TOK, 2 * HD), bf16),
        jax.ShapeDtypeStruct((2, NQ, HD), bf16),
        jax.ShapeDtypeStruct((TOK, D), bf16),
        jax.ShapeDtypeStruct((TOK, D), f32),
        jax.ShapeDtypeStruct((HD, NQ), f32),
        jax.ShapeDtypeStruct((1, NQ), f32),
        jax.ShapeDtypeStruct((2, TOK, HD), f32),
        jax.ShapeDtypeStruct((D, COLUMNS), bf16),
        jax.ShapeDtypeStruct((D, COLUMNS), bf16),
    ]
    return pl.pallas_call(
        attend_kernel,
        out_shape=[
            *state,
            jax.ShapeDtypeStruct((4, 2, TOK, D), bf16),
            jax.ShapeDtypeStruct((4, TOK, HEADS * HD), bf16),
        ],
        in_specs=[SMEM] + [VMEM] * 5 + [ANY] * 4,
        out_specs=[ANY] * 11,
        scratch_shapes=[
            pltpu.VMEM((2, 8, NQ), f32),
            pltpu.VMEM((2, HD, NQ), f32),
            pltpu.VMEM((2, HD, NQ), f32),
            pltpu.VMEM((8, NQ), f32),
            pltpu.VMEM((HD, NQ), f32),
            pltpu.VMEM((HD, NQ), f32),
            pltpu.VMEM((D, (HEADS + 2) * HD), bf16),
            pltpu.VMEM((HEADS * HD, D), bf16),
            pltpu.VMEM((TOK, HEADS * HD), bf16),
            *[pltpu.VMEM((TOK, D), bf16)] * 2,
            *[pltpu.VMEM(a.shape, a.dtype) for a in state],
            *[pltpu.VMEM((D, WINDOW), bf16)] * 2,
            *sems(52),
            pltpu.SemaphoreType.DMA((15,)),
        ],
        compiler_params=params(1),
    )(*arrays)


def mlp_kernel(*refs):
    resid, gain, og, aa, w_out_hbm, og_hbm, gate_hbm, up_w_hbm, w_down_hbm = refs[:9]
    back_hbm, grads_hbm, gains_hbm, gate_sum_hbm, near_hbm, far_hbm, up_hbm, down_hbm, aa_all = refs[9:18]
    wd, og_all, act_all, grad_hidden, hidden, ggp, gup, bk, dn, bk_core, dn_core, bk_sent, bk_in = refs[18:31]
    nb, rn, gate_terms, gate_in, gate_w, up_w, up_terms, down_terms, down_sum, dn_in, w_out = refs[31:42]
    grad_resid, grads, gain_terms, gate_sum, down_near, send_sems, recv_sems, local_sems = refs[42:]
    me = here()
    z, y, c = me["z"], me["y"], me["c"]
    partner, other = at(me, c=1), at(me, n=1)
    ys = {d: at(me, y=d) for d in (1, 2, 3)}
    zs = {d: at(me, z=d) for d in (1, 2, 3)}
    everyone_in = hail([partner, other, *ys.values(), *zs.values()])
    moves, kept_back = Moves(local_sems), []
    load_gate, load_up = moves.start(gate_hbm, gate_w), moves.start(up_w_hbm, up_w)
    units = pl.ds(pl.multiple_of((y * 2 + c) * UNITS, 16), UNITS)
    load_down, load_og = moves.start(w_down_hbm.at[units], wd), moves.start(og_hbm, og_all)
    load_out = moves.start(w_out_hbm, w_out)
    kept_back.append(moves.start(aa, aa_all.at[y, c]))
    everyone_in()
    copies = Copies(send_sems, recv_sems)
    half = TOK // 2
    halves = (pl.ds(0, half), pl.ds(half, half))
    gain = gain[...].reshape(1, D)

    def inverse_of(rows):
        return lax.rsqrt(jnp.mean(rows * rows, axis=-1, keepdims=True) + rms_eps)

    own = act_all.at[y, c]
    far, to_core = {}, {0: [], 1: [], 2: [], 3: []}
    for rows in halves:
        total = resid[rows, :]
        act_all[y, c, rows] = (total * inverse_of(total) * gain).astype(bf16)
        to_core[0].append(copies.send(own.at[rows], own.at[rows], partner))
        for d in (1, 3):
            far[d, len(to_core[0]) - 1] = copies.send(own.at[rows], own.at[rows], ys[d])
    load_down.wait()
    load_og.wait()
    pair = (2 * TOK, D)

    def hidden_back(d):
        yi = step(me, "y", d)
        grad_hidden[yi] = nt(og_all[yi].reshape(pair), wd[...])

    hidden_back(0)
    load_gate.wait()
    load_up.wait()
    bk_cores, dn_cores, bk_moves = {}, {}, {}

    def block(d, beside=None):
        yi = step(me, "y", d)
        rows = act_all[yi].reshape(pair)
        gate = nn(rows, gate_w[:, :UNITS])
        up = nn(rows, up_w[:, :UNITS])
        sigmoid = 1.0 / (1.0 + jnp.exp(-gate))
        silu = gate * sigmoid
        grads = grad_hidden[yi]
        hidden[yi] = (silu * up).astype(bf16)
        ggp[yi] = (grads * up * (sigmoid * (1.0 + gate * (1.0 - sigmoid)))).astype(bf16)
        gup[yi] = (grads * silu).astype(bf16)
        if beside is not None:
            pass_block(beside)
        both = nt(ggp[yi], gate_w[:, :UNITS]) + nt(gup[yi], up_w[:, :UNITS])
        bk[yi] = both.astype(bf16).reshape(2, TOK, D)
        bk_cores[d] = copies.send(bk.at[yi, 1 - c], bk_core.at[yi], partner)
    low, high = halves

    def pass_block(d):
        yi = step(me, "y", d)
        bk_cores[d].wait_recv()
        for k, rows in enumerate((low, high)):
            bk_sent[yi, rows] = (
                bk[yi, c, rows].astype(f32) + bk_core[yi, rows].astype(f32)
            ).astype(bf16)
            if d:
                bk_moves[d, k] = copies.send(
                    bk_sent.at[yi, rows], bk_in.at[d - 1, rows], ys[d]
                )

    def down_block(d):
        yi = step(me, "y", d)
        dn[yi] = nn(hidden[yi], wd[...]).astype(bf16).reshape(2, TOK, D)
        dn_cores[d] = copies.send(dn.at[yi, 1 - c], dn_core.at[yi], partner)

    def sum_down(d):
        yi = step(me, "y", d)
        dn_cores[d].wait_recv()
        down_sum[yi] = (dn[yi, c].astype(f32) + dn_core[yi].astype(f32)).astype(bf16)

    for copy in to_core[0]:
        copy.wait_recv()
    block(0)
    for d in (3, 1, 2):
        hidden_back(d)
    relay = {}
    for k, rows in enumerate(halves):
        for d in (1, 3):
            far[d, k].wait_recv()
            got = act_all.at[lax.rem(y + (4 - d), 4), c, rows]
            to_core[4 - d].append(copies.send(got, got, partner))
            if d == 1 + 2 * k:
                relay[d] = copies.send(got, got, ys[d])
    aa_rows = Rows(me, copies, aa, aa_all)
    aa_rows.start(1, 3, 2)
    aa_rows.pair()
    for copy in to_core[3]:
        copy.wait_recv()
    block(3, 0)
    for d, rows in ((1, low), (3, high)):
        relay[d].wait_recv()
        got = act_all.at[step(me, "y", 2), c, rows]
        to_core[2].append(copies.send(got, got, partner))
    for copy in to_core[1]:
        copy.wait_recv()
    block(1, 3)
    for copy in to_core[2]:
        copy.wait_recv()
    block(2, 1)

    everything = (GROUP * TOK, D)
    all_units = (GROUP * TOK, UNITS)
    gate_terms[...] = tn(ggp[...].reshape(all_units), act_all[...].reshape(everything)).astype(bf16)

    def z_cols(d):
        return pl.ds(pl.multiple_of(step(me, "z", d) * 384, 384), 384)

    gate_moves = {
        d: copies.send(gate_terms.at[:, z_cols(d)], gate_in.at[d - 1], zs[d]) for d in (1, 3, 2)
    }
    pass_block(2)
    aa_rows.pass_on(1, 3, 2)
    for d in (1, 3, 2, 0):
        down_block(d)
    up_terms[...] = tn(gup[...].reshape(all_units), act_all[...].reshape(everything)).astype(bf16)
    kept_back.append(moves.start(up_terms, up_hbm))
    for d in range(4):
        sum_down(d)
    swaps_back = []
    for k, rows in enumerate((low, high)):
        back = bk_sent[y, rows].astype(f32)
        for d in (1, 3, 2):
            bk_moves[d, k].wait_recv()
            back = back + bk_in[d - 1, rows].astype(f32)
        nb[rows] = back.astype(bf16)
        swaps_back.append(copies.send(nb.at[rows], rn.at[rows], other))
    dn_moves = {
        d: copies.send(down_sum.at[step(me, "y", d)], dn_in.at[d // 2], ys[d]) for d in (1, 3)
    }
    kept_back.append(moves.start(down_sum.at[step(me, "y", 2)], far_hbm))
    for zi in range(4):
        columns = og_all[:, :, :, pl.ds(384 * zi, 384)].reshape(GROUP * TOK, 384)
        sums = whole_tiles(tn(columns, hidden[...].reshape(all_units)).astype(bf16))
        down_terms[zi] = sums.reshape(4, 2, 48, COLUMNS)
    kept_back.append(moves.start(down_terms, down_hbm))
    aa_rows.complete(1, 3, 2)
    for copy in swaps_back:
        copy.wait_recv()
    grad_act = nb[...].astype(f32) + rn[...].astype(f32)
    inverse = inverse_of(resid[...])
    normed = resid[...] * inverse
    gain_terms[...] = jnp.sum(grad_act * normed, axis=0, keepdims=True)
    grad_normed = grad_act * gain
    inner = jnp.mean(grad_normed * normed, axis=-1, keepdims=True)
    grad_resid[...] = og[...].astype(f32) + inverse * (grad_normed - normed * inner)
    load_out.wait()
    grads[...] = nt(grad_resid[...].astype(bf16), w_out[...]).astype(bf16)
    for vmem, hbm in ((grad_resid, back_hbm), (grads, grads_hbm), (gain_terms, gains_hbm)):
        kept_back.append(moves.start(vmem, hbm))
    for d in (1, 3, 2):
        gate_moves[d].wait_recv()
    gate_sum[...] = whole_tiles((gate_terms[:, z_cols(0)].astype(f32) + three(gate_in)).T.astype(bf16))
    kept_back.append(moves.start(gate_sum, gate_sum_hbm))
    total = down_sum[y].astype(f32)
    for d in (1, 3):
        dn_moves[d].wait_recv()
        total = total + dn_in[d // 2].astype(f32)
    down_near[...] = total
    kept_back.append(moves.start(down_near, near_hbm))
    aa_rows.wait()
    moves.finish(kept_back)
    copies.finish()


def feed_forward(*arrays):
    rows = pltpu.VMEM((TOK, D), bf16)
    return pl.pallas_call(
        mlp_kernel,
        out_shape=[
            jax.ShapeDtypeStruct((TOK, D), f32),
            jax.ShapeDtypeStruct((TOK, HEADS * HD), bf16),
            jax.ShapeDtypeStruct((1, D), f32),
            jax.ShapeDtypeStruct((D // 4, COLUMNS), bf16),
            jax.ShapeDtypeStruct((TOK, D), f32),
            jax.ShapeDtypeStruct((TOK, D), bf16),
            jax.ShapeDtypeStruct((UNITS, D), bf16),
            jax.ShapeDtypeStruct((4, 4, 2, 48, COLUMNS), bf16),
            jax.ShapeDtypeStruct((4, 2, TOK, D), bf16),
        ],
        in_specs=[VMEM] * 4 + [ANY] * 5,
        out_specs=[ANY] * 9,
        scratch_shapes=[
            pltpu.VMEM((UNITS, D), bf16),
            pltpu.VMEM((4, 2, TOK, D), bf16),
            pltpu.VMEM((4, 2, TOK, D), bf16),
            pltpu.VMEM((4, 2 * TOK, UNITS), f32),
            *[pltpu.VMEM((4, 2 * TOK, UNITS), bf16)] * 3,
            *[pltpu.VMEM((4, 2, TOK, D), bf16)] * 2,
            *[pltpu.VMEM((4, TOK, D), bf16)] * 3,
            pltpu.VMEM((3, TOK, D), bf16),
            rows,
            rows,
            pltpu.VMEM((UNITS, D), bf16),
            pltpu.VMEM((3, UNITS, D // 4), bf16),
            *[pltpu.VMEM((D, COLUMNS), bf16)] * 2,
            pltpu.VMEM((UNITS, D), bf16),
            pltpu.VMEM((4, 4, 2, 48, COLUMNS), bf16),
            pltpu.VMEM((4, TOK, D), bf16),
            pltpu.VMEM((2, TOK, D), bf16),
            pltpu.VMEM((HEADS * HD, D), bf16),
            pltpu.VMEM((TOK, D), f32),
            pltpu.VMEM((TOK, HEADS * HD), bf16),
            pltpu.VMEM((1, D), f32),
            pltpu.VMEM((D // 4, COLUMNS), bf16),
            pltpu.VMEM((TOK, D), f32),
            *sems(48),
            pltpu.SemaphoreType.DMA((14,)),
        ],
        compiler_params=params(2),
    )(*arrays)


def back_kernel(*refs):
    lengths, lse, grad_resid, grads_in, gain, mlp_gain_terms = refs[:6]
    x_hbm, rope_hbm, gate_sum, down_far, q_hbm, kv_hbm, exact_hbm, resid_hbm, near_hbm = refs[6:15]
    al_hbm, w_qkv_hbm, act_hbm, up_terms, wd_terms = refs[15:20]
    results_hbm = refs[20:28]
    (g, stats, acc, acc_in, dkv, r1a, r1b, ta, tb, r2a, r2b, u, r3, w_qkv, act_all, gbt, gbt_all, al_all) = refs[28:46]
    gp, gp_flat, gp_all, part, part_other, small, e1, e2, e3, f1, f2 = refs[46:57]
    up_own, up_in, up_mid, wd_own, wd_across, wd_sum, wd_in, wd_mid, wd_second = refs[57:66]
    gate_second, up_second = refs[66:68]
    summed, third_in = refs[68:71], refs[71:74]
    q_terms, q_first, q_mid, q_second, q_summed, q_third = refs[74:80]
    down_in, down_part, down_other, q, kv, exact, resid, down_near, o_half, o_core, o_sum, o_in, o_mid, o_across, o_fin, o_third, *refs = refs[80:]
    x, rope, in_grad, layer_out, sum_gate, sum_up, sum_down, sum_qkv, sum_out, small_out, *refs = refs
    send_sems, recv_sems, local_sems = refs

    me = here()
    ids, start = token_rows(me, lengths)
    z, y, xh, c, n = (me[a] for a in AXES)
    partner, across, other = at(me, c=1), at(me, xh=1), at(me, n=1)
    ys = {d: at(me, y=d) for d in (1, 2, 3)}
    zs = {d: at(me, z=d) for d in (1, 2, 3)}
    near_moves = [(d, e) for d in (1, 3, 2, 0) for e in (0, 1) if d or e]
    near = {m: at(me, y=m[0], xh=m[1]) for m in near_moves}
    group = {m: at(me, y=m[0], c=m[1]) for m in near_moves}
    def strip(yi, xi):
        return pl.ds(pl.multiple_of(96 * yi + 48 * xi, 48), 48)

    everyone_in = hail([other, *zs.values(), *near.values(), *(group[m] for m in near_moves if m[1])])
    moves, kept_back = Moves(local_sems), []
    load = moves.start

    def keep_result(k, vmem):
        kept_back.append(moves.start(vmem, results_hbm[k]))

    loads = [load(exact_hbm, exact), load(q_hbm, q), load(kv_hbm, kv)]
    load_resid, load_near = load(resid_hbm, resid), load(near_hbm, down_near)
    load_x, load_rope = load(x_hbm, x), load(rope_hbm, rope)
    load_strip = load(gate_sum.at[strip(y, xh)], gate_second.at[y, xh])
    half = TOK // 2
    low, high = pl.ds(0, half), pl.ds(half, half)
    gbt[...] = grad_resid[...].T.astype(bf16).reshape(4, 4, 96, TOK)
    for h in range(HEADS):
        g[c, pl.ds(h * TOK, TOK), :] = grads_in[:, h * HD : (h + 1) * HD]
    loads[0].wait()
    stats[c, 0:1, :] = lse[...]
    stats[c, 1:2, :] = jnp.sum(g[c].astype(f32).T * exact[...], axis=0, keepdims=True)
    stats[c, 2:8, :] = jnp.zeros((6, NQ), f32)
    everyone_in()
    copies = Copies(send_sems, recv_sems)
    shared = [copies.send(g.at[c], g.at[c], partner), copies.send(stats.at[c], stats.at[c], partner)]

    def z_cols(d):
        return pl.ds(pl.multiple_of(step(me, "z", d) * 384, 384), 384)

    second = {}

    def send_second(i, source, in_ref):
        for m in near_moves:
            second[i, m] = copies.send(
                source(step(me, "y", m[0]), step(me, "xh", m[1])), in_ref.at[y, xh], near[m]
            )

    def send_mid(i, total, mid_ref, in_ref):
        turned = total.T.astype(bf16)
        if turned.shape[1] == UNITS:
            turned = whole_tiles(turned)
        for yi in range(4):
            for xi in range(2):
                rows = 96 * yi + 48 * xi
                mid_ref[yi, xi] = turned[rows : rows + 48]
        send_second(i, lambda yi, xi: mid_ref.at[yi, xi], in_ref)
        in_ref[y, xh] = mid_ref[y, xh]

    keep, give = pl.ds(pl.multiple_of(24 * c, 8), 24), pl.ds(pl.multiple_of(24 * (1 - c), 8), 24)
    third = {}
    all_summed = [*summed, q_summed]
    all_second = [gate_second, up_second, None, q_second]
    all_third = [*third_in, q_third]
    outs = (sum_gate, sum_up, sum_down, sum_qkv)

    def collect(i):
        if i == 2:
            for d in (1, 3, 2):
                second[2, d].wait_recv()
            summed[2][...] = wd_second[...].astype(f32)
        else:
            for m in near_moves:
                second[i, m].wait_recv()
            all_summed[i][...] = all_second[i][:, 0].astype(f32) + all_second[i][:, 1].astype(f32)
        third[i] = copies.send(all_summed[i].at[:, give], all_third[i], partner)

    def deliver(i):
        third[i].wait_recv()
        for yi in range(4):
            mine_sum, their_sum = all_summed[i][yi, keep], all_third[i][yi]
            pair = (jnp.where(c == 0, mine_sum, their_sum), jnp.where(c == 0, their_sum, mine_sum))
            for e in range(2):
                k = 2 * yi + e
                width = UNITS if i < 3 else HD
                outs[i][:, pl.ds(k * width, width)] = pair[e][:, :width]

    send_second(0, lambda yi, xi: gate_sum.at[strip(yi, xi)], gate_second)
    gbt_moves = {
        d: copies.send(gbt.at[:, step(me, "y", d)], gbt_all.at[y], ys[d]) for d in (1, 3, 2)
    }
    gbt_all[y] = gbt[:, y]
    down_move = copies.send(down_far, down_in, ys[2])
    first = {}
    for d in (1, 3, 2):
        first[d] = copies.send(up_terms.at[:, z_cols(d)], up_in.at[d - 1], zs[d])
    wd_move = copies.send(wd_terms.at[:, :, 1 - xh], wd_across, across)

    load_al = load(al_hbm, al_all)
    load_w = load(w_qkv_hbm, w_qkv)
    load_act = load(act_hbm, act_all)
    load_up = load(up_terms.at[:, z_cols(0)], up_own)
    load_wd = load(wd_terms.at[:, :, xh], wd_own)

    for copy in shared:
        copy.wait_recv()
    for copy in loads[1:]:
        copy.wait()
    acc[...] = jnp.zeros_like(acc)
    last = shard_of(me) // BLOCK_SHARDS

    def of_both(row):
        return jnp.concatenate([stats[0, row : row + 1, :], stats[1, row : row + 1, :]], axis=1)

    log_total, balance = of_both(0), of_both(1)
    earlier = jnp.where(start < last * KEY_BLOCK, log_total, -big_negative)
    keys_here = 2 * TOK

    def block(index, masked, shift):
        zi, yi = index // 4, lax.rem(index, 4)
        keys = kv[zi, yi, :, :, pl.ds(0, HD)].reshape(keys_here, HD)
        values = kv[zi, yi, :, :, pl.ds(HD, HD)].reshape(keys_here, HD)
        keys_t = keys.T
        dk = jnp.zeros((keys_here, HD), f32)
        dv = jnp.zeros((keys_here, HD), f32)
        for chunk in range(2 * NQ // Q_CHUNK):
            core, cs = divmod(chunk * Q_CHUNK, NQ)
            cs = pl.ds(cs, Q_CHUNK)
            piece = slice(chunk * Q_CHUNK, (chunk + 1) * Q_CHUNK)
            qc, gc = q[core, cs, :], g[core, cs, :]
            probs = jnp.exp2(nt(keys, qc) * SCALE_LOG2 - shift[:, piece])
            if masked:
                place = lax.broadcasted_iota(jnp.int32, (keys_here, Q_CHUNK), 0)
                key_ids = index * KEY_BLOCK + c * TOK + place + place // TOK * TOK
                allowed = (key_ids >= start[:, piece]) & (key_ids <= ids[:, piece])
                probs = jnp.where(allowed, probs, 0.0)
            grads = (probs * (nt(values, gc) - balance[:, piece])).astype(bf16)
            dv = dv + nn(probs.astype(bf16), gc)
            dk = dk + nn(grads, qc)
            acc[core, :, cs] = acc[core, :, cs] + nn(keys_t, grads)
        dkv[zi, yi, :, :, pl.ds(0, HD)] = (dk * SCALE).astype(bf16).reshape(2, TOK, HD)
        dkv[zi, yi, :, :, pl.ds(HD, HD)] = dv.astype(bf16).reshape(2, TOK, HD)

    def segment(zi):
        @pl.loop(0, 4)
        def _(yi):
            index = 4 * zi + yi
            edge = (index == 0) | (index == last)

            @pl.when(edge & (index <= last))
            def _():
                block(index, True, jnp.where(index == last, log_total, earlier))

            @pl.when((index < last) & jnp.logical_not(edge))
            def _():
                block(index, False, earlier)

            @pl.when(index > last)
            def _():
                dkv[zi, yi] = jnp.zeros((2, TOK, 2 * HD), bf16)

    first_a, first_b, second_a, second_b = {}, {}, {}, {}

    def settle(d):
        zi = step(me, "z", d)
        if d:
            first_a[d] = copies.send(dkv.at[zi, :, :, low], r1a.at[d - 1], zs[d])
        for e in (1, 3, 2):
            first_b[d, e] = copies.send(
                dkv.at[zi, step(me, "y", e), :, high], r1b.at[e - 1, zi], ys[e]
            )

    segment(step(me, "z", 1))
    settle(1)
    segment(step(me, "z", 2))
    settle(2)
    segment(step(me, "z", 3))
    settle(3)
    load_al.wait()
    for d in (1, 3, 2):
        gbt_moves[d].wait_recv()
    every_al = al_all[...].reshape(4 * TOK, HEADS * HD)
    for zi in range(4):
        lhs = jnp.concatenate([gbt_all[yi, zi] for yi in range(4)], axis=1)
        terms = nn(lhs, every_al).astype(bf16)
        o_half[0, zi] = terms[:, : HEADS * HD // 2]
        o_half[1, zi] = terms[:, HEADS * HD // 2 :]
    o_move = copies.send(o_half.at[1 - c], o_core, partner)
    segment(z)
    settle(0)
    queries_back = copies.send(acc.at[1 - c], acc_in, partner)
    down_move.wait_recv()
    load_near.wait()
    down_part[...] = (down_near[...] + down_in[...].astype(f32)).astype(bf16)
    down_swap = copies.send(down_part, down_other, other)
    for d in (1, 3, 2):
        first_a[d].wait_recv()
    ta[...] = (dkv[z, :, :, low].astype(f32) + three(r1a)).astype(bf16)
    for d in (1, 3, 2):
        second_a[d] = copies.send(ta.at[step(me, "y", d)], r2a.at[d - 1], ys[d])
    for copy in first_b.values():
        copy.wait_recv()
    tb[...] = (dkv[:, y, :, high].astype(f32) + three(r1b)).astype(bf16)
    for d in (1, 3, 2):
        second_b[d] = copies.send(tb.at[step(me, "z", d)], r2b.at[d - 1], zs[d])
    for d in (1, 3, 2):
        second_a[d].wait_recv()
        second_b[d].wait_recv()
    ua = ta[y].astype(f32) + three(r2a)
    ub = tb[z].astype(f32) + three(r2b)
    u[:, low] = ua.astype(bf16)
    u[:, high] = ub.astype(bf16)
    kv_last = copies.send(u.at[1 - xh], r3, across)
    load_wd.wait()
    wd_move.wait_recv()
    for zi in range(4):
        wd_sum[zi] = (wd_own[zi].astype(f32) + wd_across[zi].astype(f32)).astype(bf16)
    wd_first = {d: copies.send(wd_sum.at[step(me, "z", d)], wd_in.at[d - 1], zs[d]) for d in (1, 3, 2)}
    o_move.wait_recv()
    o_sum[...] = (o_half[c].astype(f32) + o_core[...].astype(f32)).astype(bf16)
    queries_back.wait_recv()
    load_rope.wait()
    load_x.wait()
    turned_back = ((acc[c] + acc_in[...]) * SCALE).T

    def revert(rows):
        return rows * rope[0] - pltpu.roll(rows, HD // 2, 1) * rope[1]

    def keep_head(h, rows):
        low_rows = rows.astype(bf16)
        gp[h] = low_rows
        gp_flat[:, pl.ds(h * HD, HD)] = low_rows
        small[pl.ds(24 + h, 1), :] = jnp.sum(low_rows.astype(f32), axis=0, keepdims=True)

    def to_small(first_row, row):
        for k in range(D // 128):
            small[pl.ds(first_row + k, 1), :] = row[:, k * 128 : (k + 1) * 128]

    small[...] = jnp.zeros_like(small)
    to_small(12, mlp_gain_terms[...])
    for h in range(HEADS):
        keep_head(h, revert(turned_back[h * TOK : (h + 1) * TOK]))
    load_w.wait()
    front = HEADS * HD
    partial = nt(gp_flat[:, pl.ds(0, front)], w_qkv[:, pl.ds(0, front)])

    kv_last.wait_recv()
    grad_kv = u[xh].astype(f32) + r3[...].astype(f32)
    keep_head(HEADS, revert(grad_kv[:, :HD]))
    keep_head(HEADS + 1, grad_kv[:, HD:])
    gp_moves = [
        copies.send(gp.at[step(me, "y", m[0]) * 2 + step(me, "c", m[1])], gp_all.at[y, c], group[m])
        for m in near_moves
    ]
    gp_all[y, c] = gp[y * 2 + c]
    back = pl.ds(front, 2 * HD)
    part[...] = (partial + nt(gp_flat[:, back], w_qkv[:, back])).astype(bf16)
    swap = copies.send(part, part_other, other)
    load_up.wait()
    for d in (1, 3, 2):
        first[d].wait_recv()
    send_mid(1, up_own[...].astype(f32) + three(up_in), up_mid, up_second)
    load_strip.wait()
    collect(0)
    load_act.wait()
    for copy in gp_moves:
        copy.wait_recv()
    q_terms[...] = tn(
        gp_all[...].reshape(GROUP * TOK, HD), act_all[...].reshape(GROUP * TOK, D)
    ).astype(bf16)

    q_one = {d: copies.send(q_terms.at[:, z_cols(d)], q_first.at[d - 1], zs[d]) for d in (1, 3, 2)}
    o_first = {d: copies.send(o_sum.at[step(me, "z", d)], o_in.at[d - 1], zs[d]) for d in (1, 3, 2)}
    down_swap.wait_recv()
    load_resid.wait()
    layer_out[...] = (
        resid[...] + (down_part[...].astype(f32) + down_other[...].astype(f32))
    ).astype(bf16)
    keep_result(1, layer_out)
    swap.wait_recv()
    grad_act = part[...].astype(f32) + part_other[...].astype(f32)
    rows = x[...].astype(f32)
    inverse = lax.rsqrt(jnp.mean(rows * rows, axis=-1, keepdims=True) + rms_eps)
    normed = rows * inverse
    to_small(0, jnp.sum(grad_act * normed, axis=0, keepdims=True))
    small_one = {d: copies.send(small, e1.at[d - 1], zs[d]) for d in (1, 3, 2)}
    grad_normed = grad_act * gain[...].reshape(1, D)
    inner = jnp.mean(grad_normed * normed, axis=-1, keepdims=True)
    in_grad[...] = (grad_resid[...] + inverse * (grad_normed - normed * inner)).astype(bf16)

    keep_result(0, in_grad)
    for d in (1, 3, 2):
        wd_first[d].wait_recv()
    wd_mid[...] = (wd_sum[z].astype(f32) + three(wd_in)).astype(bf16)
    for d in (1, 3, 2):
        second[2, d] = copies.send(wd_mid.at[step(me, "y", d)], wd_second.at[y], ys[d])
    wd_second[y] = wd_mid[y]
    for d in (1, 3, 2):
        q_one[d].wait_recv()
    send_mid(3, q_terms[:, z_cols(0)].astype(f32) + three(q_first), q_mid, q_second)
    for d in (1, 3, 2):
        o_first[d].wait_recv()
    o_total = (o_sum[z].astype(f32) + three(o_in)).astype(bf16)
    o_mid[0], o_mid[1] = o_total[:48], o_total[48:]
    o_last = copies.send(o_mid.at[1 - xh], o_across, across)
    for d in (1, 3, 2):
        small_one[d].wait_recv()
    f1[...] = small[...] + three(e1)
    small_two = {m: copies.send(f1, e2.at[k], near[m]) for k, m in enumerate(near_moves)}
    o_last.wait_recv()
    o_fin[...] = o_mid[xh].astype(f32) + o_across[...].astype(f32)
    o_end = copies.send(o_fin.at[give], o_third, partner)
    collect(1)
    deliver(0)
    keep_result(2, sum_gate)
    deliver(1)
    keep_result(3, sum_up)
    collect(2)
    collect(3)
    for m in near_moves:
        small_two[m].wait_recv()
    f2[...] = f1[...]
    for k in range(len(near_moves)):
        f2[...] = f2[...] + e2[k]
    small_three = copies.send(f2, e3, partner)
    deliver(2)
    keep_result(4, sum_down)
    deliver(3)
    keep_result(5, sum_qkv)
    o_end.wait_recv()
    o_mine, o_theirs = o_fin[keep], o_third[...]
    sum_out[:, : HEADS * HD // 2] = jnp.where(c == 0, o_mine, o_theirs)
    sum_out[:, HEADS * HD // 2 :] = jnp.where(c == 0, o_theirs, o_mine)
    keep_result(6, sum_out)
    small_three.wait_recv()
    small_out[...] = f2[...] + e3[...]
    keep_result(7, small_out)
    moves.finish(kept_back)
    copies.finish()


def back(*arrays):
    half = TOK // 2
    wide = 2 * HD
    results_of = [
        jax.ShapeDtypeStruct((TOK, D), bf16),
        jax.ShapeDtypeStruct((TOK, D), bf16),
        *[jax.ShapeDtypeStruct((24, FF // 2), f32)] * 3,
        jax.ShapeDtypeStruct((24, (HEADS + 2) * HD), f32),
        jax.ShapeDtypeStruct((24, HEADS * HD), f32),
        jax.ShapeDtypeStruct((40, 128), f32),
    ]
    return pl.pallas_call(
        back_kernel,
        out_shape=results_of,
        in_specs=[SMEM] + [VMEM] * 5 + [ANY] * 14,
        out_specs=[ANY] * 8,
        scratch_shapes=[
            pltpu.VMEM((2, NQ, HD), bf16),
            pltpu.VMEM((2, 8, NQ), f32),
            pltpu.VMEM((2, HD, NQ), f32),
            pltpu.VMEM((HD, NQ), f32),
            pltpu.VMEM((4, 4, 2, TOK, wide), bf16),
            pltpu.VMEM((3, 4, 2, half, wide), bf16),
            pltpu.VMEM((3, 4, 2, half, wide), bf16),
            pltpu.VMEM((4, 2, half, wide), bf16),
            pltpu.VMEM((4, 2, half, wide), bf16),
            pltpu.VMEM((3, 2, half, wide), bf16),
            pltpu.VMEM((3, 2, half, wide), bf16),
            pltpu.VMEM((2, TOK, wide), bf16),
            pltpu.VMEM((TOK, wide), bf16),
            pltpu.VMEM((D, (HEADS + 2) * HD), bf16),
            pltpu.VMEM((4, 2, TOK, D), bf16),
            pltpu.VMEM((4, 4, 96, TOK), bf16),
            pltpu.VMEM((4, 4, 96, TOK), bf16),
            pltpu.VMEM((4, TOK, HEADS * HD), bf16),
            pltpu.VMEM((HEADS + 2, TOK, HD), bf16),
            pltpu.VMEM((TOK, (HEADS + 2) * HD), bf16),
            pltpu.VMEM((4, 2, TOK, HD), bf16),
            pltpu.VMEM((TOK, D), bf16),
            pltpu.VMEM((TOK, D), bf16),
            pltpu.VMEM((40, 128), f32),
            pltpu.VMEM((3, 40, 128), f32),
            pltpu.VMEM((7, 40, 128), f32),
            pltpu.VMEM((40, 128), f32),
            pltpu.VMEM((40, 128), f32),
            pltpu.VMEM((40, 128), f32),
            pltpu.VMEM((UNITS, 384), bf16),
            pltpu.VMEM((3, UNITS, 384), bf16),
            pltpu.VMEM((4, 2, 48, COLUMNS), bf16),
            *[pltpu.VMEM((4, 4, 48, COLUMNS), bf16)] * 3,
            pltpu.VMEM((3, 4, 48, COLUMNS), bf16),
            *[pltpu.VMEM((4, 48, COLUMNS), bf16)] * 2,
            *[pltpu.VMEM((4, 2, 48, COLUMNS), bf16)] * 2,
            *[pltpu.VMEM((4, 48, COLUMNS), f32)] * 3,
            *[pltpu.VMEM((4, 24, COLUMNS), f32)] * 3,
            pltpu.VMEM((HD, D), bf16),
            pltpu.VMEM((3, HD, 384), bf16),
            pltpu.VMEM((4, 2, 48, HD), bf16),
            pltpu.VMEM((4, 2, 48, HD), bf16),
            pltpu.VMEM((4, 48, HD), f32),
            pltpu.VMEM((4, 24, HD), f32),
            pltpu.VMEM((TOK, D), bf16),
            pltpu.VMEM((TOK, D), bf16),
            pltpu.VMEM((TOK, D), bf16),
            pltpu.VMEM((2, NQ, HD), bf16),
            pltpu.VMEM((4, 4, 2, TOK, wide), bf16),
            pltpu.VMEM((HD, NQ), f32),
            pltpu.VMEM((TOK, D), f32),
            pltpu.VMEM((TOK, D), f32),
            pltpu.VMEM((2, 4, 96, HEADS * HD // 2), bf16),
            *[pltpu.VMEM((4, 96, HEADS * HD // 2), bf16)] * 2,
            pltpu.VMEM((3, 96, HEADS * HD // 2), bf16),
            pltpu.VMEM((2, 48, HEADS * HD // 2), bf16),
            pltpu.VMEM((48, HEADS * HD // 2), bf16),
            pltpu.VMEM((48, HEADS * HD // 2), f32),
            pltpu.VMEM((24, HEADS * HD // 2), f32),
            pltpu.VMEM((TOK, D), bf16),
            pltpu.VMEM((2, TOK, HD), f32),
            *[pltpu.VMEM(a.shape, a.dtype) for a in results_of],
            *sems(93),
            pltpu.SemaphoreType.DMA((21,)),
        ],
        compiler_params=params(9, 62),
    )(*arrays)


def results_kernel(*refs):
    wholes, small, copied = refs[:7], refs[7], refs[8:15]
    small_outs, (norm_attn, norm_mlp, bias, value_bias) = refs[15:19], refs[19:23]
    *held, into, out_of = refs[23:]
    shard = shard_of(here())
    loads, stores = Moves(into), Moves(out_of)
    for a, b in zip(wholes, held):
        loads.start(a, b)
    rows = jnp.concatenate(
        [
            jnp.concatenate([small[12 * i + k : 12 * i + k + 1, :] for k in range(12)], axis=1)
            for i in range(2)
        ],
        axis=0,
    )
    turned = pltpu.roll(rows, lax.rem(D - 24 * shard, D), 1)
    norm_attn[...] = turned[0:1, :24]
    norm_mlp[...] = turned[1:2, :24]
    heads = pltpu.roll(small[24 : 24 + HEADS + 2, :], lax.rem(HD - 2 * shard, HD), 1)
    bias[0] = heads[: HEADS + 1, :2].T
    value_bias[...] = heads[HEADS + 1 :, :2]
    for a, b in zip(refs[19:23], small_outs):
        stores.start(a, b)
    for load, a, b in zip(loads.started, held, copied):
        load.wait()
        stores.start(a, b)
    stores.finish(stores.started)


def results(*arrays):
    *wholes, small = arrays
    small_ones = [
        jax.ShapeDtypeStruct((1, 24), f32),
        jax.ShapeDtypeStruct((1, 24), f32),
        jax.ShapeDtypeStruct((1, 2, HEADS + 1), f32),
        jax.ShapeDtypeStruct((1, 2), f32),
    ]
    return pl.pallas_call(
        results_kernel,
        out_shape=[*[jax.ShapeDtypeStruct(a.shape, a.dtype) for a in wholes], *small_ones],
        in_specs=[ANY] * 7 + [VMEM],
        out_specs=[ANY] * 11,
        scratch_shapes=[
            *[pltpu.VMEM(a.shape, a.dtype) for a in (*small_ones, *wholes)],
            pltpu.SemaphoreType.DMA((7,)),
            pltpu.SemaphoreType.DMA((11,)),
        ],
    )(*wholes, small)


def shards(
    layer_in, lengths, norm_attn, w_qkv, qkv_bias, w_out, norm_mlp, w_gate, w_up, w_down, out_grad
):
    half = HD // 2
    freqs = np.float32(rope_base) ** (-2.0 * np.arange(half, dtype=np.float32) / HD)
    freqs = np.concatenate([freqs, freqs]).astype(np.float32)[None]
    kv, queries, act_attn, resid, exact, lse, rope, gate_w, up_w, out_grad_all, low_all = attend(
        lengths, layer_in, norm_attn, qkv_bias, freqs, out_grad, w_qkv, w_out, w_gate, w_up
    )
    (
        grad_resid, grads, gain_terms, gate_sum, down_near, down_far,
        up_terms, down_terms, act_attn_all,
    ) = feed_forward(
        resid, norm_mlp, out_grad, act_attn, w_out, out_grad_all, gate_w, up_w, w_down
    )
    sums = back(
        lengths, lse, grad_resid, grads, norm_attn, gain_terms, layer_in, rope, gate_sum, down_far,
        queries, kv, exact, resid, down_near, low_all, w_qkv, act_attn_all, up_terms, down_terms,
    )
    in_grad, layer_out, sum_gate, sum_up, sum_down, sum_qkv, sum_out, *rest = results(*sums)
    sum_norm_attn, sum_norm_mlp, bias, value_bias = rest
    return (
        layer_out,
        in_grad,
        sum_norm_attn[0],
        sum_qkv,
        bias.swapaxes(1, 2),
        value_bias,
        sum_out.T,
        sum_norm_mlp[0],
        sum_gate,
        sum_up,
        sum_down.T,
    )


def solution(mesh):
    torus = Mesh(mesh.devices.reshape(4, 4, 2, 2, 2), AXES)
    in_specs = (
        P(WIDE, None),
        P(),
        P(),
        P(None, "n"),
        P("n", None),
        P("n", None),
        P(),
        P(None, "n"),
        P(None, "n"),
        P("n", None),
        P(WIDE, None),
    )
    out_specs = (
        P(WIDE, None),
        P(WIDE, None),
        P(WIDE),
        P(WIDE, "n"),
        P("n", None, WIDE),
        P("n", WIDE),
        P("n", WIDE),
        P(WIDE),
        P(WIDE, "n"),
        P(WIDE, "n"),
        P("n", WIDE),
    )
    return jax.shard_map(
        shards, mesh=torus, in_specs=in_specs, out_specs=out_specs, check_vma=False
    )
```

```python
import functools
import math

import jax
import jax.numpy as jnp
import numpy as np
from jax import lax
from jax.experimental import pallas as pl
from jax.experimental.pallas import tpu as pltpu
from jax.sharding import Mesh
from jax.sharding import PartitionSpec as P

HD = 128
QH = 12
KVH = 2
HEADS = QH // KVH
D = 1536
FF = 8960
TOK = 128
TOKENS = 8192
SEQS = 4
NQ = HEADS * TOK
GROUP = 8
UNITS = FF // 2 // GROUP
WINDOW = 768
COLUMNS = 640

AXES = ("z", "y", "xh", "c", "n")
SIZE = {"z": 4, "y": 4, "xh": 2, "c": 2, "n": 2}
WIDE = ("z", "y", "xh", "c")
MESH = pl.DeviceIdType.MESH

rms_eps = 1e-06
rope_base = 10000.0
big_negative = -1e30
SCALE = HD ** (-0.5)
SCALE_LOG2 = SCALE * math.log2(math.e)
KEY_BLOCK = 512
BLOCK_SHARDS = KEY_BLOCK // TOK
Q_CHUNK = 256

bf16 = jnp.bfloat16
f32 = jnp.float32
VMEM = pl.BlockSpec(memory_space=pltpu.VMEM)
SMEM = pl.BlockSpec(memory_space=pltpu.SMEM)
ANY = pl.BlockSpec(memory_space=pl.ANY)


def nn(a, b):
    return lax.dot_general(a, b, (((1,), (0,)), ((), ())), preferred_element_type=f32)


def nt(a, b):
    return lax.dot_general(a, b, (((1,), (1,)), ((), ())), preferred_element_type=f32)


def tn(a, b):
    return lax.dot_general(a, b, (((0,), (0,)), ((), ())), preferred_element_type=f32)


def here():
    return {a: lax.axis_index(a) for a in AXES}


def step(me, axis, by):
    return lax.rem(me[axis] + by, SIZE[axis])


def at(me, **moved):
    return tuple(step(me, a, moved[a]) if a in moved else me[a] for a in AXES)


def sequence_starts(ids, lengths):
    starts, end = jnp.zeros_like(ids), 0
    for s in range(SEQS):
        end = end + lengths[s]
        starts = starts + jnp.where(ids >= end, lengths[s], 0)
    return starts


def token_rows(me, lengths):
    column = lax.broadcasted_iota(jnp.int32, (1, 2 * NQ), 1)
    ids = shard_of(me) // 2 * (2 * TOK) + column // NQ * TOK + column % TOK
    return ids, sequence_starts(ids, lengths)


def hail(peers):
    barrier = pltpu.get_barrier_semaphore()
    for p in peers:
        pl.semaphore_signal(barrier, inc=1, device_id=p, device_id_type=MESH)
    return lambda: pl.semaphore_wait(barrier, len(peers))


def greet(peers):
    hail(peers)()


class Copies:
    def __init__(self, send_sems, recv_sems):
        self.send_sems, self.recv_sems, self.used, self.started = send_sems, recv_sems, 0, []

    def make(self, src, dst, target):
        self.used += 1
        return self.numbered(self.used - 1, src, dst, target)

    def numbered(self, k, src, dst, target):
        return pltpu.make_async_remote_copy(
            src_ref=src,
            dst_ref=dst,
            send_sem=self.send_sems.at[k],
            recv_sem=self.recv_sems.at[k],
            device_id=target,
            device_id_type=MESH,
        )

    def send(self, src, dst, target):
        copy = self.make(src, dst, target)
        copy.start()
        self.started.append(copy)
        return copy

    def finish(self):
        for copy in self.started:
            copy.wait_send()


class Moves:
    def __init__(self, move_sems):
        self.move_sems, self.started = move_sems, []

    def start(self, src, dst):
        copy = pltpu.make_async_copy(src, dst, self.move_sems.at[len(self.started)])
        copy.start()
        self.started.append(copy)
        return copy

    def finish(self, copies):
        for copy in copies:
            copy.wait()


def sems(count):
    return [pltpu.SemaphoreType.DMA((count,)), pltpu.SemaphoreType.DMA((count,))]


def params(ident, mib=60):
    return pltpu.CompilerParams(
        collective_id=ident, has_side_effects=True, vmem_limit_bytes=mib * 2**20
    )


def whole_tiles(values):
    pad = jnp.zeros((values.shape[0], COLUMNS - values.shape[1]), values.dtype)
    return jnp.concatenate([values, pad], axis=1)


def three(ref):
    return ref[0].astype(f32) + ref[1].astype(f32) + ref[2].astype(f32)


def shard_of(me):
    return ((me["z"] * 4 + me["y"]) * 2 + me["xh"]) * 2 + me["c"]


class Rows:
    def __init__(self, me, copies, source, slots):
        self.me, self.copies, self.source, self.slots = me, copies, source, slots
        half = TOK // 2
        n = me["n"]
        self.mine = pl.ds(pl.multiple_of(half * n, half), half)
        self.theirs = pl.ds(pl.multiple_of(half * (1 - n), half), half)
        self.own = slots.at[me["y"], me["c"]]
        self.near, self.far, self.across = [], {}, {}

    def pair(self):
        self.near.append(self.copies.send(self.source, self.own, at(self.me, c=1)))

    def slot(self, d, rows):
        return self.slots.at[lax.rem(self.me["y"] + (4 - d), 4), self.me["c"], rows]

    def start(self, *steps):
        for d in steps:
            self.far[d] = self.copies.send(
                self.source.at[self.mine], self.own.at[self.mine], at(self.me, y=d)
            )

    def pass_on(self, *steps):
        for d in steps:
            self.far[d].wait_recv()
            got = self.slot(d, self.mine)
            self.across[d] = self.copies.send(got, got, at(self.me, n=1))
            self.near.append(self.copies.send(got, got, at(self.me, c=1)))

    def complete(self, *steps):
        for d in steps:
            self.across[d].wait_recv()
            got = self.slot(d, self.theirs)
            self.near.append(self.copies.send(got, got, at(self.me, c=1)))

    def wait(self):
        for copy in self.near:
            copy.wait_recv()


def attend_kernel(
    lengths, x, gain, bias, freqs, og, w_qkv_hbm, w_out_hbm, w_gate_hbm, w_up_hbm,
    kv_hbm, q_hbm, aa_part, resid_hbm, exact_hbm, lse_hbm, rope_hbm, gate_hbm, up_hbm, og_all, al_all,
    stats, acc, low_acc, stats_in, acc_in, low_in, w_qkv, w_out, o, pa, pb,
    kv, q, act, resid, exact, lse, rope, gate_w, up_w, wide_gate, wide_up, send_sems, recv_sems, local_sems,
):
    me = here()
    moves, kept_back = Moves(local_sems), []
    load_w = moves.start(w_qkv_hbm, w_qkv)
    ids, start = token_rows(me, lengths)
    z, y, xh, c = me["z"], me["y"], me["xh"], me["c"]
    partner, across, other = at(me, c=1), at(me, xh=1), at(me, n=1)
    ys = {d: at(me, y=d) for d in (1, 2, 3)}
    zs = {d: at(me, z=d) for d in (1, 2, 3)}
    everyone_in = hail([partner, across, other, *ys.values(), *zs.values()])
    rows = x[...].astype(f32)
    inverse = lax.rsqrt(jnp.mean(rows * rows, axis=-1, keepdims=True) + rms_eps)
    act[...] = (rows * inverse * gain[...].reshape(1, D)).astype(bf16)
    token = shard_of(me) * TOK + lax.broadcasted_iota(jnp.int32, (TOK, 1), 0)
    angles = (token - sequence_starts(token, lengths)).astype(f32) * freqs[...]
    cosine = jnp.cos(angles)
    turned = jnp.sin(angles)
    first_half = lax.broadcasted_iota(jnp.int32, (TOK, HD), 1) < HD // 2
    sine = jnp.where(first_half, -turned, turned)
    rope[0], rope[1] = cosine, sine
    kept_back.append(moves.start(rope, rope_hbm))
    front = HEADS * HD

    def turn(values):
        return values * cosine + pltpu.roll(values, HD // 2, 1) * sine

    load_w.wait()
    back = nn(act[...], w_qkv[:, front:]) + bias[:, front:]
    mine = kv.at[z, y, xh]
    mine[:, pl.ds(0, HD)] = turn(back[:, :HD]).astype(bf16)
    mine[:, pl.ds(HD, HD)] = back[:, HD:].astype(bf16)
    everyone_in()
    kept_back.append(moves.start(act, aa_part.at[y]))
    load_out = moves.start(w_out_hbm, w_out)
    copies = Copies(send_sems, recv_sems)
    rows_of_og = Rows(me, copies, og, og_all)
    rows_of_og.start(1, 3)
    first = copies.send(mine, mine, across)
    ahead = nn(act[...], w_qkv[:, :front]) + bias[:, :front]
    for h in range(HEADS):
        head = turn(ahead[:, h * HD : (h + 1) * HD]).astype(bf16)
        q[c, pl.ds(h * TOK, TOK), :] = head
    share_q = copies.send(q.at[c], q.at[c], partner)
    rows_of_og.pair()
    kept_back.append(moves.start(og, og_all.at[y, c]))
    stats[:, 0:1, :] = jnp.full((2, 1, NQ), big_negative, f32)
    stats[:, 1:8, :] = jnp.zeros((2, 7, NQ), f32)
    acc[...] = jnp.zeros_like(acc)
    low_acc[...] = jnp.zeros_like(low_acc)
    last = shard_of(me) // BLOCK_SHARDS
    kept = start < last * KEY_BLOCK
    half = TOK // 2
    keys_here = 2 * half

    early = sequence_starts(last * KEY_BLOCK - 1, lengths)

    def take(parts, masked=False, from_first=False):
        def both(columns):
            return jnp.concatenate(
                [
                    kv[zi, yi, :, pl.ds(pl.multiple_of(half * k, half), half), columns].reshape(
                        keys_here, HD
                    )
                    for zi, yi, k in parts
                ],
                axis=0,
            )

        def key_ids(columns):
            place = lax.broadcasted_iota(jnp.int32, (keys_here, columns), 0)
            place = place + place // half * (2 * TOK - half)
            return jnp.concatenate(
                [(4 * zi + yi) * KEY_BLOCK + c * TOK + half * k + place for zi, yi, k in parts], axis=0
            )

        keys, values = both(pl.ds(0, HD)), both(pl.ds(HD, HD)).T
        if from_first:
            barred = jnp.where(key_ids(1) >= early, 0.0, big_negative)
        for chunk in range(2 * NQ // Q_CHUNK):
            core, cs = divmod(chunk * Q_CHUNK, NQ)
            cs = pl.ds(cs, Q_CHUNK)
            here_cols = slice(chunk * Q_CHUNK, (chunk + 1) * Q_CHUNK)
            scores = nt(keys, q[core, cs, :]) * SCALE_LOG2
            if masked:
                which = key_ids(Q_CHUNK)
                allowed = (which >= start[:, here_cols]) & (which <= ids[:, here_cols])
                scores = jnp.where(allowed, scores, big_negative)
            if from_first:
                scores = scores + barred
            old = stats[core, 0:1, cs]
            new = jnp.maximum(old, jnp.max(scores, axis=0, keepdims=True))
            if masked:
                probs = jnp.where(allowed, jnp.exp2(scores - new), 0.0)
            else:
                taken = kept[:, here_cols]
                new = jnp.where(taken, new, old)
                probs = jnp.exp2(scores - jnp.where(taken, new, -big_negative))
            fade = jnp.exp2(old - new)
            stats[core, 0:1, cs] = new
            stats[core, 1:2, cs] = stats[core, 1:2, cs] * fade + jnp.sum(probs, axis=0, keepdims=True)
            upper = probs.astype(bf16)
            rest = (probs - upper.astype(f32)).astype(bf16)
            acc[core, :, cs] = acc[core, :, cs] * fade + nn(values, upper)
            low_acc[core, :, cs] = low_acc[core, :, cs] * fade + nn(values, rest)

    def pair(za, ya, zb, yb):
        a, b = 4 * za + ya, 4 * zb + yb
        spots = [(za, ya, 0), (zb, yb, 1)]
        before_last = jnp.maximum(a, b) < last
        has_first = jnp.minimum(a, b) == 0

        @pl.when(before_last & jnp.logical_not(has_first))
        def _():
            take(spots)

        @pl.when(before_last & has_first)
        def _():
            take(spots, from_first=True)

        @pl.when(jnp.logical_not(before_last))
        def _():
            @pl.loop(0, 2)
            def _(k):
                zi, yi = jnp.where(k == 0, za, zb), jnp.where(k == 0, ya, yb)
                index = 4 * zi + yi
                edge = (index == 0) | (index == last)

                @pl.when(edge & (index <= last))
                def _():
                    take([(zi, yi, k)], masked=True)

                @pl.when((index < last) & jnp.logical_not(edge))
                def _():
                    take([(zi, yi, k)])

    def two_pairs(one, two):
        spots = [(*one[:2], 0), (*one[2:], 1), (*two[:2], 0), (*two[2:], 1)]
        index = [4 * zi + yi for zi, yi, _ in spots]
        least = jnp.minimum(jnp.minimum(index[0], index[1]), jnp.minimum(index[2], index[3]))
        most = jnp.maximum(jnp.maximum(index[0], index[1]), jnp.maximum(index[2], index[3]))
        @pl.when((most < last) & (least > 0))
        def _():
            take(spots)

        @pl.when((most < last) & (least == 0))
        def _():
            take(spots, from_first=True)

        @pl.when(most >= last)
        def _():
            @pl.loop(0, 2)
            def _(i):
                pair(*(jnp.where(i == 0, a, b) for a, b in zip(one, two)))

    first.wait_recv()
    low, high = pl.ds(0, half), pl.ds(half, half)

    def slot(zi, yi, rows):
        return kv.at[zi, yi, :, rows]

    def before(axis, d):
        return lax.rem(me[axis] + (4 - d), 4)

    first_low, first_high = {}, {}
    for d in (1, 3, 2):
        first_low[d] = copies.send(slot(z, y, low), slot(z, y, low), ys[d])
        first_high[d] = copies.send(slot(z, y, high), slot(z, y, high), zs[d])
    share_q.wait_recv()

    kept_back.append(moves.start(q, q_hbm))
    first_unit = (y * 2 + c) * UNITS
    tile = jnp.minimum(first_unit // 128, FF // 2 // 128 - WINDOW // 128)
    window = pl.ds(pl.multiple_of(tile * 128, 128), WINDOW)
    load_gate = moves.start(w_gate_hbm.at[:, window], wide_gate)
    load_up = moves.start(w_up_hbm.at[:, window], wide_up)
    take([(z, y, 0), (z, y, 1)], masked=True)
    second_from = copies.used
    copies.used += 24
    for i, e in enumerate((0, 1, 3, 2)):
        yi, zi = before("y", e), before("z", e)
        if e:
            first_low[e].wait_recv()
            first_high[e].wait_recv()
        for j, d in enumerate((1, 3, 2)):
            k = second_from + 2 * (3 * i + j)
            for copy in (
                copies.numbered(k, slot(z, yi, low), slot(z, yi, low), zs[d]),
                copies.numbered(k + 1, slot(zi, y, high), slot(zi, y, high), ys[d]),
            ):
                copy.start()
                copies.started.append(copy)
    rows_of_og.start(2)
    rows_of_og.pass_on(1, 3)

    @pl.loop(1, 4)
    def _(e):
        pair(z, before("y", e), before("z", e), y)

    def places(k):
        i, j = k // 3, lax.rem(k, 3)
        e = jnp.where(i < 2, i, 5 - i)
        d = jnp.where(j < 2, 1 + 2 * j, 2)
        return before("z", d), before("y", e), before("z", e), before("y", d)

    def arrive(k):
        za, ya, zb, yb = places(k)
        one, two = slot(za, ya, low), slot(zb, yb, high)
        copies.numbered(second_from + 2 * k, one, one, zs[1]).wait_recv()
        copies.numbered(second_from + 2 * k + 1, two, two, ys[1]).wait_recv()

    def two_arrive(i):
        arrive(2 * i)
        arrive(2 * i + 1)
        two_pairs(places(2 * i), places(2 * i + 1))

    pl.loop(0, 4)(two_arrive)
    rows_of_og.pass_on(2)
    mine = rows_of_og.mine
    aa_far = [copies.send(act.at[mine], aa_part.at[y, mine], ys[d]) for d in (1, 3, 2)]
    pl.loop(4, 6)(two_arrive)
    kept_back.append(moves.start(kv, kv_hbm))
    merge = [
        copies.send(stats.at[1 - c], stats_in, partner),
        copies.send(acc.at[1 - c], acc_in, partner),
        copies.send(low_acc.at[1 - c], low_in, partner),
    ]
    rows_of_og.complete(1, 3, 2)
    for copy in merge:
        copy.wait_recv()
    own_top, in_top = stats[c, 0:1, :], stats_in[0:1, :]
    top = jnp.maximum(own_top, in_top)
    own_part, in_part = jnp.exp2(own_top - top), jnp.exp2(in_top - top)
    total = stats[c, 1:2, :] * own_part + stats_in[1:2, :] * in_part
    inverse = 1.0 / total
    own_part, in_part = own_part * inverse, in_part * inverse
    rows = acc[c] * own_part + acc_in[...] * in_part
    exact[...] = rows + (low_acc[c] * own_part + low_in[...] * in_part)
    rows = rows.T.astype(bf16)
    for h in range(HEADS):
        o[:, pl.ds(h * HD, HD)] = rows[h * TOK : (h + 1) * TOK]
    load_out.wait()
    pa[...] = nn(o[...], w_out[...]).astype(bf16)
    swap = copies.send(pa, pb, other)
    own_al = al_all.at[y]
    al_moves = {d: copies.send(o, own_al, ys[d]) for d in (1, 3, 2)}
    kept_back.append(moves.start(o, own_al))
    lse[...] = top + jnp.log2(total)
    kept_back.append(moves.start(lse, lse_hbm))
    kept_back.append(moves.start(exact, exact_hbm))
    shift = lax.rem(WINDOW - (first_unit - tile * 128), WINDOW)
    for load, part, weights, whole in (
        (load_gate, wide_gate, gate_w, gate_hbm),
        (load_up, wide_up, up_w, up_hbm),
    ):
        load.wait()

        @pl.loop(0, D // 128)
        def _(index, part=part, weights=weights):
            rows = pl.ds(pl.multiple_of(index * 128, 128), 128)
            rolled = pltpu.roll(part[rows, :].astype(f32), shift, 1)
            weights[rows, :] = rolled[:, :COLUMNS].astype(bf16)

        kept_back.append(moves.start(weights, whole))
    rows_of_og.wait()
    swap.wait_recv()
    resid[...] = x[...].astype(f32) + (pa[...].astype(f32) + pb[...].astype(f32))
    kept_back.append(moves.start(resid, resid_hbm))
    for copy in (*aa_far, *al_moves.values()):
        copy.wait_recv()
    moves.finish(kept_back)
    copies.finish()


def attend(*arrays):
    state = [
        jax.ShapeDtypeStruct((4, 4, 2, TOK, 2 * HD), bf16),
        jax.ShapeDtypeStruct((2, NQ, HD), bf16),
        jax.ShapeDtypeStruct((TOK, D), bf16),
        jax.ShapeDtypeStruct((TOK, D), f32),
        jax.ShapeDtypeStruct((HD, NQ), f32),
        jax.ShapeDtypeStruct((1, NQ), f32),
        jax.ShapeDtypeStruct((2, TOK, HD), f32),
        jax.ShapeDtypeStruct((D, COLUMNS), bf16),
        jax.ShapeDtypeStruct((D, COLUMNS), bf16),
    ]
    return pl.pallas_call(
        attend_kernel,
        out_shape=[
            *state[:2],
            jax.ShapeDtypeStruct((4, TOK, D), bf16),
            *state[3:],
            jax.ShapeDtypeStruct((4, 2, TOK, D), bf16),
            jax.ShapeDtypeStruct((4, TOK, HEADS * HD), bf16),
        ],
        in_specs=[SMEM] + [VMEM] * 5 + [ANY] * 4,
        out_specs=[ANY] * 11,
        scratch_shapes=[
            pltpu.VMEM((2, 8, NQ), f32),
            pltpu.VMEM((2, HD, NQ), f32),
            pltpu.VMEM((2, HD, NQ), f32),
            pltpu.VMEM((8, NQ), f32),
            pltpu.VMEM((HD, NQ), f32),
            pltpu.VMEM((HD, NQ), f32),
            pltpu.VMEM((D, (HEADS + 2) * HD), bf16),
            pltpu.VMEM((HEADS * HD, D), bf16),
            pltpu.VMEM((TOK, HEADS * HD), bf16),
            *[pltpu.VMEM((TOK, D), bf16)] * 2,
            *[pltpu.VMEM(a.shape, a.dtype) for a in state],
            *[pltpu.VMEM((D, WINDOW), bf16)] * 2,
            *sems(55),
            pltpu.SemaphoreType.DMA((15,)),
        ],
        compiler_params=params(1),
    )(*arrays)


def mlp_kernel(*refs):
    resid, gain, og, w_out_hbm, og_hbm, gate_hbm, up_w_hbm, w_down_hbm, aa_part = refs[:9]
    back_hbm, grads_hbm, gains_hbm, gate_sum_hbm, near_hbm, far_hbm, up_hbm, down_hbm, aa_all = refs[9:18]
    wd, og_all, act_all, grad_hidden, hidden, ggp, gup, bk, dn, bk_core, dn_core, bk_sent, bk_in = refs[18:31]
    nb, rn, gate_terms, gate_in, gate_w, up_w, up_terms, down_terms, down_sum, dn_in, w_out = refs[31:42]
    grad_resid, grads, gain_terms, gate_sum, down_near, send_sems, recv_sems, local_sems = refs[42:]
    me = here()
    z, y, c = me["z"], me["y"], me["c"]
    partner, other = at(me, c=1), at(me, n=1)
    ys = {d: at(me, y=d) for d in (1, 2, 3)}
    zs = {d: at(me, z=d) for d in (1, 2, 3)}
    everyone_in = hail([partner, other, *ys.values(), *zs.values()])
    moves, kept_back = Moves(local_sems), []
    load_gate, load_up = moves.start(gate_hbm, gate_w), moves.start(up_w_hbm, up_w)
    units = pl.ds(pl.multiple_of((y * 2 + c) * UNITS, 16), UNITS)
    load_down, load_og = moves.start(w_down_hbm.at[units], wd), moves.start(og_hbm, og_all)
    load_out = moves.start(w_out_hbm, w_out)
    everyone_in()
    copies = Copies(send_sems, recv_sems)
    half = TOK // 2
    halves = (pl.ds(0, half), pl.ds(half, half))
    gain = gain[...].reshape(1, D)

    def inverse_of(rows):
        return lax.rsqrt(jnp.mean(rows * rows, axis=-1, keepdims=True) + rms_eps)

    own = act_all.at[y, c]
    far, to_core = {}, {0: [], 1: [], 2: [], 3: []}
    for rows in halves:
        total = resid[rows, :]
        act_all[y, c, rows] = (total * inverse_of(total) * gain).astype(bf16)
        to_core[0].append(copies.send(own.at[rows], own.at[rows], partner))
        for d in (1, 3):
            far[d, len(to_core[0]) - 1] = copies.send(own.at[rows], own.at[rows], ys[d])
    load_down.wait()
    load_og.wait()
    pair = (2 * TOK, D)

    def hidden_back(d):
        yi = step(me, "y", d)
        grad_hidden[yi] = nt(og_all[yi].reshape(pair), wd[...])

    hidden_back(0)
    load_gate.wait()
    load_up.wait()
    bk_cores, dn_cores, bk_moves = {}, {}, {}

    def block(d, beside=None):
        yi = step(me, "y", d)
        rows = act_all[yi].reshape(pair)
        gate = nn(rows, gate_w[:, :UNITS])
        up = nn(rows, up_w[:, :UNITS])
        sigmoid = 1.0 / (1.0 + jnp.exp(-gate))
        silu = gate * sigmoid
        grads = grad_hidden[yi]
        hidden[yi] = (silu * up).astype(bf16)
        ggp[yi] = (grads * up * (sigmoid * (1.0 + gate * (1.0 - sigmoid)))).astype(bf16)
        gup[yi] = (grads * silu).astype(bf16)
        if beside is not None:
            pass_block(beside)
        both = nt(ggp[yi], gate_w[:, :UNITS]) + nt(gup[yi], up_w[:, :UNITS])
        bk[yi] = both.astype(bf16).reshape(2, TOK, D)
        bk_cores[d] = copies.send(bk.at[yi, 1 - c], bk_core.at[yi], partner)
    low, high = halves

    def pass_block(d):
        yi = step(me, "y", d)
        bk_cores[d].wait_recv()
        for k, rows in enumerate((low, high)):
            bk_sent[yi, rows] = (
                bk[yi, c, rows].astype(f32) + bk_core[yi, rows].astype(f32)
            ).astype(bf16)
            if d:
                bk_moves[d, k] = copies.send(
                    bk_sent.at[yi, rows], bk_in.at[d - 1, rows], ys[d]
                )

    def down_block(d):
        yi = step(me, "y", d)
        dn[yi] = nn(hidden[yi], wd[...]).astype(bf16).reshape(2, TOK, D)
        dn_cores[d] = copies.send(dn.at[yi, 1 - c], dn_core.at[yi], partner)

    def sum_down(d):
        yi = step(me, "y", d)
        dn_cores[d].wait_recv()
        down_sum[yi] = (dn[yi, c].astype(f32) + dn_core[yi].astype(f32)).astype(bf16)

    for copy in to_core[0]:
        copy.wait_recv()
    block(0)
    n = me["n"]
    mine = pl.ds(pl.multiple_of(half * n, half), half)
    theirs = pl.ds(pl.multiple_of(half * (1 - n), half), half)
    aa_near = [copies.send(aa_part.at[y], aa_all.at[y, c], partner)]
    aa_across = {}
    for d in (1, 3, 2):
        yi = step(me, "y", d)
        got, slot = aa_part.at[yi, mine], aa_all.at[yi, c, mine]
        aa_across[d] = copies.send(got, slot, other)
        aa_near.append(copies.send(got, slot, partner))
    for d in (3, 1, 2):
        hidden_back(d)
    relay = {}
    for k, rows in enumerate(halves):
        for d in (1, 3):
            far[d, k].wait_recv()
            got = act_all.at[lax.rem(y + (4 - d), 4), c, rows]
            to_core[4 - d].append(copies.send(got, got, partner))
            if d == 1 + 2 * k:
                relay[d] = copies.send(got, got, ys[d])
    for copy in to_core[3]:
        copy.wait_recv()
    block(3, 0)
    for d, rows in ((1, low), (3, high)):
        relay[d].wait_recv()
        got = act_all.at[step(me, "y", 2), c, rows]
        to_core[2].append(copies.send(got, got, partner))
    for copy in to_core[1]:
        copy.wait_recv()
    block(1, 3)
    for copy in to_core[2]:
        copy.wait_recv()
    block(2, 1)

    everything = (GROUP * TOK, D)
    all_units = (GROUP * TOK, UNITS)
    gate_terms[...] = tn(ggp[...].reshape(all_units), act_all[...].reshape(everything)).astype(bf16)

    def z_cols(d):
        return pl.ds(pl.multiple_of(step(me, "z", d) * 384, 384), 384)

    gate_moves = {
        d: copies.send(gate_terms.at[:, z_cols(d)], gate_in.at[d - 1], zs[d]) for d in (1, 3, 2)
    }
    pass_block(2)
    for d in (1, 3, 2, 0):
        down_block(d)
    up_terms[...] = tn(gup[...].reshape(all_units), act_all[...].reshape(everything)).astype(bf16)
    kept_back.append(moves.start(up_terms, up_hbm))
    for d in range(4):
        sum_down(d)
    dn_moves = {
        d: copies.send(down_sum.at[step(me, "y", d)], dn_in.at[d // 2], ys[d]) for d in (1, 3)
    }
    kept_back.append(moves.start(down_sum.at[step(me, "y", 2)], far_hbm))
    swaps_back = []
    for k, rows in enumerate((low, high)):
        back = bk_sent[y, rows].astype(f32)
        for d in (1, 3, 2):
            bk_moves[d, k].wait_recv()
            back = back + bk_in[d - 1, rows].astype(f32)
        nb[rows] = back.astype(bf16)
        swaps_back.append(copies.send(nb.at[rows], rn.at[rows], other))
    for zi in range(4):
        columns = og_all[:, :, :, pl.ds(384 * zi, 384)].reshape(GROUP * TOK, 384)
        sums = whole_tiles(tn(columns, hidden[...].reshape(all_units)).astype(bf16))
        down_terms[zi] = sums.reshape(4, 2, 48, COLUMNS)
    kept_back.append(moves.start(down_terms, down_hbm))
    for d in (1, 3, 2):
        aa_across[d].wait_recv()
        got = aa_all.at[step(me, "y", d), c, theirs]
        aa_near.append(copies.send(got, got, partner))
    for copy in swaps_back:
        copy.wait_recv()
    grad_act = nb[...].astype(f32) + rn[...].astype(f32)
    inverse = inverse_of(resid[...])
    normed = resid[...] * inverse
    gain_terms[...] = jnp.sum(grad_act * normed, axis=0, keepdims=True)
    grad_normed = grad_act * gain
    inner = jnp.mean(grad_normed * normed, axis=-1, keepdims=True)
    grad_resid[...] = og[...].astype(f32) + inverse * (grad_normed - normed * inner)
    load_out.wait()
    grads[...] = nt(grad_resid[...].astype(bf16), w_out[...]).astype(bf16)
    for vmem, hbm in ((grad_resid, back_hbm), (grads, grads_hbm), (gain_terms, gains_hbm)):
        kept_back.append(moves.start(vmem, hbm))
    for d in (1, 3, 2):
        gate_moves[d].wait_recv()
    gate_sum[...] = whole_tiles((gate_terms[:, z_cols(0)].astype(f32) + three(gate_in)).T.astype(bf16))
    kept_back.append(moves.start(gate_sum, gate_sum_hbm))
    total = down_sum[y].astype(f32)
    for d in (1, 3):
        dn_moves[d].wait_recv()
        total = total + dn_in[d // 2].astype(f32)
    down_near[...] = total
    kept_back.append(moves.start(down_near, near_hbm))
    for copy in aa_near:
        copy.wait_recv()
    moves.finish(kept_back)
    copies.finish()


def feed_forward(*arrays):
    rows = pltpu.VMEM((TOK, D), bf16)
    return pl.pallas_call(
        mlp_kernel,
        out_shape=[
            jax.ShapeDtypeStruct((TOK, D), f32),
            jax.ShapeDtypeStruct((TOK, HEADS * HD), bf16),
            jax.ShapeDtypeStruct((1, D), f32),
            jax.ShapeDtypeStruct((D // 4, COLUMNS), bf16),
            jax.ShapeDtypeStruct((TOK, D), f32),
            jax.ShapeDtypeStruct((TOK, D), bf16),
            jax.ShapeDtypeStruct((UNITS, D), bf16),
            jax.ShapeDtypeStruct((4, 4, 2, 48, COLUMNS), bf16),
            jax.ShapeDtypeStruct((4, 2, TOK, D), bf16),
        ],
        in_specs=[VMEM] * 3 + [ANY] * 6,
        out_specs=[ANY] * 9,
        scratch_shapes=[
            pltpu.VMEM((UNITS, D), bf16),
            pltpu.VMEM((4, 2, TOK, D), bf16),
            pltpu.VMEM((4, 2, TOK, D), bf16),
            pltpu.VMEM((4, 2 * TOK, UNITS), f32),
            *[pltpu.VMEM((4, 2 * TOK, UNITS), bf16)] * 3,
            *[pltpu.VMEM((4, 2, TOK, D), bf16)] * 2,
            *[pltpu.VMEM((4, TOK, D), bf16)] * 3,
            pltpu.VMEM((3, TOK, D), bf16),
            rows,
            rows,
            pltpu.VMEM((UNITS, D), bf16),
            pltpu.VMEM((3, UNITS, D // 4), bf16),
            *[pltpu.VMEM((D, COLUMNS), bf16)] * 2,
            pltpu.VMEM((UNITS, D), bf16),
            pltpu.VMEM((4, 4, 2, 48, COLUMNS), bf16),
            pltpu.VMEM((4, TOK, D), bf16),
            pltpu.VMEM((2, TOK, D), bf16),
            pltpu.VMEM((HEADS * HD, D), bf16),
            pltpu.VMEM((TOK, D), f32),
            pltpu.VMEM((TOK, HEADS * HD), bf16),
            pltpu.VMEM((1, D), f32),
            pltpu.VMEM((D // 4, COLUMNS), bf16),
            pltpu.VMEM((TOK, D), f32),
            *sems(45),
            pltpu.SemaphoreType.DMA((13,)),
        ],
        compiler_params=params(2),
    )(*arrays)


def back_kernel(*refs):
    lengths, lse, grad_resid, grads_in, gain, mlp_gain_terms = refs[:6]
    x_hbm, rope_hbm, gate_sum, down_far, q_hbm, kv_hbm, exact_hbm, resid_hbm, near_hbm = refs[6:15]
    al_hbm, w_qkv_hbm, act_hbm, up_terms, wd_terms, aa_part = refs[15:21]
    results_hbm = refs[21:29]
    (g, stats, acc, acc_in, dkv, r1a, r1b, ta, tb, r2a, r2b, u, r3, w_qkv, act_all, gbt, gbt_all, al_all) = refs[29:47]
    gp, gp_flat, gp_all, part, part_other, small, e1, e2, e3, f1, f2 = refs[47:58]
    up_own, up_in, up_mid, wd_own, wd_across, wd_sum, wd_in, wd_mid, wd_second = refs[58:67]
    gate_second, up_second = refs[67:69]
    summed, third_in = refs[69:72], refs[72:75]
    q_terms, q_first, q_mid, q_second, q_summed, q_third = refs[75:81]
    down_in, down_part, down_other, q, kv, exact, resid, down_near, o_half, o_core, o_sum, o_in, o_mid, o_across, o_fin, o_third, *refs = refs[81:]
    x, rope, in_grad, layer_out, sum_gate, sum_up, sum_down, sum_qkv, sum_out, small_out, *refs = refs
    send_sems, recv_sems, local_sems = refs

    me = here()
    ids, start = token_rows(me, lengths)
    z, y, xh, c, n = (me[a] for a in AXES)
    partner, across, other = at(me, c=1), at(me, xh=1), at(me, n=1)
    ys = {d: at(me, y=d) for d in (1, 2, 3)}
    zs = {d: at(me, z=d) for d in (1, 2, 3)}
    near_moves = [(d, e) for d in (1, 3, 2, 0) for e in (0, 1) if d or e]
    near = {m: at(me, y=m[0], xh=m[1]) for m in near_moves}
    group = {m: at(me, y=m[0], c=m[1]) for m in near_moves}
    def strip(yi, xi):
        return pl.ds(pl.multiple_of(96 * yi + 48 * xi, 48), 48)

    everyone_in = hail([other, *zs.values(), *near.values(), *(group[m] for m in near_moves if m[1])])
    moves, kept_back = Moves(local_sems), []
    load = moves.start

    def keep_result(k, vmem):
        kept_back.append(moves.start(vmem, results_hbm[k]))

    loads = [load(exact_hbm, exact), load(q_hbm, q), load(kv_hbm, kv)]
    load_resid, load_near = load(resid_hbm, resid), load(near_hbm, down_near)
    load_x, load_rope = load(x_hbm, x), load(rope_hbm, rope)
    load_strip = load(gate_sum.at[strip(y, xh)], gate_second.at[y, xh])
    half = TOK // 2
    low, high = pl.ds(0, half), pl.ds(half, half)
    gbt[...] = grad_resid[...].T.astype(bf16).reshape(4, 4, 96, TOK)
    for h in range(HEADS):
        g[c, pl.ds(h * TOK, TOK), :] = grads_in[:, h * HD : (h + 1) * HD]
    loads[0].wait()
    stats[c, 0:1, :] = lse[...]
    stats[c, 1:2, :] = jnp.sum(g[c].astype(f32).T * exact[...], axis=0, keepdims=True)
    stats[c, 2:8, :] = jnp.zeros((6, NQ), f32)
    everyone_in()
    copies = Copies(send_sems, recv_sems)
    shared = [copies.send(g.at[c], g.at[c], partner), copies.send(stats.at[c], stats.at[c], partner)]

    def z_cols(d):
        return pl.ds(pl.multiple_of(step(me, "z", d) * 384, 384), 384)

    second = {}

    def send_second(i, source, in_ref):
        for m in near_moves:
            second[i, m] = copies.send(
                source(step(me, "y", m[0]), step(me, "xh", m[1])), in_ref.at[y, xh], near[m]
            )

    def send_mid(i, total, mid_ref, in_ref):
        turned = total.T.astype(bf16)
        if turned.shape[1] == UNITS:
            turned = whole_tiles(turned)
        for yi in range(4):
            for xi in range(2):
                rows = 96 * yi + 48 * xi
                mid_ref[yi, xi] = turned[rows : rows + 48]
        send_second(i, lambda yi, xi: mid_ref.at[yi, xi], in_ref)
        in_ref[y, xh] = mid_ref[y, xh]

    keep, give = pl.ds(pl.multiple_of(24 * c, 8), 24), pl.ds(pl.multiple_of(24 * (1 - c), 8), 24)
    third = {}
    all_summed = [*summed, q_summed]
    all_second = [gate_second, up_second, None, q_second]
    all_third = [*third_in, q_third]
    outs = (sum_gate, sum_up, sum_down, sum_qkv)

    def collect(i):
        if i == 2:
            for d in (1, 3, 2):
                second[2, d].wait_recv()
            summed[2][...] = wd_second[...].astype(f32)
        else:
            for m in near_moves:
                second[i, m].wait_recv()
            all_summed[i][...] = all_second[i][:, 0].astype(f32) + all_second[i][:, 1].astype(f32)
        third[i] = copies.send(all_summed[i].at[:, give], all_third[i], partner)

    def deliver(i):
        third[i].wait_recv()
        for yi in range(4):
            mine_sum, their_sum = all_summed[i][yi, keep], all_third[i][yi]
            pair = (jnp.where(c == 0, mine_sum, their_sum), jnp.where(c == 0, their_sum, mine_sum))
            for e in range(2):
                k = 2 * yi + e
                width = UNITS if i < 3 else HD
                outs[i][:, pl.ds(k * width, width)] = pair[e][:, :width]

    send_second(0, lambda yi, xi: gate_sum.at[strip(yi, xi)], gate_second)
    gbt_moves = {
        d: copies.send(gbt.at[:, step(me, "y", d)], gbt_all.at[y], ys[d]) for d in (1, 3, 2)
    }
    gbt_all[y] = gbt[:, y]
    down_move = copies.send(down_far, down_in, ys[2])
    first = {}
    for d in (1, 3, 2):
        first[d] = copies.send(up_terms.at[:, z_cols(d)], up_in.at[d - 1], zs[d])
    wd_move = copies.send(wd_terms.at[:, :, 1 - xh], wd_across, across)

    load_al = load(al_hbm, al_all)
    load_w = load(w_qkv_hbm, w_qkv)
    mine = pl.ds(pl.multiple_of(half * n, half), half)
    theirs = pl.ds(pl.multiple_of(half * (1 - n), half), half)
    load_act = [load(aa_part.at[y], act_all.at[y, c]), load(act_hbm.at[:, 1 - c], act_all.at[:, 1 - c])]
    for d in (1, 2, 3):
        yi = step(me, "y", d)
        load_act.append(load(aa_part.at[yi, mine], act_all.at[yi, c, mine]))
        load_act.append(load(act_hbm.at[yi, c, theirs], act_all.at[yi, c, theirs]))
    load_up = load(up_terms.at[:, z_cols(0)], up_own)
    load_wd = load(wd_terms.at[:, :, xh], wd_own)

    for copy in shared:
        copy.wait_recv()
    for copy in loads[1:]:
        copy.wait()
    acc[...] = jnp.zeros_like(acc)
    last = shard_of(me) // BLOCK_SHARDS

    def of_both(row):
        return jnp.concatenate([stats[0, row : row + 1, :], stats[1, row : row + 1, :]], axis=1)

    log_total, balance = of_both(0), of_both(1)
    earlier = jnp.where(start < last * KEY_BLOCK, log_total, -big_negative)
    keys_here = 2 * TOK

    def block(index, masked, shift):
        zi, yi = index // 4, lax.rem(index, 4)
        keys = kv[zi, yi, :, :, pl.ds(0, HD)].reshape(keys_here, HD)
        values = kv[zi, yi, :, :, pl.ds(HD, HD)].reshape(keys_here, HD)
        keys_t = keys.T
        dk = jnp.zeros((keys_here, HD), f32)
        dv = jnp.zeros((keys_here, HD), f32)
        for chunk in range(2 * NQ // Q_CHUNK):
            core, cs = divmod(chunk * Q_CHUNK, NQ)
            cs = pl.ds(cs, Q_CHUNK)
            piece = slice(chunk * Q_CHUNK, (chunk + 1) * Q_CHUNK)
            qc, gc = q[core, cs, :], g[core, cs, :]
            probs = jnp.exp2(nt(keys, qc) * SCALE_LOG2 - shift[:, piece])
            if masked:
                place = lax.broadcasted_iota(jnp.int32, (keys_here, Q_CHUNK), 0)
                key_ids = index * KEY_BLOCK + c * TOK + place + place // TOK * TOK
                allowed = (key_ids >= start[:, piece]) & (key_ids <= ids[:, piece])
                probs = jnp.where(allowed, probs, 0.0)
            grads = (probs * (nt(values, gc) - balance[:, piece])).astype(bf16)
            dv = dv + nn(probs.astype(bf16), gc)
            dk = dk + nn(grads, qc)
            acc[core, :, cs] = acc[core, :, cs] + nn(keys_t, grads)
        dkv[zi, yi, :, :, pl.ds(0, HD)] = (dk * SCALE).astype(bf16).reshape(2, TOK, HD)
        dkv[zi, yi, :, :, pl.ds(HD, HD)] = dv.astype(bf16).reshape(2, TOK, HD)

    def segment(zi):
        @pl.loop(0, 4)
        def _(yi):
            index = 4 * zi + yi
            edge = (index == 0) | (index == last)

            @pl.when(edge & (index <= last))
            def _():
                block(index, True, jnp.where(index == last, log_total, earlier))

            @pl.when((index < last) & jnp.logical_not(edge))
            def _():
                block(index, False, earlier)

            @pl.when(index > last)
            def _():
                dkv[zi, yi] = jnp.zeros((2, TOK, 2 * HD), bf16)

    first_a, first_b, second_a, second_b = {}, {}, {}, {}

    def settle(d):
        zi = step(me, "z", d)
        if d:
            first_a[d] = copies.send(dkv.at[zi, :, :, low], r1a.at[d - 1], zs[d])
        for e in (1, 3, 2):
            first_b[d, e] = copies.send(
                dkv.at[zi, step(me, "y", e), :, high], r1b.at[e - 1, zi], ys[e]
            )

    segment(step(me, "z", 1))
    settle(1)
    segment(step(me, "z", 2))
    settle(2)
    segment(step(me, "z", 3))
    settle(3)
    load_al.wait()
    for d in (1, 3, 2):
        gbt_moves[d].wait_recv()
    every_al = al_all[...].reshape(4 * TOK, HEADS * HD)
    for zi in range(4):
        lhs = jnp.concatenate([gbt_all[yi, zi] for yi in range(4)], axis=1)
        terms = nn(lhs, every_al).astype(bf16)
        o_half[0, zi] = terms[:, : HEADS * HD // 2]
        o_half[1, zi] = terms[:, HEADS * HD // 2 :]
    o_move = copies.send(o_half.at[1 - c], o_core, partner)
    segment(z)
    settle(0)
    queries_back = copies.send(acc.at[1 - c], acc_in, partner)
    down_move.wait_recv()
    load_near.wait()
    down_part[...] = (down_near[...] + down_in[...].astype(f32)).astype(bf16)
    down_swap = copies.send(down_part, down_other, other)
    for d in (1, 3, 2):
        first_a[d].wait_recv()
    ta[...] = (dkv[z, :, :, low].astype(f32) + three(r1a)).astype(bf16)
    for d in (1, 3, 2):
        second_a[d] = copies.send(ta.at[step(me, "y", d)], r2a.at[d - 1], ys[d])
    for copy in first_b.values():
        copy.wait_recv()
    tb[...] = (dkv[:, y, :, high].astype(f32) + three(r1b)).astype(bf16)
    for d in (1, 3, 2):
        second_b[d] = copies.send(tb.at[step(me, "z", d)], r2b.at[d - 1], zs[d])
    for d in (1, 3, 2):
        second_a[d].wait_recv()
        second_b[d].wait_recv()
    ua = ta[y].astype(f32) + three(r2a)
    ub = tb[z].astype(f32) + three(r2b)
    u[:, low] = ua.astype(bf16)
    u[:, high] = ub.astype(bf16)
    kv_last = copies.send(u.at[1 - xh], r3, across)
    o_move.wait_recv()
    o_sum[...] = (o_half[c].astype(f32) + o_core[...].astype(f32)).astype(bf16)
    o_first = {d: copies.send(o_sum.at[step(me, "z", d)], o_in.at[d - 1], zs[d]) for d in (1, 3, 2)}
    load_wd.wait()
    wd_move.wait_recv()
    for zi in range(4):
        wd_sum[zi] = (wd_own[zi].astype(f32) + wd_across[zi].astype(f32)).astype(bf16)
    wd_first = {d: copies.send(wd_sum.at[step(me, "z", d)], wd_in.at[d - 1], zs[d]) for d in (1, 3, 2)}
    queries_back.wait_recv()
    load_rope.wait()
    load_x.wait()
    turned_back = ((acc[c] + acc_in[...]) * SCALE).T

    def revert(rows):
        return rows * rope[0] - pltpu.roll(rows, HD // 2, 1) * rope[1]

    def keep_head(h, rows):
        low_rows = rows.astype(bf16)
        gp[h] = low_rows
        gp_flat[:, pl.ds(h * HD, HD)] = low_rows
        small[pl.ds(24 + h, 1), :] = jnp.sum(low_rows.astype(f32), axis=0, keepdims=True)

    def to_small(first_row, row):
        for k in range(D // 128):
            small[pl.ds(first_row + k, 1), :] = row[:, k * 128 : (k + 1) * 128]

    small[...] = jnp.zeros_like(small)
    to_small(12, mlp_gain_terms[...])
    for h in range(HEADS):
        keep_head(h, revert(turned_back[h * TOK : (h + 1) * TOK]))
    load_w.wait()
    front = HEADS * HD
    partial = nt(gp_flat[:, pl.ds(0, front)], w_qkv[:, pl.ds(0, front)])

    kv_last.wait_recv()
    grad_kv = u[xh].astype(f32) + r3[...].astype(f32)
    keep_head(HEADS, revert(grad_kv[:, :HD]))
    keep_head(HEADS + 1, grad_kv[:, HD:])
    gp_moves = [
        copies.send(gp.at[step(me, "y", m[0]) * 2 + step(me, "c", m[1])], gp_all.at[y, c], group[m])
        for m in near_moves
    ]
    gp_all[y, c] = gp[y * 2 + c]
    back = pl.ds(front, 2 * HD)
    part[...] = (partial + nt(gp_flat[:, back], w_qkv[:, back])).astype(bf16)
    swap = copies.send(part, part_other, other)
    load_up.wait()
    for d in (1, 3, 2):
        first[d].wait_recv()
    send_mid(1, up_own[...].astype(f32) + three(up_in), up_mid, up_second)
    load_strip.wait()
    collect(0)
    for copy in load_act:
        copy.wait()
    for copy in gp_moves:
        copy.wait_recv()
    q_terms[...] = tn(
        gp_all[...].reshape(GROUP * TOK, HD), act_all[...].reshape(GROUP * TOK, D)
    ).astype(bf16)

    q_one = {d: copies.send(q_terms.at[:, z_cols(d)], q_first.at[d - 1], zs[d]) for d in (1, 3, 2)}
    down_swap.wait_recv()
    load_resid.wait()
    layer_out[...] = (
        resid[...] + (down_part[...].astype(f32) + down_other[...].astype(f32))
    ).astype(bf16)
    keep_result(1, layer_out)
    swap.wait_recv()
    grad_act = part[...].astype(f32) + part_other[...].astype(f32)
    rows = x[...].astype(f32)
    inverse = lax.rsqrt(jnp.mean(rows * rows, axis=-1, keepdims=True) + rms_eps)
    normed = rows * inverse
    to_small(0, jnp.sum(grad_act * normed, axis=0, keepdims=True))
    small_one = {d: copies.send(small, e1.at[d - 1], zs[d]) for d in (1, 3, 2)}
    grad_normed = grad_act * gain[...].reshape(1, D)
    inner = jnp.mean(grad_normed * normed, axis=-1, keepdims=True)
    in_grad[...] = (grad_resid[...] + inverse * (grad_normed - normed * inner)).astype(bf16)

    keep_result(0, in_grad)
    for d in (1, 3, 2):
        wd_first[d].wait_recv()
    wd_mid[...] = (wd_sum[z].astype(f32) + three(wd_in)).astype(bf16)
    for d in (1, 3, 2):
        second[2, d] = copies.send(wd_mid.at[step(me, "y", d)], wd_second.at[y], ys[d])
    wd_second[y] = wd_mid[y]
    for d in (1, 3, 2):
        q_one[d].wait_recv()
    send_mid(3, q_terms[:, z_cols(0)].astype(f32) + three(q_first), q_mid, q_second)
    for d in (1, 3, 2):
        o_first[d].wait_recv()
    o_total = (o_sum[z].astype(f32) + three(o_in)).astype(bf16)
    o_mid[0], o_mid[1] = o_total[:48], o_total[48:]
    o_last = copies.send(o_mid.at[1 - xh], o_across, across)
    for d in (1, 3, 2):
        small_one[d].wait_recv()
    f1[...] = small[...] + three(e1)
    small_two = {m: copies.send(f1, e2.at[k], near[m]) for k, m in enumerate(near_moves)}
    o_last.wait_recv()
    o_fin[...] = o_mid[xh].astype(f32) + o_across[...].astype(f32)
    o_end = copies.send(o_fin.at[give], o_third, partner)
    collect(1)
    deliver(0)
    keep_result(2, sum_gate)
    deliver(1)
    keep_result(3, sum_up)
    collect(2)
    collect(3)
    for m in near_moves:
        small_two[m].wait_recv()
    f2[...] = f1[...]
    for k in range(len(near_moves)):
        f2[...] = f2[...] + e2[k]
    small_three = copies.send(f2, e3, partner)
    deliver(2)
    keep_result(4, sum_down)
    deliver(3)
    keep_result(5, sum_qkv)
    o_end.wait_recv()
    o_mine, o_theirs = o_fin[keep], o_third[...]
    sum_out[:, : HEADS * HD // 2] = jnp.where(c == 0, o_mine, o_theirs)
    sum_out[:, HEADS * HD // 2 :] = jnp.where(c == 0, o_theirs, o_mine)
    keep_result(6, sum_out)
    small_three.wait_recv()
    small_out[...] = f2[...] + e3[...]
    keep_result(7, small_out)
    moves.finish(kept_back)
    copies.finish()


def back(*arrays):
    half = TOK // 2
    wide = 2 * HD
    results_of = [
        jax.ShapeDtypeStruct((TOK, D), bf16),
        jax.ShapeDtypeStruct((TOK, D), bf16),
        *[jax.ShapeDtypeStruct((24, FF // 2), f32)] * 3,
        jax.ShapeDtypeStruct((24, (HEADS + 2) * HD), f32),
        jax.ShapeDtypeStruct((24, HEADS * HD), f32),
        jax.ShapeDtypeStruct((40, 128), f32),
    ]
    return pl.pallas_call(
        back_kernel,
        out_shape=results_of,
        in_specs=[SMEM] + [VMEM] * 5 + [ANY] * 15,
        out_specs=[ANY] * 8,
        scratch_shapes=[
            pltpu.VMEM((2, NQ, HD), bf16),
            pltpu.VMEM((2, 8, NQ), f32),
            pltpu.VMEM((2, HD, NQ), f32),
            pltpu.VMEM((HD, NQ), f32),
            pltpu.VMEM((4, 4, 2, TOK, wide), bf16),
            pltpu.VMEM((3, 4, 2, half, wide), bf16),
            pltpu.VMEM((3, 4, 2, half, wide), bf16),
            pltpu.VMEM((4, 2, half, wide), bf16),
            pltpu.VMEM((4, 2, half, wide), bf16),
            pltpu.VMEM((3, 2, half, wide), bf16),
            pltpu.VMEM((3, 2, half, wide), bf16),
            pltpu.VMEM((2, TOK, wide), bf16),
            pltpu.VMEM((TOK, wide), bf16),
            pltpu.VMEM((D, (HEADS + 2) * HD), bf16),
            pltpu.VMEM((4, 2, TOK, D), bf16),
            pltpu.VMEM((4, 4, 96, TOK), bf16),
            pltpu.VMEM((4, 4, 96, TOK), bf16),
            pltpu.VMEM((4, TOK, HEADS * HD), bf16),
            pltpu.VMEM((HEADS + 2, TOK, HD), bf16),
            pltpu.VMEM((TOK, (HEADS + 2) * HD), bf16),
            pltpu.VMEM((4, 2, TOK, HD), bf16),
            pltpu.VMEM((TOK, D), bf16),
            pltpu.VMEM((TOK, D), bf16),
            pltpu.VMEM((40, 128), f32),
            pltpu.VMEM((3, 40, 128), f32),
            pltpu.VMEM((7, 40, 128), f32),
            pltpu.VMEM((40, 128), f32),
            pltpu.VMEM((40, 128), f32),
            pltpu.VMEM((40, 128), f32),
            pltpu.VMEM((UNITS, 384), bf16),
            pltpu.VMEM((3, UNITS, 384), bf16),
            pltpu.VMEM((4, 2, 48, COLUMNS), bf16),
            *[pltpu.VMEM((4, 4, 48, COLUMNS), bf16)] * 3,
            pltpu.VMEM((3, 4, 48, COLUMNS), bf16),
            *[pltpu.VMEM((4, 48, COLUMNS), bf16)] * 2,
            *[pltpu.VMEM((4, 2, 48, COLUMNS), bf16)] * 2,
            *[pltpu.VMEM((4, 48, COLUMNS), f32)] * 3,
            *[pltpu.VMEM((4, 24, COLUMNS), f32)] * 3,
            pltpu.VMEM((HD, D), bf16),
            pltpu.VMEM((3, HD, 384), bf16),
            pltpu.VMEM((4, 2, 48, HD), bf16),
            pltpu.VMEM((4, 2, 48, HD), bf16),
            pltpu.VMEM((4, 48, HD), f32),
            pltpu.VMEM((4, 24, HD), f32),
            pltpu.VMEM((TOK, D), bf16),
            pltpu.VMEM((TOK, D), bf16),
            pltpu.VMEM((TOK, D), bf16),
            pltpu.VMEM((2, NQ, HD), bf16),
            pltpu.VMEM((4, 4, 2, TOK, wide), bf16),
            pltpu.VMEM((HD, NQ), f32),
            pltpu.VMEM((TOK, D), f32),
            pltpu.VMEM((TOK, D), f32),
            pltpu.VMEM((2, 4, 96, HEADS * HD // 2), bf16),
            *[pltpu.VMEM((4, 96, HEADS * HD // 2), bf16)] * 2,
            pltpu.VMEM((3, 96, HEADS * HD // 2), bf16),
            pltpu.VMEM((2, 48, HEADS * HD // 2), bf16),
            pltpu.VMEM((48, HEADS * HD // 2), bf16),
            pltpu.VMEM((48, HEADS * HD // 2), f32),
            pltpu.VMEM((24, HEADS * HD // 2), f32),
            pltpu.VMEM((TOK, D), bf16),
            pltpu.VMEM((2, TOK, HD), f32),
            *[pltpu.VMEM(a.shape, a.dtype) for a in results_of],
            *sems(93),
            pltpu.SemaphoreType.DMA((28,)),
        ],
        compiler_params=params(9, 62),
    )(*arrays)


def results_kernel(*refs):
    wholes, small, copied = refs[:7], refs[7], refs[8:15]
    small_outs, (norm_attn, norm_mlp, bias, value_bias) = refs[15:19], refs[19:23]
    *held, into, out_of = refs[23:]
    shard = shard_of(here())
    loads, stores = Moves(into), Moves(out_of)
    for a, b in zip(wholes, held):
        loads.start(a, b)
    rows = jnp.concatenate(
        [
            jnp.concatenate([small[12 * i + k : 12 * i + k + 1, :] for k in range(12)], axis=1)
            for i in range(2)
        ],
        axis=0,
    )
    turned = pltpu.roll(rows, lax.rem(D - 24 * shard, D), 1)
    norm_attn[...] = turned[0:1, :24]
    norm_mlp[...] = turned[1:2, :24]
    heads = pltpu.roll(small[24 : 24 + HEADS + 2, :], lax.rem(HD - 2 * shard, HD), 1)
    bias[0] = heads[: HEADS + 1, :2].T
    value_bias[...] = heads[HEADS + 1 :, :2]
    for a, b in zip(refs[19:23], small_outs):
        stores.start(a, b)
    for load, a, b in zip(loads.started, held, copied):
        load.wait()
        stores.start(a, b)
    stores.finish(stores.started)


def results(*arrays):
    *wholes, small = arrays
    small_ones = [
        jax.ShapeDtypeStruct((1, 24), f32),
        jax.ShapeDtypeStruct((1, 24), f32),
        jax.ShapeDtypeStruct((1, 2, HEADS + 1), f32),
        jax.ShapeDtypeStruct((1, 2), f32),
    ]
    return pl.pallas_call(
        results_kernel,
        out_shape=[*[jax.ShapeDtypeStruct(a.shape, a.dtype) for a in wholes], *small_ones],
        in_specs=[ANY] * 7 + [VMEM],
        out_specs=[ANY] * 11,
        scratch_shapes=[
            *[pltpu.VMEM(a.shape, a.dtype) for a in (*small_ones, *wholes)],
            pltpu.SemaphoreType.DMA((7,)),
            pltpu.SemaphoreType.DMA((11,)),
        ],
    )(*wholes, small)


def shards(
    layer_in, lengths, norm_attn, w_qkv, qkv_bias, w_out, norm_mlp, w_gate, w_up, w_down, out_grad
):
    half = HD // 2
    freqs = np.float32(rope_base) ** (-2.0 * np.arange(half, dtype=np.float32) / HD)
    freqs = np.concatenate([freqs, freqs]).astype(np.float32)[None]
    kv, queries, act_part, resid, exact, lse, rope, gate_w, up_w, out_grad_all, low_all = attend(
        lengths, layer_in, norm_attn, qkv_bias, freqs, out_grad, w_qkv, w_out, w_gate, w_up
    )
    (
        grad_resid, grads, gain_terms, gate_sum, down_near, down_far,
        up_terms, down_terms, act_attn_all,
    ) = feed_forward(
        resid, norm_mlp, out_grad, w_out, out_grad_all, gate_w, up_w, w_down, act_part
    )
    sums = back(
        lengths, lse, grad_resid, grads, norm_attn, gain_terms, layer_in, rope, gate_sum, down_far,
        queries, kv, exact, resid, down_near, low_all, w_qkv, act_attn_all, up_terms, down_terms,
        act_part,
    )
    in_grad, layer_out, sum_gate, sum_up, sum_down, sum_qkv, sum_out, *rest = results(*sums)
    sum_norm_attn, sum_norm_mlp, bias, value_bias = rest
    return (
        layer_out,
        in_grad,
        sum_norm_attn[0],
        sum_qkv,
        bias.swapaxes(1, 2),
        value_bias,
        sum_out.T,
        sum_norm_mlp[0],
        sum_gate,
        sum_up,
        sum_down.T,
    )


def solution(mesh):
    torus = Mesh(mesh.devices.reshape(4, 4, 2, 2, 2), AXES)
    in_specs = (
        P(WIDE, None),
        P(),
        P(),
        P(None, "n"),
        P("n", None),
        P("n", None),
        P(),
        P(None, "n"),
        P(None, "n"),
        P("n", None),
        P(WIDE, None),
    )
    out_specs = (
        P(WIDE, None),
        P(WIDE, None),
        P(WIDE),
        P(WIDE, "n"),
        P("n", None, WIDE),
        P("n", WIDE),
        P("n", WIDE),
        P(WIDE),
        P(WIDE, "n"),
        P(WIDE, "n"),
        P("n", WIDE),
    )
    return jax.shard_map(
        shards, mesh=torus, in_specs=in_specs, out_specs=out_specs, check_vma=False
    )
```

```python
import functools
import math

import jax
import jax.numpy as jnp
import numpy as np
from jax import lax
from jax.experimental import pallas as pl
from jax.experimental.pallas import tpu as pltpu
from jax.sharding import Mesh
from jax.sharding import PartitionSpec as P

HD = 128
QH = 12
KVH = 2
HEADS = QH // KVH
D = 1536
FF = 8960
TOK = 128
TOKENS = 8192
SEQS = 4
NQ = HEADS * TOK
GROUP = 8
UNITS = FF // 2 // GROUP
WINDOW = 768
COLUMNS = 640

AXES = ("z", "y", "xh", "c", "n")
SIZE = {"z": 4, "y": 4, "xh": 2, "c": 2, "n": 2}
WIDE = ("z", "y", "xh", "c")
MESH = pl.DeviceIdType.MESH

rms_eps = 1e-06
rope_base = 10000.0
big_negative = -1e30
SCALE = HD ** (-0.5)
SCALE_LOG2 = SCALE * math.log2(math.e)
KEY_BLOCK = 512
BLOCK_SHARDS = KEY_BLOCK // TOK
Q_CHUNK = 256

bf16 = jnp.bfloat16
f32 = jnp.float32
VMEM = pl.BlockSpec(memory_space=pltpu.VMEM)
SMEM = pl.BlockSpec(memory_space=pltpu.SMEM)
ANY = pl.BlockSpec(memory_space=pl.ANY)


def nn(a, b):
    return lax.dot_general(a, b, (((1,), (0,)), ((), ())), preferred_element_type=f32)


def nt(a, b):
    return lax.dot_general(a, b, (((1,), (1,)), ((), ())), preferred_element_type=f32)


def tn(a, b):
    return lax.dot_general(a, b, (((0,), (0,)), ((), ())), preferred_element_type=f32)


def here():
    return {a: lax.axis_index(a) for a in AXES}


def step(me, axis, by):
    return lax.rem(me[axis] + by, SIZE[axis])


def at(me, **moved):
    return tuple(step(me, a, moved[a]) if a in moved else me[a] for a in AXES)


def sequence_starts(ids, lengths):
    starts, end = jnp.zeros_like(ids), 0
    for s in range(SEQS):
        end = end + lengths[s]
        starts = starts + jnp.where(ids >= end, lengths[s], 0)
    return starts


def token_rows(me, lengths):
    column = lax.broadcasted_iota(jnp.int32, (1, 2 * NQ), 1)
    ids = shard_of(me) // 2 * (2 * TOK) + column // NQ * TOK + column % TOK
    return ids, sequence_starts(ids, lengths)


def hail(peers):
    barrier = pltpu.get_barrier_semaphore()
    for p in peers:
        pl.semaphore_signal(barrier, inc=1, device_id=p, device_id_type=MESH)
    return lambda: pl.semaphore_wait(barrier, len(peers))


def greet(peers):
    hail(peers)()


class Copies:
    def __init__(self, send_sems, recv_sems):
        self.send_sems, self.recv_sems, self.used, self.started = send_sems, recv_sems, 0, []

    def make(self, src, dst, target):
        self.used += 1
        return self.numbered(self.used - 1, src, dst, target)

    def numbered(self, k, src, dst, target):
        return pltpu.make_async_remote_copy(
            src_ref=src,
            dst_ref=dst,
            send_sem=self.send_sems.at[k],
            recv_sem=self.recv_sems.at[k],
            device_id=target,
            device_id_type=MESH,
        )

    def send(self, src, dst, target):
        copy = self.make(src, dst, target)
        copy.start()
        self.started.append(copy)
        return copy

    def finish(self):
        for copy in self.started:
            copy.wait_send()


class Moves:
    def __init__(self, move_sems):
        self.move_sems, self.started = move_sems, []

    def start(self, src, dst):
        copy = pltpu.make_async_copy(src, dst, self.move_sems.at[len(self.started)])
        copy.start()
        self.started.append(copy)
        return copy

    def finish(self, copies):
        for copy in copies:
            copy.wait()


def sems(count):
    return [pltpu.SemaphoreType.DMA((count,)), pltpu.SemaphoreType.DMA((count,))]


def params(ident, mib=60):
    return pltpu.CompilerParams(
        collective_id=ident, has_side_effects=True, vmem_limit_bytes=mib * 2**20
    )


def whole_tiles(values):
    pad = jnp.zeros((values.shape[0], COLUMNS - values.shape[1]), values.dtype)
    return jnp.concatenate([values, pad], axis=1)


def three(ref):
    return ref[0].astype(f32) + ref[1].astype(f32) + ref[2].astype(f32)


def shard_of(me):
    return ((me["z"] * 4 + me["y"]) * 2 + me["xh"]) * 2 + me["c"]


class Rows:
    def __init__(self, me, copies, source, slots):
        self.me, self.copies, self.source, self.slots = me, copies, source, slots
        half = TOK // 2
        n = me["n"]
        self.mine = pl.ds(pl.multiple_of(half * n, half), half)
        self.theirs = pl.ds(pl.multiple_of(half * (1 - n), half), half)
        self.own = slots.at[me["y"], me["c"]]
        self.near, self.far, self.across = [], {}, {}

    def pair(self):
        self.near.append(self.copies.send(self.source, self.own, at(self.me, c=1)))

    def slot(self, d, rows):
        return self.slots.at[lax.rem(self.me["y"] + (4 - d), 4), self.me["c"], rows]

    def start(self, *steps):
        for d in steps:
            self.far[d] = self.copies.send(
                self.source.at[self.mine], self.own.at[self.mine], at(self.me, y=d)
            )

    def pass_on(self, *steps):
        for d in steps:
            self.far[d].wait_recv()
            got = self.slot(d, self.mine)
            self.across[d] = self.copies.send(got, got, at(self.me, n=1))
            self.near.append(self.copies.send(got, got, at(self.me, c=1)))

    def complete(self, *steps):
        for d in steps:
            self.across[d].wait_recv()
            got = self.slot(d, self.theirs)
            self.near.append(self.copies.send(got, got, at(self.me, c=1)))

    def wait(self):
        for copy in self.near:
            copy.wait_recv()


def attend_kernel(
    lengths, x, gain, bias, freqs, og, w_qkv_hbm, w_out_hbm, w_gate_hbm, w_up_hbm,
    kv_hbm, q_hbm, aa_part, resid_hbm, exact_hbm, lse_hbm, rope_hbm, gate_hbm, up_hbm, og_all, al_all,
    stats, acc, low_acc, stats_in, acc_in, low_in, w_qkv, w_out, o, pa, pb,
    kv, q, act, resid, exact, lse, rope, gate_w, up_w, wide_gate, wide_up, send_sems, recv_sems, local_sems,
):
    me = here()
    moves, kept_back = Moves(local_sems), []
    load_w = moves.start(w_qkv_hbm, w_qkv)
    ids, start = token_rows(me, lengths)
    z, y, xh, c = me["z"], me["y"], me["xh"], me["c"]
    partner, across, other = at(me, c=1), at(me, xh=1), at(me, n=1)
    ys = {d: at(me, y=d) for d in (1, 2, 3)}
    zs = {d: at(me, z=d) for d in (1, 2, 3)}
    everyone_in = hail([partner, across, other, *ys.values(), *zs.values()])
    rows = x[...].astype(f32)
    inverse = lax.rsqrt(jnp.mean(rows * rows, axis=-1, keepdims=True) + rms_eps)
    act[...] = (rows * inverse * gain[...].reshape(1, D)).astype(bf16)
    token = shard_of(me) * TOK + lax.broadcasted_iota(jnp.int32, (TOK, 1), 0)
    angles = (token - sequence_starts(token, lengths)).astype(f32) * freqs[...]
    cosine = jnp.cos(angles)
    turned = jnp.sin(angles)
    first_half = lax.broadcasted_iota(jnp.int32, (TOK, HD), 1) < HD // 2
    sine = jnp.where(first_half, -turned, turned)
    rope[0], rope[1] = cosine, sine
    kept_back.append(moves.start(rope, rope_hbm))
    front = HEADS * HD

    def turn(values):
        return values * cosine + pltpu.roll(values, HD // 2, 1) * sine

    load_w.wait()
    back = nn(act[...], w_qkv[:, front:]) + bias[:, front:]
    mine = kv.at[z, y, xh]
    mine[:, pl.ds(0, HD)] = turn(back[:, :HD]).astype(bf16)
    mine[:, pl.ds(HD, HD)] = back[:, HD:].astype(bf16)
    everyone_in()
    kept_back.append(moves.start(act, aa_part.at[y]))
    load_out = moves.start(w_out_hbm, w_out)
    copies = Copies(send_sems, recv_sems)
    rows_of_og = Rows(me, copies, og, og_all)
    rows_of_og.start(1, 3)
    first = copies.send(mine, mine, across)
    ahead = nn(act[...], w_qkv[:, :front]) + bias[:, :front]
    for h in range(HEADS):
        head = turn(ahead[:, h * HD : (h + 1) * HD]).astype(bf16)
        q[c, pl.ds(h * TOK, TOK), :] = head
    share_q = copies.send(q.at[c], q.at[c], partner)
    rows_of_og.pair()
    kept_back.append(moves.start(og, og_all.at[y, c]))
    stats[:, 0:1, :] = jnp.full((2, 1, NQ), big_negative, f32)
    stats[:, 1:8, :] = jnp.zeros((2, 7, NQ), f32)
    acc[...] = jnp.zeros_like(acc)
    low_acc[...] = jnp.zeros_like(low_acc)
    last = shard_of(me) // BLOCK_SHARDS
    kept = start < last * KEY_BLOCK
    half = TOK // 2
    keys_here = 2 * half

    early = sequence_starts(last * KEY_BLOCK - 1, lengths)

    def take(parts, masked=False, from_first=False):
        def both(columns):
            return jnp.concatenate(
                [
                    kv[zi, yi, :, pl.ds(pl.multiple_of(half * k, half), half), columns].reshape(
                        keys_here, HD
                    )
                    for zi, yi, k in parts
                ],
                axis=0,
            )

        def key_ids(columns):
            place = lax.broadcasted_iota(jnp.int32, (keys_here, columns), 0)
            place = place + place // half * (2 * TOK - half)
            return jnp.concatenate(
                [(4 * zi + yi) * KEY_BLOCK + c * TOK + half * k + place for zi, yi, k in parts], axis=0
            )

        keys, values = both(pl.ds(0, HD)), both(pl.ds(HD, HD)).T
        if from_first:
            barred = jnp.where(key_ids(1) >= early, 0.0, big_negative)
        for chunk in range(2 * NQ // Q_CHUNK):
            core, cs = divmod(chunk * Q_CHUNK, NQ)
            cs = pl.ds(cs, Q_CHUNK)
            here_cols = slice(chunk * Q_CHUNK, (chunk + 1) * Q_CHUNK)
            scores = nt(keys, q[core, cs, :]) * SCALE_LOG2
            if masked:
                which = key_ids(Q_CHUNK)
                allowed = (which >= start[:, here_cols]) & (which <= ids[:, here_cols])
                scores = jnp.where(allowed, scores, big_negative)
            if from_first:
                scores = scores + barred
            old = stats[core, 0:1, cs]
            new = jnp.maximum(old, jnp.max(scores, axis=0, keepdims=True))
            if masked:
                probs = jnp.where(allowed, jnp.exp2(scores - new), 0.0)
            else:
                taken = kept[:, here_cols]
                new = jnp.where(taken, new, old)
                probs = jnp.exp2(scores - jnp.where(taken, new, -big_negative))
            fade = jnp.exp2(old - new)
            stats[core, 0:1, cs] = new
            stats[core, 1:2, cs] = stats[core, 1:2, cs] * fade + jnp.sum(probs, axis=0, keepdims=True)
            upper = probs.astype(bf16)
            rest = (probs - upper.astype(f32)).astype(bf16)
            acc[core, :, cs] = acc[core, :, cs] * fade + nn(values, upper)
            low_acc[core, :, cs] = low_acc[core, :, cs] * fade + nn(values, rest)

    def pair(za, ya, zb, yb):
        a, b = 4 * za + ya, 4 * zb + yb
        spots = [(za, ya, 0), (zb, yb, 1)]
        before_last = jnp.maximum(a, b) < last
        has_first = jnp.minimum(a, b) == 0

        @pl.when(before_last & jnp.logical_not(has_first))
        def _():
            take(spots)

        @pl.when(before_last & has_first)
        def _():
            take(spots, from_first=True)

        @pl.when(jnp.logical_not(before_last))
        def _():
            @pl.loop(0, 2)
            def _(k):
                zi, yi = jnp.where(k == 0, za, zb), jnp.where(k == 0, ya, yb)
                index = 4 * zi + yi
                edge = (index == 0) | (index == last)

                @pl.when(edge & (index <= last))
                def _():
                    take([(zi, yi, k)], masked=True)

                @pl.when((index < last) & jnp.logical_not(edge))
                def _():
                    take([(zi, yi, k)])

    def two_pairs(one, two):
        spots = [(*one[:2], 0), (*one[2:], 1), (*two[:2], 0), (*two[2:], 1)]
        index = [4 * zi + yi for zi, yi, _ in spots]
        least = jnp.minimum(jnp.minimum(index[0], index[1]), jnp.minimum(index[2], index[3]))
        most = jnp.maximum(jnp.maximum(index[0], index[1]), jnp.maximum(index[2], index[3]))
        @pl.when((most < last) & (least > 0))
        def _():
            take(spots)

        @pl.when((most < last) & (least == 0))
        def _():
            take(spots, from_first=True)

        @pl.when(most >= last)
        def _():
            @pl.loop(0, 2)
            def _(i):
                pair(*(jnp.where(i == 0, a, b) for a, b in zip(one, two)))

    first.wait_recv()
    low, high = pl.ds(0, half), pl.ds(half, half)

    def slot(zi, yi, rows):
        return kv.at[zi, yi, :, rows]

    def before(axis, d):
        return lax.rem(me[axis] + (4 - d), 4)

    first_low, first_high = {}, {}
    for d in (1, 3, 2):
        first_low[d] = copies.send(slot(z, y, low), slot(z, y, low), ys[d])
        first_high[d] = copies.send(slot(z, y, high), slot(z, y, high), zs[d])
    share_q.wait_recv()

    kept_back.append(moves.start(q, q_hbm))
    first_unit = (y * 2 + c) * UNITS
    tile = jnp.minimum(first_unit // 128, FF // 2 // 128 - WINDOW // 128)
    window = pl.ds(pl.multiple_of(tile * 128, 128), WINDOW)
    load_gate = moves.start(w_gate_hbm.at[:, window], wide_gate)
    load_up = moves.start(w_up_hbm.at[:, window], wide_up)
    take([(z, y, 0), (z, y, 1)], masked=True)
    second_from = copies.used
    copies.used += 24
    for i, e in enumerate((0, 1, 3, 2)):
        yi, zi = before("y", e), before("z", e)
        if e:
            first_low[e].wait_recv()
            first_high[e].wait_recv()
        for j, d in enumerate((1, 3, 2)):
            k = second_from + 2 * (3 * i + j)
            for copy in (
                copies.numbered(k, slot(z, yi, low), slot(z, yi, low), zs[d]),
                copies.numbered(k + 1, slot(zi, y, high), slot(zi, y, high), ys[d]),
            ):
                copy.start()
                copies.started.append(copy)
    rows_of_og.start(2)
    rows_of_og.pass_on(1, 3)

    @pl.loop(1, 4)
    def _(e):
        pair(z, before("y", e), before("z", e), y)

    def places(k):
        i, j = k // 3, lax.rem(k, 3)
        e = jnp.where(i < 2, i, 5 - i)
        d = jnp.where(j < 2, 1 + 2 * j, 2)
        return before("z", d), before("y", e), before("z", e), before("y", d)

    def arrive(k):
        za, ya, zb, yb = places(k)
        one, two = slot(za, ya, low), slot(zb, yb, high)
        copies.numbered(second_from + 2 * k, one, one, zs[1]).wait_recv()
        copies.numbered(second_from + 2 * k + 1, two, two, ys[1]).wait_recv()

    def two_arrive(i):
        arrive(2 * i)
        arrive(2 * i + 1)
        two_pairs(places(2 * i), places(2 * i + 1))

    pl.loop(0, 4)(two_arrive)
    rows_of_og.pass_on(2)
    mine = rows_of_og.mine
    aa_far = [copies.send(act.at[mine], aa_part.at[y, mine], ys[d]) for d in (1, 3, 2)]
    pl.loop(4, 6)(two_arrive)
    kept_back.append(moves.start(kv, kv_hbm))
    merge = [
        copies.send(stats.at[1 - c], stats_in, partner),
        copies.send(acc.at[1 - c], acc_in, partner),
        copies.send(low_acc.at[1 - c], low_in, partner),
    ]
    rows_of_og.complete(1, 3, 2)
    for copy in merge:
        copy.wait_recv()
    own_top, in_top = stats[c, 0:1, :], stats_in[0:1, :]
    top = jnp.maximum(own_top, in_top)
    own_part, in_part = jnp.exp2(own_top - top), jnp.exp2(in_top - top)
    total = stats[c, 1:2, :] * own_part + stats_in[1:2, :] * in_part
    inverse = 1.0 / total
    own_part, in_part = own_part * inverse, in_part * inverse
    rows = acc[c] * own_part + acc_in[...] * in_part
    exact[...] = rows + (low_acc[c] * own_part + low_in[...] * in_part)
    rows = rows.T.astype(bf16)
    for h in range(HEADS):
        o[:, pl.ds(h * HD, HD)] = rows[h * TOK : (h + 1) * TOK]
    load_out.wait()
    pa[...] = nn(o[...], w_out[...]).astype(bf16)
    swap = copies.send(pa, pb, other)
    own_al = al_all.at[y]
    al_moves = {d: copies.send(o, own_al, ys[d]) for d in (1, 3, 2)}
    kept_back.append(moves.start(o, own_al))
    lse[...] = top + jnp.log2(total)
    kept_back.append(moves.start(lse, lse_hbm))
    kept_back.append(moves.start(exact, exact_hbm))
    shift = lax.rem(WINDOW - (first_unit - tile * 128), WINDOW)
    for load, part, weights, whole in (
        (load_gate, wide_gate, gate_w, gate_hbm),
        (load_up, wide_up, up_w, up_hbm),
    ):
        load.wait()

        @pl.loop(0, D // 128)
        def _(index, part=part, weights=weights):
            rows = pl.ds(pl.multiple_of(index * 128, 128), 128)
            rolled = pltpu.roll(part[rows, :].astype(f32), shift, 1)
            weights[rows, :] = rolled[:, :COLUMNS].astype(bf16)

        kept_back.append(moves.start(weights, whole))
    rows_of_og.wait()
    swap.wait_recv()
    resid[...] = x[...].astype(f32) + (pa[...].astype(f32) + pb[...].astype(f32))
    kept_back.append(moves.start(resid, resid_hbm))
    for copy in (*aa_far, *al_moves.values()):
        copy.wait_recv()
    moves.finish(kept_back)
    copies.finish()


def attend(*arrays):
    state = [
        jax.ShapeDtypeStruct((4, 4, 2, TOK, 2 * HD), bf16),
        jax.ShapeDtypeStruct((2, NQ, HD), bf16),
        jax.ShapeDtypeStruct((TOK, D), bf16),
        jax.ShapeDtypeStruct((TOK, D), f32),
        jax.ShapeDtypeStruct((HD, NQ), f32),
        jax.ShapeDtypeStruct((1, NQ), f32),
        jax.ShapeDtypeStruct((2, TOK, HD), f32),
        jax.ShapeDtypeStruct((D, COLUMNS), bf16),
        jax.ShapeDtypeStruct((D, COLUMNS), bf16),
    ]
    return pl.pallas_call(
        attend_kernel,
        out_shape=[
            *state[:2],
            jax.ShapeDtypeStruct((4, TOK, D), bf16),
            *state[3:],
            jax.ShapeDtypeStruct((4, 2, TOK, D), bf16),
            jax.ShapeDtypeStruct((4, TOK, HEADS * HD), bf16),
        ],
        in_specs=[SMEM] + [VMEM] * 5 + [ANY] * 4,
        out_specs=[ANY] * 11,
        scratch_shapes=[
            pltpu.VMEM((2, 8, NQ), f32),
            pltpu.VMEM((2, HD, NQ), f32),
            pltpu.VMEM((2, HD, NQ), f32),
            pltpu.VMEM((8, NQ), f32),
            pltpu.VMEM((HD, NQ), f32),
            pltpu.VMEM((HD, NQ), f32),
            pltpu.VMEM((D, (HEADS + 2) * HD), bf16),
            pltpu.VMEM((HEADS * HD, D), bf16),
            pltpu.VMEM((TOK, HEADS * HD), bf16),
            *[pltpu.VMEM((TOK, D), bf16)] * 2,
            *[pltpu.VMEM(a.shape, a.dtype) for a in state],
            *[pltpu.VMEM((D, WINDOW), bf16)] * 2,
            *sems(55),
            pltpu.SemaphoreType.DMA((15,)),
        ],
        compiler_params=params(1),
    )(*arrays)


def mlp_kernel(*refs):
    resid, gain, og, w_out_hbm, og_hbm, gate_hbm, up_w_hbm, w_down_hbm, aa_part = refs[:9]
    back_hbm, grads_hbm, gains_hbm, gate_sum_hbm, near_hbm, far_hbm, up_hbm, down_hbm, aa_all = refs[9:18]
    wd, og_all, act_all, grad_hidden, hidden, ggp, gup, bk, dn, bk_core, dn_core, bk_sent, bk_in = refs[18:31]
    nb, rn, gate_terms, gate_in, gate_w, up_w, up_terms, down_terms, down_sum, dn_in, w_out = refs[31:42]
    grad_resid, grads, gain_terms, gate_sum, down_near, send_sems, recv_sems, local_sems = refs[42:]
    me = here()
    z, y, c = me["z"], me["y"], me["c"]
    partner, other = at(me, c=1), at(me, n=1)
    ys = {d: at(me, y=d) for d in (1, 2, 3)}
    zs = {d: at(me, z=d) for d in (1, 2, 3)}
    everyone_in = hail([partner, other, *ys.values(), *zs.values()])
    moves, kept_back = Moves(local_sems), []
    load_gate, load_up = moves.start(gate_hbm, gate_w), moves.start(up_w_hbm, up_w)
    units = pl.ds(pl.multiple_of((y * 2 + c) * UNITS, 16), UNITS)
    load_down, load_og = moves.start(w_down_hbm.at[units], wd), moves.start(og_hbm, og_all)
    load_out = moves.start(w_out_hbm, w_out)
    everyone_in()
    copies = Copies(send_sems, recv_sems)
    half = TOK // 2
    halves = (pl.ds(0, half), pl.ds(half, half))
    gain = gain[...].reshape(1, D)

    def inverse_of(rows):
        return lax.rsqrt(jnp.mean(rows * rows, axis=-1, keepdims=True) + rms_eps)

    own = act_all.at[y, c]
    far, to_core = {}, {0: [], 1: [], 2: [], 3: []}
    for rows in halves:
        total = resid[rows, :]
        act_all[y, c, rows] = (total * inverse_of(total) * gain).astype(bf16)
        to_core[0].append(copies.send(own.at[rows], own.at[rows], partner))
        for d in (1, 3):
            far[d, len(to_core[0]) - 1] = copies.send(own.at[rows], own.at[rows], ys[d])
    load_down.wait()
    load_og.wait()
    pair = (2 * TOK, D)

    def hidden_back(d):
        yi = step(me, "y", d)
        grad_hidden[yi] = nt(og_all[yi].reshape(pair), wd[...])

    hidden_back(0)
    load_gate.wait()
    load_up.wait()
    bk_cores, dn_cores, bk_moves = {}, {}, {}

    def block(d, beside=None):
        yi = step(me, "y", d)
        rows = act_all[yi].reshape(pair)
        gate = nn(rows, gate_w[:, :UNITS])
        up = nn(rows, up_w[:, :UNITS])
        sigmoid = 1.0 / (1.0 + jnp.exp(-gate))
        silu = gate * sigmoid
        grads = grad_hidden[yi]
        hidden[yi] = (silu * up).astype(bf16)
        ggp[yi] = (grads * up * (sigmoid * (1.0 + gate * (1.0 - sigmoid)))).astype(bf16)
        gup[yi] = (grads * silu).astype(bf16)
        if beside is not None:
            pass_block(beside)
        both = nt(ggp[yi], gate_w[:, :UNITS]) + nt(gup[yi], up_w[:, :UNITS])
        bk[yi] = both.astype(bf16).reshape(2, TOK, D)
        bk_cores[d] = copies.send(bk.at[yi, 1 - c], bk_core.at[yi], partner)
    low, high = halves

    def pass_block(d):
        yi = step(me, "y", d)
        bk_cores[d].wait_recv()
        for k, rows in enumerate((low, high)):
            bk_sent[yi, rows] = (
                bk[yi, c, rows].astype(f32) + bk_core[yi, rows].astype(f32)
            ).astype(bf16)
            if d:
                bk_moves[d, k] = copies.send(
                    bk_sent.at[yi, rows], bk_in.at[d - 1, rows], ys[d]
                )

    def down_block(d):
        yi = step(me, "y", d)
        dn[yi] = nn(hidden[yi], wd[...]).astype(bf16).reshape(2, TOK, D)
        dn_cores[d] = copies.send(dn.at[yi, 1 - c], dn_core.at[yi], partner)

    def sum_down(d):
        yi = step(me, "y", d)
        dn_cores[d].wait_recv()
        down_sum[yi] = (dn[yi, c].astype(f32) + dn_core[yi].astype(f32)).astype(bf16)

    for copy in to_core[0]:
        copy.wait_recv()
    block(0)
    n = me["n"]
    mine = pl.ds(pl.multiple_of(half * n, half), half)
    theirs = pl.ds(pl.multiple_of(half * (1 - n), half), half)
    aa_near = [copies.send(aa_part.at[y], aa_all.at[y, c], partner)]
    aa_across = {}
    for d in (1, 3, 2):
        yi = step(me, "y", d)
        got, slot = aa_part.at[yi, mine], aa_all.at[yi, c, mine]
        aa_across[d] = copies.send(got, slot, other)
        aa_near.append(copies.send(got, slot, partner))
    for d in (3, 1, 2):
        hidden_back(d)
    relay = {}
    for k, rows in enumerate(halves):
        for d in (1, 3):
            far[d, k].wait_recv()
            got = act_all.at[lax.rem(y + (4 - d), 4), c, rows]
            to_core[4 - d].append(copies.send(got, got, partner))
            if d == 1 + 2 * k:
                relay[d] = copies.send(got, got, ys[d])
    for copy in to_core[3]:
        copy.wait_recv()
    block(3, 0)
    for d, rows in ((1, low), (3, high)):
        relay[d].wait_recv()
        got = act_all.at[step(me, "y", 2), c, rows]
        to_core[2].append(copies.send(got, got, partner))
    for copy in to_core[1]:
        copy.wait_recv()
    block(1, 3)
    for copy in to_core[2]:
        copy.wait_recv()
    block(2, 1)

    everything = (GROUP * TOK, D)
    all_units = (GROUP * TOK, UNITS)
    gate_terms[...] = tn(ggp[...].reshape(all_units), act_all[...].reshape(everything)).astype(bf16)

    def z_cols(d):
        return pl.ds(pl.multiple_of(step(me, "z", d) * 384, 384), 384)

    gate_moves = {
        d: copies.send(gate_terms.at[:, z_cols(d)], gate_in.at[d - 1], zs[d]) for d in (1, 3, 2)
    }
    pass_block(2)
    for d in (1, 3, 2, 0):
        down_block(d)
    up_terms[...] = tn(gup[...].reshape(all_units), act_all[...].reshape(everything)).astype(bf16)
    kept_back.append(moves.start(up_terms, up_hbm))
    for d in range(4):
        sum_down(d)
    dn_moves = {
        d: copies.send(down_sum.at[step(me, "y", d)], dn_in.at[d // 2], ys[d]) for d in (1, 3)
    }
    kept_back.append(moves.start(down_sum.at[step(me, "y", 2)], far_hbm))
    swaps_back = []
    for k, rows in enumerate((low, high)):
        back = bk_sent[y, rows].astype(f32)
        for d in (1, 3, 2):
            bk_moves[d, k].wait_recv()
            back = back + bk_in[d - 1, rows].astype(f32)
        nb[rows] = back.astype(bf16)
        swaps_back.append(copies.send(nb.at[rows], rn.at[rows], other))
    for zi in range(4):
        columns = og_all[:, :, :, pl.ds(384 * zi, 384)].reshape(GROUP * TOK, 384)
        sums = whole_tiles(tn(columns, hidden[...].reshape(all_units)).astype(bf16))
        down_terms[zi] = sums.reshape(4, 2, 48, COLUMNS)
    kept_back.append(moves.start(down_terms, down_hbm))
    for d in (1, 3, 2):
        aa_across[d].wait_recv()
        got = aa_all.at[step(me, "y", d), c, theirs]
        aa_near.append(copies.send(got, got, partner))
    for copy in swaps_back:
        copy.wait_recv()
    grad_act = nb[...].astype(f32) + rn[...].astype(f32)
    inverse = inverse_of(resid[...])
    normed = resid[...] * inverse
    gain_terms[...] = jnp.sum(grad_act * normed, axis=0, keepdims=True)
    grad_normed = grad_act * gain
    inner = jnp.mean(grad_normed * normed, axis=-1, keepdims=True)
    grad_resid[...] = og[...].astype(f32) + inverse * (grad_normed - normed * inner)
    load_out.wait()
    grads[...] = nt(grad_resid[...].astype(bf16), w_out[...]).astype(bf16)
    for vmem, hbm in ((grad_resid, back_hbm), (grads, grads_hbm), (gain_terms, gains_hbm)):
        kept_back.append(moves.start(vmem, hbm))
    for d in (1, 3, 2):
        gate_moves[d].wait_recv()
    gate_sum[...] = whole_tiles((gate_terms[:, z_cols(0)].astype(f32) + three(gate_in)).T.astype(bf16))
    kept_back.append(moves.start(gate_sum, gate_sum_hbm))
    total = down_sum[y].astype(f32)
    for d in (1, 3):
        dn_moves[d].wait_recv()
        total = total + dn_in[d // 2].astype(f32)
    down_near[...] = total
    kept_back.append(moves.start(down_near, near_hbm))
    for copy in aa_near:
        copy.wait_recv()
    moves.finish(kept_back)
    copies.finish()


def feed_forward(*arrays):
    rows = pltpu.VMEM((TOK, D), bf16)
    return pl.pallas_call(
        mlp_kernel,
        out_shape=[
            jax.ShapeDtypeStruct((TOK, D), f32),
            jax.ShapeDtypeStruct((TOK, HEADS * HD), bf16),
            jax.ShapeDtypeStruct((1, D), f32),
            jax.ShapeDtypeStruct((D // 4, COLUMNS), bf16),
            jax.ShapeDtypeStruct((TOK, D), f32),
            jax.ShapeDtypeStruct((TOK, D), bf16),
            jax.ShapeDtypeStruct((UNITS, D), bf16),
            jax.ShapeDtypeStruct((4, 4, 2, 48, COLUMNS), bf16),
            jax.ShapeDtypeStruct((4, 2, TOK, D), bf16),
        ],
        in_specs=[VMEM] * 3 + [ANY] * 6,
        out_specs=[ANY] * 9,
        scratch_shapes=[
            pltpu.VMEM((UNITS, D), bf16),
            pltpu.VMEM((4, 2, TOK, D), bf16),
            pltpu.VMEM((4, 2, TOK, D), bf16),
            pltpu.VMEM((4, 2 * TOK, UNITS), f32),
            *[pltpu.VMEM((4, 2 * TOK, UNITS), bf16)] * 3,
            *[pltpu.VMEM((4, 2, TOK, D), bf16)] * 2,
            *[pltpu.VMEM((4, TOK, D), bf16)] * 3,
            pltpu.VMEM((3, TOK, D), bf16),
            rows,
            rows,
            pltpu.VMEM((UNITS, D), bf16),
            pltpu.VMEM((3, UNITS, D // 4), bf16),
            *[pltpu.VMEM((D, COLUMNS), bf16)] * 2,
            pltpu.VMEM((UNITS, D), bf16),
            pltpu.VMEM((4, 4, 2, 48, COLUMNS), bf16),
            pltpu.VMEM((4, TOK, D), bf16),
            pltpu.VMEM((2, TOK, D), bf16),
            pltpu.VMEM((HEADS * HD, D), bf16),
            pltpu.VMEM((TOK, D), f32),
            pltpu.VMEM((TOK, HEADS * HD), bf16),
            pltpu.VMEM((1, D), f32),
            pltpu.VMEM((D // 4, COLUMNS), bf16),
            pltpu.VMEM((TOK, D), f32),
            *sems(45),
            pltpu.SemaphoreType.DMA((13,)),
        ],
        compiler_params=params(2),
    )(*arrays)


def back_kernel(*refs):
    lengths, lse, grad_resid, grads_in, gain, mlp_gain_terms = refs[:6]
    x_hbm, rope_hbm, gate_sum, down_far, q_hbm, kv_hbm, exact_hbm, resid_hbm, near_hbm = refs[6:15]
    al_hbm, w_qkv_hbm, act_hbm, up_terms, wd_terms, aa_part = refs[15:21]
    results_hbm = refs[21:29]
    (g, stats, acc, acc_in, dkv, r1a, r1b, ta, tb, r2a, r2b, u, r3, w_qkv, act_all, gbt, gbt_all, al_all) = refs[29:47]
    gp, gp_flat, gp_all, part, part_other, small, e1, e2, e3, f1, f2 = refs[47:58]
    up_own, up_in, up_mid, wd_own, wd_across, wd_sum, wd_in, wd_mid, wd_second = refs[58:67]
    gate_second, up_second = refs[67:69]
    summed, third_in = refs[69:72], refs[72:75]
    q_terms, q_first, q_mid, q_second, q_summed, q_third = refs[75:81]
    down_in, down_part, down_other, q, kv, exact, resid, down_near, o_half, o_core, o_sum, o_in, o_mid, o_across, o_fin, o_third, *refs = refs[81:]
    x, rope, in_grad, layer_out, sum_gate, sum_up, sum_down, sum_qkv, sum_out, small_out, *refs = refs
    send_sems, recv_sems, local_sems = refs

    me = here()
    ids, start = token_rows(me, lengths)
    z, y, xh, c, n = (me[a] for a in AXES)
    partner, across, other = at(me, c=1), at(me, xh=1), at(me, n=1)
    ys = {d: at(me, y=d) for d in (1, 2, 3)}
    zs = {d: at(me, z=d) for d in (1, 2, 3)}
    near_moves = [(d, e) for d in (1, 3, 2, 0) for e in (0, 1) if d or e]
    near = {m: at(me, y=m[0], xh=m[1]) for m in near_moves}
    group = {m: at(me, y=m[0], c=m[1]) for m in near_moves}
    def strip(yi, xi):
        return pl.ds(pl.multiple_of(96 * yi + 48 * xi, 48), 48)

    everyone_in = hail([other, *zs.values(), *near.values(), *(group[m] for m in near_moves if m[1])])
    moves, kept_back = Moves(local_sems), []
    load = moves.start

    def keep_result(k, vmem):
        kept_back.append(moves.start(vmem, results_hbm[k]))

    loads = [load(exact_hbm, exact), load(q_hbm, q), load(kv_hbm, kv)]
    load_resid, load_near = load(resid_hbm, resid), load(near_hbm, down_near)
    load_x, load_rope = load(x_hbm, x), load(rope_hbm, rope)
    load_strip = load(gate_sum.at[strip(y, xh)], gate_second.at[y, xh])
    half = TOK // 2
    low, high = pl.ds(0, half), pl.ds(half, half)
    gbt[...] = grad_resid[...].T.astype(bf16).reshape(4, 4, 96, TOK)
    for h in range(HEADS):
        g[c, pl.ds(h * TOK, TOK), :] = grads_in[:, h * HD : (h + 1) * HD]
    loads[0].wait()
    stats[c, 0:1, :] = lse[...]
    stats[c, 1:2, :] = jnp.sum(g[c].astype(f32).T * exact[...], axis=0, keepdims=True)
    stats[c, 2:8, :] = jnp.zeros((6, NQ), f32)
    everyone_in()
    copies = Copies(send_sems, recv_sems)
    shared = [copies.send(g.at[c], g.at[c], partner), copies.send(stats.at[c], stats.at[c], partner)]

    def z_cols(d):
        return pl.ds(pl.multiple_of(step(me, "z", d) * 384, 384), 384)

    second = {}

    def send_second(i, source, in_ref):
        for m in near_moves:
            second[i, m] = copies.send(
                source(step(me, "y", m[0]), step(me, "xh", m[1])), in_ref.at[y, xh], near[m]
            )

    def send_mid(i, total, mid_ref, in_ref):
        turned = total.T.astype(bf16)
        if turned.shape[1] == UNITS:
            turned = whole_tiles(turned)
        for yi in range(4):
            for xi in range(2):
                rows = 96 * yi + 48 * xi
                mid_ref[yi, xi] = turned[rows : rows + 48]
        send_second(i, lambda yi, xi: mid_ref.at[yi, xi], in_ref)
        in_ref[y, xh] = mid_ref[y, xh]

    keep, give = pl.ds(pl.multiple_of(24 * c, 8), 24), pl.ds(pl.multiple_of(24 * (1 - c), 8), 24)
    third = {}
    all_summed = [*summed, q_summed]
    all_second = [gate_second, up_second, None, q_second]
    all_third = [*third_in, q_third]
    outs = (sum_gate, sum_up, sum_down, sum_qkv)

    def collect(i):
        if i == 2:
            for d in (1, 3, 2):
                second[2, d].wait_recv()
            summed[2][...] = wd_second[...].astype(f32)
        else:
            for m in near_moves:
                second[i, m].wait_recv()
            all_summed[i][...] = all_second[i][:, 0].astype(f32) + all_second[i][:, 1].astype(f32)
        third[i] = copies.send(all_summed[i].at[:, give], all_third[i], partner)

    def deliver(i):
        third[i].wait_recv()
        for yi in range(4):
            mine_sum, their_sum = all_summed[i][yi, keep], all_third[i][yi]
            pair = (jnp.where(c == 0, mine_sum, their_sum), jnp.where(c == 0, their_sum, mine_sum))
            for e in range(2):
                k = 2 * yi + e
                width = UNITS if i < 3 else HD
                outs[i][:, pl.ds(k * width, width)] = pair[e][:, :width]

    send_second(0, lambda yi, xi: gate_sum.at[strip(yi, xi)], gate_second)
    gbt_moves = {
        d: copies.send(gbt.at[:, step(me, "y", d)], gbt_all.at[y], ys[d]) for d in (1, 3, 2)
    }
    gbt_all[y] = gbt[:, y]
    down_move = copies.send(down_far, down_in, ys[2])
    first = {}
    for d in (1, 3, 2):
        first[d] = copies.send(up_terms.at[:, z_cols(d)], up_in.at[d - 1], zs[d])
    wd_move = copies.send(wd_terms.at[:, :, 1 - xh], wd_across, across)

    load_al = load(al_hbm, al_all)
    load_w = load(w_qkv_hbm, w_qkv)
    mine = pl.ds(pl.multiple_of(half * n, half), half)
    theirs = pl.ds(pl.multiple_of(half * (1 - n), half), half)
    load_act = [load(aa_part.at[y], act_all.at[y, c]), load(act_hbm.at[:, 1 - c], act_all.at[:, 1 - c])]
    for d in (1, 2, 3):
        yi = step(me, "y", d)
        load_act.append(load(aa_part.at[yi, mine], act_all.at[yi, c, mine]))
        load_act.append(load(act_hbm.at[yi, c, theirs], act_all.at[yi, c, theirs]))
    load_up = load(up_terms.at[:, z_cols(0)], up_own)
    load_wd = load(wd_terms.at[:, :, xh], wd_own)

    for copy in shared:
        copy.wait_recv()
    for copy in loads[1:]:
        copy.wait()
    acc[...] = jnp.zeros_like(acc)
    last = shard_of(me) // BLOCK_SHARDS

    def of_both(row):
        return jnp.concatenate([stats[0, row : row + 1, :], stats[1, row : row + 1, :]], axis=1)

    log_total, balance = of_both(0), of_both(1)
    earlier = jnp.where(start < last * KEY_BLOCK, log_total, -big_negative)
    keys_here = 2 * TOK

    def block(index, masked, shift):
        zi, yi = index // 4, lax.rem(index, 4)
        keys = kv[zi, yi, :, :, pl.ds(0, HD)].reshape(keys_here, HD)
        values = kv[zi, yi, :, :, pl.ds(HD, HD)].reshape(keys_here, HD)
        keys_t = keys.T
        dk = jnp.zeros((keys_here, HD), f32)
        dv = jnp.zeros((keys_here, HD), f32)
        for chunk in range(2 * NQ // Q_CHUNK):
            core, cs = divmod(chunk * Q_CHUNK, NQ)
            cs = pl.ds(cs, Q_CHUNK)
            piece = slice(chunk * Q_CHUNK, (chunk + 1) * Q_CHUNK)
            qc, gc = q[core, cs, :], g[core, cs, :]
            probs = jnp.exp2(nt(keys, qc) * SCALE_LOG2 - shift[:, piece])
            if masked:
                place = lax.broadcasted_iota(jnp.int32, (keys_here, Q_CHUNK), 0)
                key_ids = index * KEY_BLOCK + c * TOK + place + place // TOK * TOK
                allowed = (key_ids >= start[:, piece]) & (key_ids <= ids[:, piece])
                probs = jnp.where(allowed, probs, 0.0)
            grads = (probs * (nt(values, gc) - balance[:, piece])).astype(bf16)
            dv = dv + nn(probs.astype(bf16), gc)
            dk = dk + nn(grads, qc)
            acc[core, :, cs] = acc[core, :, cs] + nn(keys_t, grads)
        dkv[zi, yi, :, :, pl.ds(0, HD)] = (dk * SCALE).astype(bf16).reshape(2, TOK, HD)
        dkv[zi, yi, :, :, pl.ds(HD, HD)] = dv.astype(bf16).reshape(2, TOK, HD)

    def segment(zi):
        @pl.loop(0, 4)
        def _(yi):
            index = 4 * zi + yi
            edge = (index == 0) | (index == last)

            @pl.when(edge & (index <= last))
            def _():
                block(index, True, jnp.where(index == last, log_total, earlier))

            @pl.when((index < last) & jnp.logical_not(edge))
            def _():
                block(index, False, earlier)

            @pl.when(index > last)
            def _():
                dkv[zi, yi] = jnp.zeros((2, TOK, 2 * HD), bf16)

    first_a, first_b, second_a, second_b = {}, {}, {}, {}

    def settle(d):
        zi = step(me, "z", d)
        if d:
            first_a[d] = copies.send(dkv.at[zi, :, :, low], r1a.at[d - 1], zs[d])
        for e in (1, 3, 2):
            first_b[d, e] = copies.send(
                dkv.at[zi, step(me, "y", e), :, high], r1b.at[e - 1, zi], ys[e]
            )

    segment(step(me, "z", 1))
    settle(1)
    segment(step(me, "z", 2))
    settle(2)
    segment(step(me, "z", 3))
    settle(3)
    load_al.wait()
    for d in (1, 3, 2):
        gbt_moves[d].wait_recv()
    every_al = al_all[...].reshape(4 * TOK, HEADS * HD)
    for zi in range(4):
        lhs = jnp.concatenate([gbt_all[yi, zi] for yi in range(4)], axis=1)
        terms = nn(lhs, every_al).astype(bf16)
        o_half[0, zi] = terms[:, : HEADS * HD // 2]
        o_half[1, zi] = terms[:, HEADS * HD // 2 :]
    o_move = copies.send(o_half.at[1 - c], o_core, partner)
    segment(z)
    settle(0)
    queries_back = copies.send(acc.at[1 - c], acc_in, partner)
    down_move.wait_recv()
    load_near.wait()
    down_part[...] = (down_near[...] + down_in[...].astype(f32)).astype(bf16)
    down_swap = copies.send(down_part, down_other, other)
    for d in (1, 3, 2):
        first_a[d].wait_recv()
    ta[...] = (dkv[z, :, :, low].astype(f32) + three(r1a)).astype(bf16)
    for d in (1, 3, 2):
        second_a[d] = copies.send(ta.at[step(me, "y", d)], r2a.at[d - 1], ys[d])
    for copy in first_b.values():
        copy.wait_recv()
    tb[...] = (dkv[:, y, :, high].astype(f32) + three(r1b)).astype(bf16)
    for d in (1, 3, 2):
        second_b[d] = copies.send(tb.at[step(me, "z", d)], r2b.at[d - 1], zs[d])
    for d in (1, 3, 2):
        second_a[d].wait_recv()
        second_b[d].wait_recv()
    ua = ta[y].astype(f32) + three(r2a)
    ub = tb[z].astype(f32) + three(r2b)
    u[:, low] = ua.astype(bf16)
    u[:, high] = ub.astype(bf16)
    kv_last = copies.send(u.at[1 - xh], r3, across)
    o_move.wait_recv()
    o_sum[...] = (o_half[c].astype(f32) + o_core[...].astype(f32)).astype(bf16)
    o_first = {d: copies.send(o_sum.at[step(me, "z", d)], o_in.at[d - 1], zs[d]) for d in (1, 3, 2)}
    load_wd.wait()
    wd_move.wait_recv()
    for zi in range(4):
        wd_sum[zi] = (wd_own[zi].astype(f32) + wd_across[zi].astype(f32)).astype(bf16)
    wd_first = {d: copies.send(wd_sum.at[step(me, "z", d)], wd_in.at[d - 1], zs[d]) for d in (1, 3, 2)}
    queries_back.wait_recv()
    load_rope.wait()
    load_x.wait()
    turned_back = ((acc[c] + acc_in[...]) * SCALE).T

    def revert(rows):
        return rows * rope[0] - pltpu.roll(rows, HD // 2, 1) * rope[1]

    def keep_head(h, rows):
        low_rows = rows.astype(bf16)
        gp[h] = low_rows
        gp_flat[:, pl.ds(h * HD, HD)] = low_rows
        small[pl.ds(24 + h, 1), :] = jnp.sum(low_rows.astype(f32), axis=0, keepdims=True)

    def to_small(first_row, row):
        for k in range(D // 128):
            small[pl.ds(first_row + k, 1), :] = row[:, k * 128 : (k + 1) * 128]

    small[...] = jnp.zeros_like(small)
    to_small(12, mlp_gain_terms[...])
    for h in range(HEADS):
        keep_head(h, revert(turned_back[h * TOK : (h + 1) * TOK]))
    load_w.wait()
    front = HEADS * HD
    partial = nt(gp_flat[:, pl.ds(0, front)], w_qkv[:, pl.ds(0, front)])

    kv_last.wait_recv()
    grad_kv = u[xh].astype(f32) + r3[...].astype(f32)
    keep_head(HEADS, revert(grad_kv[:, :HD]))
    keep_head(HEADS + 1, grad_kv[:, HD:])
    gp_moves = [
        copies.send(gp.at[step(me, "y", m[0]) * 2 + step(me, "c", m[1])], gp_all.at[y, c], group[m])
        for m in near_moves
    ]
    gp_all[y, c] = gp[y * 2 + c]
    back = pl.ds(front, 2 * HD)
    part[...] = (partial + nt(gp_flat[:, back], w_qkv[:, back])).astype(bf16)
    swap = copies.send(part, part_other, other)
    load_up.wait()
    for d in (1, 3, 2):
        first[d].wait_recv()
    send_mid(1, up_own[...].astype(f32) + three(up_in), up_mid, up_second)
    load_strip.wait()
    collect(0)
    for copy in load_act:
        copy.wait()
    for copy in gp_moves:
        copy.wait_recv()
    q_terms[...] = tn(
        gp_all[...].reshape(GROUP * TOK, HD), act_all[...].reshape(GROUP * TOK, D)
    ).astype(bf16)

    q_one = {d: copies.send(q_terms.at[:, z_cols(d)], q_first.at[d - 1], zs[d]) for d in (1, 3, 2)}
    for d in (1, 3, 2):
        o_first[d].wait_recv()
    o_total = (o_sum[z].astype(f32) + three(o_in)).astype(bf16)
    o_mid[0], o_mid[1] = o_total[:48], o_total[48:]
    o_last = copies.send(o_mid.at[1 - xh], o_across, across)
    down_swap.wait_recv()
    load_resid.wait()
    layer_out[...] = (
        resid[...] + (down_part[...].astype(f32) + down_other[...].astype(f32))
    ).astype(bf16)
    keep_result(1, layer_out)
    deliver(0)
    keep_result(2, sum_gate)
    swap.wait_recv()
    grad_act = part[...].astype(f32) + part_other[...].astype(f32)
    rows = x[...].astype(f32)
    inverse = lax.rsqrt(jnp.mean(rows * rows, axis=-1, keepdims=True) + rms_eps)
    normed = rows * inverse
    to_small(0, jnp.sum(grad_act * normed, axis=0, keepdims=True))
    small_one = {d: copies.send(small, e1.at[d - 1], zs[d]) for d in (1, 3, 2)}
    grad_normed = grad_act * gain[...].reshape(1, D)
    inner = jnp.mean(grad_normed * normed, axis=-1, keepdims=True)
    in_grad[...] = (grad_resid[...] + inverse * (grad_normed - normed * inner)).astype(bf16)

    keep_result(0, in_grad)
    for d in (1, 3, 2):
        wd_first[d].wait_recv()
    wd_mid[...] = (wd_sum[z].astype(f32) + three(wd_in)).astype(bf16)
    for d in (1, 3, 2):
        second[2, d] = copies.send(wd_mid.at[step(me, "y", d)], wd_second.at[y], ys[d])
    wd_second[y] = wd_mid[y]
    for d in (1, 3, 2):
        q_one[d].wait_recv()
    send_mid(3, q_terms[:, z_cols(0)].astype(f32) + three(q_first), q_mid, q_second)
    for d in (1, 3, 2):
        small_one[d].wait_recv()
    f1[...] = small[...] + three(e1)
    small_two = {m: copies.send(f1, e2.at[k], near[m]) for k, m in enumerate(near_moves)}
    o_last.wait_recv()
    o_fin[...] = o_mid[xh].astype(f32) + o_across[...].astype(f32)
    o_end = copies.send(o_fin.at[give], o_third, partner)
    collect(1)
    deliver(1)
    keep_result(3, sum_up)
    collect(2)
    collect(3)
    for m in near_moves:
        small_two[m].wait_recv()
    f2[...] = f1[...]
    for k in range(len(near_moves)):
        f2[...] = f2[...] + e2[k]
    small_three = copies.send(f2, e3, partner)
    deliver(2)
    keep_result(4, sum_down)
    deliver(3)
    keep_result(5, sum_qkv)
    o_end.wait_recv()
    o_mine, o_theirs = o_fin[keep], o_third[...]
    sum_out[:, : HEADS * HD // 2] = jnp.where(c == 0, o_mine, o_theirs)
    sum_out[:, HEADS * HD // 2 :] = jnp.where(c == 0, o_theirs, o_mine)
    keep_result(6, sum_out)
    small_three.wait_recv()
    small_out[...] = f2[...] + e3[...]
    keep_result(7, small_out)
    moves.finish(kept_back)
    copies.finish()


def back(*arrays):
    half = TOK // 2
    wide = 2 * HD
    results_of = [
        jax.ShapeDtypeStruct((TOK, D), bf16),
        jax.ShapeDtypeStruct((TOK, D), bf16),
        *[jax.ShapeDtypeStruct((24, FF // 2), f32)] * 3,
        jax.ShapeDtypeStruct((24, (HEADS + 2) * HD), f32),
        jax.ShapeDtypeStruct((24, HEADS * HD), f32),
        jax.ShapeDtypeStruct((40, 128), f32),
    ]
    return pl.pallas_call(
        back_kernel,
        out_shape=results_of,
        in_specs=[SMEM] + [VMEM] * 5 + [ANY] * 15,
        out_specs=[ANY] * 8,
        scratch_shapes=[
            pltpu.VMEM((2, NQ, HD), bf16),
            pltpu.VMEM((2, 8, NQ), f32),
            pltpu.VMEM((2, HD, NQ), f32),
            pltpu.VMEM((HD, NQ), f32),
            pltpu.VMEM((4, 4, 2, TOK, wide), bf16),
            pltpu.VMEM((3, 4, 2, half, wide), bf16),
            pltpu.VMEM((3, 4, 2, half, wide), bf16),
            pltpu.VMEM((4, 2, half, wide), bf16),
            pltpu.VMEM((4, 2, half, wide), bf16),
            pltpu.VMEM((3, 2, half, wide), bf16),
            pltpu.VMEM((3, 2, half, wide), bf16),
            pltpu.VMEM((2, TOK, wide), bf16),
            pltpu.VMEM((TOK, wide), bf16),
            pltpu.VMEM((D, (HEADS + 2) * HD), bf16),
            pltpu.VMEM((4, 2, TOK, D), bf16),
            pltpu.VMEM((4, 4, 96, TOK), bf16),
            pltpu.VMEM((4, 4, 96, TOK), bf16),
            pltpu.VMEM((4, TOK, HEADS * HD), bf16),
            pltpu.VMEM((HEADS + 2, TOK, HD), bf16),
            pltpu.VMEM((TOK, (HEADS + 2) * HD), bf16),
            pltpu.VMEM((4, 2, TOK, HD), bf16),
            pltpu.VMEM((TOK, D), bf16),
            pltpu.VMEM((TOK, D), bf16),
            pltpu.VMEM((40, 128), f32),
            pltpu.VMEM((3, 40, 128), f32),
            pltpu.VMEM((7, 40, 128), f32),
            pltpu.VMEM((40, 128), f32),
            pltpu.VMEM((40, 128), f32),
            pltpu.VMEM((40, 128), f32),
            pltpu.VMEM((UNITS, 384), bf16),
            pltpu.VMEM((3, UNITS, 384), bf16),
            pltpu.VMEM((4, 2, 48, COLUMNS), bf16),
            *[pltpu.VMEM((4, 4, 48, COLUMNS), bf16)] * 3,
            pltpu.VMEM((3, 4, 48, COLUMNS), bf16),
            *[pltpu.VMEM((4, 48, COLUMNS), bf16)] * 2,
            *[pltpu.VMEM((4, 2, 48, COLUMNS), bf16)] * 2,
            *[pltpu.VMEM((4, 48, COLUMNS), f32)] * 3,
            *[pltpu.VMEM((4, 24, COLUMNS), f32)] * 3,
            pltpu.VMEM((HD, D), bf16),
            pltpu.VMEM((3, HD, 384), bf16),
            pltpu.VMEM((4, 2, 48, HD), bf16),
            pltpu.VMEM((4, 2, 48, HD), bf16),
            pltpu.VMEM((4, 48, HD), f32),
            pltpu.VMEM((4, 24, HD), f32),
            pltpu.VMEM((TOK, D), bf16),
            pltpu.VMEM((TOK, D), bf16),
            pltpu.VMEM((TOK, D), bf16),
            pltpu.VMEM((2, NQ, HD), bf16),
            pltpu.VMEM((4, 4, 2, TOK, wide), bf16),
            pltpu.VMEM((HD, NQ), f32),
            pltpu.VMEM((TOK, D), f32),
            pltpu.VMEM((TOK, D), f32),
            pltpu.VMEM((2, 4, 96, HEADS * HD // 2), bf16),
            *[pltpu.VMEM((4, 96, HEADS * HD // 2), bf16)] * 2,
            pltpu.VMEM((3, 96, HEADS * HD // 2), bf16),
            pltpu.VMEM((2, 48, HEADS * HD // 2), bf16),
            pltpu.VMEM((48, HEADS * HD // 2), bf16),
            pltpu.VMEM((48, HEADS * HD // 2), f32),
            pltpu.VMEM((24, HEADS * HD // 2), f32),
            pltpu.VMEM((TOK, D), bf16),
            pltpu.VMEM((2, TOK, HD), f32),
            *[pltpu.VMEM(a.shape, a.dtype) for a in results_of],
            *sems(93),
            pltpu.SemaphoreType.DMA((28,)),
        ],
        compiler_params=params(9, 62),
    )(*arrays)


def results_kernel(*refs):
    wholes, small, copied = refs[:7], refs[7], refs[8:15]
    small_outs, (norm_attn, norm_mlp, bias, value_bias) = refs[15:19], refs[19:23]
    *held, into, out_of = refs[23:]
    shard = shard_of(here())
    loads, stores = Moves(into), Moves(out_of)
    for a, b in zip(wholes, held):
        loads.start(a, b)
    rows = jnp.concatenate(
        [
            jnp.concatenate([small[12 * i + k : 12 * i + k + 1, :] for k in range(12)], axis=1)
            for i in range(2)
        ],
        axis=0,
    )
    turned = pltpu.roll(rows, lax.rem(D - 24 * shard, D), 1)
    norm_attn[...] = turned[0:1, :24]
    norm_mlp[...] = turned[1:2, :24]
    heads = pltpu.roll(small[24 : 24 + HEADS + 2, :], lax.rem(HD - 2 * shard, HD), 1)
    bias[0] = heads[: HEADS + 1, :2].T
    value_bias[...] = heads[HEADS + 1 :, :2]
    for a, b in zip(refs[19:23], small_outs):
        stores.start(a, b)
    for load, a, b in zip(loads.started, held, copied):
        load.wait()
        stores.start(a, b)
    stores.finish(stores.started)


def results(*arrays):
    *wholes, small = arrays
    small_ones = [
        jax.ShapeDtypeStruct((1, 24), f32),
        jax.ShapeDtypeStruct((1, 24), f32),
        jax.ShapeDtypeStruct((1, 2, HEADS + 1), f32),
        jax.ShapeDtypeStruct((1, 2), f32),
    ]
    return pl.pallas_call(
        results_kernel,
        out_shape=[*[jax.ShapeDtypeStruct(a.shape, a.dtype) for a in wholes], *small_ones],
        in_specs=[ANY] * 7 + [VMEM],
        out_specs=[ANY] * 11,
        scratch_shapes=[
            *[pltpu.VMEM(a.shape, a.dtype) for a in (*small_ones, *wholes)],
            pltpu.SemaphoreType.DMA((7,)),
            pltpu.SemaphoreType.DMA((11,)),
        ],
    )(*wholes, small)


def shards(
    layer_in, lengths, norm_attn, w_qkv, qkv_bias, w_out, norm_mlp, w_gate, w_up, w_down, out_grad
):
    half = HD // 2
    freqs = np.float32(rope_base) ** (-2.0 * np.arange(half, dtype=np.float32) / HD)
    freqs = np.concatenate([freqs, freqs]).astype(np.float32)[None]
    kv, queries, act_part, resid, exact, lse, rope, gate_w, up_w, out_grad_all, low_all = attend(
        lengths, layer_in, norm_attn, qkv_bias, freqs, out_grad, w_qkv, w_out, w_gate, w_up
    )
    (
        grad_resid, grads, gain_terms, gate_sum, down_near, down_far,
        up_terms, down_terms, act_attn_all,
    ) = feed_forward(
        resid, norm_mlp, out_grad, w_out, out_grad_all, gate_w, up_w, w_down, act_part
    )
    sums = back(
        lengths, lse, grad_resid, grads, norm_attn, gain_terms, layer_in, rope, gate_sum, down_far,
        queries, kv, exact, resid, down_near, low_all, w_qkv, act_attn_all, up_terms, down_terms,
        act_part,
    )
    in_grad, layer_out, sum_gate, sum_up, sum_down, sum_qkv, sum_out, *rest = results(*sums)
    sum_norm_attn, sum_norm_mlp, bias, value_bias = rest
    return (
        layer_out,
        in_grad,
        sum_norm_attn[0],
        sum_qkv,
        bias.swapaxes(1, 2),
        value_bias,
        sum_out.T,
        sum_norm_mlp[0],
        sum_gate,
        sum_up,
        sum_down.T,
    )


def solution(mesh):
    torus = Mesh(mesh.devices.reshape(4, 4, 2, 2, 2), AXES)
    in_specs = (
        P(WIDE, None),
        P(),
        P(),
        P(None, "n"),
        P("n", None),
        P("n", None),
        P(),
        P(None, "n"),
        P(None, "n"),
        P("n", None),
        P(WIDE, None),
    )
    out_specs = (
        P(WIDE, None),
        P(WIDE, None),
        P(WIDE),
        P(WIDE, "n"),
        P("n", None, WIDE),
        P("n", WIDE),
        P("n", WIDE),
        P(WIDE),
        P(WIDE, "n"),
        P(WIDE, "n"),
        P("n", WIDE),
    )
    return jax.shard_map(
        shards, mesh=torus, in_specs=in_specs, out_specs=out_specs, check_vma=False
    )
```
